128 devices in a mesh: section: 2 (over z_lo), fsdp: 8 (over y, core), replica: 8 (over x, z_hi).
Axes of the slice: x: 4, y: 4, z: 4 (z_hi: 2, z_lo: 2; z = z_hi * 2 + z_lo), core: 2. Of those that a mesh axis runs over, the one named last changes fastest.
Arguments:
- inputs: bfloat16 [2, 8, 512, 1088], P(None, 'replica', 'fsdp'), may hold values from -6 to 6
- cotangent: bfloat16 [2, 8, 512, 1088], P(None, 'replica', 'fsdp'), may hold values from -6 to 6
- weight_attn: bfloat16 [2, 1088, 3264], P('section', 'fsdp'), may hold values from -0.1875 to 0.1875
- weight_out: bfloat16 [2, 1088, 1088], P('section', 'fsdp'), may hold values from -1.5 to 1.5
- weight_up: bfloat16 [2, 1088, 4352], P('section', 'fsdp'), may hold values from -0.1875 to 0.1875
- weight_down: bfloat16 [2, 4352, 1088], P('section', 'fsdp'), may hold values from -0.09375 to 0.09375
- bias_attn: bfloat16 [2, 2176], P('section', 'fsdp'), may hold values from -3 to 3
- bias_out: bfloat16 [2, 1088], P('section', 'fsdp'), may hold values from -2 to 2
- bias_up: bfloat16 [2, 4352], P('section', 'fsdp'), may hold values from -3 to 3
- bias_down: bfloat16 [2, 1088], P('section', 'fsdp'), may hold values from -2 to 2
- norm_gain: bfloat16 [2, 2, 1088], P('section', None, 'fsdp'), may hold values from 0.5 to 1.5
- norm_bias: bfloat16 [2, 2, 1088], P('section', None, 'fsdp'), may hold values from -1.5 to 1.5
Outputs:
- acts: bfloat16 [2, 2, 8, 512, 1088], P('section', None, 'replica', 'fsdp')
- in_grads: bfloat16 [2, 2, 8, 512, 1088], P('section', None, 'replica', 'fsdp')
- grad_attn: float32 [2, 1088, 3264], P('section', 'fsdp')
- grad_out: float32 [2, 1088, 1088], P('section', 'fsdp')
- grad_up: float32 [2, 1088, 4352], P('section', 'fsdp')
- grad_down: float32 [2, 4352, 1088], P('section', 'fsdp')
- grad_bias_attn: float32 [2, 2176], P('section', 'fsdp')
- grad_bias_out: float32 [2, 1088], P('section', 'fsdp')
- grad_bias_up: float32 [2, 4352], P('section', 'fsdp')
- grad_bias_down: float32 [2, 1088], P('section', 'fsdp')
- grad_gain: float32 [2, 2, 1088], P('section', None, 'fsdp')
- grad_shift: float32 [2, 2, 1088], P('section', None, 'fsdp')
The draws below stay inside these ranges and needn't reach their ends.
All inputs are finite; a program needn't handle non-finite values.
Results may differ from the reference program's by a relative error of at most 0.02.
Values may be sent and summed in bfloat16 or wider, within the bound.
A program may use at most 192 MiB of HBM per device.

```python
import jax
import jax.numpy as jnp
from jax import lax

D = 1088
FF = 4352
HEADS = 17
HEAD_DIM = 64
MICRO = 2
LENGTH = 512
SEQS = 8


def level_of(key, dims, cuts, smallest, top_value):
    level = 1.0
    for dim, shards_of in cuts:
        heights = jax.random.uniform(jax.random.fold_in(jax.random.fold_in(key, 6), dim), (shards_of,), jnp.float32, smallest / len(cuts), top_value / len(cuts))
        level = level * jnp.repeat(jnp.exp(heights), dims[dim] // shards_of).reshape((-1,) + (1,) * (len(dims) - 1 - dim))
    return level


def centred(key, dims, width, limit, cuts=(), kind=jnp.bfloat16):
    entries = width * jax.random.normal(key, dims, jnp.float32)
    if cuts:
        entries = entries * level_of(key, dims, cuts, -0.22, 0.18)
    return jnp.clip(entries, -limit, limit).astype(kind)


def setup_inputs(seed: int = 0) -> dict:
    splits = jax.random.split(jax.random.key(seed), 13)
    return {
        "inputs": centred(splits[0], (MICRO, SEQS, LENGTH, D), 1.0, 6.0, ((1, 8), (2, 8))),
        "cotangent": centred(splits[1], (MICRO, SEQS, LENGTH, D), 1.0, 6.0, ((1, 8), (2, 8))),
        "weight_attn": centred(splits[2], (2, D, 3 * D), D ** -0.5, 0.1875, ((0, 2), (1, 8))),
        "weight_out": centred(splits[3], (2, D, D), (D // 64) ** -0.5, 1.5, ((0, 2), (1, 8))),
        "weight_up": centred(splits[4], (2, D, FF), D ** -0.5, 0.1875, ((0, 2), (1, 8))),
        "weight_down": centred(splits[5], (2, FF, D), FF ** -0.5, 0.09375, ((0, 2), (1, 8))),
        "bias_attn": centred(splits[6], (2, 2 * D), 0.5, 3.0, ((0, 2), (1, 8))),
        "bias_out": centred(splits[7], (2, D), 0.3, 2.0, ((0, 2), (1, 8))),
        "bias_up": centred(splits[8], (2, FF), 0.5, 3.0, ((0, 2), (1, 8))),
        "bias_down": centred(splits[9], (2, D), 0.3, 2.0, ((0, 2), (1, 8))),
        "norm_gain": jnp.clip(1.0 + 0.1 * jax.random.normal(splits[10], (2, 2, D), jnp.float32), 0.5, 1.5).astype(jnp.bfloat16),
        "norm_bias": centred(splits[11], (2, 2, D), 0.2, 1.5, ((0, 2), (2, 8))),
    }


@jax.custom_vjp
def low(v):
    return lax.optimization_barrier(v.astype(jnp.bfloat16)).astype(jnp.float32)

@jax.custom_vjp
def low_back(v):
    return v

def low_keep(v):
    return (low(v), None)

def low_pass(kept, grad):
    return (grad,)

def back_keep(v):
    return (v, None)

def back_low(kept, grad):
    return (low(grad),)
low.defvjp(low_keep, low_pass)
low_back.defvjp(back_keep, back_low)

def norm_rows(values, gain_row, shift_row):
    centre = values - lax.optimization_barrier(jnp.mean(values, axis=-1, keepdims=True))
    spread = lax.optimization_barrier(jnp.mean(centre * centre, axis=-1, keepdims=True))
    return centre * lax.rsqrt(spread + 1e-05) * gain_row + shift_row

def linear(left_side, right_side):
    return jnp.einsum('bti,ij->btj', left_side, right_side, precision=lax.Precision.HIGHEST)

def layer(stream, params):
    weight_attn, weight_out, weight_up, weight_down, bias_attn, bias_out, bias_up, bias_down, gains_all, shifts_all = params
    batch_size = stream.shape[0]
    normed = low(norm_rows(stream, gains_all[0], shifts_all[0]))
    bias_full = jnp.concatenate([bias_attn[:D], jnp.zeros((D,), jnp.float32), bias_attn[D:]])
    joined = low_back(low(linear(normed, weight_attn) + bias_full))
    queries = joined[:, :, :D].reshape(batch_size, LENGTH, HEADS, HEAD_DIM)
    keys_all = joined[:, :, D:2 * D].reshape(batch_size, LENGTH, HEADS, HEAD_DIM)
    values = joined[:, :, 2 * D:].reshape(batch_size, LENGTH, HEADS, HEAD_DIM)
    scores = low_back(jnp.einsum('bqhd,bkhd->bhqk', queries, keys_all, precision=lax.Precision.HIGHEST) * HEAD_DIM ** (-0.5))
    places = jnp.arange(LENGTH)
    causal = places[:, None] >= places[None, :]
    masked = jnp.where(causal, scores, -1e+30)
    attention = low(jax.nn.softmax(masked, axis=-1))
    attended = jnp.einsum('bhqk,bkhd->bqhd', attention, values, precision=lax.Precision.HIGHEST)
    attended = low_back(low(attended.reshape(batch_size, LENGTH, D)))
    middle = stream + low_back(linear(attended, weight_out) + bias_out)
    normed_two = low(norm_rows(middle, gains_all[1], shifts_all[1]))
    hidden_pre = low_back(linear(normed_two, weight_up) + bias_up)
    active = low(jax.nn.gelu(hidden_pre, approximate=True))
    return middle + low_back(linear(active, weight_down) + bias_down)

def reference(inputs, cotangent, weight_attn, weight_out, weight_up, weight_down, bias_attn, bias_out, bias_up, bias_down, norm_gain, norm_bias):
    params = tuple((array_one.astype(jnp.float32) for array_one in (weight_attn, weight_out, weight_up, weight_down, bias_attn, bias_out, bias_up, bias_down, norm_gain, norm_bias)))
    first_layer = tuple((array_one[0] for array_one in params))
    second = tuple((array_one[1] for array_one in params))
    stream = inputs.astype(jnp.float32)
    nudge_zero = jnp.zeros(stream.shape, jnp.float32)

    def two_layers(stream, first_layer, second, nudge_zero):

        def one_block(unused_carry, block_pair):
            block_in, block_nudge = block_pair
            hidden = low_back(low(layer(block_in, first_layer)) + block_nudge)
            return (unused_carry, (layer(hidden, second), hidden))
        unused_carry, (result, hidden) = lax.scan(jax.checkpoint(one_block), jnp.zeros((), jnp.float32), (stream, nudge_zero))
        return (result, hidden)
    result, pullback, hidden = jax.vjp(two_layers, stream, first_layer, second, nudge_zero, has_aux=True)
    grad_stream, grad_first, grad_second, grad_nudge = pullback(cotangent.astype(jnp.float32))
    acts = jnp.stack([hidden, result]).astype(jnp.bfloat16)
    in_grads = jnp.stack([grad_stream, grad_nudge]).astype(jnp.bfloat16)
    stacked = [jnp.stack([array_one, array_two]) for array_one, array_two in zip(grad_first, grad_second)]
    return (acts, in_grads, stacked[0], stacked[1], stacked[2], stacked[3], stacked[4], stacked[5], stacked[6], stacked[7], stacked[8], stacked[9])
```

```python
import functools

import jax
import jax.numpy as jnp
from jax import lax
from jax.experimental import pallas as pl
from jax.experimental.pallas import tpu as pltpu
from jax.sharding import PartitionSpec as P

D = 1088
FF = 4352
HEADS = 17
HD = 64
BLK = 64
CHIPS = 4
ROWS = BLK * CHIPS
SLOTS = 5
TH = SLOTS * HD
TQKV = 3 * TH
SCALE = HD**-0.5
EPS = 1e-5
MESH = pl.DeviceIdType.MESH
BF = jnp.bfloat16
F32 = jnp.float32
ANY = pl.BlockSpec(memory_space=pl.ANY)
VMEM = pl.BlockSpec(memory_space=pltpu.VMEM)
DMA = pltpu.SemaphoreType.DMA
LIMIT = 56 * 1024 * 1024


def dot(a, b):
    return lax.dot_general(a, b, (((1,), (0,)), ((), ())), preferred_element_type=F32)


def dot_nt(a, b):
    return lax.dot_general(a, b, (((1,), (1,)), ((), ())), preferred_element_type=F32)


def dot_tn(a, b):
    return lax.dot_general(a, b, (((0,), (0,)), ((), ())), preferred_element_type=F32)


def chunks(n, size=256):
    return [(i, min(size, n - i)) for i in range(0, n, size)]


def place():
    f = lax.axis_index("fsdp")
    return f // 2, f % 2


def ring(y, k):
    return lax.rem(y + k, CHIPS)


def at_chip(y, c):
    return {"fsdp": 2 * y + c}


def greet(targets):
    barrier = pltpu.get_barrier_semaphore()
    for target in targets:
        pl.semaphore_signal(barrier, inc=1, device_id=target, device_id_type=MESH)
    return functools.partial(pl.semaphore_wait, barrier, len(targets))


def remote(src, dst, send, recv, target):
    return pltpu.make_async_remote_copy(
        src_ref=src, dst_ref=dst, send_sem=send, recv_sem=recv, device_id=target, device_id_type=MESH
    )


def slot(ref, y):
    return ref.at[pl.ds(pl.multiple_of(y * BLK, BLK), BLK)]


ORDER = (2, 1, 3)


def gather_start(full, y, c, send, recv):
    for k in ORDER:
        remote(slot(full, y), slot(full, y), send.at[k - 1], recv.at[k - 1], at_chip(ring(y, k), c)).start()


def gather_wait(full, y, c, send, recv):
    for k in (1, 3, 2):
        source = ring(y, 4 - k)
        remote(slot(full, source), slot(full, source), send.at[k - 1], recv.at[k - 1], at_chip(ring(y, k), c)).wait()


def scatter_start(acc, out_buf, in_buf, y, c, send, recv):
    for k in ORDER:
        target = ring(y, k)
        out_buf[k - 1] = slot(acc, target)[...].astype(BF)
        remote(out_buf.at[k - 1], in_buf.at[k - 1], send.at[k - 1], recv.at[k - 1], at_chip(target, c)).start()


def scatter_wait(acc, out_buf, in_buf, y, c, send, recv):
    total = slot(acc, y)[...]
    for k in (1, 3, 2):
        remote(out_buf.at[k - 1], in_buf.at[k - 1], send.at[k - 1], recv.at[k - 1], at_chip(ring(y, k), c)).wait()
        total = total + in_buf[k - 1].astype(F32)
    return total


def stats(v):
    centre = v - jnp.mean(v, axis=-1, keepdims=True)
    scale = lax.rsqrt(jnp.mean(centre * centre, axis=-1, keepdims=True) + EPS)
    return centre * scale, scale


def norm(v, gain, shift):
    return stats(v)[0] * gain + shift


def norm_back(d, v, gain):
    vh, scale = stats(v)
    q = d * gain
    grad = scale * (q - jnp.mean(q, axis=-1, keepdims=True) - vh * jnp.mean(q * vh, axis=-1, keepdims=True))
    return grad, jnp.sum(d * vh, axis=0, keepdims=True), jnp.sum(d, axis=0, keepdims=True)


GELU_A = 0.7978845608028654
GELU_B = 0.044715


def gelu(h):
    return 0.5 * h * (1.0 + jnp.tanh(GELU_A * (h + GELU_B * h * h * h)))


def gelu_slope(h):
    t = jnp.tanh(GELU_A * (h + GELU_B * h * h * h))
    return 0.5 * (1.0 + t) + 0.5 * h * (1.0 - t * t) * (GELU_A * (1.0 + 3.0 * GELU_B * h * h))


def masks(c):
    row = lax.broadcasted_iota(jnp.int32, (ROWS, ROWS), 0)
    col = lax.broadcasted_iota(jnp.int32, (ROWS, ROWS), 1)
    own = row >= col
    other = (row // BLK) >= (col // BLK) + (1 - c)
    return own, other


def load(pairs, sems):
    copies = [pltpu.make_async_copy(src, dst, sems.at[i]) for i, (src, dst) in enumerate(pairs)]
    for copy in copies:
        copy.start()
    return copies


def attend_forward(x, w_hbm, wo_hbm, vecs, bias, middle, normed, queries, kv, kv_other, logsum, attended,
                   w, wo, acc, out_buf, in_buf, ls, gs, gr, ss, sr, ks, kr):
    y, c = place()
    peers = [at_chip(ring(y, k), c) for k in (1, 2, 3)]
    sibling = at_chip(y, 1 - c)
    arrived = greet(peers + [sibling])
    weights = load([(w_hbm, w), (wo_hbm, wo)], ls)
    slot(normed, y)[...] = norm(x[...], vecs[0:1], vecs[1:2]).astype(BF)
    arrived()
    gather_start(normed, y, c, gs, gr)
    own, other = masks(c)
    weights[0].wait()
    gather_wait(normed, y, c, gs, gr)
    rows = normed[...]
    for at, size in chunks(2 * TH):
        kv[:, at : at + size] = (dot(rows, w[:, at : at + size]) + bias[0:1, at : at + size]).astype(BF)
    swap = remote(kv, kv_other, ks, kr, sibling)
    swap.start()
    queries[...] = (dot(rows, w[:, 2 * TH :]) + bias[0:1, 2 * TH :]).astype(BF)
    swap.wait()
    for h in range(SLOTS):
        at = h * HD
        q = queries[:, at : at + HD]
        s_own = jnp.where(own, dot_nt(q, kv[:, at : at + HD]) * SCALE, -1e30)
        s_other = jnp.where(other, dot_nt(q, kv_other[:, at : at + HD]) * SCALE, -1e30)
        top = jnp.maximum(jnp.max(s_own, axis=-1, keepdims=True), jnp.max(s_other, axis=-1, keepdims=True))
        e_own = jnp.exp(s_own - top)
        e_other = jnp.exp(s_other - top)
        total = jnp.sum(e_own, axis=-1, keepdims=True) + jnp.sum(e_other, axis=-1, keepdims=True)
        logsum[:, h : h + 1] = top + jnp.log(total)
        inverse = 1.0 / total
        a_own = (e_own * inverse).astype(BF)
        a_other = (e_other * inverse).astype(BF)
        out = dot(a_own, kv[:, TH + at : TH + at + HD]) + dot(a_other, kv_other[:, TH + at : TH + at + HD])
        attended[:, at : at + HD] = out.astype(BF)
    weights[1].wait()
    mixed = attended[...]
    for at, size in chunks(D):
        acc[:, at : at + size] = dot(mixed, wo[:, at : at + size])
    scatter_start(acc, out_buf, in_buf, y, c, ss, sr)
    base = x[...] + vecs[4:5]
    middle[...] = base + scatter_wait(acc, out_buf, in_buf, y, c, ss, sr)


def feed_forward(middle, wu_hbm, wd_hbm, vecs, result, normed, hidden, active,
                 wu, wd, acc, out_buf, in_buf, ls, gs, gr, ss, sr):
    y, c = place()
    arrived = greet([at_chip(ring(y, k), c) for k in (1, 2, 3)])
    weights = load([(wu_hbm, wu), (wd_hbm, wd)], ls)
    slot(normed, y)[...] = norm(middle[...], vecs[2:3], vecs[3:4]).astype(BF)
    arrived()
    gather_start(normed, y, c, gs, gr)
    weights[0].wait()
    gather_wait(normed, y, c, gs, gr)
    rows = normed[...]
    for at, size in chunks(D):
        h = dot(rows, wu[:, at : at + size]) + vecs[6:7, at : at + size]
        hidden[:, at : at + size] = h
        active[:, at : at + size] = gelu(h).astype(BF)
    weights[1].wait()
    rows = active[...]
    for at, size in chunks(D):
        acc[:, at : at + size] = dot(rows, wd[:, at : at + size])
    scatter_start(acc, out_buf, in_buf, y, c, ss, sr)
    base = middle[...] + vecs[5:6]
    result[...] = base + scatter_wait(acc, out_buf, in_buf, y, c, ss, sr)


def feed_back(grad, wu_hbm, wd_hbm, vecs, middle, normed, hidden, active, grad_middle, grad_up, grad_down, small,
              wu, wd, full, gh, acc, out_buf, in_buf, ls, gs, gr, ss, sr):
    y, c = place()
    arrived = greet([at_chip(ring(y, k), c) for k in (1, 2, 3)])
    weights = load([(wu_hbm, wu), (wd_hbm, wd)], ls)
    own_rows = grad[...].astype(BF)
    slot(full, y)[...] = own_rows
    arrived()
    gather_start(full, y, c, gs, gr)
    small[...] = jnp.zeros_like(small)
    small[3:4] = jnp.sum(own_rows.astype(F32), axis=0, keepdims=True)
    weights[1].wait()
    gather_wait(full, y, c, gs, gr)
    rows = full[...]
    for at, size in chunks(D):
        slope = gelu_slope(hidden[:, at : at + size])
        part = (dot_nt(rows, wd[at : at + size, :]) * slope).astype(BF)
        gh[:, at : at + size] = part
        small[2:3, at : at + size] = jnp.sum(part.astype(F32), axis=0, keepdims=True)
    weights[0].wait()
    rows = gh[...]
    for at, size in chunks(D):
        acc[:, at : at + size] = dot_nt(rows, wu[at : at + size, :])
    scatter_start(acc, out_buf, in_buf, y, c, ss, sr)
    for at, size in chunks(D):
        grad_up[at : at + size, :] = dot_tn(normed[:, at : at + size], gh[...]).astype(BF)
        grad_down[at : at + size, :] = dot_tn(active[:, at : at + size], full[...]).astype(BF)
    d = scatter_wait(acc, out_buf, in_buf, y, c, ss, sr)
    back, gain, shift = norm_back(d, middle[...], vecs[2:3])
    small[0:1] = gain
    small[1:2] = shift
    grad_middle[...] = grad[...] + back


def attend_back(grad, w_hbm, wo_hbm, vecs, x, normed, queries, kv, kv_other, logsum, attended,
                grad_x, grad_attn, grad_out, small, small_bias,
                w, wo, full, ga, gj, part_out, part_in, part_own, acc, out_buf, in_buf, ls, gs, gr, ss, sr, ks, kr):
    y, c = place()
    peers = [at_chip(ring(y, k), c) for k in (1, 2, 3)]
    sibling = at_chip(y, 1 - c)
    arrived = greet(peers + [sibling])
    weights = load([(w_hbm, w), (wo_hbm, wo)], ls)
    own_rows = grad[...].astype(BF)
    slot(full, y)[...] = own_rows
    arrived()
    gather_start(full, y, c, gs, gr)
    small[...] = jnp.zeros_like(small)
    small[2:3] = jnp.sum(own_rows.astype(F32), axis=0, keepdims=True)
    own, other = masks(c)
    weights[1].wait()
    gather_wait(full, y, c, gs, gr)
    ga[...] = dot_nt(full[...], wo[...]).astype(BF)
    for h in range(SLOTS):
        at = h * HD
        q = queries[:, at : at + HD]
        g = ga[:, at : at + HD]
        lse = logsum[:, h : h + 1]
        k_own, k_other = kv[:, at : at + HD], kv_other[:, at : at + HD]
        v_own, v_other = kv[:, TH + at : TH + at + HD], kv_other[:, TH + at : TH + at + HD]
        p_own = jnp.exp(jnp.where(own, dot_nt(q, k_own) * SCALE, -1e30) - lse)
        p_other = jnp.exp(jnp.where(other, dot_nt(q, k_other) * SCALE, -1e30) - lse)
        gp_own = dot_nt(g, v_own)
        gp_other = dot_nt(g, v_other)
        delta = jnp.sum(p_own * gp_own, axis=-1, keepdims=True) + jnp.sum(p_other * gp_other, axis=-1, keepdims=True)
        s_own = (p_own * (gp_own - delta)).astype(BF)
        s_other = (p_other * (gp_other - delta)).astype(BF)
        gj[:, 2 * TH + at : 2 * TH + at + HD] = ((dot(s_own, k_own) + dot(s_other, k_other)) * SCALE).astype(BF)
        part_own[:, at : at + HD] = dot_tn(s_own, q) * SCALE
        part_out[:, at : at + HD] = (dot_tn(s_other, q) * SCALE).astype(BF)
        part_own[:, TH + at : TH + at + HD] = dot_tn(p_own.astype(BF), g)
        part_out[:, TH + at : TH + at + HD] = dot_tn(p_other.astype(BF), g).astype(BF)
    swap = remote(part_out, part_in, ks, kr, sibling)
    swap.start()
    for at, size in chunks(D):
        grad_out[:, at : at + size] = dot_tn(attended[...], full[:, at : at + size]).astype(BF)
    weights[0].wait()
    swap.wait()
    gj[:, : 2 * TH] = (part_own[...] + part_in[...].astype(F32)).astype(BF)
    rows = gj[...]
    for at, size in chunks(D):
        acc[:, at : at + size] = dot_nt(rows, w[at : at + size, :])
    scatter_start(acc, out_buf, in_buf, y, c, ss, sr)
    for at, size in chunks(D):
        grad_attn[at : at + size, :] = dot_tn(normed[:, at : at + size], gj[...]).astype(BF)
    small_bias[...] = jnp.zeros_like(small_bias)
    small_bias[0:1] = jnp.sum(gj[...].astype(F32), axis=0, keepdims=True)
    d = scatter_wait(acc, out_buf, in_buf, y, c, ss, sr)
    back, gain, shift = norm_back(d, x[...], vecs[0:1])
    small[0:1] = gain
    small[1:2] = shift
    grad_x[...] = grad[...] + back


def shape(dims, kind):
    return jax.ShapeDtypeStruct(dims, kind)


MOVE = [
    pltpu.VMEM((ROWS, D), F32),
    pltpu.VMEM((3, BLK, D), BF),
    pltpu.VMEM((3, BLK, D), BF),
    DMA((2,)),
    DMA((3,)),
    DMA((3,)),
    DMA((3,)),
    DMA((3,)),
]


def call(body, name, number, outs, ins, scratch):
    return pl.pallas_call(
        body,
        name=name,
        out_shape=outs,
        in_specs=ins,
        out_specs=[VMEM] * len(outs),
        scratch_shapes=scratch,
        compiler_params=pltpu.CompilerParams(collective_id=number, has_side_effects=True, vmem_limit_bytes=LIMIT),
    )


def run_attend_forward(x, w, wo, vecs, bias):
    outs = [
        shape((BLK, D), F32),
        shape((ROWS, D), BF),
        shape((ROWS, TH), BF),
        shape((ROWS, 2 * TH), BF),
        shape((ROWS, 2 * TH), BF),
        shape((ROWS, 128), F32),
        shape((ROWS, TH), BF),
    ]
    scratch = [pltpu.VMEM((D, TQKV), BF), pltpu.VMEM((TH, D), BF)] + MOVE + [DMA, DMA]
    return call(attend_forward, "attend_forward", 0, outs, [VMEM, ANY, ANY, VMEM, VMEM], scratch)(x, w, wo, vecs, bias)


def run_feed_forward(middle, wu, wd, vecs):
    outs = [shape((BLK, D), F32), shape((ROWS, D), BF), shape((ROWS, D), F32), shape((ROWS, D), BF)]
    scratch = [pltpu.VMEM((D, D), BF), pltpu.VMEM((D, D), BF)] + MOVE
    return call(feed_forward, "feed_forward", 1, outs, [VMEM, ANY, ANY, VMEM], scratch)(middle, wu, wd, vecs)


def run_feed_back(grad, wu, wd, vecs, middle, normed, hidden, active):
    outs = [shape((BLK, D), F32), shape((D, D), BF), shape((D, D), BF), shape((8, D), F32)]
    scratch = [
        pltpu.VMEM((D, D), BF),
        pltpu.VMEM((D, D), BF),
        pltpu.VMEM((ROWS, D), BF),
        pltpu.VMEM((ROWS, D), BF),
    ] + MOVE
    return call(feed_back, "feed_back", 2, outs, [VMEM, ANY, ANY] + [VMEM] * 5, scratch)(
        grad, wu, wd, vecs, middle, normed, hidden, active
    )


def run_attend_back(grad, w, wo, vecs, x, saved):
    outs = [
        shape((BLK, D), F32),
        shape((D, TQKV), BF),
        shape((TH, D), BF),
        shape((8, D), F32),
        shape((8, TQKV), F32),
    ]
    scratch = [
        pltpu.VMEM((D, TQKV), BF),
        pltpu.VMEM((TH, D), BF),
        pltpu.VMEM((ROWS, D), BF),
        pltpu.VMEM((ROWS, TH), BF),
        pltpu.VMEM((ROWS, TQKV), BF),
        pltpu.VMEM((ROWS, 2 * TH), BF),
        pltpu.VMEM((ROWS, 2 * TH), BF),
        pltpu.VMEM((ROWS, 2 * TH), F32),
    ] + MOVE + [DMA, DMA]
    return call(attend_back, "attend_back", 3, outs, [VMEM, ANY, ANY] + [VMEM] * 8, scratch)(
        grad, w, wo, vecs, x, *saved
    )


def spread(send_a, send_u, send_d, send_o, send_v, wa, wu, wd, wo, wv, local, ysend, yrecv, zsend, zrecv, csend, crecv):
    s = lax.axis_index("section")
    y, c = place()
    replica = lax.axis_index("replica")
    flipped = replica // 2 * 2 + (1 - replica % 2)
    near = {"section": 1 - s}
    far = {"section": 1 - s, "replica": flipped}
    sibling = at_chip(y, 1 - c)
    peers = [at_chip(ring(y, k), c) for k in (1, 2, 3)]
    arrived = greet(peers + [sibling, near, far])
    keeps = load(
        [
            (send_a.at[y], wa.at[s, y, c]),
            (send_u.at[y], wu.at[s, y, c]),
            (send_d, wd.at[s, c]),
            (send_o, wo.at[s, c]),
            (send_v, wv.at[s, y, c]),
        ],
        local,
    )
    arrived()

    def along_y(k, back):
        target = ring(y, k)
        place_in = ring(y, 4 - k) if back else y
        return [
            remote(send_v, wv.at[s, place_in, c], ysend.at[0, k - 1], yrecv.at[0, k - 1], at_chip(target, c)),
            remote(send_a.at[target], wa.at[s, place_in, c], ysend.at[1, k - 1], yrecv.at[1, k - 1], at_chip(target, c)),
            remote(send_u.at[target], wu.at[s, place_in, c], ysend.at[2, k - 1], yrecv.at[2, k - 1], at_chip(target, c)),
        ]

    def along_z(layer):
        return [
            remote(wv.at[layer, :, c], wv.at[layer, :, c], zsend.at[0], zrecv.at[0], near),
            remote(wa.at[layer, 0:2, c], wa.at[layer, 0:2, c], zsend.at[1], zrecv.at[1], near),
            remote(wa.at[layer, 2:4, c], wa.at[layer, 2:4, c], zsend.at[2], zrecv.at[2], far),
            remote(wo.at[layer, c], wo.at[layer, c], zsend.at[3], zrecv.at[3], far),
            remote(wu.at[layer, 0:2, c], wu.at[layer, 0:2, c], zsend.at[4], zrecv.at[4], near),
            remote(wu.at[layer, 2:4, c], wu.at[layer, 2:4, c], zsend.at[5], zrecv.at[5], far),
            remote(wd.at[layer, c, 0:272], wd.at[layer, c, 0:272], zsend.at[6], zrecv.at[6], near),
            remote(wd.at[layer, c, 272:544], wd.at[layer, c, 272:544], zsend.at[7], zrecv.at[7], far),
        ]

    def across(layer, i, core):
        return [
            remote(wv.at[layer, :, core], wv.at[layer, :, core], csend.at[i, 0], crecv.at[i, 0], sibling),
            remote(wa.at[layer, :, core], wa.at[layer, :, core], csend.at[i, 1], crecv.at[i, 1], sibling),
            remote(wo.at[layer, core], wo.at[layer, core], csend.at[i, 2], crecv.at[i, 2], sibling),
            remote(wu.at[layer, :, core], wu.at[layer, :, core], csend.at[i, 3], crecv.at[i, 3], sibling),
            remote(wd.at[layer, core], wd.at[layer, core], csend.at[i, 4], crecv.at[i, 4], sibling),
        ]

    sent_y = [along_y(k, False) for k in (1, 2, 3)]
    got_y = [along_y(k, True) for k in (1, 2, 3)]
    sent_z, got_z = along_z(s), along_z(1 - s)
    sent_c = [across(s, 0, c), across(1 - s, 1, c)]
    got_c = [across(s, 0, 1 - c), across(1 - s, 1, 1 - c)]
    for kind in range(3):
        for k in (1, 0, 2):
            sent_y[k][kind].start()
    keeps[2].wait()
    keeps[3].wait()
    sent_z[3].start()
    sent_c[0][2].start()
    for kind, keep, zs, cross in ((0, 4, (0,), 0), (1, 0, (1, 2), 1), (2, 1, (4, 5, 6, 7), 3)):
        keeps[keep].wait()
        for k in range(3):
            got_y[k][kind].wait_recv()
        for z in zs:
            sent_z[z].start()
        sent_c[0][cross].start()
    sent_c[0][4].start()
    for zs, cross in (((0,), 0), ((1, 2), 1), ((3,), 2), ((4, 5), 3), ((6, 7), 4)):
        for z in zs:
            got_z[z].wait_recv()
        sent_c[1][cross].start()
    for i in range(2):
        for cross in range(5):
            got_c[i][cross].wait_recv()
    for k in range(3):
        for kind in range(3):
            sent_y[k][kind].wait_send()
    for z in range(8):
        sent_z[z].wait_send()
    for i in range(2):
        for cross in range(5):
            sent_c[i][cross].wait_send()


def run_spread(a, u, d, o, v):
    outs = [
        shape((2, 4, 2, 136, TQKV), BF),
        shape((2, 4, 2, 136, D), BF),
        shape((2, 2, 544, D), BF),
        shape((2, 2, 192, D), BF),
        shape((2, 4, 2, 16, 128), BF),
    ]
    return pl.pallas_call(
        spread,
        name="spread",
        out_shape=outs,
        in_specs=[ANY] * 5,
        out_specs=[ANY] * 5,
        scratch_shapes=[DMA((5,)), DMA((3, 3)), DMA((3, 3)), DMA((8,)), DMA((8,)), DMA((2, 5)), DMA((2, 5))],
        compiler_params=pltpu.CompilerParams(collective_id=4, has_side_effects=True),
    )(a, u, d, o, v)


def collect(wide, tall, out_wide, out_tall, own_w, own_t, in_w, in_t, out_w, local, csend, crecv, ysend, yrecv):
    y, c = place()
    sibling = at_chip(y, 1 - c)
    arrived = greet([at_chip(ring(y, k), c) for k in (1, 2, 3)] + [sibling])
    keeps = load([(wide.at[:, c], own_w), (tall.at[c], own_t)], local)
    arrived()
    swaps = [
        remote(wide.at[:, 1 - c], in_w, csend.at[0], crecv.at[0], sibling),
        remote(tall.at[1 - c], in_t, csend.at[1], crecv.at[1], sibling),
    ]
    for swap in swaps:
        swap.start()
    keeps[0].wait()
    swaps[0].wait()
    for k in ORDER:
        target = ring(y, k)
        out_w[target] = (own_w[target].astype(F32) + in_w[target].astype(F32)).astype(BF)
        remote(out_w.at[target], out_wide.at[y], ysend.at[k - 1], yrecv.at[k - 1], at_chip(target, c)).start()
    out_wide[y] = (own_w[y].astype(F32) + in_w[y].astype(F32)).astype(BF)
    keeps[1].wait()
    swaps[1].wait()
    out_tall[...] = (own_t[...].astype(F32) + in_t[...].astype(F32)).astype(BF)
    for k in (1, 3, 2):
        remote(out_w.at[ring(y, k)], out_wide.at[ring(y, 4 - k)], ysend.at[k - 1], yrecv.at[k - 1],
               at_chip(ring(y, k), c)).wait()


def run_collect(wide, tall, number):
    width = wide.shape[-1]
    rows = tall.shape[1]
    outs = [shape((4, 136, width), BF), shape((rows, D), BF)]
    wide_buf, tall_buf = pltpu.VMEM((4, 136, width), BF), pltpu.VMEM((rows, D), BF)
    return pl.pallas_call(
        collect,
        name="collect_%d" % number,
        out_shape=outs,
        in_specs=[ANY] * 2,
        out_specs=[VMEM] * 2,
        scratch_shapes=[wide_buf, tall_buf, wide_buf, tall_buf, wide_buf, DMA((2,)), DMA((2,)), DMA((2,)), DMA((3,)), DMA((3,))],
        compiler_params=pltpu.CompilerParams(collective_id=number, has_side_effects=True, vmem_limit_bytes=LIMIT),
    )(wide, tall)


def by_chip(options, y):
    return lax.dynamic_index_in_dim(jnp.stack(options), y, 0, keepdims=False)


def split_heads(block):
    zero = jnp.zeros(block.shape[:-1] + (HD,), block.dtype)
    return [
        jnp.concatenate([block[..., 256 * j : 256 * j + 256], block[..., 1024:] if j == 3 else zero], axis=-1)
        for j in range(CHIPS)
    ]


def join_heads(blocks):
    return jnp.concatenate([blocks[j][..., :256] for j in range(CHIPS)] + [blocks[3][..., 256:]], axis=-1)


def on_device(inputs, cotangent, weight_attn, weight_out, weight_up, weight_down, bias_attn, bias_out, bias_up,
              bias_down, norm_gain, norm_bias):
    s = lax.axis_index("section")
    f = lax.axis_index("fsdp")
    y, c = f // 2, f % 2
    wa = weight_attn[0]
    q_blocks, k_blocks, v_blocks = (split_heads(wa[:, i * D : (i + 1) * D]) for i in range(3))
    send_a = jnp.stack(
        [jnp.concatenate([k_blocks[j], v_blocks[j], q_blocks[j]], axis=-1) for j in range(CHIPS)]
    )
    send_u = jnp.stack([weight_up[0][:, j * D : (j + 1) * D] for j in range(CHIPS)])
    tail = lax.ppermute(weight_out[0, 88:], "fsdp", [(i, (i + 2) % 8) for i in range(8)])
    send_o = jnp.concatenate([weight_out[0], tail, jnp.zeros((8, D), BF)], axis=0)
    send_v = jnp.concatenate(
        [bias_attn[0], bias_out[0], bias_up[0], bias_down[0], norm_gain[0].reshape(-1), norm_bias[0].reshape(-1),
         jnp.zeros((416,), BF)]
    ).reshape(16, 128)
    wa, wu, wd, wo, wv = run_spread(send_a, send_u, weight_down[0], send_o, send_v)
    wa = wa.reshape(2, D, TQKV)
    wu = wu.reshape(2, D, D)
    wd = wd.reshape(2, D, D)
    wv = wv.reshape(2, 8, 2048).astype(F32)

    def layer_params(e):
        rows = jnp.concatenate([wo[e, 1, 136:184], wo[e, 0, :136], wo[e, 1, :136]], axis=0)
        main = lax.dynamic_slice_in_dim(rows, 48 - 16 * y, 256, 0)
        extra = jnp.where(y == 3, rows[256:320], jnp.zeros((HD, D), BF))
        out_rows = jnp.concatenate([main, extra], axis=0)
        v = wv[e]
        attn = v[:, :272].reshape(-1)
        gains = v[:, 1088:1360].reshape(8, 2, 136).transpose(1, 0, 2).reshape(2, D)
        shifts = v[:, 1360:1632].reshape(8, 2, 136).transpose(1, 0, 2).reshape(2, D)
        up = lax.dynamic_slice_in_dim(v, 2 * y, 2, 0)[:, 408:952].reshape(1, D)
        vecs = jnp.concatenate(
            [gains[0:1], shifts[0:1], gains[1:2], shifts[1:2], v[:, 272:408].reshape(1, D), v[:, 952:1088].reshape(1, D),
             up, jnp.zeros((1, D), F32)], axis=0
        )
        bq, bv = by_chip(split_heads(attn[:D]), y), by_chip(split_heads(attn[D:]), y)
        bias = jnp.concatenate([jnp.zeros((TH,), F32), bv, bq])[None]
        return wa[e], out_rows, wu[e], wd[e], vecs, jnp.pad(bias, ((0, 7), (0, 0)))

    params = [layer_params(e) for e in range(2)]
    micro = lax.dynamic_index_in_dim(inputs, s, 0, keepdims=False)[0]
    stream = micro.astype(F32)
    saved, acts = [], []
    for e in range(2):
        w, wo_e, wu_e, wd_e, vecs, bias = params[e]
        middle, *kept = run_attend_forward(stream, w, wo_e, vecs, bias)
        result, *kept_two = run_feed_forward(middle, wu_e, wd_e, vecs)
        saved.append((stream, kept, middle, kept_two))
        acts.append(result.astype(BF))
        stream = acts[-1].astype(F32)
    grad = lax.dynamic_index_in_dim(cotangent, s, 0, keepdims=False)[0].astype(F32)
    in_grads, weight_grads, small_grads = [None, None], [None, None], [None, None]
    for e in (1, 0):
        w, wo_e, wu_e, wd_e, vecs, bias = params[e]
        x, kept, middle, kept_two = saved[e]
        grad_middle, grad_up, grad_down, small_two = run_feed_back(grad, wu_e, wd_e, vecs, middle, *kept_two)
        up, down = run_collect(grad_up.reshape(4, 2, 136, D), grad_down.reshape(2, 544, D), 5)
        up = lax.psum(up, ("section", "replica"))
        down = lax.psum(down, ("section", "replica"))
        grad_x, grad_attn, grad_out, small_one, small_bias = run_attend_back(grad_middle, w, wo_e, vecs, x, kept)
        in_grads[e] = grad_x.astype(BF)
        grad = in_grads[e].astype(F32)
        after = lax.ppermute(grad_out[:64], "fsdp", [(i, (i - 2) % 8) for i in range(8)])
        after = jnp.where(y == 3, grad_out[256:], after)
        chip_rows = lax.dynamic_slice_in_dim(jnp.concatenate([grad_out[:256], after], axis=0), 16 * y, 272, 0)
        attn, out = run_collect(grad_attn.reshape(4, 2, 136, TQKV), chip_rows.reshape(2, 136, D), 6)
        attn = lax.psum(attn, ("section", "replica"))
        out = lax.psum(out, ("section", "replica"))
        weight_grads[e] = (attn, out, up, down)
        bq = lax.dynamic_update_slice(jnp.zeros((4, TH), F32), small_bias[0:1, 2 * TH :], (y, 0))
        bv = lax.dynamic_update_slice(jnp.zeros((4, TH), F32), small_bias[0:1, TH : 2 * TH], (y, 0))
        bu = lax.dynamic_update_slice(jnp.zeros((4, D), F32), small_two[2:3], (y, 0))
        small_grads[e] = jnp.concatenate(
            [join_heads(bq), join_heads(bv), small_one[2], bu.reshape(-1), small_two[3],
             small_one[0], small_two[0], small_one[1], small_two[1]]
        )
    small = lax.psum(jnp.stack(small_grads), ("section", "fsdp", "replica"))
    attn, out, up, down = (jnp.where(s == 0, a, b).astype(F32) for a, b in zip(weight_grads[0], weight_grads[1]))
    small = lax.dynamic_index_in_dim(small, s, 0, keepdims=False)
    attn = jnp.concatenate(
        [join_heads([attn[j][:, i * TH : (i + 1) * TH] for j in range(CHIPS)]) for i in (2, 0, 1)], axis=-1
    )
    up = jnp.concatenate([up[j] for j in range(CHIPS)], axis=-1)

    def piece(at, total):
        size = total // 8
        return lax.dynamic_slice_in_dim(small, at + f * size, size, 0)

    def pair(at):
        return jnp.stack([piece(at, D), piece(at + D, D)])

    def swap_layers(values):
        mine = jnp.where(s == 0, values[0], values[1])
        theirs = jnp.where(s == 0, values[1], values[0])
        received = lax.ppermute(theirs, "section", [(0, 1), (1, 0)])
        pair_up = jnp.stack([jnp.where(s == 0, mine, received), jnp.where(s == 0, received, mine)])
        return pair_up[None, :, None]

    return (
        swap_layers(acts),
        swap_layers(in_grads),
        attn[None],
        out[None],
        up[None],
        down[None],
        piece(0, 2176)[None],
        piece(2176, D)[None],
        piece(3264, FF)[None],
        piece(7616, D)[None],
        pair(8704)[None],
        pair(10880)[None],
    )


def solution(mesh):
    placed = (
        P(None, "replica", "fsdp", None),
        P(None, "replica", "fsdp", None),
        P("section", "fsdp", None),
        P("section", "fsdp", None),
        P("section", "fsdp", None),
        P("section", "fsdp", None),
        P("section", "fsdp"),
        P("section", "fsdp"),
        P("section", "fsdp"),
        P("section", "fsdp"),
        P("section", None, "fsdp"),
        P("section", None, "fsdp"),
    )
    return jax.shard_map(
        on_device,
        mesh=mesh,
        in_specs=placed,
        out_specs=(
            P("section", None, "replica", "fsdp", None),
            P("section", None, "replica", "fsdp", None),
        )
        + placed[2:],
        check_vma=False,
    )
```

```python
import functools

import jax
import jax.numpy as jnp
from jax import lax
from jax.experimental import pallas as pl
from jax.experimental.pallas import tpu as pltpu
from jax.sharding import PartitionSpec as P

D = 1088
FF = 4352
HEADS = 17
HD = 64
BLK = 64
CHIPS = 4
ROWS = BLK * CHIPS
SLOTS = 5
TH = SLOTS * HD
TQKV = 3 * TH
SCALE = HD**-0.5
EPS = 1e-5
MESH = pl.DeviceIdType.MESH
BF = jnp.bfloat16
F32 = jnp.float32
ANY = pl.BlockSpec(memory_space=pl.ANY)
VMEM = pl.BlockSpec(memory_space=pltpu.VMEM)
DMA = pltpu.SemaphoreType.DMA
LIMIT = 56 * 1024 * 1024
COST = pl.CostEstimate(flops=10_000_000, bytes_accessed=10_000, transcendentals=0)


def dot(a, b):
    return lax.dot_general(a, b, (((1,), (0,)), ((), ())), preferred_element_type=F32)


def dot_nt(a, b):
    return lax.dot_general(a, b, (((1,), (1,)), ((), ())), preferred_element_type=F32)


def dot_tn(a, b):
    return lax.dot_general(a, b, (((0,), (0,)), ((), ())), preferred_element_type=F32)


def chunks(n, size=256):
    return [(i, min(size, n - i)) for i in range(0, n, size)]


def place():
    f = lax.axis_index("fsdp")
    return f // 2, f % 2


def ring(y, k):
    return lax.rem(y + k, CHIPS)


def at_chip(y, c):
    return {"fsdp": 2 * y + c}


def greet(targets):
    barrier = pltpu.get_barrier_semaphore()
    for target in targets:
        pl.semaphore_signal(barrier, inc=1, device_id=target, device_id_type=MESH)
    return functools.partial(pl.semaphore_wait, barrier, len(targets))


def remote(src, dst, send, recv, target):
    return pltpu.make_async_remote_copy(
        src_ref=src, dst_ref=dst, send_sem=send, recv_sem=recv, device_id=target, device_id_type=MESH
    )


def slot(ref, y):
    return ref.at[pl.ds(pl.multiple_of(y * BLK, BLK), BLK)]


ORDER = (2, 1, 3)


def gather_start(full, y, c, send, recv):
    for k in ORDER:
        remote(slot(full, y), slot(full, y), send.at[k - 1], recv.at[k - 1], at_chip(ring(y, k), c)).start()


def gather_wait(full, y, c, send, recv):
    for k in (1, 3, 2):
        source = ring(y, 4 - k)
        remote(slot(full, source), slot(full, source), send.at[k - 1], recv.at[k - 1], at_chip(ring(y, k), c)).wait()


def scatter_start(acc, out_buf, in_buf, y, c, send, recv):
    for k in ORDER:
        target = ring(y, k)
        out_buf[k - 1] = slot(acc, target)[...].astype(BF)
        remote(out_buf.at[k - 1], in_buf.at[k - 1], send.at[k - 1], recv.at[k - 1], at_chip(target, c)).start()


def scatter_wait(acc, out_buf, in_buf, y, c, send, recv):
    total = slot(acc, y)[...]
    for k in (1, 3, 2):
        remote(out_buf.at[k - 1], in_buf.at[k - 1], send.at[k - 1], recv.at[k - 1], at_chip(ring(y, k), c)).wait()
        total = total + in_buf[k - 1].astype(F32)
    return total


def stats(v):
    centre = v - jnp.mean(v, axis=-1, keepdims=True)
    scale = lax.rsqrt(jnp.mean(centre * centre, axis=-1, keepdims=True) + EPS)
    return centre * scale, scale


def norm(v, gain, shift):
    return stats(v)[0] * gain + shift


def norm_back(d, v, gain):
    vh, scale = stats(v)
    q = d * gain
    grad = scale * (q - jnp.mean(q, axis=-1, keepdims=True) - vh * jnp.mean(q * vh, axis=-1, keepdims=True))
    return grad, jnp.sum(d * vh, axis=0, keepdims=True), jnp.sum(d, axis=0, keepdims=True)


GELU_A = 0.7978845608028654
GELU_B = 0.044715


def gelu(h):
    return 0.5 * h * (1.0 + jnp.tanh(GELU_A * (h + GELU_B * h * h * h)))


def gelu_slope(h):
    t = jnp.tanh(GELU_A * (h + GELU_B * h * h * h))
    return 0.5 * (1.0 + t) + 0.5 * h * (1.0 - t * t) * (GELU_A * (1.0 + 3.0 * GELU_B * h * h))


def masks(c):
    row = lax.broadcasted_iota(jnp.int32, (ROWS, ROWS), 0)
    col = lax.broadcasted_iota(jnp.int32, (ROWS, ROWS), 1)
    own = row >= col
    other = (row // BLK) >= (col // BLK) + (1 - c)
    return own, other


def load(pairs, sems):
    copies = [pltpu.make_async_copy(src, dst, sems.at[i]) for i, (src, dst) in enumerate(pairs)]
    for copy in copies:
        copy.start()
    return copies


def out_rows(wo_hbm, wo, e, y):
    start = pl.multiple_of(48 - 16 * y, 16)
    return [(wo_hbm.at[e, pl.ds(start, 256)], wo.at[0:256]), (wo_hbm.at[e, 256:320], wo.at[256:320])]


def out_wait(weights, wo, y):
    weights[1].wait()
    weights[2].wait()

    @pl.when(y < 3)
    def _():
        wo[256:320] = jnp.zeros((HD, D), BF)


def chip_row(y, rows):
    return jnp.where(lax.broadcasted_iota(jnp.int32, (CHIPS, 1), 0) == y, rows, 0.0)


def head_bias(vecs, row, y):
    last = jnp.where(y == 3, vecs[row : row + 1, 1024:D], 0.0)
    return jnp.concatenate([vecs[row : row + 1, pl.ds(pl.multiple_of(256 * y, 256), 256)], last], axis=-1)


def attend_forward(e, x, w_hbm, wo_hbm, vecs, middle, normed, queries, kv, kv_other, logsum, attended,
                   w, wo, acc, out_buf, in_buf, ls, gs, gr, ss, sr, ks, kr):
    y, c = place()
    peers = [at_chip(ring(y, k), c) for k in (1, 2, 3)]
    sibling = at_chip(y, 1 - c)
    arrived = greet(peers + [sibling])
    weights = load([(w_hbm.at[e], w)] + out_rows(wo_hbm, wo, e, y), ls)
    slot(normed, y)[...] = norm(x[...], vecs[0:1], vecs[1:2]).astype(BF)
    arrived()
    gather_start(normed, y, c, gs, gr)
    own, other = masks(c)
    weights[0].wait()
    gather_wait(normed, y, c, gs, gr)
    rows = normed[...]
    bias = jnp.concatenate([jnp.zeros((1, TH), F32), head_bias(vecs, 11, y)], axis=-1)
    for at, size in chunks(2 * TH):
        kv[:, at : at + size] = (dot(rows, w[:, at : at + size]) + bias[:, at : at + size]).astype(BF)
    swap = remote(kv, kv_other, ks, kr, sibling)
    swap.start()
    queries[...] = (dot(rows, w[:, 2 * TH :]) + head_bias(vecs, 10, y)).astype(BF)
    swap.wait()
    for h in range(SLOTS):
        at = h * HD
        q = queries[:, at : at + HD]
        s_own = jnp.where(own, dot_nt(q, kv[:, at : at + HD]) * SCALE, -1e30)
        s_other = jnp.where(other, dot_nt(q, kv_other[:, at : at + HD]) * SCALE, -1e30)
        top = jnp.maximum(jnp.max(s_own, axis=-1, keepdims=True), jnp.max(s_other, axis=-1, keepdims=True))
        e_own = jnp.exp(s_own - top)
        e_other = jnp.exp(s_other - top)
        total = jnp.sum(e_own, axis=-1, keepdims=True) + jnp.sum(e_other, axis=-1, keepdims=True)
        logsum[:, h : h + 1] = top + jnp.log(total)
        inverse = 1.0 / total
        a_own = (e_own * inverse).astype(BF)
        a_other = (e_other * inverse).astype(BF)
        out = dot(a_own, kv[:, TH + at : TH + at + HD]) + dot(a_other, kv_other[:, TH + at : TH + at + HD])
        attended[:, at : at + HD] = out.astype(BF)
    out_wait(weights, wo, y)
    mixed = attended[...]
    for at, size in chunks(D):
        acc[:, at : at + size] = dot(mixed, wo[:, at : at + size])
    scatter_start(acc, out_buf, in_buf, y, c, ss, sr)
    base = x[...] + vecs[4:5]
    middle[...] = base + scatter_wait(acc, out_buf, in_buf, y, c, ss, sr)


def feed_forward(e, middle, wu_hbm, wd_hbm, vecs, result, normed, hidden, active,
                 wu, wd, acc, out_buf, in_buf, ls, gs, gr, ss, sr):
    y, c = place()
    arrived = greet([at_chip(ring(y, k), c) for k in (1, 2, 3)])
    weights = load([(wu_hbm.at[e], wu), (wd_hbm.at[e], wd)], ls)
    slot(normed, y)[...] = norm(middle[...], vecs[2:3], vecs[3:4]).astype(BF)
    arrived()
    gather_start(normed, y, c, gs, gr)
    bias = jnp.sum(chip_row(y, vecs[6:10]), axis=0, keepdims=True)
    weights[0].wait()
    gather_wait(normed, y, c, gs, gr)
    rows = normed[...]
    for at, size in chunks(D):
        h = dot(rows, wu[:, at : at + size]) + bias[:, at : at + size]
        hidden[:, at : at + size] = h
        active[:, at : at + size] = gelu(h).astype(BF)
    weights[1].wait()
    rows = active[...]
    for at, size in chunks(D):
        acc[:, at : at + size] = dot(rows, wd[:, at : at + size])
    scatter_start(acc, out_buf, in_buf, y, c, ss, sr)
    base = middle[...] + vecs[5:6]
    result[...] = base + scatter_wait(acc, out_buf, in_buf, y, c, ss, sr)


def feed_back(e, grad, wu_hbm, wd_hbm, vecs, middle, normed, hidden, active, grad_middle, grad_up, grad_down, small,
              wu, wd, full, gh, acc, out_buf, in_buf, ls, gs, gr, ss, sr):
    y, c = place()
    arrived = greet([at_chip(ring(y, k), c) for k in (1, 2, 3)])
    weights = load([(wu_hbm.at[e], wu), (wd_hbm.at[e], wd)], ls)
    own_rows = grad[...].astype(BF)
    slot(full, y)[...] = own_rows
    arrived()
    gather_start(full, y, c, gs, gr)
    small[...] = jnp.zeros_like(small)
    small[3:4] = jnp.sum(own_rows.astype(F32), axis=0, keepdims=True)
    weights[1].wait()
    gather_wait(full, y, c, gs, gr)
    rows = full[...]
    for at, size in chunks(D):
        slope = gelu_slope(hidden[:, at : at + size])
        part = (dot_nt(rows, wd[at : at + size, :]) * slope).astype(BF)
        gh[:, at : at + size] = part
        small[2:3, at : at + size] = jnp.sum(part.astype(F32), axis=0, keepdims=True)
    weights[0].wait()
    rows = gh[...]
    for at, size in chunks(D):
        acc[:, at : at + size] = dot_nt(rows, wu[at : at + size, :])
    scatter_start(acc, out_buf, in_buf, y, c, ss, sr)
    for at, size in chunks(D):
        grad_up[at : at + size, :] = dot_tn(normed[:, at : at + size], gh[...]).astype(BF)
        grad_down[at : at + size, :] = dot_tn(active[:, at : at + size], full[...]).astype(BF)
    d = scatter_wait(acc, out_buf, in_buf, y, c, ss, sr)
    back, gain, shift = norm_back(d, middle[...], vecs[2:3])
    small[0:1] = gain
    small[1:2] = shift
    grad_middle[...] = grad[...] + back


def attend_back(e, grad, w_hbm, wo_hbm, vecs, x, normed, queries, kv, kv_other, logsum, attended,
                grad_x, grad_attn, grad_out, small, small_bias,
                w, wo, full, ga, gj, part_out, part_in, part_own, acc, out_buf, in_buf, ls, gs, gr, ss, sr, ks, kr):
    y, c = place()
    peers = [at_chip(ring(y, k), c) for k in (1, 2, 3)]
    sibling = at_chip(y, 1 - c)
    arrived = greet(peers + [sibling])
    weights = load([(w_hbm.at[e], w)] + out_rows(wo_hbm, wo, e, y), ls)
    own_rows = grad[...].astype(BF)
    slot(full, y)[...] = own_rows
    arrived()
    gather_start(full, y, c, gs, gr)
    small[...] = jnp.zeros_like(small)
    small[2:3] = jnp.sum(own_rows.astype(F32), axis=0, keepdims=True)
    own, other = masks(c)
    out_wait(weights, wo, y)
    gather_wait(full, y, c, gs, gr)
    ga[...] = dot_nt(full[...], wo[...]).astype(BF)
    for h in range(SLOTS):
        at = h * HD
        q = queries[:, at : at + HD]
        g = ga[:, at : at + HD]
        lse = logsum[:, h : h + 1]
        k_own, k_other = kv[:, at : at + HD], kv_other[:, at : at + HD]
        v_own, v_other = kv[:, TH + at : TH + at + HD], kv_other[:, TH + at : TH + at + HD]
        p_own = jnp.exp(jnp.where(own, dot_nt(q, k_own) * SCALE, -1e30) - lse)
        p_other = jnp.exp(jnp.where(other, dot_nt(q, k_other) * SCALE, -1e30) - lse)
        gp_own = dot_nt(g, v_own)
        gp_other = dot_nt(g, v_other)
        delta = jnp.sum(p_own * gp_own, axis=-1, keepdims=True) + jnp.sum(p_other * gp_other, axis=-1, keepdims=True)
        s_own = (p_own * (gp_own - delta)).astype(BF)
        s_other = (p_other * (gp_other - delta)).astype(BF)
        gj[:, 2 * TH + at : 2 * TH + at + HD] = ((dot(s_own, k_own) + dot(s_other, k_other)) * SCALE).astype(BF)
        part_own[:, at : at + HD] = dot_tn(s_own, q) * SCALE
        part_out[:, at : at + HD] = (dot_tn(s_other, q) * SCALE).astype(BF)
        part_own[:, TH + at : TH + at + HD] = dot_tn(p_own.astype(BF), g)
        part_out[:, TH + at : TH + at + HD] = dot_tn(p_other.astype(BF), g).astype(BF)
    swap = remote(part_out, part_in, ks, kr, sibling)
    swap.start()
    for at, size in chunks(D):
        grad_out[:, at : at + size] = dot_tn(attended[...], full[:, at : at + size]).astype(BF)
    weights[0].wait()
    swap.wait()
    gj[:, : 2 * TH] = (part_own[...] + part_in[...].astype(F32)).astype(BF)
    rows = gj[...]
    for at, size in chunks(D):
        acc[:, at : at + size] = dot_nt(rows, w[at : at + size, :])
    scatter_start(acc, out_buf, in_buf, y, c, ss, sr)
    for at, size in chunks(D):
        grad_attn[at : at + size, :] = dot_tn(normed[:, at : at + size], gj[...]).astype(BF)
    small_bias[...] = jnp.zeros_like(small_bias)
    small_bias[0:1] = jnp.sum(gj[...].astype(F32), axis=0, keepdims=True)
    d = scatter_wait(acc, out_buf, in_buf, y, c, ss, sr)
    back, gain, shift = norm_back(d, x[...], vecs[0:1])
    small[0:1] = gain
    small[1:2] = shift
    grad_x[...] = grad[...] + back


def shape(dims, kind):
    return jax.ShapeDtypeStruct(dims, kind)


MOVE = [
    pltpu.VMEM((ROWS, D), F32),
    pltpu.VMEM((3, BLK, D), BF),
    pltpu.VMEM((3, BLK, D), BF),
    DMA((3,)),
    DMA((3,)),
    DMA((3,)),
    DMA((3,)),
    DMA((3,)),
]


def call(body, name, number, outs, ins, scratch):
    return pl.pallas_call(
        body,
        name=name,
        out_shape=outs,
        in_specs=ins,
        out_specs=[VMEM] * len(outs),
        scratch_shapes=scratch,
        cost_estimate=COST,
        compiler_params=pltpu.CompilerParams(collective_id=number, has_side_effects=True, vmem_limit_bytes=LIMIT),
    )


def run_attend_forward(e, x, w, wo, vecs):
    outs = [
        shape((BLK, D), F32),
        shape((ROWS, D), BF),
        shape((ROWS, TH), BF),
        shape((ROWS, 2 * TH), BF),
        shape((ROWS, 2 * TH), BF),
        shape((ROWS, 128), F32),
        shape((ROWS, TH), BF),
    ]
    scratch = [pltpu.VMEM((D, TQKV), BF), pltpu.VMEM((TH, D), BF)] + MOVE + [DMA, DMA]
    return call(functools.partial(attend_forward, e), "attend_forward_%d" % e, e, outs, [VMEM, ANY, ANY, VMEM], scratch)(x, w, wo, vecs)


def run_feed_forward(e, middle, wu, wd, vecs):
    outs = [shape((BLK, D), F32), shape((ROWS, D), BF), shape((ROWS, D), F32), shape((ROWS, D), BF)]
    scratch = [pltpu.VMEM((D, D), BF), pltpu.VMEM((D, D), BF)] + MOVE
    return call(functools.partial(feed_forward, e), "feed_forward_%d" % e, 2 + e, outs, [VMEM, ANY, ANY, VMEM], scratch)(middle, wu, wd, vecs)


def run_feed_back(e, grad, wu, wd, vecs, middle, normed, hidden, active):
    outs = [shape((BLK, D), F32), shape((D, D), BF), shape((D, D), BF), shape((8, D), F32)]
    scratch = [
        pltpu.VMEM((D, D), BF),
        pltpu.VMEM((D, D), BF),
        pltpu.VMEM((ROWS, D), BF),
        pltpu.VMEM((ROWS, D), BF),
    ] + MOVE
    return call(functools.partial(feed_back, e), "feed_back_%d" % e, 4 + e, outs, [VMEM, ANY, ANY] + [VMEM] * 5, scratch)(
        grad, wu, wd, vecs, middle, normed, hidden, active
    )


def run_attend_back(e, grad, w, wo, vecs, x, saved):
    outs = [
        shape((BLK, D), F32),
        shape((D, TQKV), BF),
        shape((TH, D), BF),
        shape((8, D), F32),
        shape((8, TQKV), F32),
    ]
    scratch = [
        pltpu.VMEM((D, TQKV), BF),
        pltpu.VMEM((TH, D), BF),
        pltpu.VMEM((ROWS, D), BF),
        pltpu.VMEM((ROWS, TH), BF),
        pltpu.VMEM((ROWS, TQKV), BF),
        pltpu.VMEM((ROWS, 2 * TH), BF),
        pltpu.VMEM((ROWS, 2 * TH), BF),
        pltpu.VMEM((ROWS, 2 * TH), F32),
    ] + MOVE + [DMA, DMA]
    return call(functools.partial(attend_back, e), "attend_back_%d" % e, 6 + e, outs, [VMEM, ANY, ANY] + [VMEM] * 8, scratch)(
        grad, w, wo, vecs, x, *saved
    )


def spread(send_a, send_u, send_d, send_o, send_v, wa, wu, wd, wo, wv, local, ysend, yrecv, zsend, zrecv, csend, crecv):
    s = lax.axis_index("section")
    y, c = place()
    replica = lax.axis_index("replica")
    flipped = replica // 2 * 2 + (1 - replica % 2)
    near = {"section": 1 - s}
    far = {"section": 1 - s, "replica": flipped}
    sibling = at_chip(y, 1 - c)
    peers = [at_chip(ring(y, k), c) for k in (1, 2, 3)]
    arrived = greet(peers + [sibling, near, far])
    keeps = load(
        [
            (send_a.at[y], wa.at[s, y, c]),
            (send_u.at[y], wu.at[s, y, c]),
            (send_d, wd.at[s, c]),
            (send_o, wo.at[s, c]),
            (send_v, wv.at[s, y, c]),
        ],
        local,
    )
    arrived()

    def along_y(k, back):
        target = ring(y, k)
        place_in = ring(y, 4 - k) if back else y
        return [
            remote(send_v, wv.at[s, place_in, c], ysend.at[0, k - 1], yrecv.at[0, k - 1], at_chip(target, c)),
            remote(send_a.at[target], wa.at[s, place_in, c], ysend.at[1, k - 1], yrecv.at[1, k - 1], at_chip(target, c)),
            remote(send_u.at[target], wu.at[s, place_in, c], ysend.at[2, k - 1], yrecv.at[2, k - 1], at_chip(target, c)),
        ]

    def along_z(layer):
        return [
            remote(wv.at[layer, :, c], wv.at[layer, :, c], zsend.at[0], zrecv.at[0], near),
            remote(wa.at[layer, 0:2, c], wa.at[layer, 0:2, c], zsend.at[1], zrecv.at[1], near),
            remote(wa.at[layer, 2:4, c], wa.at[layer, 2:4, c], zsend.at[2], zrecv.at[2], far),
            remote(wo.at[layer, c], wo.at[layer, c], zsend.at[3], zrecv.at[3], far),
            remote(wu.at[layer, 0:2, c], wu.at[layer, 0:2, c], zsend.at[4], zrecv.at[4], near),
            remote(wu.at[layer, 2:4, c], wu.at[layer, 2:4, c], zsend.at[5], zrecv.at[5], far),
            remote(wd.at[layer, c, 0:272], wd.at[layer, c, 0:272], zsend.at[6], zrecv.at[6], near),
            remote(wd.at[layer, c, 272:544], wd.at[layer, c, 272:544], zsend.at[7], zrecv.at[7], far),
        ]

    def across(layer, i, core):
        return [
            remote(wv.at[layer, :, core], wv.at[layer, :, core], csend.at[i, 0], crecv.at[i, 0], sibling),
            remote(wa.at[layer, :, core], wa.at[layer, :, core], csend.at[i, 1], crecv.at[i, 1], sibling),
            remote(wo.at[layer, core], wo.at[layer, core], csend.at[i, 2], crecv.at[i, 2], sibling),
            remote(wu.at[layer, :, core], wu.at[layer, :, core], csend.at[i, 3], crecv.at[i, 3], sibling),
            remote(wd.at[layer, core], wd.at[layer, core], csend.at[i, 4], crecv.at[i, 4], sibling),
        ]

    sent_y = [along_y(k, False) for k in (1, 2, 3)]
    got_y = [along_y(k, True) for k in (1, 2, 3)]
    sent_z, got_z = along_z(s), along_z(1 - s)
    sent_c = [across(s, 0, c), across(1 - s, 1, c)]
    got_c = [across(s, 0, 1 - c), across(1 - s, 1, 1 - c)]
    for kind in (0, 1):
        for k in (1, 0, 2):
            sent_y[k][kind].start()
    keeps[3].wait()
    sent_z[3].start()
    sent_c[0][2].start()
    keeps[2].wait()
    sent_z[6].start()
    sent_z[7].start()
    sent_c[0][4].start()
    for kind, keep, zs, cross in ((0, 4, (0,), 0), (1, 0, (1, 2), 1)):
        keeps[keep].wait()
        for k in range(3):
            got_y[k][kind].wait_recv()
        for z in zs:
            sent_z[z].start()
        sent_c[0][cross].start()
    for k in (1, 0, 2):
        sent_y[k][2].start()
    for zs, cross in (((3,), 2), ((6, 7), 4), ((0,), 0), ((1, 2), 1)):
        for z in zs:
            got_z[z].wait_recv()
        sent_c[1][cross].start()
    keeps[1].wait()
    for k in range(3):
        got_y[k][2].wait_recv()
    for z in (4, 5):
        sent_z[z].start()
    sent_c[0][3].start()
    for z in (4, 5):
        got_z[z].wait_recv()
    sent_c[1][3].start()
    for i in range(2):
        for cross in range(5):
            got_c[i][cross].wait_recv()
    for k in range(3):
        for kind in range(3):
            sent_y[k][kind].wait_send()
    for z in range(8):
        sent_z[z].wait_send()
    for i in range(2):
        for cross in range(5):
            sent_c[i][cross].wait_send()


def run_spread(a, u, d, o, v):
    outs = [
        shape((2, 4, 2, 136, TQKV), BF),
        shape((2, 4, 2, 136, D), BF),
        shape((2, 2, 544, D), BF),
        shape((2, 2, 192, D), BF),
        shape((2, 4, 2, 16, D), BF),
    ]
    return pl.pallas_call(
        spread,
        name="spread",
        out_shape=outs,
        in_specs=[ANY] * 5,
        out_specs=[ANY] * 5,
        scratch_shapes=[DMA((5,)), DMA((3, 3)), DMA((3, 3)), DMA((8,)), DMA((8,)), DMA((2, 5)), DMA((2, 5))],
        compiler_params=pltpu.CompilerParams(collective_id=8, has_side_effects=True),
    )(a, u, d, o, v)


def wide_start(wide, own_w, in_w, out_w, out_wide, keep, swap, y, c, ysend, yrecv):
    keep.wait()
    swap.wait()
    for k in ORDER:
        target = ring(y, k)
        out_w[target] = (own_w[target].astype(F32) + in_w[target].astype(F32)).astype(BF)
        remote(out_w.at[target], out_wide.at[y], ysend.at[k - 1], yrecv.at[k - 1], at_chip(target, c)).start()
    out_wide[y] = (own_w[y].astype(F32) + in_w[y].astype(F32)).astype(BF)


def wide_wait(out_w, out_wide, y, c, ysend, yrecv):
    for k in (1, 3, 2):
        remote(out_w.at[ring(y, k)], out_wide.at[ring(y, 4 - k)], ysend.at[k - 1], yrecv.at[k - 1],
               at_chip(ring(y, k), c)).wait()


def collect_feed(wide, tall, out_wide, out_tall, own_w, own_t, in_w, in_t, out_w, local, csend, crecv, ysend, yrecv):
    y, c = place()
    sibling = at_chip(y, 1 - c)
    arrived = greet([at_chip(ring(y, k), c) for k in (1, 2, 3)] + [sibling])
    keeps = load([(wide.at[:, c], own_w), (tall.at[c], own_t)], local)
    arrived()
    swaps = [
        remote(wide.at[:, 1 - c], in_w, csend.at[0], crecv.at[0], sibling),
        remote(tall.at[1 - c], in_t, csend.at[1], crecv.at[1], sibling),
    ]
    for swap in swaps:
        swap.start()
    wide_start(wide, own_w, in_w, out_w, out_wide, keeps[0], swaps[0], y, c, ysend, yrecv)
    keeps[1].wait()
    swaps[1].wait()
    out_tall[...] = (own_t[...].astype(F32) + in_t[...].astype(F32)).astype(BF)
    wide_wait(out_w, out_wide, y, c, ysend, yrecv)


def collect_attend(wide, rows, one, two, heads, out_wide, out_rows_ref, out_small,
                   own_w, own_r, in_w, in_r, out_w, edge, small, in_small, in_small_y,
                   local, csend, crecv, ysend, yrecv, esend, erecv, ssend, srecv):
    y, c = place()
    sibling = at_chip(y, 1 - c)
    arrived = greet([at_chip(ring(y, k), c) for k in (1, 2, 3)] + [sibling])
    keeps = load([(wide.at[:, c], own_w), (rows, own_r)], local)
    small[...] = jnp.zeros_like(small)
    small[0:2] = one[0:2]
    small[2:4] = two[0:2]
    small[4:5] = one[2:3]
    small[5:6] = two[3:4]
    small[6:10] = chip_row(y, two[2:3])
    for row, at in ((10, 2 * TH), (11, TH)):
        small[row : row + 1, pl.ds(pl.multiple_of(256 * y, 256), 256)] = heads[0:1, at : at + 256]

        @pl.when(y == 3)
        def _():
            small[row : row + 1, 1024:D] = heads[0:1, at + 256 : at + TH]

    arrived()
    swaps = [
        remote(wide.at[:, 1 - c], in_w, csend.at[0], crecv.at[0], sibling),
        remote(rows, in_r, csend.at[1], crecv.at[1], sibling),
        remote(small, in_small, csend.at[2], crecv.at[2], sibling),
    ]
    for swap in swaps:
        swap.start()
    wide_start(wide, own_w, in_w, out_w, out_wide, keeps[0], swaps[0], y, c, ysend, yrecv)
    keeps[1].wait()
    swaps[1].wait()
    own_r[...] = (own_r[...].astype(F32) + in_r[...].astype(F32)).astype(BF)
    shift = remote(own_r.at[0:HD], edge, esend, erecv, at_chip(ring(y, 3), c))
    shift.start()
    swaps[2].wait()
    small[...] = small[...] + in_small[...]
    for k in (1, 2, 3):
        remote(small, in_small_y.at[k - 1], ssend.at[k - 1], srecv.at[k - 1], at_chip(ring(y, k), c)).start()
    shift.wait()

    @pl.when(y < 3)
    def _():
        own_r[256:320] = edge[...]

    out_rows_ref[...] = own_r[pl.ds(pl.multiple_of(16 * y, 16), 272)]
    total = small[...]
    for k in (1, 2, 3):
        remote(small, in_small_y.at[k - 1], ssend.at[k - 1], srecv.at[k - 1], at_chip(ring(y, k), c)).wait()
        total = total + in_small_y[k - 1]
    out_small[...] = total
    wide_wait(out_w, out_wide, y, c, ysend, yrecv)


def run_collect_feed(e, wide, tall):
    outs = [shape((4, 136, D), BF), shape((544, D), BF)]
    wide_buf, tall_buf = pltpu.VMEM((4, 136, D), BF), pltpu.VMEM((544, D), BF)
    scratch = [wide_buf, tall_buf, wide_buf, tall_buf, wide_buf, DMA((2,)), DMA((2,)), DMA((2,)), DMA((3,)), DMA((3,))]
    return call(collect_feed, "collect_feed_%d" % e, 9 + e, outs, [ANY] * 2, scratch)(wide, tall)


def run_collect_attend(e, wide, rows, one, two, heads):
    outs = [shape((4, 136, TQKV), BF), shape((272, D), BF), shape((16, D), F32)]
    wide_buf, rows_buf, small_buf = pltpu.VMEM((4, 136, TQKV), BF), pltpu.VMEM((TH, D), BF), pltpu.VMEM((16, D), F32)
    scratch = [wide_buf, rows_buf, wide_buf, rows_buf, wide_buf, pltpu.VMEM((HD, D), BF), small_buf, small_buf,
               pltpu.VMEM((3, 16, D), F32), DMA((2,)), DMA((3,)), DMA((3,)), DMA((3,)), DMA((3,)), DMA, DMA,
               DMA((3,)), DMA((3,))]
    return call(collect_attend, "collect_attend_%d" % e, 11 + e, outs, [ANY] * 2 + [VMEM] * 3, scratch)(
        wide, rows, one, two, heads
    )


def split_heads(block):
    zero = jnp.zeros(block.shape[:-1] + (HD,), block.dtype)
    return [
        jnp.concatenate([block[..., 256 * j : 256 * j + 256], block[..., 1024:] if j == 3 else zero], axis=-1)
        for j in range(CHIPS)
    ]


def join_heads(blocks):
    return jnp.concatenate([blocks[j][..., :256] for j in range(CHIPS)] + [blocks[3][..., 256:]], axis=-1)


def on_device(inputs, cotangent, weight_attn, weight_out, weight_up, weight_down, bias_attn, bias_out, bias_up,
              bias_down, norm_gain, norm_bias):
    s = lax.axis_index("section")
    f = lax.axis_index("fsdp")
    y, c = f // 2, f % 2
    wa = weight_attn[0]
    q_blocks, k_blocks, v_blocks = (split_heads(wa[:, i * D : (i + 1) * D]) for i in range(3))
    send_a = jnp.stack(
        [jnp.concatenate([k_blocks[j], v_blocks[j], q_blocks[j]], axis=-1) for j in range(CHIPS)]
    )
    send_u = jnp.stack([weight_up[0][:, j * D : (j + 1) * D] for j in range(CHIPS)])
    tail = lax.ppermute(weight_out[0, 88:], "fsdp", [(i, (i + 2) % 8) for i in range(8)])
    send_o = jnp.concatenate([weight_out[0], tail, jnp.zeros((8, D), BF)], axis=0)
    vectors = jnp.stack([norm_gain[0, 0], norm_bias[0, 0], norm_gain[0, 1], norm_bias[0, 1], bias_out[0], bias_down[0]])
    send_v = jnp.concatenate(
        [
            lax.dynamic_update_slice(jnp.zeros((6, D), BF), vectors, (0, 136 * f)),
            lax.dynamic_update_slice(jnp.zeros((4, D), BF), bias_up, (y, 544 * c)),
            lax.dynamic_update_slice(jnp.zeros((6, D), BF), bias_attn, (f // 4, 272 * (f % 4))),
        ]
    )
    wa, wu, wd, wo, wv = run_spread(send_a, send_u, weight_down[0], send_o, send_v)
    wa = wa.reshape(2, D, TQKV)
    wu = wu.reshape(2, D, D)
    wd = wd.reshape(2, D, D)
    wo = jnp.concatenate([wo[:, 1, 136:184], wo[:, 0, :136], wo[:, 1, :136]], axis=1)
    vecs = jnp.sum(wv.astype(F32), axis=(1, 2))
    micro = lax.dynamic_index_in_dim(inputs, s, 0, keepdims=False)[0]
    stream = micro.astype(F32)
    saved, acts = [], []
    for e in range(2):
        middle, *kept = run_attend_forward(e, stream, wa, wo, vecs[e])
        result, *kept_two = run_feed_forward(e, middle, wu, wd, vecs[e])
        saved.append((stream, kept, middle, kept_two))
        acts.append(result.astype(BF))
        stream = acts[-1].astype(F32)
    grad = lax.dynamic_index_in_dim(cotangent, s, 0, keepdims=False)[0].astype(F32)
    in_grads, weight_grads = [None, None], [None, None]
    for e in (1, 0):
        x, kept, middle, kept_two = saved[e]
        grad_middle, grad_up, grad_down, two = run_feed_back(e, grad, wu, wd, vecs[e], middle, *kept_two)
        if e == 0:
            grad_up, weight_grads[1] = lax.optimization_barrier((grad_up, weight_grads[1]))
        up, down = run_collect_feed(e, grad_up.reshape(4, 2, 136, D), grad_down.reshape(2, 544, D))
        grad_middle, up, down = lax.optimization_barrier((grad_middle, up, down))
        up, down = lax.psum((up, down), ("replica", "section"))
        grad_x, grad_attn, grad_out, one, heads = run_attend_back(e, grad_middle, wa, wo, vecs[e], x, kept)
        in_grads[e] = grad_x.astype(BF)
        grad = in_grads[e].astype(F32)
        attn, out, small = run_collect_attend(e, grad_attn.reshape(4, 2, 136, TQKV), grad_out, one, two, heads)
        out = lax.dynamic_slice_in_dim(out, 136 * c, 136, 0)
        out = jnp.concatenate([out, small.astype(BF)], axis=0)
        grad, attn, out, up, down = lax.optimization_barrier((grad, attn, out, up, down))
        attn, out = lax.psum((attn, out), ("section", "replica"))
        out, small = out[:136], out[136:]
        weight_grads[e] = (attn, out, up, down, small)
    attn, out, up, down, small = (
        jnp.where(s == 0, a, b).astype(F32) for a, b in zip(weight_grads[0], weight_grads[1])
    )
    attn = jnp.concatenate(
        [join_heads([attn[j][:, i * TH : (i + 1) * TH] for j in range(CHIPS)]) for i in (2, 0, 1)], axis=-1
    )
    up = jnp.concatenate([up[j] for j in range(CHIPS)], axis=-1)
    pieces = lax.dynamic_slice(small, (0, 136 * f), (6, 136))
    piece_up = lax.dynamic_slice(small, (6 + y, 544 * c), (1, 544))
    piece_attn = lax.dynamic_slice(small, (10 + f // 4, 272 * (f % 4)), (1, 272))

    def swap_layers(values):
        mine = jnp.where(s == 0, values[0], values[1])
        theirs = jnp.where(s == 0, values[1], values[0])
        received = lax.ppermute(theirs, "section", [(0, 1), (1, 0)])
        pair_up = jnp.stack([jnp.where(s == 0, mine, received), jnp.where(s == 0, received, mine)])
        return pair_up[None, :, None]

    return (
        swap_layers(acts),
        swap_layers(in_grads),
        attn[None],
        out[None],
        up[None],
        down[None],
        piece_attn,
        pieces[4:5],
        piece_up,
        pieces[5:6],
        pieces[0:4:2][None],
        pieces[1:4:2][None],
    )


def solution(mesh):
    placed = (
        P(None, "replica", "fsdp", None),
        P(None, "replica", "fsdp", None),
        P("section", "fsdp", None),
        P("section", "fsdp", None),
        P("section", "fsdp", None),
        P("section", "fsdp", None),
        P("section", "fsdp"),
        P("section", "fsdp"),
        P("section", "fsdp"),
        P("section", "fsdp"),
        P("section", None, "fsdp"),
        P("section", None, "fsdp"),
    )
    return jax.shard_map(
        on_device,
        mesh=mesh,
        in_specs=placed,
        out_specs=(
            P("section", None, "replica", "fsdp", None),
            P("section", None, "replica", "fsdp", None),
        )
        + placed[2:],
        check_vma=False,
    )
```

```python
import functools

import jax
import jax.numpy as jnp
from jax import lax
from jax.experimental import pallas as pl
from jax.experimental.pallas import tpu as pltpu
from jax.sharding import PartitionSpec as P

D = 1088
FF = 4352
HEADS = 17
HD = 64
BLK = 64
CHIPS = 4
ROWS = BLK * CHIPS
SLOTS = 5
TH = SLOTS * HD
TQKV = 3 * TH
SCALE = HD**-0.5
EPS = 1e-5
MESH = pl.DeviceIdType.MESH
BF = jnp.bfloat16
F32 = jnp.float32
ANY = pl.BlockSpec(memory_space=pl.ANY)
VMEM = pl.BlockSpec(memory_space=pltpu.VMEM)
DMA = pltpu.SemaphoreType.DMA
LIMIT = 56 * 1024 * 1024
COST = pl.CostEstimate(flops=10_000_000, bytes_accessed=10_000, transcendentals=0)


def dot(a, b):
    return lax.dot_general(a, b, (((1,), (0,)), ((), ())), preferred_element_type=F32)


def dot_nt(a, b):
    return lax.dot_general(a, b, (((1,), (1,)), ((), ())), preferred_element_type=F32)


def dot_tn(a, b):
    return lax.dot_general(a, b, (((0,), (0,)), ((), ())), preferred_element_type=F32)


def chunks(n, size=256):
    return [(i, min(size, n - i)) for i in range(0, n, size)]


def place():
    f = lax.axis_index("fsdp")
    return f // 2, f % 2


def ring(y, k):
    return lax.rem(y + k, CHIPS)


def at_chip(y, c):
    return {"fsdp": 2 * y + c}


def greet(targets):
    barrier = pltpu.get_barrier_semaphore()
    for target in targets:
        pl.semaphore_signal(barrier, inc=1, device_id=target, device_id_type=MESH)
    return functools.partial(pl.semaphore_wait, barrier, len(targets))


def remote(src, dst, send, recv, target):
    return pltpu.make_async_remote_copy(
        src_ref=src, dst_ref=dst, send_sem=send, recv_sem=recv, device_id=target, device_id_type=MESH
    )


def slot(ref, y):
    return ref.at[pl.ds(pl.multiple_of(y * BLK, BLK), BLK)]


ORDER = (2, 1, 3)


def gather_start(full, y, c, send, recv):
    for k in ORDER:
        remote(slot(full, y), slot(full, y), send.at[k - 1], recv.at[k - 1], at_chip(ring(y, k), c)).start()


def gather_wait(full, y, c, send, recv):
    for k in (1, 3, 2):
        source = ring(y, 4 - k)
        remote(slot(full, source), slot(full, source), send.at[k - 1], recv.at[k - 1], at_chip(ring(y, k), c)).wait()


def scatter_start(acc, out_buf, in_buf, y, c, send, recv):
    for k in ORDER:
        target = ring(y, k)
        out_buf[k - 1] = slot(acc, target)[...].astype(BF)
        remote(out_buf.at[k - 1], in_buf.at[k - 1], send.at[k - 1], recv.at[k - 1], at_chip(target, c)).start()


def scatter_wait(acc, out_buf, in_buf, y, c, send, recv):
    total = slot(acc, y)[...]
    for k in (1, 3, 2):
        remote(out_buf.at[k - 1], in_buf.at[k - 1], send.at[k - 1], recv.at[k - 1], at_chip(ring(y, k), c)).wait()
        total = total + in_buf[k - 1].astype(F32)
    return total


def stats(v):
    centre = v - jnp.mean(v, axis=-1, keepdims=True)
    scale = lax.rsqrt(jnp.mean(centre * centre, axis=-1, keepdims=True) + EPS)
    return centre * scale, scale


def norm(v, gain, shift):
    return stats(v)[0] * gain + shift


def norm_back(d, v, gain):
    vh, scale = stats(v)
    q = d * gain
    grad = scale * (q - jnp.mean(q, axis=-1, keepdims=True) - vh * jnp.mean(q * vh, axis=-1, keepdims=True))
    return grad, jnp.sum(d * vh, axis=0, keepdims=True), jnp.sum(d, axis=0, keepdims=True)


GELU_A = 0.7978845608028654
GELU_B = 0.044715


def gelu(h):
    return 0.5 * h * (1.0 + jnp.tanh(GELU_A * (h + GELU_B * h * h * h)))


def gelu_slope(h):
    t = jnp.tanh(GELU_A * (h + GELU_B * h * h * h))
    return 0.5 * (1.0 + t) + 0.5 * h * (1.0 - t * t) * (GELU_A * (1.0 + 3.0 * GELU_B * h * h))


def masks(c):
    row = lax.broadcasted_iota(jnp.int32, (ROWS, ROWS), 0)
    col = lax.broadcasted_iota(jnp.int32, (ROWS, ROWS), 1)
    own = row >= col
    other = (row // BLK) >= (col // BLK) + (1 - c)
    return own, other


def load(pairs, sems):
    copies = [pltpu.make_async_copy(src, dst, sems.at[i]) for i, (src, dst) in enumerate(pairs)]
    for copy in copies:
        copy.start()
    return copies


def out_rows(wo_hbm, wo, e, y):
    start = pl.multiple_of(48 - 16 * y, 16)
    return [(wo_hbm.at[e, pl.ds(start, 256)], wo.at[0:256]), (wo_hbm.at[e, 256:320], wo.at[256:320])]


def out_wait(weights, wo, y):
    weights[1].wait()
    weights[2].wait()

    @pl.when(y < 3)
    def _():
        wo[256:320] = jnp.zeros((HD, D), BF)


def chip_row(y, rows):
    return jnp.where(lax.broadcasted_iota(jnp.int32, (CHIPS, 1), 0) == y, rows, 0.0)


def head_bias(vecs, row, y):
    last = jnp.where(y == 3, vecs[row : row + 1, 1024:D], 0.0)
    return jnp.concatenate([vecs[row : row + 1, pl.ds(pl.multiple_of(256 * y, 256), 256)], last], axis=-1)


def attend_forward(e, x, w_hbm, wo_hbm, vecs, middle, normed, queries, kv, kv_other, logsum, attended,
                   w, wo, acc, out_buf, in_buf, ls, gs, gr, ss, sr, ks, kr):
    y, c = place()
    peers = [at_chip(ring(y, k), c) for k in (1, 2, 3)]
    sibling = at_chip(y, 1 - c)
    arrived = greet(peers + [sibling])
    weights = load([(w_hbm.at[e], w)] + out_rows(wo_hbm, wo, e, y), ls)
    slot(normed, y)[...] = norm(x[...], vecs[0:1], vecs[1:2]).astype(BF)
    arrived()
    gather_start(normed, y, c, gs, gr)
    own, other = masks(c)
    weights[0].wait()
    gather_wait(normed, y, c, gs, gr)
    rows = normed[...]
    bias = jnp.concatenate([jnp.zeros((1, TH), F32), head_bias(vecs, 11, y)], axis=-1)
    for at, size in chunks(2 * TH):
        kv[:, at : at + size] = (dot(rows, w[:, at : at + size]) + bias[:, at : at + size]).astype(BF)
    swap = remote(kv, kv_other, ks, kr, sibling)
    swap.start()
    queries[...] = (dot(rows, w[:, 2 * TH :]) + head_bias(vecs, 10, y)).astype(BF)
    swap.wait()
    for h in range(SLOTS):
        at = h * HD
        q = queries[:, at : at + HD]
        s_own = jnp.where(own, dot_nt(q, kv[:, at : at + HD]) * SCALE, -1e30)
        s_other = jnp.where(other, dot_nt(q, kv_other[:, at : at + HD]) * SCALE, -1e30)
        top = jnp.maximum(jnp.max(s_own, axis=-1, keepdims=True), jnp.max(s_other, axis=-1, keepdims=True))
        e_own = jnp.exp(s_own - top)
        e_other = jnp.exp(s_other - top)
        total = jnp.sum(e_own, axis=-1, keepdims=True) + jnp.sum(e_other, axis=-1, keepdims=True)
        logsum[:, h : h + 1] = top + jnp.log(total)
        inverse = 1.0 / total
        a_own = (e_own * inverse).astype(BF)
        a_other = (e_other * inverse).astype(BF)
        out = dot(a_own, kv[:, TH + at : TH + at + HD]) + dot(a_other, kv_other[:, TH + at : TH + at + HD])
        attended[:, at : at + HD] = out.astype(BF)
    out_wait(weights, wo, y)
    mixed = attended[...]
    for at, size in chunks(D):
        acc[:, at : at + size] = dot(mixed, wo[:, at : at + size])
    scatter_start(acc, out_buf, in_buf, y, c, ss, sr)
    base = x[...] + vecs[4:5]
    middle[...] = base + scatter_wait(acc, out_buf, in_buf, y, c, ss, sr)


def feed_forward(e, middle, wu_hbm, wd_hbm, vecs, result, normed, hidden, active,
                 wu, wd, acc, out_buf, in_buf, ls, gs, gr, ss, sr):
    y, c = place()
    arrived = greet([at_chip(ring(y, k), c) for k in (1, 2, 3)])
    weights = load([(wu_hbm.at[e], wu), (wd_hbm.at[e], wd)], ls)
    slot(normed, y)[...] = norm(middle[...], vecs[2:3], vecs[3:4]).astype(BF)
    arrived()
    gather_start(normed, y, c, gs, gr)
    bias = jnp.sum(chip_row(y, vecs[6:10]), axis=0, keepdims=True)
    weights[0].wait()
    gather_wait(normed, y, c, gs, gr)
    rows = normed[...]
    for at, size in chunks(D):
        h = dot(rows, wu[:, at : at + size]) + bias[:, at : at + size]
        hidden[:, at : at + size] = h
        active[:, at : at + size] = gelu(h).astype(BF)
    weights[1].wait()
    rows = active[...]
    for at, size in chunks(D):
        acc[:, at : at + size] = dot(rows, wd[:, at : at + size])
    scatter_start(acc, out_buf, in_buf, y, c, ss, sr)
    base = middle[...] + vecs[5:6]
    result[...] = base + scatter_wait(acc, out_buf, in_buf, y, c, ss, sr)


def feed_back(e, grad, wu_hbm, wd_hbm, vecs, middle, normed, hidden, active, grad_middle, grad_up, grad_down, small,
              wu, wd, full, gh, acc, out_buf, in_buf, ls, gs, gr, ss, sr, reduce=None):
    y, c = place()
    peers = [at_chip(ring(y, k), c) for k in (1, 2, 3)]
    arrived = greet(peers) if reduce is None else greet_owners(peers + [at_chip(y, 1 - c)], reduce.pieces.layer)
    weights = load([(wu_hbm.at[e], wu), (wd_hbm.at[e], wd)], ls)
    own_rows = grad[...].astype(BF)
    slot(full, y)[...] = own_rows
    arrived()
    gather_start(full, y, c, gs, gr)
    if reduce is not None:
        reduce.begin(y, c)
    small[...] = jnp.zeros_like(small)
    small[3:4] = jnp.sum(own_rows.astype(F32), axis=0, keepdims=True)
    weights[1].wait()
    gather_wait(full, y, c, gs, gr)
    if reduce is not None:
        reduce.middle(y, c)
    rows = full[...]
    for at, size in chunks(D):
        slope = gelu_slope(hidden[:, at : at + size])
        part = (dot_nt(rows, wd[at : at + size, :]) * slope).astype(BF)
        gh[:, at : at + size] = part
        small[2:3, at : at + size] = jnp.sum(part.astype(F32), axis=0, keepdims=True)
    weights[0].wait()
    rows = gh[...]
    for at, size in chunks(D):
        acc[:, at : at + size] = dot_nt(rows, wu[at : at + size, :])
    scatter_start(acc, out_buf, in_buf, y, c, ss, sr)
    for at, size in chunks(D):
        grad_up[at : at + size, :] = dot_tn(normed[:, at : at + size], gh[...]).astype(BF)
        grad_down[at : at + size, :] = dot_tn(active[:, at : at + size], full[...]).astype(BF)
    d = scatter_wait(acc, out_buf, in_buf, y, c, ss, sr)
    back, gain, shift = norm_back(d, middle[...], vecs[2:3])
    small[0:1] = gain
    small[1:2] = shift
    grad_middle[...] = grad[...] + back
    if reduce is not None:
        reduce.finish()


def attend_back(e, grad, w_hbm, wo_hbm, vecs, x, normed, queries, kv, kv_other, logsum, attended,
                grad_x, grad_attn, grad_out, small, small_bias,
                w, wo, full, ga, gj, part_out, part_in, part_own, rows_out, edge, acc, out_buf, in_buf, ls, gs, gr, ss, sr, ks, kr, es, er,
                reduce):
    y, c = place()
    peers = [at_chip(ring(y, k), c) for k in (1, 2, 3)]
    sibling = at_chip(y, 1 - c)
    arrived = greet_owners(peers + [sibling], e)
    weights = load([(w_hbm.at[e], w)] + out_rows(wo_hbm, wo, e, y), ls)
    own_rows = grad[...].astype(BF)
    slot(full, y)[...] = own_rows
    arrived()
    gather_start(full, y, c, gs, gr)
    reduce.begin(y, c)
    small[...] = jnp.zeros_like(small)
    small[2:3] = jnp.sum(own_rows.astype(F32), axis=0, keepdims=True)
    own, other = masks(c)
    out_wait(weights, wo, y)
    gather_wait(full, y, c, gs, gr)
    reduce.middle(y, c)
    ga[...] = dot_nt(full[...], wo[...]).astype(BF)
    for h in range(SLOTS):
        at = h * HD
        q = queries[:, at : at + HD]
        g = ga[:, at : at + HD]
        lse = logsum[:, h : h + 1]
        k_own, k_other = kv[:, at : at + HD], kv_other[:, at : at + HD]
        v_own, v_other = kv[:, TH + at : TH + at + HD], kv_other[:, TH + at : TH + at + HD]
        p_own = jnp.exp(jnp.where(own, dot_nt(q, k_own) * SCALE, -1e30) - lse)
        p_other = jnp.exp(jnp.where(other, dot_nt(q, k_other) * SCALE, -1e30) - lse)
        gp_own = dot_nt(g, v_own)
        gp_other = dot_nt(g, v_other)
        delta = jnp.sum(p_own * gp_own, axis=-1, keepdims=True) + jnp.sum(p_other * gp_other, axis=-1, keepdims=True)
        s_own = (p_own * (gp_own - delta)).astype(BF)
        s_other = (p_other * (gp_other - delta)).astype(BF)
        gj[:, 2 * TH + at : 2 * TH + at + HD] = ((dot(s_own, k_own) + dot(s_other, k_other)) * SCALE).astype(BF)
        part_own[:, at : at + HD] = dot_tn(s_own, q) * SCALE
        part_out[:, at : at + HD] = (dot_tn(s_other, q) * SCALE).astype(BF)
        part_own[:, TH + at : TH + at + HD] = dot_tn(p_own.astype(BF), g)
        part_out[:, TH + at : TH + at + HD] = dot_tn(p_other.astype(BF), g).astype(BF)
    swap = remote(part_out, part_in, ks, kr, sibling)
    swap.start()
    for at, size in chunks(D):
        rows_out[:, at : at + size] = dot_tn(attended[...], full[:, at : at + size]).astype(BF)
    lend = remote(rows_out.at[0:HD], edge, es, er, at_chip(ring(y, 3), c))
    lend.start()
    weights[0].wait()
    swap.wait()
    gj[:, : 2 * TH] = (part_own[...] + part_in[...].astype(F32)).astype(BF)
    rows = gj[...]
    for at, size in chunks(D):
        acc[:, at : at + size] = dot_nt(rows, w[at : at + size, :])
    scatter_start(acc, out_buf, in_buf, y, c, ss, sr)
    for at, size in chunks(D):
        grad_attn[at : at + size, :] = dot_tn(normed[:, at : at + size], gj[...]).astype(BF)
    small_bias[...] = jnp.zeros_like(small_bias)
    small_bias[0:1] = jnp.sum(gj[...].astype(F32), axis=0, keepdims=True)
    d = scatter_wait(acc, out_buf, in_buf, y, c, ss, sr)
    back, gain, shift = norm_back(d, x[...], vecs[0:1])
    small[0:1] = gain
    small[1:2] = shift
    grad_x[...] = grad[...] + back
    lend.wait()

    @pl.when(y < 3)
    def _():
        rows_out[256:320] = edge[...]

    grad_out[...] = rows_out[pl.ds(pl.multiple_of(16 * y, 16), 272)]
    reduce.finish()


def plane():
    s, r = lax.axis_index("section"), lax.axis_index("replica")
    return s, r // 2, r % 2, s * 8 + r


def at_plane(q):
    return {"section": q // 8, "replica": lax.rem(q, 8)}


def greet_owners(targets, layer):
    s, x, h, me = plane()
    barrier = pltpu.get_barrier_semaphore()
    for target in targets:
        pl.semaphore_signal(barrier, inc=1, device_id=target, device_id_type=MESH)

    @pl.when(s == layer)
    def _():
        for j in range(1, 16):
            q = lax.rem(me + j, 16)
            pl.semaphore_signal(barrier, inc=1, device_id=at_plane(q), device_id_type=MESH)

    return lambda: pl.semaphore_wait(barrier, len(targets) + jnp.where(s == layer, 7, 8))


class Pieces:
    def __init__(self, layer, groups, send, recv):
        self.layer, self.groups, self.send, self.recv = layer, groups, send, recv

    def copies(self):
        s, x, h, me = plane()
        for g, (half, pieces, landing, out) in enumerate(self.groups):
            for dx in (2, 1, 3, 0):
                xt = lax.rem(x + dx, 4)
                owner = self.layer * 8 + xt * 2 + half
                rel = lax.rem(me - owner + 15, 16)
                copy = remote(pieces.at[xt], landing.at[rel], self.send.at[g, dx], self.recv.at[g, rel], at_plane(owner))
                yield me != owner, copy

    def start(self):
        for remote_one, copy in self.copies():
            pl.when(remote_one)(copy.start)

    def finish(self):
        s, x, h, me = plane()
        for remote_one, copy in self.copies():
            pl.when(remote_one)(copy.wait_send)
        for g, (half, pieces, landing, out) in enumerate(self.groups):
            mine = jnp.logical_and(s == self.layer, h == half)

            def collect(g=g, pieces=pieces, landing=landing, out=out):
                for rel in range(15):
                    remote(pieces.at[x], landing.at[rel], self.send.at[g, 0], self.recv.at[g, rel], at_plane(me)).wait_recv()
                for at in range(0, 136, 8):
                    total = pieces[x, at : at + 8].astype(F32)
                    for rel in range(15):
                        total = total + landing[rel, at : at + 8].astype(F32)
                    out[at : at + 8] = total.astype(BF)

            pl.when(mine)(collect)


class FeedReduce:
    def __init__(self, layer, up, down, out, own, other, landing, ls, cs, cr, send, recv):
        self.sources = (up, down)
        self.out, self.own, self.other = out, own, other
        self.ls, self.cs, self.cr = ls, cs, cr
        self.pieces = Pieces(layer, [(0, own.at[0], landing, out), (1, own.at[1], landing, out)], send, recv)

    def keeps(self, c):
        up, down = self.sources
        return [
            pltpu.make_async_copy(up.at[:, c], self.own.at[0], self.ls.at[0]),
            pltpu.make_async_copy(down.at[c], self.own.at[1], self.ls.at[1]),
        ]

    def swaps(self, y, c):
        up, down = self.sources
        sibling = at_chip(y, 1 - c)
        return [
            remote(up.at[:, 1 - c], self.other.at[0], self.cs.at[0], self.cr.at[0], sibling),
            remote(down.at[1 - c], self.other.at[1], self.cs.at[1], self.cr.at[1], sibling),
        ]

    def begin(self, y, c):
        for copy in self.keeps(c) + self.swaps(y, c):
            copy.start()
        self.out[...] = jnp.zeros_like(self.out)

    def middle(self, y, c):
        for copy in self.keeps(c) + self.swaps(y, c):
            copy.wait()

        def add(i, carry):
            self.own[i // 4, i % 4] = (
                self.own[i // 4, i % 4].astype(F32) + self.other[i // 4, i % 4].astype(F32)
            ).astype(BF)
            return carry

        lax.fori_loop(0, 8, add, 0)
        self.pieces.start()

    def finish(self):
        self.pieces.finish()


FEED_SCRATCH = [
    pltpu.VMEM((2, 4, 136, D), BF),
    pltpu.VMEM((2, 4, 136, D), BF),
    pltpu.VMEM((15, 136, D), BF),
    DMA((2,)),
    DMA((2,)),
    DMA((2,)),
    DMA((2, 4)),
    DMA((2, 15)),
]


class AttendReduce:
    def __init__(self, layer, wide, rows, out_a, out_b, out_o, own_w, other_w, own_r, other_r, pa, pb, po,
                 land_a, land_b, land_o, ls, cs, cr, send, recv):
        self.wide, self.rows = wide, rows
        self.outs = (out_a, out_b, out_o)
        self.own_w, self.other_w, self.own_r, self.other_r = own_w, other_w, own_r, other_r
        self.pa, self.pb, self.po = pa, pb, po
        self.ls, self.cs, self.cr = ls, cs, cr
        self.pieces = Pieces(
            layer, [(0, pa, land_a, out_a), (1, pb, land_b, out_b), (1, po, land_o, out_o)], send, recv
        )

    def keeps(self, c):
        return [
            pltpu.make_async_copy(self.wide.at[:, c], self.own_w, self.ls.at[0]),
            pltpu.make_async_copy(self.rows.at[c], self.own_r, self.ls.at[1]),
        ]

    def swaps(self, y, c):
        sibling = at_chip(y, 1 - c)
        return [
            remote(self.wide.at[:, 1 - c], self.other_w, self.cs.at[0], self.cr.at[0], sibling),
            remote(self.rows.at[1 - c], self.other_r, self.cs.at[1], self.cr.at[1], sibling),
        ]

    def begin(self, y, c):
        for copy in self.keeps(c) + self.swaps(y, c):
            copy.start()
        for out in self.outs:
            out[...] = jnp.zeros_like(out)

    def middle(self, y, c):
        for copy in self.keeps(c) + self.swaps(y, c):
            copy.wait()
        for i in range(4):
            block = self.own_w[i].astype(F32) + self.other_w[i].astype(F32)
            self.pa[i] = block[:, :640].astype(BF)
            self.pb[i] = block[:, 640:].astype(BF)
            chunk = self.own_r[:, 256 * i : 256 * i + 256].astype(F32) + self.other_r[:, 256 * i : 256 * i + 256].astype(F32)
            self.po[i, :, :256] = chunk.astype(BF)
            if i < 3:
                self.po[i, :, 256:] = jnp.zeros((136, HD), BF)
        chunk = self.own_r[:, 1024:].astype(F32) + self.other_r[:, 1024:].astype(F32)
        self.po[3, :, 256:] = chunk.astype(BF)
        self.pieces.start()

    def finish(self):
        self.pieces.finish()


ATTEND_SCRATCH = [
    pltpu.VMEM((4, 136, TQKV), BF),
    pltpu.VMEM((4, 136, TQKV), BF),
    pltpu.VMEM((136, D), BF),
    pltpu.VMEM((136, D), BF),
    pltpu.VMEM((4, 136, 640), BF),
    pltpu.VMEM((4, 136, 320), BF),
    pltpu.VMEM((4, 136, 320), BF),
    pltpu.VMEM((15, 136, 640), BF),
    pltpu.VMEM((15, 136, 320), BF),
    pltpu.VMEM((15, 136, 320), BF),
    DMA((2,)),
    DMA((2,)),
    DMA((2,)),
    DMA((3, 4)),
    DMA((3, 15)),
]


def feed_back_reduce(e, layer, grad, wu_hbm, wd_hbm, vecs, middle, normed, hidden, active, wide, rows,
                     grad_middle, grad_up, grad_down, small, out_a, out_b, out_o, *scratch):
    own, extra = scratch[: 4 + len(MOVE)], scratch[4 + len(MOVE) :]
    reduce = AttendReduce(layer, wide, rows, out_a, out_b, out_o, *extra)
    feed_back(e, grad, wu_hbm, wd_hbm, vecs, middle, normed, hidden, active, grad_middle, grad_up, grad_down, small,
              *own, reduce=reduce)


def attend_back_reduce(e, grad, w_hbm, wo_hbm, vecs, x, normed, queries, kv, kv_other, logsum, attended, up, down,
                       grad_x, grad_attn, grad_out, small, small_bias, out, *scratch):
    extra = scratch[len(scratch) - len(FEED_SCRATCH) :]
    own = scratch[: len(scratch) - len(FEED_SCRATCH)]
    reduce = FeedReduce(e, up, down, out, *extra)
    attend_back(e, grad, w_hbm, wo_hbm, vecs, x, normed, queries, kv, kv_other, logsum, attended,
                grad_x, grad_attn, grad_out, small, small_bias, *own, reduce=reduce)


def shape(dims, kind):
    return jax.ShapeDtypeStruct(dims, kind)


MOVE = [
    pltpu.VMEM((ROWS, D), F32),
    pltpu.VMEM((3, BLK, D), BF),
    pltpu.VMEM((3, BLK, D), BF),
    DMA((3,)),
    DMA((3,)),
    DMA((3,)),
    DMA((3,)),
    DMA((3,)),
]


def call(body, name, number, outs, ins, scratch):
    return pl.pallas_call(
        body,
        name=name,
        out_shape=outs,
        in_specs=ins,
        out_specs=[VMEM] * len(outs),
        scratch_shapes=scratch,
        cost_estimate=COST,
        compiler_params=pltpu.CompilerParams(collective_id=number, has_side_effects=True, vmem_limit_bytes=LIMIT),
    )


def run_attend_forward(e, x, w, wo, vecs):
    outs = [
        shape((BLK, D), F32),
        shape((ROWS, D), BF),
        shape((ROWS, TH), BF),
        shape((ROWS, 2 * TH), BF),
        shape((ROWS, 2 * TH), BF),
        shape((ROWS, 128), F32),
        shape((ROWS, TH), BF),
    ]
    scratch = [pltpu.VMEM((D, TQKV), BF), pltpu.VMEM((TH, D), BF)] + MOVE + [DMA, DMA]
    return call(functools.partial(attend_forward, e), "attend_forward_%d" % e, e, outs, [VMEM, ANY, ANY, VMEM], scratch)(x, w, wo, vecs)


def run_feed_forward(e, middle, wu, wd, vecs):
    outs = [shape((BLK, D), F32), shape((ROWS, D), BF), shape((ROWS, D), F32), shape((ROWS, D), BF)]
    scratch = [pltpu.VMEM((D, D), BF), pltpu.VMEM((D, D), BF)] + MOVE
    return call(functools.partial(feed_forward, e), "feed_forward_%d" % e, 2 + e, outs, [VMEM, ANY, ANY, VMEM], scratch)(middle, wu, wd, vecs)


PIECE_A = shape((136, 640), BF)
PIECE_B = shape((136, 320), BF)
PIECE_U = shape((136, D), BF)


def run_feed_back(e, grad, wu, wd, vecs, middle, normed, hidden, active, before=None):
    outs = [shape((BLK, D), F32), shape((D, D), BF), shape((D, D), BF), shape((8, D), F32)]
    scratch = [
        pltpu.VMEM((D, D), BF),
        pltpu.VMEM((D, D), BF),
        pltpu.VMEM((ROWS, D), BF),
        pltpu.VMEM((ROWS, D), BF),
    ] + MOVE
    ins = [VMEM, ANY, ANY] + [VMEM] * 5
    if before is None:
        return call(functools.partial(feed_back, e), "feed_back_%d" % e, 4 + e, outs, ins, scratch)(
            grad, wu, wd, vecs, middle, normed, hidden, active
        )
    outs += [PIECE_A, PIECE_B, PIECE_B]
    body = functools.partial(feed_back_reduce, e, 1 - e)
    return call(body, "feed_back_%d" % e, 4 + e, outs, ins + [ANY, ANY], scratch + ATTEND_SCRATCH)(
        grad, wu, wd, vecs, middle, normed, hidden, active, *before
    )


def run_attend_back(e, grad, w, wo, vecs, x, saved, up, down):
    outs = [
        shape((BLK, D), F32),
        shape((D, TQKV), BF),
        shape((272, D), BF),
        shape((8, D), F32),
        shape((8, TQKV), F32),
        PIECE_U,
    ]
    scratch = [
        pltpu.VMEM((D, TQKV), BF),
        pltpu.VMEM((TH, D), BF),
        pltpu.VMEM((ROWS, D), BF),
        pltpu.VMEM((ROWS, TH), BF),
        pltpu.VMEM((ROWS, TQKV), BF),
        pltpu.VMEM((ROWS, 2 * TH), BF),
        pltpu.VMEM((ROWS, 2 * TH), BF),
        pltpu.VMEM((ROWS, 2 * TH), F32),
        pltpu.VMEM((TH, D), BF),
        pltpu.VMEM((HD, D), BF),
    ] + MOVE + [DMA, DMA, DMA, DMA] + FEED_SCRATCH
    body = functools.partial(attend_back_reduce, e)
    return call(body, "attend_back_%d" % e, 6 + e, outs, [VMEM, ANY, ANY] + [VMEM] * 8 + [ANY, ANY], scratch)(
        grad, w, wo, vecs, x, *saved, up, down
    )


def spread(send_a, send_u, send_d, send_o, send_v, wa, wu, wd, wo, wv, local, ysend, yrecv, zsend, zrecv, csend, crecv):
    s = lax.axis_index("section")
    y, c = place()
    replica = lax.axis_index("replica")
    flipped = replica // 2 * 2 + (1 - replica % 2)
    near = {"section": 1 - s}
    far = {"section": 1 - s, "replica": flipped}
    sibling = at_chip(y, 1 - c)
    peers = [at_chip(ring(y, k), c) for k in (1, 2, 3)]
    arrived = greet(peers + [sibling, near, far])
    keeps = load(
        [
            (send_a.at[y], wa.at[s, y, c]),
            (send_u.at[y], wu.at[s, y, c]),
            (send_d, wd.at[s, c]),
            (send_o, wo.at[s, c]),
            (send_v, wv.at[s, y, c]),
        ],
        local,
    )
    arrived()

    def along_y(k, back):
        target = ring(y, k)
        place_in = ring(y, 4 - k) if back else y
        return [
            remote(send_v, wv.at[s, place_in, c], ysend.at[0, k - 1], yrecv.at[0, k - 1], at_chip(target, c)),
            remote(send_a.at[target], wa.at[s, place_in, c], ysend.at[1, k - 1], yrecv.at[1, k - 1], at_chip(target, c)),
            remote(send_u.at[target], wu.at[s, place_in, c], ysend.at[2, k - 1], yrecv.at[2, k - 1], at_chip(target, c)),
        ]

    def along_z(layer):
        return [
            remote(wv.at[layer, :, c], wv.at[layer, :, c], zsend.at[0], zrecv.at[0], near),
            remote(wa.at[layer, 0:2, c], wa.at[layer, 0:2, c], zsend.at[1], zrecv.at[1], near),
            remote(wa.at[layer, 2:4, c], wa.at[layer, 2:4, c], zsend.at[2], zrecv.at[2], far),
            remote(wo.at[layer, c], wo.at[layer, c], zsend.at[3], zrecv.at[3], far),
            remote(wu.at[layer, 0:2, c], wu.at[layer, 0:2, c], zsend.at[4], zrecv.at[4], near),
            remote(wu.at[layer, 2:4, c], wu.at[layer, 2:4, c], zsend.at[5], zrecv.at[5], far),
            remote(wd.at[layer, c, 0:272], wd.at[layer, c, 0:272], zsend.at[6], zrecv.at[6], near),
            remote(wd.at[layer, c, 272:544], wd.at[layer, c, 272:544], zsend.at[7], zrecv.at[7], far),
        ]

    def across(layer, i, core):
        return [
            remote(wv.at[layer, :, core], wv.at[layer, :, core], csend.at[i, 0], crecv.at[i, 0], sibling),
            remote(wa.at[layer, :, core], wa.at[layer, :, core], csend.at[i, 1], crecv.at[i, 1], sibling),
            remote(wo.at[layer, core], wo.at[layer, core], csend.at[i, 2], crecv.at[i, 2], sibling),
            remote(wu.at[layer, :, core], wu.at[layer, :, core], csend.at[i, 3], crecv.at[i, 3], sibling),
            remote(wd.at[layer, core], wd.at[layer, core], csend.at[i, 4], crecv.at[i, 4], sibling),
        ]

    sent_y = [along_y(k, False) for k in (1, 2, 3)]
    got_y = [along_y(k, True) for k in (1, 2, 3)]
    sent_z, got_z = along_z(s), along_z(1 - s)
    sent_c = [across(s, 0, c), across(1 - s, 1, c)]
    got_c = [across(s, 0, 1 - c), across(1 - s, 1, 1 - c)]
    for kind in (0, 1):
        for k in (1, 0, 2):
            sent_y[k][kind].start()
    keeps[3].wait()
    sent_z[3].start()
    sent_c[0][2].start()
    keeps[2].wait()
    sent_z[6].start()
    sent_z[7].start()
    sent_c[0][4].start()
    for kind, keep, zs, cross in ((0, 4, (0,), 0), (1, 0, (1, 2), 1)):
        keeps[keep].wait()
        for k in range(3):
            got_y[k][kind].wait_recv()
        for z in zs:
            sent_z[z].start()
        sent_c[0][cross].start()
    for k in (1, 0, 2):
        sent_y[k][2].start()
    for zs, cross in (((3,), 2), ((6, 7), 4), ((0,), 0), ((1, 2), 1)):
        for z in zs:
            got_z[z].wait_recv()
        sent_c[1][cross].start()
    keeps[1].wait()
    for k in range(3):
        got_y[k][2].wait_recv()
    for z in (4, 5):
        sent_z[z].start()
    sent_c[0][3].start()
    for z in (4, 5):
        got_z[z].wait_recv()
    sent_c[1][3].start()
    for i in range(2):
        for cross in range(5):
            got_c[i][cross].wait_recv()
    for k in range(3):
        for kind in range(3):
            sent_y[k][kind].wait_send()
    for z in range(8):
        sent_z[z].wait_send()
    for i in range(2):
        for cross in range(5):
            sent_c[i][cross].wait_send()


def run_spread(a, u, d, o, v):
    outs = [
        shape((2, 4, 2, 136, TQKV), BF),
        shape((2, 4, 2, 136, D), BF),
        shape((2, 2, 544, D), BF),
        shape((2, 2, 192, D), BF),
        shape((2, 4, 2, 16, D), BF),
    ]
    return pl.pallas_call(
        spread,
        name="spread",
        out_shape=outs,
        in_specs=[ANY] * 5,
        out_specs=[ANY] * 5,
        scratch_shapes=[DMA((5,)), DMA((3, 3)), DMA((3, 3)), DMA((8,)), DMA((8,)), DMA((2, 5)), DMA((2, 5))],
        compiler_params=pltpu.CompilerParams(collective_id=8, has_side_effects=True),
    )(a, u, d, o, v)


def build_small(buf, one, two, heads, y):
    buf[...] = jnp.zeros_like(buf)
    buf[0:2] = one[0:2]
    buf[2:4] = two[0:2]
    buf[4:5] = one[2:3]
    buf[5:6] = two[3:4]
    buf[6:10] = chip_row(y, two[2:3])
    for row, at in ((10, 2 * TH), (11, TH)):
        buf[row : row + 1, pl.ds(pl.multiple_of(256 * y, 256), 256)] = heads[0:1, at : at + 256]

        @pl.when(y == 3)
        def _(row=row, at=at):
            buf[row : row + 1, 1024:D] = heads[0:1, at + 256 : at + TH]


def gather_pieces(wide, rows, piece_u, in_a, in_b, in_o, one_0, two_0, heads_0, one_1, two_1, heads_1,
                  up, down, out_a, out_b, out_o, out_small,
                  red_a, red_b, red_o, small, small_c, small_y, small_x, small_z, gs, gr, cs, cr, ys, yr, zs, zr, *extra):
    y, c = place()
    s, x, h, me = plane()
    r = 2 * x + h
    sibling = at_chip(y, 1 - c)
    peers = [at_chip(ring(y, k), c) for k in (1, 2, 3)]
    reduce = AttendReduce(0, wide, rows, red_a, red_b, red_o, *extra)
    barrier = pltpu.get_barrier_semaphore()
    others = [at_plane(lax.rem(me + j, 16)) for j in range(1, 16)]
    sources = [
        {"fsdp": 2 * ring(y, k) + c, "replica": 2 * y + half} for k in (1, 2, 3) for half in (0, 1)
    ]
    for target in peers + [sibling] + others + sources:
        pl.semaphore_signal(barrier, inc=1, device_id=target, device_id_type=MESH)
    build_small(small.at[0], one_0, two_0, heads_0, y)
    build_small(small.at[1], one_1, two_1, heads_1, y)
    pl.semaphore_wait(barrier, 19 + jnp.where(x == y, 0, 8))
    reduce.begin(y, c)
    cross = remote(small, small_c, cs, cr, sibling)
    cross.start()

    kinds = [
        (piece_u, up, 0, True),
        (piece_u, down, 1, False),
        (red_a, out_a, 0, True),
        (red_b, out_b, 1, True),
        (red_o, out_o, 1, False),
    ]

    def sends(i):
        piece, out, half, moves = kinds[i]
        copies = []
        for j in (4, 2, 6, 3, 5, 1, 7, 0):
            target = lax.rem(r + j, 8)
            row = x if moves else y
            index = y if moves else x
            copy = remote(piece, out.at[index], gs.at[i, j], gr.at[i, index], {"fsdp": 2 * row + c, "replica": target})
            copies.append((j, copy))
        return copies

    def start(i):
        piece, out, half, moves = kinds[i]

        @pl.when(h == half)
        def _():
            for j, copy in sends(i):
                if j:
                    copy.start()
                elif moves:
                    pl.when(x != y)(copy.start)

                    @pl.when(x == y)
                    def _():
                        out[y] = piece[...]
                else:
                    out[x] = piece[...]

    def finish(i):
        piece, out, half, moves = kinds[i]

        @pl.when(h == half)
        def _():
            for j, copy in sends(i):
                if j:
                    copy.wait_send()
                elif moves:
                    pl.when(x != y)(copy.wait_send)

        for index in range(4):
            own = jnp.logical_and(h == half, index == (y if moves else x))
            if moves:
                own = jnp.logical_and(own, x == y)
            copy = remote(piece, out.at[index], gs.at[i, 0], gr.at[i, index], sibling)
            pl.when(jnp.logical_not(own))(copy.wait_recv)

    start(0)
    start(1)
    reduce.middle(y, c)
    cross.wait()
    small[...] = small[...] + small_c[...]
    hops = [remote(small, small_y.at[k - 1], ys.at[k - 1], yr.at[k - 1], peers[k - 1]) for k in (1, 2, 3)]
    for hop in hops:
        hop.start()
    for hop in hops:
        hop.wait()
    small_x[...] = (small[...] + small_y[0] + small_y[1] + small_y[2]).astype(BF)

    def plane_copies():
        for j in range(1, 16):
            q = lax.rem(me + j, 16)
            yield remote(small_x.at[q // 8], small_z.at[15 - j], zs.at[j - 1], zr.at[15 - j], at_plane(q))

    for copy in plane_copies():
        copy.start()
    reduce.finish()

    @pl.when(s == 1)
    def _():
        red_a[...] = in_a[...]
        red_b[...] = in_b[...]
        red_o[...] = in_o[...]

    for i in (2, 3, 4):
        start(i)
    total = small_x[s].astype(F32)
    for j, copy in enumerate(plane_copies()):
        copy.wait_send()
    for j in range(15):
        remote(small_x.at[0], small_z.at[j], zs.at[j], zr.at[j], sibling).wait_recv()
        total = total + small_z[j].astype(F32)
    out_small[...] = total
    for i in range(5):
        finish(i)


def run_gather_pieces(wide, rows, piece_u, pieces, smalls):
    outs = [
        shape((4, 136, D), BF),
        shape((4, 136, D), BF),
        shape((4, 136, 640), BF),
        shape((4, 136, 320), BF),
        shape((4, 136, 320), BF),
        shape((16, D), F32),
    ]
    scratch = [
        pltpu.VMEM((136, 640), BF),
        pltpu.VMEM((136, 320), BF),
        pltpu.VMEM((136, 320), BF),
        pltpu.VMEM((2, 16, D), F32),
        pltpu.VMEM((2, 16, D), F32),
        pltpu.VMEM((3, 2, 16, D), F32),
        pltpu.VMEM((2, 16, D), BF),
        pltpu.VMEM((15, 16, D), BF),
        DMA((5, 8)),
        DMA((5, 4)),
        DMA,
        DMA,
        DMA((3,)),
        DMA((3,)),
        DMA((15,)),
        DMA((15,)),
    ] + ATTEND_SCRATCH
    return call(gather_pieces, "gather_pieces", 9, outs, [ANY, ANY] + [VMEM] * 10, scratch)(
        wide, rows, piece_u, *pieces, *smalls
    )


def split_heads(block):
    zero = jnp.zeros(block.shape[:-1] + (HD,), block.dtype)
    return [
        jnp.concatenate([block[..., 256 * j : 256 * j + 256], block[..., 1024:] if j == 3 else zero], axis=-1)
        for j in range(CHIPS)
    ]


def join_heads(blocks):
    return jnp.concatenate([blocks[j][..., :256] for j in range(CHIPS)] + [blocks[3][..., 256:]], axis=-1)


def on_device(inputs, cotangent, weight_attn, weight_out, weight_up, weight_down, bias_attn, bias_out, bias_up,
              bias_down, norm_gain, norm_bias):
    s = lax.axis_index("section")
    f = lax.axis_index("fsdp")
    y, c = f // 2, f % 2
    wa = weight_attn[0]
    q_blocks, k_blocks, v_blocks = (split_heads(wa[:, i * D : (i + 1) * D]) for i in range(3))
    send_a = jnp.stack(
        [jnp.concatenate([k_blocks[j], v_blocks[j], q_blocks[j]], axis=-1) for j in range(CHIPS)]
    )
    send_u = jnp.stack([weight_up[0][:, j * D : (j + 1) * D] for j in range(CHIPS)])
    tail = lax.ppermute(weight_out[0, 88:], "fsdp", [(i, (i + 2) % 8) for i in range(8)])
    send_o = jnp.concatenate([weight_out[0], tail, jnp.zeros((8, D), BF)], axis=0)
    vectors = jnp.stack([norm_gain[0, 0], norm_bias[0, 0], norm_gain[0, 1], norm_bias[0, 1], bias_out[0], bias_down[0]])
    send_v = jnp.concatenate(
        [
            lax.dynamic_update_slice(jnp.zeros((6, D), BF), vectors, (0, 136 * f)),
            lax.dynamic_update_slice(jnp.zeros((4, D), BF), bias_up, (y, 544 * c)),
            lax.dynamic_update_slice(jnp.zeros((6, D), BF), bias_attn, (f // 4, 272 * (f % 4))),
        ]
    )
    wa, wu, wd, wo, wv = run_spread(send_a, send_u, weight_down[0], send_o, send_v)
    wa = wa.reshape(2, D, TQKV)
    wu = wu.reshape(2, D, D)
    wd = wd.reshape(2, D, D)
    wo = jnp.concatenate([wo[:, 1, 136:184], wo[:, 0, :136], wo[:, 1, :136]], axis=1)
    vecs = jnp.sum(wv.astype(F32), axis=(1, 2))
    micro = lax.dynamic_index_in_dim(inputs, s, 0, keepdims=False)[0]
    stream = micro.astype(F32)
    saved, acts = [], []
    for e in range(2):
        middle, *kept = run_attend_forward(e, stream, wa, wo, vecs[e])
        result, *kept_two = run_feed_forward(e, middle, wu, wd, vecs[e])
        saved.append((stream, kept, middle, kept_two))
        acts.append(result.astype(BF))
        stream = acts[-1].astype(F32)
    grad = lax.dynamic_index_in_dim(cotangent, s, 0, keepdims=False)[0].astype(F32)
    in_grads, smalls, piece_u, before = [None, None], [None, None], [None, None], None
    for e in (1, 0):
        x, kept, middle, kept_two = saved[e]
        grad_middle, grad_up, grad_down, two, *pieces = run_feed_back(
            e, grad, wu, wd, vecs[e], middle, *kept_two, before=before
        )
        grad_x, grad_attn, grad_out, one, heads, piece_u[e] = run_attend_back(
            e, grad_middle, wa, wo, vecs[e], x, kept, grad_up.reshape(4, 2, 136, D), grad_down.reshape(2, 4, 136, D)
        )
        in_grads[e] = grad_x.astype(BF)
        grad = in_grads[e].astype(F32)
        before = (grad_attn.reshape(4, 2, 136, TQKV), grad_out.reshape(2, 136, D))
        smalls[e] = (one, two, heads)
    up, down, part_a, part_b, part_o, small = run_gather_pieces(
        *before, jnp.where(s == 0, piece_u[0], piece_u[1]), pieces, smalls[0] + smalls[1]
    )
    up, part_a, part_b, part_o = (a.astype(F32) for a in (up, part_a, part_b, part_o))
    attn = [jnp.concatenate([part_a[j], part_b[j]], axis=-1) for j in range(CHIPS)]
    attn = jnp.concatenate(
        [join_heads([attn[j][:, i * TH : (i + 1) * TH] for j in range(CHIPS)]) for i in (2, 0, 1)], axis=-1
    )
    out = join_heads([part_o[j] for j in range(CHIPS)])
    up = jnp.concatenate([up[j] for j in range(CHIPS)], axis=-1)
    down = down.reshape(544, D).astype(F32)
    pieces = lax.dynamic_slice(small, (0, 136 * f), (6, 136))
    piece_up = lax.dynamic_slice(small, (6 + y, 544 * c), (1, 544))
    piece_attn = lax.dynamic_slice(small, (10 + f // 4, 272 * (f % 4)), (1, 272))

    def swap_layers(values):
        mine = jnp.where(s == 0, values[0], values[1])
        theirs = jnp.where(s == 0, values[1], values[0])
        received = lax.ppermute(theirs, "section", [(0, 1), (1, 0)])
        pair_up = jnp.stack([jnp.where(s == 0, mine, received), jnp.where(s == 0, received, mine)])
        return pair_up[None, :, None]

    return (
        swap_layers(acts),
        swap_layers(in_grads),
        attn[None],
        out[None],
        up[None],
        down[None],
        piece_attn,
        pieces[4:5],
        piece_up,
        pieces[5:6],
        pieces[0:4:2][None],
        pieces[1:4:2][None],
    )


def solution(mesh):
    placed = (
        P(None, "replica", "fsdp", None),
        P(None, "replica", "fsdp", None),
        P("section", "fsdp", None),
        P("section", "fsdp", None),
        P("section", "fsdp", None),
        P("section", "fsdp", None),
        P("section", "fsdp"),
        P("section", "fsdp"),
        P("section", "fsdp"),
        P("section", "fsdp"),
        P("section", None, "fsdp"),
        P("section", None, "fsdp"),
    )
    return jax.shard_map(
        on_device,
        mesh=mesh,
        in_specs=placed,
        out_specs=(
            P("section", None, "replica", "fsdp", None),
            P("section", None, "replica", "fsdp", None),
        )
        + placed[2:],
        check_vma=False,
    )
```

```python
import functools

import jax
import jax.numpy as jnp
from jax import lax
from jax.experimental import pallas as pl
from jax.experimental.pallas import tpu as pltpu
from jax.sharding import PartitionSpec as P

D = 1088
FF = 4352
HEADS = 17
HD = 64
BLK = 64
CHIPS = 4
ROWS = BLK * CHIPS
SLOTS = 5
TH = SLOTS * HD
TQKV = 3 * TH
SCALE = HD**-0.5
EPS = 1e-5
MESH = pl.DeviceIdType.MESH
BF = jnp.bfloat16
F32 = jnp.float32
ANY = pl.BlockSpec(memory_space=pl.ANY)
VMEM = pl.BlockSpec(memory_space=pltpu.VMEM)
DMA = pltpu.SemaphoreType.DMA
LIMIT = 56 * 1024 * 1024
COST = pl.CostEstimate(flops=10_000_000, bytes_accessed=10_000, transcendentals=0)


def dot(a, b):
    return lax.dot_general(a, b, (((1,), (0,)), ((), ())), preferred_element_type=F32)


def dot_nt(a, b):
    return lax.dot_general(a, b, (((1,), (1,)), ((), ())), preferred_element_type=F32)


def dot_tn(a, b):
    return lax.dot_general(a, b, (((0,), (0,)), ((), ())), preferred_element_type=F32)


def chunks(n, size=256):
    return [(i, min(size, n - i)) for i in range(0, n, size)]


def place():
    f = lax.axis_index("fsdp")
    return f // 2, f % 2


def ring(y, k):
    return lax.rem(y + k, CHIPS)


def at_chip(y, c):
    return {"fsdp": 2 * y + c}


def greet(targets):
    barrier = pltpu.get_barrier_semaphore()
    for target in targets:
        pl.semaphore_signal(barrier, inc=1, device_id=target, device_id_type=MESH)
    return functools.partial(pl.semaphore_wait, barrier, len(targets))


def remote(src, dst, send, recv, target):
    return pltpu.make_async_remote_copy(
        src_ref=src, dst_ref=dst, send_sem=send, recv_sem=recv, device_id=target, device_id_type=MESH
    )


def slot(ref, y):
    return ref.at[pl.ds(pl.multiple_of(y * BLK, BLK), BLK)]


ORDER = (2, 1, 3)


def gather_start(full, y, c, send, recv):
    for k in ORDER:
        remote(slot(full, y), slot(full, y), send.at[k - 1], recv.at[k - 1], at_chip(ring(y, k), c)).start()


def gather_wait(full, y, c, send, recv):
    for k in (1, 3, 2):
        source = ring(y, 4 - k)
        remote(slot(full, source), slot(full, source), send.at[k - 1], recv.at[k - 1], at_chip(ring(y, k), c)).wait()


def scatter_start(acc, out_buf, in_buf, y, c, send, recv):
    for k in ORDER:
        target = ring(y, k)
        out_buf[k - 1] = slot(acc, target)[...].astype(BF)
        remote(out_buf.at[k - 1], in_buf.at[k - 1], send.at[k - 1], recv.at[k - 1], at_chip(target, c)).start()


def scatter_wait(acc, out_buf, in_buf, y, c, send, recv):
    total = slot(acc, y)[...]
    for k in (1, 3, 2):
        remote(out_buf.at[k - 1], in_buf.at[k - 1], send.at[k - 1], recv.at[k - 1], at_chip(ring(y, k), c)).wait()
        total = total + in_buf[k - 1].astype(F32)
    return total


def stats(v):
    centre = v - jnp.mean(v, axis=-1, keepdims=True)
    scale = lax.rsqrt(jnp.mean(centre * centre, axis=-1, keepdims=True) + EPS)
    return centre * scale, scale


def norm(v, gain, shift):
    return stats(v)[0] * gain + shift


def norm_back(d, v, gain):
    vh, scale = stats(v)
    q = d * gain
    grad = scale * (q - jnp.mean(q, axis=-1, keepdims=True) - vh * jnp.mean(q * vh, axis=-1, keepdims=True))
    return grad, jnp.sum(d * vh, axis=0, keepdims=True), jnp.sum(d, axis=0, keepdims=True)


GELU_A = 0.7978845608028654
GELU_B = 0.044715


def gelu(h):
    return 0.5 * h * (1.0 + jnp.tanh(GELU_A * (h + GELU_B * h * h * h)))


def gelu_slope(h):
    t = jnp.tanh(GELU_A * (h + GELU_B * h * h * h))
    return 0.5 * (1.0 + t) + 0.5 * h * (1.0 - t * t) * (GELU_A * (1.0 + 3.0 * GELU_B * h * h))


def masks(c):
    row = lax.broadcasted_iota(jnp.int32, (ROWS, ROWS), 0)
    col = lax.broadcasted_iota(jnp.int32, (ROWS, ROWS), 1)
    own = row >= col
    other = (row // BLK) >= (col // BLK) + (1 - c)
    return own, other


def load(pairs, sems):
    copies = [pltpu.make_async_copy(src, dst, sems.at[i]) for i, (src, dst) in enumerate(pairs)]
    for copy in copies:
        copy.start()
    return copies


def out_rows(wo_hbm, wo, e, y):
    start = pl.multiple_of(48 - 16 * y, 16)
    return [(wo_hbm.at[e, pl.ds(start, 256)], wo.at[0:256]), (wo_hbm.at[e, 256:320], wo.at[256:320])]


def out_wait(weights, wo, y):
    weights[1].wait()
    weights[2].wait()

    @pl.when(y < 3)
    def _():
        wo[256:320] = jnp.zeros((HD, D), BF)


def chip_row(y, rows):
    return jnp.where(lax.broadcasted_iota(jnp.int32, (CHIPS, 1), 0) == y, rows, 0.0)


def head_bias(vecs, row, y):
    last = jnp.where(y == 3, vecs[row : row + 1, 1024:D], 0.0)
    return jnp.concatenate([vecs[row : row + 1, pl.ds(pl.multiple_of(256 * y, 256), 256)], last], axis=-1)


def attend_forward(e, x, w_hbm, wo_hbm, vecs, middle, normed, queries, kv, kv_other, logsum, attended,
                   w, wo, acc, out_buf, in_buf, ls, gs, gr, ss, sr, ks, kr):
    y, c = place()
    peers = [at_chip(ring(y, k), c) for k in (1, 2, 3)]
    sibling = at_chip(y, 1 - c)
    arrived = greet(peers + [sibling])
    weights = load([(w_hbm.at[e], w)] + out_rows(wo_hbm, wo, e, y), ls)
    slot(normed, y)[...] = norm(x[...], vecs[0:1], vecs[1:2]).astype(BF)
    arrived()
    gather_start(normed, y, c, gs, gr)
    own, other = masks(c)
    weights[0].wait()
    gather_wait(normed, y, c, gs, gr)
    rows = normed[...]
    bias = jnp.concatenate([jnp.zeros((1, TH), F32), head_bias(vecs, 11, y)], axis=-1)
    for at, size in chunks(2 * TH):
        kv[:, at : at + size] = (dot(rows, w[:, at : at + size]) + bias[:, at : at + size]).astype(BF)
    swap = remote(kv, kv_other, ks, kr, sibling)
    swap.start()
    queries[...] = (dot(rows, w[:, 2 * TH :]) + head_bias(vecs, 10, y)).astype(BF)
    swap.wait()
    for h in range(SLOTS):
        at = h * HD
        q = queries[:, at : at + HD]
        s_own = jnp.where(own, dot_nt(q, kv[:, at : at + HD]) * SCALE, -1e30)
        s_other = jnp.where(other, dot_nt(q, kv_other[:, at : at + HD]) * SCALE, -1e30)
        top = jnp.maximum(jnp.max(s_own, axis=-1, keepdims=True), jnp.max(s_other, axis=-1, keepdims=True))
        e_own = jnp.exp(s_own - top)
        e_other = jnp.exp(s_other - top)
        total = jnp.sum(e_own, axis=-1, keepdims=True) + jnp.sum(e_other, axis=-1, keepdims=True)
        logsum[:, h : h + 1] = top + jnp.log(total)
        inverse = 1.0 / total
        a_own = (e_own * inverse).astype(BF)
        a_other = (e_other * inverse).astype(BF)
        out = dot(a_own, kv[:, TH + at : TH + at + HD]) + dot(a_other, kv_other[:, TH + at : TH + at + HD])
        attended[:, at : at + HD] = out.astype(BF)
    out_wait(weights, wo, y)
    mixed = attended[...]
    for at, size in chunks(D):
        acc[:, at : at + size] = dot(mixed, wo[:, at : at + size])
    scatter_start(acc, out_buf, in_buf, y, c, ss, sr)
    base = x[...] + vecs[4:5]
    middle[...] = base + scatter_wait(acc, out_buf, in_buf, y, c, ss, sr)


def feed_forward(e, middle, wu_hbm, wd_hbm, vecs, result, normed, hidden, active,
                 wu, wd, acc, out_buf, in_buf, ls, gs, gr, ss, sr):
    y, c = place()
    arrived = greet([at_chip(ring(y, k), c) for k in (1, 2, 3)])
    weights = load([(wu_hbm.at[e], wu), (wd_hbm.at[e], wd)], ls)
    slot(normed, y)[...] = norm(middle[...], vecs[2:3], vecs[3:4]).astype(BF)
    arrived()
    gather_start(normed, y, c, gs, gr)
    bias = jnp.sum(chip_row(y, vecs[6:10]), axis=0, keepdims=True)
    weights[0].wait()
    gather_wait(normed, y, c, gs, gr)
    rows = normed[...]
    for at, size in chunks(D):
        h = dot(rows, wu[:, at : at + size]) + bias[:, at : at + size]
        hidden[:, at : at + size] = h
        active[:, at : at + size] = gelu(h).astype(BF)
    weights[1].wait()
    rows = active[...]
    for at, size in chunks(D):
        acc[:, at : at + size] = dot(rows, wd[:, at : at + size])
    scatter_start(acc, out_buf, in_buf, y, c, ss, sr)
    base = middle[...] + vecs[5:6]
    result[...] = base + scatter_wait(acc, out_buf, in_buf, y, c, ss, sr)


def feed_back(e, grad, wu_hbm, wd_hbm, vecs, middle, normed, hidden, active, grad_middle, grad_up, grad_down, small,
              wu, wd, full, gh, acc, out_buf, in_buf, ls, gs, gr, ss, sr, reduce=None):
    y, c = place()
    peers = [at_chip(ring(y, k), c) for k in (1, 2, 3)]
    arrived = greet(peers if reduce is None else peers + [at_chip(y, 1 - c)] + plane_peers())
    weights = load([(wu_hbm.at[e], wu), (wd_hbm.at[e], wd)], ls)
    own_rows = grad[...].astype(BF)
    slot(full, y)[...] = own_rows
    arrived()
    gather_start(full, y, c, gs, gr)
    if reduce is not None:
        reduce.begin(y, c)
    small[...] = jnp.zeros_like(small)
    small[3:4] = jnp.sum(own_rows.astype(F32), axis=0, keepdims=True)
    weights[1].wait()
    gather_wait(full, y, c, gs, gr)
    if reduce is not None:
        reduce.middle(y, c)
    rows = full[...]
    for at, size in chunks(D):
        slope = gelu_slope(hidden[:, at : at + size])
        part = (dot_nt(rows, wd[at : at + size, :]) * slope).astype(BF)
        gh[:, at : at + size] = part
        small[2:3, at : at + size] = jnp.sum(part.astype(F32), axis=0, keepdims=True)
    weights[0].wait()
    rows = gh[...]
    for at, size in chunks(D):
        acc[:, at : at + size] = dot_nt(rows, wu[at : at + size, :])
    scatter_start(acc, out_buf, in_buf, y, c, ss, sr)
    for at, size in chunks(D):
        grad_up[at : at + size, :] = dot_tn(normed[:, at : at + size], gh[...]).astype(BF)
        grad_down[at : at + size, :] = dot_tn(active[:, at : at + size], full[...]).astype(BF)
    d = scatter_wait(acc, out_buf, in_buf, y, c, ss, sr)
    back, gain, shift = norm_back(d, middle[...], vecs[2:3])
    small[0:1] = gain
    small[1:2] = shift
    grad_middle[...] = grad[...] + back
    if reduce is not None:
        reduce.finish()


def attend_back(e, grad, w_hbm, wo_hbm, vecs, x, normed, queries, kv, kv_other, logsum, attended,
                grad_x, grad_attn, grad_out, small, small_bias,
                w, wo, full, ga, gj, part_out, part_in, part_own, rows_out, edge, acc, out_buf, in_buf, ls, gs, gr, ss, sr, ks, kr, es, er,
                reduce):
    y, c = place()
    peers = [at_chip(ring(y, k), c) for k in (1, 2, 3)]
    sibling = at_chip(y, 1 - c)
    arrived = greet(peers + [sibling] + plane_peers())
    weights = load([(w_hbm.at[e], w)] + out_rows(wo_hbm, wo, e, y), ls)
    own_rows = grad[...].astype(BF)
    slot(full, y)[...] = own_rows
    arrived()
    gather_start(full, y, c, gs, gr)
    reduce.begin(y, c)
    small[...] = jnp.zeros_like(small)
    small[2:3] = jnp.sum(own_rows.astype(F32), axis=0, keepdims=True)
    own, other = masks(c)
    out_wait(weights, wo, y)
    gather_wait(full, y, c, gs, gr)
    reduce.middle(y, c)
    ga[...] = dot_nt(full[...], wo[...]).astype(BF)
    for h in range(SLOTS):
        at = h * HD
        q = queries[:, at : at + HD]
        g = ga[:, at : at + HD]
        lse = logsum[:, h : h + 1]
        k_own, k_other = kv[:, at : at + HD], kv_other[:, at : at + HD]
        v_own, v_other = kv[:, TH + at : TH + at + HD], kv_other[:, TH + at : TH + at + HD]
        p_own = jnp.exp(jnp.where(own, dot_nt(q, k_own) * SCALE, -1e30) - lse)
        p_other = jnp.exp(jnp.where(other, dot_nt(q, k_other) * SCALE, -1e30) - lse)
        gp_own = dot_nt(g, v_own)
        gp_other = dot_nt(g, v_other)
        delta = jnp.sum(p_own * gp_own, axis=-1, keepdims=True) + jnp.sum(p_other * gp_other, axis=-1, keepdims=True)
        s_own = (p_own * (gp_own - delta)).astype(BF)
        s_other = (p_other * (gp_other - delta)).astype(BF)
        gj[:, 2 * TH + at : 2 * TH + at + HD] = ((dot(s_own, k_own) + dot(s_other, k_other)) * SCALE).astype(BF)
        part_own[:, at : at + HD] = dot_tn(s_own, q) * SCALE
        part_out[:, at : at + HD] = (dot_tn(s_other, q) * SCALE).astype(BF)
        part_own[:, TH + at : TH + at + HD] = dot_tn(p_own.astype(BF), g)
        part_out[:, TH + at : TH + at + HD] = dot_tn(p_other.astype(BF), g).astype(BF)
    swap = remote(part_out, part_in, ks, kr, sibling)
    swap.start()
    for at, size in chunks(D):
        rows_out[:, at : at + size] = dot_tn(attended[...], full[:, at : at + size]).astype(BF)
    lend = remote(rows_out.at[0:HD], edge, es, er, at_chip(ring(y, 3), c))
    lend.start()
    weights[0].wait()
    swap.wait()
    gj[:, : 2 * TH] = (part_own[...] + part_in[...].astype(F32)).astype(BF)
    rows = gj[...]
    for at, size in chunks(D):
        acc[:, at : at + size] = dot_nt(rows, w[at : at + size, :])
    scatter_start(acc, out_buf, in_buf, y, c, ss, sr)
    for at, size in chunks(D):
        grad_attn[at : at + size, :] = dot_tn(normed[:, at : at + size], gj[...]).astype(BF)
    small_bias[...] = jnp.zeros_like(small_bias)
    small_bias[0:1] = jnp.sum(gj[...].astype(F32), axis=0, keepdims=True)
    d = scatter_wait(acc, out_buf, in_buf, y, c, ss, sr)
    back, gain, shift = norm_back(d, x[...], vecs[0:1])
    small[0:1] = gain
    small[1:2] = shift
    grad_x[...] = grad[...] + back
    lend.wait()

    @pl.when(y < 3)
    def _():
        rows_out[256:320] = edge[...]

    grad_out[...] = rows_out[pl.ds(pl.multiple_of(16 * y, 16), 272)]
    reduce.finish()


def plane():
    s, r = lax.axis_index("section"), lax.axis_index("replica")
    return s, r // 2, r % 2, s * 8 + r


def at_plane(q):
    return {"section": q // 8, "replica": lax.rem(q, 8)}


def x_peers(x, h):
    return [{"replica": 2 * lax.rem(x + k, 4) + h} for k in (1, 2, 3)]


def z_peers(s, h):
    x = lax.axis_index("replica") // 2
    return [
        {"section": 1 - s},
        {"section": 1 - s, "replica": 2 * x + 1 - h},
        {"replica": 2 * x + 1 - h},
    ]


def plane_peers():
    s, x, h, me = plane()
    return x_peers(x, h) + z_peers(s, h)


class AlongX:
    def __init__(self, blocks, landing, out, send, recv):
        self.blocks, self.landing, self.out, self.send, self.recv = blocks, landing, out, send, recv

    def copies(self):
        s, x, h, me = plane()
        targets = x_peers(x, h)
        for k in ORDER:
            yield remote(
                self.blocks.at[lax.rem(x + k, 4)], self.landing.at[k - 1], self.send.at[k - 1], self.recv.at[k - 1],
                targets[k - 1],
            )

    def start(self):
        for copy in self.copies():
            copy.start()

    def finish(self):
        s, x, h, me = plane()
        for copy in self.copies():
            copy.wait()

        def add(i, carry):
            rows = pl.ds(pl.multiple_of(8 * (i % 17), 8), 8)
            total = self.blocks[x, i // 17, rows].astype(F32)
            for k in range(3):
                total = total + self.landing[k, i // 17, rows].astype(F32)
            self.out[i // 17, rows] = total.astype(BF)
            return carry

        lax.fori_loop(0, 34, add, 0)


def x_scratch(width):
    return [pltpu.VMEM((4, 2, 136, width), BF), pltpu.VMEM((3, 2, 136, width), BF), DMA((3,)), DMA((3,))]


class AlongZ:
    def __init__(self, layer, blocks, landing, out, send, recv):
        self.layer, self.blocks, self.landing, self.out, self.send, self.recv = layer, blocks, landing, out, send, recv

    def copies(self):
        s, x, h, me = plane()
        for half in (0, 1):
            owner = 2 * half + self.layer
            rel = lax.rem(2 * h + s - owner + 3, 4)
            target = {"section": jnp.int32(self.layer), "replica": 2 * x + half}
            copy = remote(self.blocks.at[half], self.landing.at[rel], self.send.at[half], self.recv.at[rel], target)
            yield 2 * h + s != owner, copy

    def start(self):
        for sends, copy in self.copies():
            pl.when(sends)(copy.start)

    def finish(self):
        s, x, h, me = plane()
        for sends, copy in self.copies():
            pl.when(sends)(copy.wait_send)

        @pl.when(s == self.layer)
        def _():
            for rel in range(3):
                remote(self.blocks.at[0], self.landing.at[rel], self.send.at[0], self.recv.at[rel], {"section": 1 - s}).wait_recv()

            def add(i, carry):
                rows = pl.ds(pl.multiple_of(8 * i, 8), 8)
                total = self.blocks[h, rows].astype(F32)
                for rel in range(3):
                    total = total + self.landing[rel, rows].astype(F32)
                self.out[rows] = total.astype(BF)
                return carry

            lax.fori_loop(0, 17, add, 0)

        @pl.when(s != self.layer)
        def _():
            self.out[...] = jnp.zeros_like(self.out)


def z_scratch(width):
    return [pltpu.VMEM((3, 136, width), BF), DMA((2,)), DMA((3,))]


class FeedReduce:
    def __init__(self, up, down, out, other, ls, cs, cr, *scratch):
        self.sources = (up, down)
        self.other, self.ls, self.cs, self.cr = other, ls, cs, cr
        self.along = AlongX(scratch[0], scratch[1], out, scratch[2], scratch[3])
        self.blocks = scratch[0]

    def keeps(self, c):
        up, down = self.sources
        return [
            pltpu.make_async_copy(up.at[:, c], self.blocks.at[:, 0], self.ls.at[0]),
            pltpu.make_async_copy(down.at[c], self.blocks.at[:, 1], self.ls.at[1]),
        ]

    def swaps(self, y, c):
        up, down = self.sources
        sibling = at_chip(y, 1 - c)
        return [
            remote(up.at[:, 1 - c], self.other.at[:, 0], self.cs.at[0], self.cr.at[0], sibling),
            remote(down.at[1 - c], self.other.at[:, 1], self.cs.at[1], self.cr.at[1], sibling),
        ]

    def begin(self, y, c):
        for copy in self.keeps(c) + self.swaps(y, c):
            copy.start()

    def middle(self, y, c):
        for copy in self.keeps(c) + self.swaps(y, c):
            copy.wait()

        def add(i, carry):
            self.blocks[i // 2, i % 2] = (
                self.blocks[i // 2, i % 2].astype(F32) + self.other[i // 2, i % 2].astype(F32)
            ).astype(BF)
            return carry

        lax.fori_loop(0, 8, add, 0)
        self.along.start()

    def finish(self):
        self.along.finish()


FEED_SCRATCH = [pltpu.VMEM((4, 2, 136, D), BF), DMA((2,)), DMA((2,)), DMA((2,))] + x_scratch(D)


class AttendReduce:
    def __init__(self, wide, rows, out, own_w, other_w, own_r, other_r, ls, cs, cr, *scratch):
        self.wide, self.rows = wide, rows
        self.own_w, self.other_w, self.own_r, self.other_r = own_w, other_w, own_r, other_r
        self.ls, self.cs, self.cr = ls, cs, cr
        self.along = AlongX(scratch[0], scratch[1], out, scratch[2], scratch[3])
        self.blocks = scratch[0]

    def keeps(self, c):
        return [
            pltpu.make_async_copy(self.wide.at[:, c], self.own_w, self.ls.at[0]),
            pltpu.make_async_copy(self.rows.at[c], self.own_r, self.ls.at[1]),
        ]

    def swaps(self, y, c):
        sibling = at_chip(y, 1 - c)
        return [
            remote(self.wide.at[:, 1 - c], self.other_w, self.cs.at[0], self.cr.at[0], sibling),
            remote(self.rows.at[1 - c], self.other_r, self.cs.at[1], self.cr.at[1], sibling),
        ]

    def begin(self, y, c):
        for copy in self.keeps(c) + self.swaps(y, c):
            copy.start()

    def middle(self, y, c):
        for copy in self.keeps(c) + self.swaps(y, c):
            copy.wait()
        blocks = self.blocks
        for i in range(4):
            block = self.own_w[i].astype(F32) + self.other_w[i].astype(F32)
            blocks[i, 0] = block[:, :640].astype(BF)
            blocks[i, 1, :, :320] = block[:, 640:].astype(BF)
            chunk = self.own_r[:, 256 * i : 256 * i + 256].astype(F32) + self.other_r[:, 256 * i : 256 * i + 256].astype(F32)
            blocks[i, 1, :, 320:576] = chunk.astype(BF)
            if i < 3:
                blocks[i, 1, :, 576:] = jnp.zeros((136, HD), BF)
        chunk = self.own_r[:, 1024:].astype(F32) + self.other_r[:, 1024:].astype(F32)
        blocks[3, 1, :, 576:] = chunk.astype(BF)
        self.along.start()

    def finish(self):
        self.along.finish()


ATTEND_SCRATCH = [
    pltpu.VMEM((4, 136, TQKV), BF),
    pltpu.VMEM((4, 136, TQKV), BF),
    pltpu.VMEM((136, D), BF),
    pltpu.VMEM((136, D), BF),
    DMA((2,)),
    DMA((2,)),
    DMA((2,)),
] + x_scratch(640)


class Both:
    def __init__(self, first, along_z):
        self.first, self.along_z = first, along_z

    def begin(self, y, c):
        self.first.begin(y, c)
        if self.along_z is not None:
            self.along_z.start()

    def middle(self, y, c):
        self.first.middle(y, c)

    def finish(self):
        self.first.finish()
        if self.along_z is not None:
            self.along_z.finish()


def feed_back_reduce(e, grad, wu_hbm, wd_hbm, vecs, middle, normed, hidden, active, wide, rows, half_u,
                     grad_middle, grad_up, grad_down, small, half_a, piece_u, *scratch):
    count = 4 + len(MOVE)
    own, extra, last = scratch[:count], scratch[count : count + len(ATTEND_SCRATCH)], scratch[count + len(ATTEND_SCRATCH) :]
    reduce = Both(AttendReduce(wide, rows, half_a, *extra), AlongZ(1 - e, half_u, last[0], piece_u, *last[1:]))
    feed_back(e, grad, wu_hbm, wd_hbm, vecs, middle, normed, hidden, active, grad_middle, grad_up, grad_down, small,
              *own, reduce=reduce)


def attend_back_reduce(e, later, grad, w_hbm, wo_hbm, vecs, x, normed, queries, kv, kv_other, logsum, attended, up, down,
                       *refs):
    refs = list(refs)
    half_a = refs.pop(0) if later else None
    outs, refs = refs[:5], refs[5:]
    half_u = refs.pop(0)
    piece_a = refs.pop(0) if later else None
    count = 14 + len(MOVE)
    own, extra, last = refs[:count], refs[count : count + len(FEED_SCRATCH)], refs[count + len(FEED_SCRATCH) :]
    along_z = AlongZ(1 - e, half_a, last[0], piece_a, *last[1:]) if later else None
    reduce = Both(FeedReduce(up, down, half_u, *extra), along_z)
    attend_back(e, grad, w_hbm, wo_hbm, vecs, x, normed, queries, kv, kv_other, logsum, attended, *outs, *own,
                reduce=reduce)


def shape(dims, kind):
    return jax.ShapeDtypeStruct(dims, kind)


MOVE = [
    pltpu.VMEM((ROWS, D), F32),
    pltpu.VMEM((3, BLK, D), BF),
    pltpu.VMEM((3, BLK, D), BF),
    DMA((3,)),
    DMA((3,)),
    DMA((3,)),
    DMA((3,)),
    DMA((3,)),
]


def call(body, name, number, outs, ins, scratch):
    return pl.pallas_call(
        body,
        name=name,
        out_shape=outs,
        in_specs=ins,
        out_specs=[VMEM] * len(outs),
        scratch_shapes=scratch,
        cost_estimate=COST,
        compiler_params=pltpu.CompilerParams(collective_id=number, has_side_effects=True, vmem_limit_bytes=LIMIT),
    )


def run_attend_forward(e, x, w, wo, vecs):
    outs = [
        shape((BLK, D), F32),
        shape((ROWS, D), BF),
        shape((ROWS, TH), BF),
        shape((ROWS, 2 * TH), BF),
        shape((ROWS, 2 * TH), BF),
        shape((ROWS, 128), F32),
        shape((ROWS, TH), BF),
    ]
    scratch = [pltpu.VMEM((D, TQKV), BF), pltpu.VMEM((TH, D), BF)] + MOVE + [DMA, DMA]
    return call(functools.partial(attend_forward, e), "attend_forward_%d" % e, e, outs, [VMEM, ANY, ANY, VMEM], scratch)(x, w, wo, vecs)


def run_feed_forward(e, middle, wu, wd, vecs):
    outs = [shape((BLK, D), F32), shape((ROWS, D), BF), shape((ROWS, D), F32), shape((ROWS, D), BF)]
    scratch = [pltpu.VMEM((D, D), BF), pltpu.VMEM((D, D), BF)] + MOVE
    return call(functools.partial(feed_forward, e), "feed_forward_%d" % e, 2 + e, outs, [VMEM, ANY, ANY, VMEM], scratch)(middle, wu, wd, vecs)


HALF_A, HALF_U = shape((2, 136, 640), BF), shape((2, 136, D), BF)
PIECE_A, PIECE_U = shape((136, 640), BF), shape((136, D), BF)


def run_feed_back(e, grad, wu, wd, vecs, middle, normed, hidden, active, before=None):
    outs = [shape((BLK, D), F32), shape((D, D), BF), shape((D, D), BF), shape((8, D), F32)]
    scratch = [
        pltpu.VMEM((D, D), BF),
        pltpu.VMEM((D, D), BF),
        pltpu.VMEM((ROWS, D), BF),
        pltpu.VMEM((ROWS, D), BF),
    ] + MOVE
    ins = [VMEM, ANY, ANY] + [VMEM] * 5
    if before is None:
        return call(functools.partial(feed_back, e), "feed_back_%d" % e, 4 + e, outs, ins, scratch)(
            grad, wu, wd, vecs, middle, normed, hidden, active
        )
    outs += [HALF_A, PIECE_U]
    scratch = scratch + ATTEND_SCRATCH + z_scratch(D)
    return call(functools.partial(feed_back_reduce, e), "feed_back_%d" % e, 4 + e, outs, ins + [ANY, ANY, VMEM], scratch)(
        grad, wu, wd, vecs, middle, normed, hidden, active, *before
    )


def run_attend_back(e, grad, w, wo, vecs, x, saved, up, down, half_a=None):
    outs = [
        shape((BLK, D), F32),
        shape((D, TQKV), BF),
        shape((272, D), BF),
        shape((8, D), F32),
        shape((8, TQKV), F32),
        HALF_U,
    ]
    scratch = [
        pltpu.VMEM((D, TQKV), BF),
        pltpu.VMEM((TH, D), BF),
        pltpu.VMEM((ROWS, D), BF),
        pltpu.VMEM((ROWS, TH), BF),
        pltpu.VMEM((ROWS, TQKV), BF),
        pltpu.VMEM((ROWS, 2 * TH), BF),
        pltpu.VMEM((ROWS, 2 * TH), BF),
        pltpu.VMEM((ROWS, 2 * TH), F32),
        pltpu.VMEM((TH, D), BF),
        pltpu.VMEM((HD, D), BF),
    ] + MOVE + [DMA, DMA, DMA, DMA] + FEED_SCRATCH
    later = half_a is not None
    body = functools.partial(attend_back_reduce, e, later)
    ins = [VMEM, ANY, ANY] + [VMEM] * 8 + [ANY, ANY]
    more = []
    if later:
        outs, scratch, ins, more = outs + [PIECE_A], scratch + z_scratch(640), ins + [VMEM], [half_a]
    return call(body, "attend_back_%d" % e, 6 + e, outs, ins, scratch)(
        grad, w, wo, vecs, x, *saved, up, down, *more
    )


def spread(send_a, send_u, send_d, send_o, send_v, wa, wu, wd, wo, wv, hold_a, hold_u, hold_d, hold_o, hold_v, local, ysend, yrecv, zsend, zrecv, csend, crecv):
    s = lax.axis_index("section")
    y, c = place()
    replica = lax.axis_index("replica")
    flipped = replica // 2 * 2 + (1 - replica % 2)
    near = {"section": 1 - s}
    far = {"section": 1 - s, "replica": flipped}
    sibling = at_chip(y, 1 - c)
    peers = [at_chip(ring(y, k), c) for k in (1, 2, 3)]
    arrived = greet(peers + [sibling, near, far])
    brought = load(
        [(send_a.at[y], hold_a), (send_u.at[y], hold_u), (send_d, hold_d), (send_o, hold_o), (send_v, hold_v)], local.at[0]
    )
    for copy in brought:
        copy.wait()
    keeps = load(
        [
            (hold_a, wa.at[s, y, c]),
            (hold_u, wu.at[s, y, c]),
            (hold_d, wd.at[s, c]),
            (hold_o, wo.at[s, c]),
            (hold_v, wv.at[s, y, c]),
        ],
        local.at[1],
    )
    arrived()

    def along_y(k, back):
        target = ring(y, k)
        place_in = ring(y, 4 - k) if back else y
        return [
            remote(send_v, wv.at[s, place_in, c], ysend.at[0, k - 1], yrecv.at[0, k - 1], at_chip(target, c)),
            remote(send_a.at[target], wa.at[s, place_in, c], ysend.at[1, k - 1], yrecv.at[1, k - 1], at_chip(target, c)),
            remote(send_u.at[target], wu.at[s, place_in, c], ysend.at[2, k - 1], yrecv.at[2, k - 1], at_chip(target, c)),
        ]

    def along_z(layer):
        return [
            remote(wv.at[layer, :, c], wv.at[layer, :, c], zsend.at[0], zrecv.at[0], near),
            remote(wa.at[layer, 0:2, c], wa.at[layer, 0:2, c], zsend.at[1], zrecv.at[1], near),
            remote(wa.at[layer, 2:4, c], wa.at[layer, 2:4, c], zsend.at[2], zrecv.at[2], far),
            remote(wo.at[layer, c], wo.at[layer, c], zsend.at[3], zrecv.at[3], far),
            remote(wu.at[layer, 0:2, c], wu.at[layer, 0:2, c], zsend.at[4], zrecv.at[4], near),
            remote(wu.at[layer, 2:4, c], wu.at[layer, 2:4, c], zsend.at[5], zrecv.at[5], far),
            remote(wd.at[layer, c, 0:272], wd.at[layer, c, 0:272], zsend.at[6], zrecv.at[6], near),
            remote(wd.at[layer, c, 272:544], wd.at[layer, c, 272:544], zsend.at[7], zrecv.at[7], far),
        ]

    def across(layer, i, core):
        return [
            remote(wv.at[layer, :, core], wv.at[layer, :, core], csend.at[i, 0], crecv.at[i, 0], sibling),
            remote(wa.at[layer, :, core], wa.at[layer, :, core], csend.at[i, 1], crecv.at[i, 1], sibling),
            remote(wo.at[layer, core], wo.at[layer, core], csend.at[i, 2], crecv.at[i, 2], sibling),
            remote(wu.at[layer, :, core], wu.at[layer, :, core], csend.at[i, 3], crecv.at[i, 3], sibling),
            remote(wd.at[layer, core], wd.at[layer, core], csend.at[i, 4], crecv.at[i, 4], sibling),
        ]

    sent_y = [along_y(k, False) for k in (1, 2, 3)]
    got_y = [along_y(k, True) for k in (1, 2, 3)]
    sent_z, got_z = along_z(s), along_z(1 - s)
    sent_c = [across(s, 0, c), across(1 - s, 1, c)]
    got_c = [across(s, 0, 1 - c), across(1 - s, 1, 1 - c)]
    for kind in (0, 1):
        for k in (1, 0, 2):
            sent_y[k][kind].start()
    keeps[3].wait()
    sent_z[3].start()
    sent_c[0][2].start()
    keeps[2].wait()
    sent_z[6].start()
    sent_z[7].start()
    sent_c[0][4].start()
    for kind, keep, zs, cross in ((0, 4, (0,), 0), (1, 0, (1, 2), 1)):
        keeps[keep].wait()
        for k in range(3):
            got_y[k][kind].wait_recv()
        for z in zs:
            sent_z[z].start()
        sent_c[0][cross].start()
    for k in (1, 0, 2):
        sent_y[k][2].start()
    for zs, cross in (((3,), 2), ((6, 7), 4), ((0,), 0), ((1, 2), 1)):
        for z in zs:
            got_z[z].wait_recv()
        sent_c[1][cross].start()
    keeps[1].wait()
    for k in range(3):
        got_y[k][2].wait_recv()
    for z in (4, 5):
        sent_z[z].start()
    sent_c[0][3].start()
    for z in (4, 5):
        got_z[z].wait_recv()
    sent_c[1][3].start()
    for i in range(2):
        for cross in range(5):
            got_c[i][cross].wait_recv()
    for k in range(3):
        for kind in range(3):
            sent_y[k][kind].wait_send()
    for z in range(8):
        sent_z[z].wait_send()
    for i in range(2):
        for cross in range(5):
            sent_c[i][cross].wait_send()


def run_spread(a, u, d, o, v):
    outs = [
        shape((2, 4, 2, 136, TQKV), BF),
        shape((2, 4, 2, 136, D), BF),
        shape((2, 2, 544, D), BF),
        shape((2, 2, 192, D), BF),
        shape((2, 4, 2, 16, D), BF),
    ]
    return pl.pallas_call(
        spread,
        name="spread",
        out_shape=outs,
        in_specs=[ANY] * 5,
        out_specs=[ANY] * 5,
        scratch_shapes=[
            pltpu.VMEM((136, TQKV), BF),
            pltpu.VMEM((136, D), BF),
            pltpu.VMEM((544, D), BF),
            pltpu.VMEM((192, D), BF),
            pltpu.VMEM((16, D), BF),
            DMA((2, 5)), DMA((3, 3)), DMA((3, 3)), DMA((8,)), DMA((8,)), DMA((2, 5)), DMA((2, 5)),
        ],
        compiler_params=pltpu.CompilerParams(collective_id=8, has_side_effects=True),
    )(a, u, d, o, v)


def build_small(buf, one, two, heads, y):
    buf[...] = jnp.zeros_like(buf)
    buf[0:2] = one[0:2]
    buf[2:4] = two[0:2]
    buf[4:5] = one[2:3]
    buf[5:6] = two[3:4]
    buf[6:10] = chip_row(y, two[2:3])
    for row, at in ((10, 2 * TH), (11, TH)):
        buf[row : row + 1, pl.ds(pl.multiple_of(256 * y, 256), 256)] = heads[0:1, at : at + 256]

        @pl.when(y == 3)
        def _(row=row, at=at):
            buf[row : row + 1, 1024:D] = heads[0:1, at + 256 : at + TH]


class Gather:
    def __init__(self, piece, moved, out, number, moves, keep_from, ts, tr, gs, gr):
        self.piece, self.moved, self.out, self.i = piece, moved, out, number
        self.moves, self.keep_from = moves, keep_from
        self.ts, self.tr, self.gs, self.gr = ts, tr, gs, gr

    def transpose(self):
        y, c = place()
        s, x, h, me = plane()
        copy = remote(self.piece, self.moved, self.ts.at[self.i], self.tr.at[self.i], {"fsdp": 2 * x + c, "replica": 2 * y + h})
        cond = x != y
        return copy, cond if self.moves else jnp.logical_and(cond, h == 0)

    def start(self):
        copy, cond = self.transpose()
        pl.when(cond)(copy.start)

    def copies(self):
        s, x, h, me = plane()
        r = 2 * x + h
        for j in (4, 2, 6, 3, 5, 1, 7):
            yield j, remote(self.piece, self.out.at[h, x], self.gs.at[self.i, j], self.gr.at[self.i, j], {"replica": lax.rem(r + j, 8)})

    def spread(self):
        s, x, h, me = plane()
        copy, cond = self.transpose()
        pl.when(cond)(copy.wait)

        @pl.when(jnp.logical_and(cond, h == 0))
        def _():
            self.piece[...] = self.moved[...]

        if self.moves:
            @pl.when(jnp.logical_and(cond, h == 1))
            def _():
                lane = lax.broadcasted_iota(jnp.int32, self.piece.shape, 1)
                merged = jnp.where(lane < self.keep_from, self.moved[...].astype(F32), self.piece[...].astype(F32))
                self.piece[...] = merged.astype(BF)

        self.out[h, x] = self.piece[...]
        for j, copy in self.copies():
            copy.start()

    def finish(self):
        s, x, h, me = plane()
        r = 2 * x + h
        for j, copy in self.copies():
            copy.wait_send()
            source = lax.rem(r - j + 8, 8)
            place_in = self.out.at[source % 2, source // 2]
            remote(place_in, place_in, self.gs.at[self.i, j], self.gr.at[self.i, j], {"replica": lax.rem(r + j, 8)}).wait_recv()


def gather_pieces(wide, rows, half_u, done_u, done_a, one_0, two_0, heads_0, one_1, two_1, heads_1,
                  out_u, out_a, out_small,
                  piece_u, moved_u, piece_a, moved_a, half_a, small, small_c, small_y, small_x, small_z,
                  ts, tr, gs, gr, cs, cr, ys, yr, zs, zr, *extra):
    y, c = place()
    s, x, h, me = plane()
    sibling = at_chip(y, 1 - c)
    peers = [at_chip(ring(y, k), c) for k in (1, 2, 3)]
    reduce = AttendReduce(wide, rows, half_a, *extra[: len(ATTEND_SCRATCH)])
    extra = extra[len(ATTEND_SCRATCH) :]
    z_u = AlongZ(0, half_u, extra[0], piece_u, extra[1], extra[2])
    z_a = AlongZ(0, half_a, extra[3], piece_a, extra[4], extra[5])
    g_u = Gather(piece_u, moved_u, out_u, 0, False, 0, ts, tr, gs, gr)
    g_a = Gather(piece_a, moved_a, out_a, 1, True, 320, ts, tr, gs, gr)
    barrier = pltpu.get_barrier_semaphore()
    for target in peers + [sibling] + [at_plane(lax.rem(me + j, 16)) for j in range(1, 16)]:
        pl.semaphore_signal(barrier, inc=1, device_id=target, device_id_type=MESH)

    @pl.when(x != y)
    def _():
        pl.semaphore_signal(barrier, inc=1, device_id={"fsdp": 2 * x + c, "replica": 2 * y + h}, device_id_type=MESH)

    build_small(small.at[0], one_0, two_0, heads_0, y)
    build_small(small.at[1], one_1, two_1, heads_1, y)
    pl.semaphore_wait(barrier, 19 + jnp.where(x == y, 0, 1))
    z_u.start()
    reduce.begin(y, c)
    cross = remote(small, small_c, cs, cr, sibling)
    cross.start()
    reduce.middle(y, c)
    cross.wait()
    small[...] = small[...] + small_c[...]
    hops = [remote(small, small_y.at[k - 1], ys.at[k - 1], yr.at[k - 1], peers[k - 1]) for k in (1, 2, 3)]
    for hop in hops:
        hop.start()
    z_u.finish()

    @pl.when(s == 1)
    def _():
        piece_u[...] = done_u[...]

    g_u.start()
    reduce.finish()
    z_a.start()
    g_u.spread()
    for hop in hops:
        hop.wait()
    small_x[...] = (small[...] + small_y[0] + small_y[1] + small_y[2]).astype(BF)

    def plane_copies():
        for j in range(1, 16):
            q = lax.rem(me + j, 16)
            yield remote(small_x.at[q // 8], small_z.at[15 - j], zs.at[j - 1], zr.at[15 - j], at_plane(q))

    for copy in plane_copies():
        copy.start()
    z_a.finish()

    @pl.when(s == 1)
    def _():
        piece_a[...] = done_a[...]

    g_a.start()
    g_a.spread()
    total = small_x[s].astype(F32)
    for copy in plane_copies():
        copy.wait_send()
    for j in range(15):
        remote(small_x.at[0], small_z.at[j], zs.at[j], zr.at[j], sibling).wait_recv()
        total = total + small_z[j].astype(F32)
    out_small[...] = total
    g_u.finish()
    g_a.finish()


def run_gather_pieces(wide, rows, half_u, done_u, done_a, smalls):
    outs = [shape((2, 4, 136, D), BF), shape((2, 4, 136, 640), BF), shape((16, D), F32)]
    scratch = [
        pltpu.VMEM((136, D), BF),
        pltpu.VMEM((136, D), BF),
        pltpu.VMEM((136, 640), BF),
        pltpu.VMEM((136, 640), BF),
        pltpu.VMEM((2, 136, 640), BF),
        pltpu.VMEM((2, 16, D), F32),
        pltpu.VMEM((2, 16, D), F32),
        pltpu.VMEM((3, 2, 16, D), F32),
        pltpu.VMEM((2, 16, D), BF),
        pltpu.VMEM((15, 16, D), BF),
        DMA((2,)),
        DMA((2,)),
        DMA((2, 8)),
        DMA((2, 8)),
        DMA,
        DMA,
        DMA((3,)),
        DMA((3,)),
        DMA((15,)),
        DMA((15,)),
    ] + ATTEND_SCRATCH + z_scratch(D) + z_scratch(640)
    return call(gather_pieces, "gather_pieces", 9, outs, [ANY, ANY] + [VMEM] * 9, scratch)(
        wide, rows, half_u, done_u, done_a, *smalls
    )


def split_heads(block):
    zero = jnp.zeros(block.shape[:-1] + (HD,), block.dtype)
    return [
        jnp.concatenate([block[..., 256 * j : 256 * j + 256], block[..., 1024:] if j == 3 else zero], axis=-1)
        for j in range(CHIPS)
    ]


def join_heads(blocks):
    return jnp.concatenate([blocks[j][..., :256] for j in range(CHIPS)] + [blocks[3][..., 256:]], axis=-1)


def on_device(inputs, cotangent, weight_attn, weight_out, weight_up, weight_down, bias_attn, bias_out, bias_up,
              bias_down, norm_gain, norm_bias):
    s = lax.axis_index("section")
    f = lax.axis_index("fsdp")
    y, c = f // 2, f % 2
    wa = weight_attn[0]
    q_blocks, k_blocks, v_blocks = (split_heads(wa[:, i * D : (i + 1) * D]) for i in range(3))
    send_a = jnp.stack(
        [jnp.concatenate([k_blocks[j], v_blocks[j], q_blocks[j]], axis=-1) for j in range(CHIPS)]
    )
    send_u = jnp.stack([weight_up[0][:, j * D : (j + 1) * D] for j in range(CHIPS)])
    tail = lax.ppermute(weight_out[0, 88:], "fsdp", [(i, (i + 2) % 8) for i in range(8)])
    send_o = jnp.concatenate([weight_out[0], tail, jnp.zeros((8, D), BF)], axis=0)
    vectors = jnp.stack([norm_gain[0, 0], norm_bias[0, 0], norm_gain[0, 1], norm_bias[0, 1], bias_out[0], bias_down[0]])
    send_v = jnp.concatenate(
        [
            lax.dynamic_update_slice(jnp.zeros((6, D), BF), vectors, (0, 136 * f)),
            lax.dynamic_update_slice(jnp.zeros((4, D), BF), bias_up, (y, 544 * c)),
            lax.dynamic_update_slice(jnp.zeros((6, D), BF), bias_attn, (f // 4, 272 * (f % 4))),
        ]
    )
    wa, wu, wd, wo, wv = run_spread(send_a, send_u, weight_down[0], send_o, send_v)
    wa = wa.reshape(2, D, TQKV)
    wu = wu.reshape(2, D, D)
    wd = wd.reshape(2, D, D)
    wo = jnp.concatenate([wo[:, 1, 136:184], wo[:, 0, :136], wo[:, 1, :136]], axis=1)
    vecs = jnp.sum(wv.astype(F32), axis=(1, 2))
    micro = lax.dynamic_index_in_dim(inputs, s, 0, keepdims=False)[0]
    stream = micro.astype(F32)
    saved, acts = [], []
    for e in range(2):
        middle, *kept = run_attend_forward(e, stream, wa, wo, vecs[e])
        result, *kept_two = run_feed_forward(e, middle, wu, wd, vecs[e])
        saved.append((stream, kept, middle, kept_two))
        acts.append(result.astype(BF))
        stream = acts[-1].astype(F32)
    grad = lax.dynamic_index_in_dim(cotangent, s, 0, keepdims=False)[0].astype(F32)
    in_grads, smalls, before, half_a = [None, None], [None, None], None, None
    for e in (1, 0):
        x, kept, middle, kept_two = saved[e]
        grad_middle, grad_up, grad_down, two, *reduced = run_feed_back(
            e, grad, wu, wd, vecs[e], middle, *kept_two, before=before
        )
        if reduced:
            half_a, done_u = reduced
        grad_x, grad_attn, grad_out, one, heads, half_u, *done_a = run_attend_back(
            e, grad_middle, wa, wo, vecs[e], x, kept, grad_up.reshape(4, 2, 136, D), grad_down.reshape(2, 4, 136, D),
            half_a,
        )
        in_grads[e] = grad_x.astype(BF)
        grad = in_grads[e].astype(F32)
        before = (grad_attn.reshape(4, 2, 136, TQKV), grad_out.reshape(2, 136, D), half_u)
        smalls[e] = (one, two, heads)
    all_u, all_a, small = run_gather_pieces(*before, done_u, *done_a, smalls[0] + smalls[1])
    all_u, all_a = all_u.astype(F32), all_a.astype(F32)
    attn = [jnp.concatenate([all_a[0, j], all_a[1, j, :, :320]], axis=-1) for j in range(CHIPS)]
    attn = jnp.concatenate(
        [join_heads([attn[j][:, i * TH : (i + 1) * TH] for j in range(CHIPS)]) for i in (2, 0, 1)], axis=-1
    )
    out = join_heads([all_a[1, j, :, 320:] for j in range(CHIPS)])
    up = jnp.concatenate([all_u[0, j] for j in range(CHIPS)], axis=-1)
    down = all_u[1].reshape(544, D)
    pieces = lax.dynamic_slice(small, (0, 136 * f), (6, 136))
    piece_up = lax.dynamic_slice(small, (6 + y, 544 * c), (1, 544))
    piece_attn = lax.dynamic_slice(small, (10 + f // 4, 272 * (f % 4)), (1, 272))

    def swap_layers(values):
        mine = jnp.where(s == 0, values[0], values[1])
        theirs = jnp.where(s == 0, values[1], values[0])
        received = lax.ppermute(theirs, "section", [(0, 1), (1, 0)])
        pair_up = jnp.stack([jnp.where(s == 0, mine, received), jnp.where(s == 0, received, mine)])
        return pair_up[None, :, None]

    return (
        swap_layers(acts),
        swap_layers(in_grads),
        attn[None],
        out[None],
        up[None],
        down[None],
        piece_attn,
        pieces[4:5],
        piece_up,
        pieces[5:6],
        pieces[0:4:2][None],
        pieces[1:4:2][None],
    )


def solution(mesh):
    placed = (
        P(None, "replica", "fsdp", None),
        P(None, "replica", "fsdp", None),
        P("section", "fsdp", None),
        P("section", "fsdp", None),
        P("section", "fsdp", None),
        P("section", "fsdp", None),
        P("section", "fsdp"),
        P("section", "fsdp"),
        P("section", "fsdp"),
        P("section", "fsdp"),
        P("section", None, "fsdp"),
        P("section", None, "fsdp"),
    )
    return jax.shard_map(
        on_device,
        mesh=mesh,
        in_specs=placed,
        out_specs=(
            P("section", None, "replica", "fsdp", None),
            P("section", None, "replica", "fsdp", None),
        )
        + placed[2:],
        check_vma=False,
    )
```

```python
import functools

import jax
import jax.numpy as jnp
from jax import lax
from jax.experimental import pallas as pl
from jax.experimental.pallas import tpu as pltpu
from jax.sharding import PartitionSpec as P

D = 1088
FF = 4352
HEADS = 17
HD = 64
BLK = 64
CHIPS = 4
ROWS = BLK * CHIPS
SLOTS = 5
TH = SLOTS * HD
TQKV = 3 * TH
SCALE = HD**-0.5
EPS = 1e-5
MESH = pl.DeviceIdType.MESH
BF = jnp.bfloat16
F32 = jnp.float32
ANY = pl.BlockSpec(memory_space=pl.ANY)
VMEM = pl.BlockSpec(memory_space=pltpu.VMEM)
DMA = pltpu.SemaphoreType.DMA
LIMIT = 56 * 1024 * 1024
COST = pl.CostEstimate(flops=10_000_000, bytes_accessed=10_000, transcendentals=0)


def dot(a, b):
    return lax.dot_general(a, b, (((1,), (0,)), ((), ())), preferred_element_type=F32)


def dot_nt(a, b):
    return lax.dot_general(a, b, (((1,), (1,)), ((), ())), preferred_element_type=F32)


def dot_tn(a, b):
    return lax.dot_general(a, b, (((0,), (0,)), ((), ())), preferred_element_type=F32)


def chunks(n, size=256):
    return [(i, min(size, n - i)) for i in range(0, n, size)]


def place():
    f = lax.axis_index("fsdp")
    return f // 2, f % 2


def ring(y, k):
    return lax.rem(y + k, CHIPS)


def at_chip(y, c):
    return {"fsdp": 2 * y + c}


def greet(targets):
    barrier = pltpu.get_barrier_semaphore()
    for target in targets:
        pl.semaphore_signal(barrier, inc=1, device_id=target, device_id_type=MESH)
    return functools.partial(pl.semaphore_wait, barrier, len(targets))


def remote(src, dst, send, recv, target):
    return pltpu.make_async_remote_copy(
        src_ref=src, dst_ref=dst, send_sem=send, recv_sem=recv, device_id=target, device_id_type=MESH
    )


def slot(ref, y):
    return ref.at[pl.ds(pl.multiple_of(y * BLK, BLK), BLK)]


ORDER = (2, 1, 3)


def gather_start(full, y, c, send, recv):
    for k in ORDER:
        remote(slot(full, y), slot(full, y), send.at[k - 1], recv.at[k - 1], at_chip(ring(y, k), c)).start()


def gather_wait(full, y, c, send, recv):
    for k in (1, 3, 2):
        source = ring(y, 4 - k)
        remote(slot(full, source), slot(full, source), send.at[k - 1], recv.at[k - 1], at_chip(ring(y, k), c)).wait()


def scatter_start(acc, out_buf, in_buf, y, c, send, recv):
    for k in ORDER:
        target = ring(y, k)
        out_buf[k - 1] = slot(acc, target)[...].astype(BF)
        remote(out_buf.at[k - 1], in_buf.at[k - 1], send.at[k - 1], recv.at[k - 1], at_chip(target, c)).start()


def scatter_wait(acc, out_buf, in_buf, y, c, send, recv):
    total = slot(acc, y)[...]
    for k in (1, 3, 2):
        remote(out_buf.at[k - 1], in_buf.at[k - 1], send.at[k - 1], recv.at[k - 1], at_chip(ring(y, k), c)).wait()
        total = total + in_buf[k - 1].astype(F32)
    return total


def stats(v):
    centre = v - jnp.mean(v, axis=-1, keepdims=True)
    scale = lax.rsqrt(jnp.mean(centre * centre, axis=-1, keepdims=True) + EPS)
    return centre * scale, scale


def norm(v, gain, shift):
    return stats(v)[0] * gain + shift


def norm_back(d, v, gain):
    vh, scale = stats(v)
    q = d * gain
    grad = scale * (q - jnp.mean(q, axis=-1, keepdims=True) - vh * jnp.mean(q * vh, axis=-1, keepdims=True))
    return grad, jnp.sum(d * vh, axis=0, keepdims=True), jnp.sum(d, axis=0, keepdims=True)


GELU_A = 0.7978845608028654
GELU_B = 0.044715


def gelu(h):
    return 0.5 * h * (1.0 + jnp.tanh(GELU_A * (h + GELU_B * h * h * h)))


def gelu_slope(h):
    t = jnp.tanh(GELU_A * (h + GELU_B * h * h * h))
    return 0.5 * (1.0 + t) + 0.5 * h * (1.0 - t * t) * (GELU_A * (1.0 + 3.0 * GELU_B * h * h))


def masks(c):
    row = lax.broadcasted_iota(jnp.int32, (ROWS, ROWS), 0)
    col = lax.broadcasted_iota(jnp.int32, (ROWS, ROWS), 1)
    own = row >= col
    other = (row // BLK) >= (col // BLK) + (1 - c)
    return own, other


def load(pairs, sems):
    copies = [pltpu.make_async_copy(src, dst, sems.at[i]) for i, (src, dst) in enumerate(pairs)]
    for copy in copies:
        copy.start()
    return copies


def out_rows(wo_hbm, wo, e, y):
    start = pl.multiple_of(48 - 16 * y, 16)
    return [(wo_hbm.at[e, pl.ds(start, 256)], wo.at[0:256]), (wo_hbm.at[e, 256:320], wo.at[256:320])]


def out_wait(weights, wo, y):
    weights[1].wait()
    weights[2].wait()

    @pl.when(y < 3)
    def _():
        wo[256:320] = jnp.zeros((HD, D), BF)


def chip_row(y, rows):
    return jnp.where(lax.broadcasted_iota(jnp.int32, (CHIPS, 1), 0) == y, rows, 0.0)


def head_bias(vecs, row, y):
    last = jnp.where(y == 3, vecs[row : row + 1, 1024:D], 0.0)
    return jnp.concatenate([vecs[row : row + 1, pl.ds(pl.multiple_of(256 * y, 256), 256)], last], axis=-1)


def attend_forward(e, x, w_hbm, wo_hbm, vecs, middle, normed, queries, kv, kv_other, logsum, attended,
                   w, wo, acc, out_buf, in_buf, ls, gs, gr, ss, sr, ks, kr):
    y, c = place()
    peers = [at_chip(ring(y, k), c) for k in (1, 2, 3)]
    sibling = at_chip(y, 1 - c)
    arrived = greet(peers + [sibling])
    weights = load([(w_hbm.at[e], w)] + out_rows(wo_hbm, wo, e, y), ls)
    slot(normed, y)[...] = norm(x[...].astype(F32), vecs[0:1], vecs[1:2]).astype(BF)
    arrived()
    gather_start(normed, y, c, gs, gr)
    own, other = masks(c)
    weights[0].wait()
    gather_wait(normed, y, c, gs, gr)
    rows = normed[...]
    bias = jnp.concatenate([jnp.zeros((1, TH), F32), head_bias(vecs, 11, y)], axis=-1)
    for at, size in chunks(2 * TH):
        kv[:, at : at + size] = (dot(rows, w[:, at : at + size]) + bias[:, at : at + size]).astype(BF)
    swap = remote(kv, kv_other, ks, kr, sibling)
    swap.start()
    queries[...] = (dot(rows, w[:, 2 * TH :]) + head_bias(vecs, 10, y)).astype(BF)
    swap.wait()
    for h in range(SLOTS):
        at = h * HD
        q = queries[:, at : at + HD]
        s_own = jnp.where(own, dot_nt(q, kv[:, at : at + HD]) * SCALE, -1e30)
        s_other = jnp.where(other, dot_nt(q, kv_other[:, at : at + HD]) * SCALE, -1e30)
        top = jnp.maximum(jnp.max(s_own, axis=-1, keepdims=True), jnp.max(s_other, axis=-1, keepdims=True))
        e_own = jnp.exp(s_own - top)
        e_other = jnp.exp(s_other - top)
        total = jnp.sum(e_own, axis=-1, keepdims=True) + jnp.sum(e_other, axis=-1, keepdims=True)
        logsum[:, h : h + 1] = top + jnp.log(total)
        inverse = 1.0 / total
        a_own = (e_own * inverse).astype(BF)
        a_other = (e_other * inverse).astype(BF)
        out = dot(a_own, kv[:, TH + at : TH + at + HD]) + dot(a_other, kv_other[:, TH + at : TH + at + HD])
        attended[:, at : at + HD] = out.astype(BF)
    out_wait(weights, wo, y)
    mixed = attended[...]
    for at, size in chunks(D):
        acc[:, at : at + size] = dot(mixed, wo[:, at : at + size])
    scatter_start(acc, out_buf, in_buf, y, c, ss, sr)
    base = x[...].astype(F32) + vecs[4:5]
    middle[...] = base + scatter_wait(acc, out_buf, in_buf, y, c, ss, sr)


def feed_forward(e, middle, wu_hbm, wd_hbm, vecs, result, normed, hidden, active,
                 wu, wd, acc, out_buf, in_buf, ls, gs, gr, ss, sr):
    y, c = place()
    arrived = greet([at_chip(ring(y, k), c) for k in (1, 2, 3)])
    weights = load([(wu_hbm.at[e], wu), (wd_hbm.at[e], wd)], ls)
    slot(normed, y)[...] = norm(middle[...], vecs[2:3], vecs[3:4]).astype(BF)
    arrived()
    gather_start(normed, y, c, gs, gr)
    bias = jnp.sum(chip_row(y, vecs[6:10]), axis=0, keepdims=True)
    weights[0].wait()
    gather_wait(normed, y, c, gs, gr)
    rows = normed[...]
    for at, size in chunks(D):
        h = dot(rows, wu[:, at : at + size]) + bias[:, at : at + size]
        hidden[:, at : at + size] = h
        active[:, at : at + size] = gelu(h).astype(BF)
    weights[1].wait()
    rows = active[...]
    for at, size in chunks(D):
        acc[:, at : at + size] = dot(rows, wd[:, at : at + size])
    scatter_start(acc, out_buf, in_buf, y, c, ss, sr)
    base = middle[...] + vecs[5:6]
    result[...] = (base + scatter_wait(acc, out_buf, in_buf, y, c, ss, sr)).astype(BF)


def feed_back(e, grad, wu_hbm, wd_hbm, vecs, middle, normed, hidden, active, grad_middle, grad_up, grad_down, small,
              wu, wd, full, gh, acc, out_buf, in_buf, ls, gs, gr, ss, sr, reduce=None):
    y, c = place()
    peers = [at_chip(ring(y, k), c) for k in (1, 2, 3)]
    arrived = greet(peers if reduce is None else peers + [at_chip(y, 1 - c)] + plane_peers())
    weights = load([(wu_hbm.at[e], wu), (wd_hbm.at[e], wd)], ls)
    own_rows = grad[...]
    slot(full, y)[...] = own_rows
    arrived()
    gather_start(full, y, c, gs, gr)
    if reduce is not None:
        reduce.begin(y, c)
    small[...] = jnp.zeros_like(small)
    small[3:4] = jnp.sum(own_rows.astype(F32), axis=0, keepdims=True)
    weights[1].wait()
    if reduce is not None:
        reduce.middle(y, c)
    gather_wait(full, y, c, gs, gr)
    rows = full[...]
    for at, size in chunks(D):
        slope = gelu_slope(hidden[:, at : at + size])
        part = (dot_nt(rows, wd[at : at + size, :]) * slope).astype(BF)
        gh[:, at : at + size] = part
        small[2:3, at : at + size] = jnp.sum(part.astype(F32), axis=0, keepdims=True)
    weights[0].wait()
    rows = gh[...]
    for at, size in chunks(D):
        acc[:, at : at + size] = dot_nt(rows, wu[at : at + size, :])
    scatter_start(acc, out_buf, in_buf, y, c, ss, sr)
    for at, size in chunks(D):
        grad_up[at : at + size, :] = dot_tn(normed[:, at : at + size], gh[...]).astype(BF)
        grad_down[at : at + size, :] = dot_tn(active[:, at : at + size], full[...]).astype(BF)
    d = scatter_wait(acc, out_buf, in_buf, y, c, ss, sr)
    back, gain, shift = norm_back(d, middle[...], vecs[2:3])
    small[0:1] = gain
    small[1:2] = shift
    grad_middle[...] = grad[...].astype(F32) + back
    if reduce is not None:
        reduce.finish()


def attend_back(e, grad, w_hbm, wo_hbm, vecs, x, normed, queries, kv, kv_other, logsum, attended,
                grad_x, grad_attn, grad_out, small, small_bias,
                w, wo, full, ga, gj, part_out, part_in, part_own, rows_out, edge, acc, out_buf, in_buf, ls, gs, gr, ss, sr, ks, kr, es, er,
                reduce):
    y, c = place()
    peers = [at_chip(ring(y, k), c) for k in (1, 2, 3)]
    sibling = at_chip(y, 1 - c)
    arrived = greet(peers + [sibling] + plane_peers())
    weights = load([(w_hbm.at[e], w)] + out_rows(wo_hbm, wo, e, y), ls)
    own_rows = grad[...].astype(BF)
    slot(full, y)[...] = own_rows
    arrived()
    gather_start(full, y, c, gs, gr)
    reduce.begin(y, c)
    small[...] = jnp.zeros_like(small)
    small[2:3] = jnp.sum(own_rows.astype(F32), axis=0, keepdims=True)
    own, other = masks(c)
    out_wait(weights, wo, y)
    reduce.middle(y, c)
    gather_wait(full, y, c, gs, gr)
    ga[...] = dot_nt(full[...], wo[...]).astype(BF)
    for h in range(SLOTS):
        at = h * HD
        q = queries[:, at : at + HD]
        g = ga[:, at : at + HD]
        lse = logsum[:, h : h + 1]
        k_own, k_other = kv[:, at : at + HD], kv_other[:, at : at + HD]
        v_own, v_other = kv[:, TH + at : TH + at + HD], kv_other[:, TH + at : TH + at + HD]
        p_own = jnp.exp(jnp.where(own, dot_nt(q, k_own) * SCALE, -1e30) - lse)
        p_other = jnp.exp(jnp.where(other, dot_nt(q, k_other) * SCALE, -1e30) - lse)
        gp_own = dot_nt(g, v_own)
        gp_other = dot_nt(g, v_other)
        delta = jnp.sum(p_own * gp_own, axis=-1, keepdims=True) + jnp.sum(p_other * gp_other, axis=-1, keepdims=True)
        s_own = (p_own * (gp_own - delta)).astype(BF)
        s_other = (p_other * (gp_other - delta)).astype(BF)
        gj[:, 2 * TH + at : 2 * TH + at + HD] = ((dot(s_own, k_own) + dot(s_other, k_other)) * SCALE).astype(BF)
        part_own[:, at : at + HD] = dot_tn(s_own, q) * SCALE
        part_out[:, at : at + HD] = (dot_tn(s_other, q) * SCALE).astype(BF)
        part_own[:, TH + at : TH + at + HD] = dot_tn(p_own.astype(BF), g)
        part_out[:, TH + at : TH + at + HD] = dot_tn(p_other.astype(BF), g).astype(BF)
    swap = remote(part_out, part_in, ks, kr, sibling)
    swap.start()
    for at, size in chunks(D):
        rows_out[:, at : at + size] = dot_tn(attended[...], full[:, at : at + size]).astype(BF)
    lend = remote(rows_out.at[0:HD], edge, es, er, at_chip(ring(y, 3), c))
    lend.start()
    weights[0].wait()
    swap.wait()
    gj[:, : 2 * TH] = (part_own[...] + part_in[...].astype(F32)).astype(BF)
    rows = gj[...]
    for at, size in chunks(D):
        acc[:, at : at + size] = dot_nt(rows, w[at : at + size, :])
    scatter_start(acc, out_buf, in_buf, y, c, ss, sr)
    for at, size in chunks(D):
        grad_attn[at : at + size, :] = dot_tn(normed[:, at : at + size], gj[...]).astype(BF)
    small_bias[...] = jnp.zeros_like(small_bias)
    small_bias[0:1] = jnp.sum(gj[...].astype(F32), axis=0, keepdims=True)
    d = scatter_wait(acc, out_buf, in_buf, y, c, ss, sr)
    back, gain, shift = norm_back(d, x[...].astype(F32), vecs[0:1])
    small[0:1] = gain
    small[1:2] = shift
    grad_x[...] = (grad[...] + back).astype(BF)
    lend.wait()

    @pl.when(y < 3)
    def _():
        rows_out[256:320] = edge[...]

    grad_out[...] = rows_out[pl.ds(pl.multiple_of(16 * y, 16), 272)]
    reduce.finish()


def plane():
    s, r = lax.axis_index("section"), lax.axis_index("replica")
    return s, r // 2, r % 2, s * 8 + r


def at_plane(q):
    return {"section": q // 8, "replica": lax.rem(q, 8)}


def x_peers(x, h):
    return [{"replica": 2 * lax.rem(x + k, 4) + h} for k in (1, 2, 3)]


def z_peers(s, h):
    x = lax.axis_index("replica") // 2
    return [
        {"section": 1 - s},
        {"section": 1 - s, "replica": 2 * x + 1 - h},
        {"replica": 2 * x + 1 - h},
    ]


def plane_peers():
    s, x, h, me = plane()
    return x_peers(x, h) + z_peers(s, h)


class AlongX:
    def __init__(self, blocks, landing, out, send, recv):
        self.blocks, self.landing, self.out, self.send, self.recv = blocks, landing, out, send, recv

    def copies(self):
        s, x, h, me = plane()
        targets = x_peers(x, h)
        for k in ORDER:
            yield remote(
                self.blocks.at[lax.rem(x + k, 4)], self.landing.at[k - 1], self.send.at[k - 1], self.recv.at[k - 1],
                targets[k - 1],
            )

    def start(self):
        for copy in self.copies():
            copy.start()

    def finish(self):
        s, x, h, me = plane()
        for copy in self.copies():
            copy.wait()

        def add(i, carry):
            rows = pl.ds(pl.multiple_of(8 * (i % 17), 8), 8)
            total = self.blocks[x, i // 17, rows].astype(F32)
            for k in range(3):
                total = total + self.landing[k, i // 17, rows].astype(F32)
            self.out[i // 17, rows] = total.astype(BF)
            return carry

        lax.fori_loop(0, 34, add, 0)


def x_scratch(width):
    return [pltpu.VMEM((4, 2, 136, width), BF), pltpu.VMEM((3, 2, 136, width), BF), DMA((3,)), DMA((3,))]


class AlongZ:
    def __init__(self, layer, blocks, landing, out, send, recv):
        self.layer, self.blocks, self.landing, self.out, self.send, self.recv = layer, blocks, landing, out, send, recv

    def copies(self):
        s, x, h, me = plane()
        for half in (0, 1):
            owner = 2 * half + self.layer
            rel = lax.rem(2 * h + s - owner + 3, 4)
            target = {"section": jnp.int32(self.layer), "replica": 2 * x + half}
            copy = remote(self.blocks, self.landing.at[rel], self.send.at[half], self.recv.at[rel], target)
            yield 2 * h + s != owner, copy

    def start(self):
        for sends, copy in self.copies():
            pl.when(sends)(copy.start)

    def finish(self):
        s, x, h, me = plane()
        for sends, copy in self.copies():
            pl.when(sends)(copy.wait_send)

        @pl.when(s == self.layer)
        def _():
            for rel in range(3):
                remote(self.blocks, self.landing.at[rel], self.send.at[0], self.recv.at[rel], {"section": 1 - s}).wait_recv()

            def add(i, carry):
                rows = pl.ds(pl.multiple_of(8 * (i % 17), 8), 8)
                total = self.blocks[i // 17, rows].astype(F32)
                for rel in range(3):
                    total = total + self.landing[rel, i // 17, rows].astype(F32)
                self.out[i // 17, rows] = total.astype(BF)
                return carry

            lax.fori_loop(0, 34, add, 0)

        @pl.when(s != self.layer)
        def _():
            self.out[...] = jnp.zeros_like(self.out)


def z_scratch(width):
    return [pltpu.VMEM((3, 2, 136, width), BF), DMA((2,)), DMA((3,))]


class FeedReduce:
    def __init__(self, up, down, out, other, ls, cs, cr, *scratch):
        self.sources = (up, down)
        self.other, self.ls, self.cs, self.cr = other, ls, cs, cr
        self.along = AlongX(scratch[0], scratch[1], out, scratch[2], scratch[3])
        self.blocks = scratch[0]

    def keeps(self, c):
        up, down = self.sources
        return [
            pltpu.make_async_copy(up.at[:, c], self.blocks.at[:, 0], self.ls.at[0]),
            pltpu.make_async_copy(down.at[c], self.blocks.at[:, 1], self.ls.at[1]),
        ]

    def swaps(self, y, c):
        up, down = self.sources
        sibling = at_chip(y, 1 - c)
        return [
            remote(up.at[:, 1 - c], self.other.at[:, 0], self.cs.at[0], self.cr.at[0], sibling),
            remote(down.at[1 - c], self.other.at[:, 1], self.cs.at[1], self.cr.at[1], sibling),
        ]

    def begin(self, y, c):
        for copy in self.keeps(c) + self.swaps(y, c):
            copy.start()

    def middle(self, y, c):
        for copy in self.keeps(c) + self.swaps(y, c):
            copy.wait()

        def add(i, carry):
            self.blocks[i // 2, i % 2] = (
                self.blocks[i // 2, i % 2].astype(F32) + self.other[i // 2, i % 2].astype(F32)
            ).astype(BF)
            return carry

        lax.fori_loop(0, 8, add, 0)
        self.along.start()

    def finish(self):
        self.along.finish()


FEED_SCRATCH = [pltpu.VMEM((4, 2, 136, D), BF), DMA((2,)), DMA((2,)), DMA((2,))] + x_scratch(D)


class AttendReduce:
    def __init__(self, wide, rows, out, own_w, other_w, own_r, other_r, ls, cs, cr, *scratch):
        self.wide, self.rows = wide, rows
        self.own_w, self.other_w, self.own_r, self.other_r = own_w, other_w, own_r, other_r
        self.ls, self.cs, self.cr = ls, cs, cr
        self.along = AlongX(scratch[0], scratch[1], out, scratch[2], scratch[3])
        self.blocks = scratch[0]

    def keeps(self, c):
        return [
            pltpu.make_async_copy(self.wide.at[:, c], self.own_w, self.ls.at[0]),
            pltpu.make_async_copy(self.rows.at[c], self.own_r, self.ls.at[1]),
        ]

    def swaps(self, y, c):
        sibling = at_chip(y, 1 - c)
        return [
            remote(self.wide.at[:, 1 - c], self.other_w, self.cs.at[0], self.cr.at[0], sibling),
            remote(self.rows.at[1 - c], self.other_r, self.cs.at[1], self.cr.at[1], sibling),
        ]

    def begin(self, y, c):
        for copy in self.keeps(c) + self.swaps(y, c):
            copy.start()

    def middle(self, y, c):
        for copy in self.keeps(c) + self.swaps(y, c):
            copy.wait()
        blocks = self.blocks
        for i in range(4):
            block = self.own_w[i].astype(F32) + self.other_w[i].astype(F32)
            blocks[i, 0] = block[:, :640].astype(BF)
            blocks[i, 1, :, :320] = block[:, 640:].astype(BF)
            chunk = self.own_r[:, 256 * i : 256 * i + 256].astype(F32) + self.other_r[:, 256 * i : 256 * i + 256].astype(F32)
            blocks[i, 1, :, 320:576] = chunk.astype(BF)
            if i < 3:
                blocks[i, 1, :, 576:] = jnp.zeros((136, HD), BF)
        chunk = self.own_r[:, 1024:].astype(F32) + self.other_r[:, 1024:].astype(F32)
        blocks[3, 1, :, 576:] = chunk.astype(BF)
        self.along.start()

    def finish(self):
        self.along.finish()


ATTEND_SCRATCH = [
    pltpu.VMEM((4, 136, TQKV), BF),
    pltpu.VMEM((4, 136, TQKV), BF),
    pltpu.VMEM((136, D), BF),
    pltpu.VMEM((136, D), BF),
    DMA((2,)),
    DMA((2,)),
    DMA((2,)),
] + x_scratch(640)


class Both:
    def __init__(self, first, along_z):
        self.first, self.along_z = first, along_z

    def begin(self, y, c):
        self.first.begin(y, c)
        if self.along_z is not None:
            self.along_z.start()

    def middle(self, y, c):
        self.first.middle(y, c)

    def finish(self):
        self.first.finish()
        if self.along_z is not None:
            self.along_z.finish()


def feed_back_reduce(e, grad, wu_hbm, wd_hbm, vecs, middle, normed, hidden, active, wide, rows, half_u,
                     grad_middle, grad_up, grad_down, small, half_a, piece_u, *scratch):
    count = 4 + len(MOVE)
    own, extra, last = scratch[:count], scratch[count : count + len(ATTEND_SCRATCH)], scratch[count + len(ATTEND_SCRATCH) :]
    reduce = Both(AttendReduce(wide, rows, half_a, *extra), AlongZ(1 - e, half_u, last[0], piece_u, *last[1:]))
    feed_back(e, grad, wu_hbm, wd_hbm, vecs, middle, normed, hidden, active, grad_middle, grad_up, grad_down, small,
              *own, reduce=reduce)


def attend_back_reduce(e, later, grad, w_hbm, wo_hbm, vecs, x, normed, queries, kv, kv_other, logsum, attended, up, down,
                       *refs):
    refs = list(refs)
    half_a = refs.pop(0) if later else None
    outs, refs = refs[:5], refs[5:]
    half_u = refs.pop(0)
    piece_a = refs.pop(0) if later else None
    count = 14 + len(MOVE)
    own, extra, last = refs[:count], refs[count : count + len(FEED_SCRATCH)], refs[count + len(FEED_SCRATCH) :]
    along_z = AlongZ(1 - e, half_a, last[0], piece_a, *last[1:]) if later else None
    reduce = Both(FeedReduce(up, down, half_u, *extra), along_z)
    attend_back(e, grad, w_hbm, wo_hbm, vecs, x, normed, queries, kv, kv_other, logsum, attended, *outs, *own,
                reduce=reduce)


def shape(dims, kind):
    return jax.ShapeDtypeStruct(dims, kind)


MOVE = [
    pltpu.VMEM((ROWS, D), F32),
    pltpu.VMEM((3, BLK, D), BF),
    pltpu.VMEM((3, BLK, D), BF),
    DMA((3,)),
    DMA((3,)),
    DMA((3,)),
    DMA((3,)),
    DMA((3,)),
]


def call(body, name, number, outs, ins, scratch):
    return pl.pallas_call(
        body,
        name=name,
        out_shape=outs,
        in_specs=ins,
        out_specs=[VMEM] * len(outs),
        scratch_shapes=scratch,
        cost_estimate=COST,
        compiler_params=pltpu.CompilerParams(collective_id=number, has_side_effects=True, vmem_limit_bytes=LIMIT),
    )


def run_attend_forward(e, x, w, wo, vecs):
    outs = [
        shape((BLK, D), F32),
        shape((ROWS, D), BF),
        shape((ROWS, TH), BF),
        shape((ROWS, 2 * TH), BF),
        shape((ROWS, 2 * TH), BF),
        shape((ROWS, 128), F32),
        shape((ROWS, TH), BF),
    ]
    scratch = [pltpu.VMEM((D, TQKV), BF), pltpu.VMEM((TH, D), BF)] + MOVE + [DMA, DMA]
    return call(functools.partial(attend_forward, e), "attend_forward_%d" % e, e, outs, [VMEM, ANY, ANY, VMEM], scratch)(x, w, wo, vecs)


def run_feed_forward(e, middle, wu, wd, vecs):
    outs = [shape((BLK, D), BF), shape((ROWS, D), BF), shape((ROWS, D), F32), shape((ROWS, D), BF)]
    scratch = [pltpu.VMEM((D, D), BF), pltpu.VMEM((D, D), BF)] + MOVE
    return call(functools.partial(feed_forward, e), "feed_forward_%d" % e, 2 + e, outs, [VMEM, ANY, ANY, VMEM], scratch)(middle, wu, wd, vecs)


HALF_A, HALF_U = shape((2, 136, 640), BF), shape((2, 136, D), BF)


def run_feed_back(e, grad, wu, wd, vecs, middle, normed, hidden, active, before=None):
    outs = [shape((BLK, D), F32), shape((D, D), BF), shape((D, D), BF), shape((8, D), F32)]
    scratch = [
        pltpu.VMEM((D, D), BF),
        pltpu.VMEM((D, D), BF),
        pltpu.VMEM((ROWS, D), BF),
        pltpu.VMEM((ROWS, D), BF),
    ] + MOVE
    ins = [VMEM, ANY, ANY] + [VMEM] * 5
    if before is None:
        return call(functools.partial(feed_back, e), "feed_back_%d" % e, 4 + e, outs, ins, scratch)(
            grad, wu, wd, vecs, middle, normed, hidden, active
        )
    outs += [HALF_A, HALF_U]
    scratch = scratch + ATTEND_SCRATCH + z_scratch(D)
    return call(functools.partial(feed_back_reduce, e), "feed_back_%d" % e, 4 + e, outs, ins + [ANY, ANY, VMEM], scratch)(
        grad, wu, wd, vecs, middle, normed, hidden, active, *before
    )


def run_attend_back(e, grad, w, wo, vecs, x, saved, up, down, half_a=None):
    outs = [
        shape((BLK, D), BF),
        shape((D, TQKV), BF),
        shape((272, D), BF),
        shape((8, D), F32),
        shape((8, TQKV), F32),
        HALF_U,
    ]
    scratch = [
        pltpu.VMEM((D, TQKV), BF),
        pltpu.VMEM((TH, D), BF),
        pltpu.VMEM((ROWS, D), BF),
        pltpu.VMEM((ROWS, TH), BF),
        pltpu.VMEM((ROWS, TQKV), BF),
        pltpu.VMEM((ROWS, 2 * TH), BF),
        pltpu.VMEM((ROWS, 2 * TH), BF),
        pltpu.VMEM((ROWS, 2 * TH), F32),
        pltpu.VMEM((TH, D), BF),
        pltpu.VMEM((HD, D), BF),
    ] + MOVE + [DMA, DMA, DMA, DMA] + FEED_SCRATCH
    later = half_a is not None
    body = functools.partial(attend_back_reduce, e, later)
    ins = [VMEM, ANY, ANY] + [VMEM] * 8 + [ANY, ANY]
    more = []
    if later:
        outs, scratch, ins, more = outs + [HALF_A], scratch + z_scratch(640), ins + [VMEM], [half_a]
    return call(body, "attend_back_%d" % e, 6 + e, outs, ins, scratch)(
        grad, w, wo, vecs, x, *saved, up, down, *more
    )


def spread(send_a, send_u, send_d, send_o, send_v, wa, wu, wd, wo, wv, hold_a, hold_u, hold_d, hold_o, hold_v, local, ysend, yrecv, zsend, zrecv, csend, crecv):
    s = lax.axis_index("section")
    y, c = place()
    replica = lax.axis_index("replica")
    flipped = replica // 2 * 2 + (1 - replica % 2)
    near = {"section": 1 - s}
    far = {"section": 1 - s, "replica": flipped}
    sibling = at_chip(y, 1 - c)
    peers = [at_chip(ring(y, k), c) for k in (1, 2, 3)]
    arrived = greet(peers + [sibling, near, far])
    brought = load(
        [(send_a.at[y], hold_a), (send_u.at[y], hold_u), (send_d, hold_d), (send_o, hold_o), (send_v, hold_v)], local.at[0]
    )
    for copy in brought:
        copy.wait()
    keeps = load(
        [
            (hold_a, wa.at[s, y, c]),
            (hold_u, wu.at[s, y, c]),
            (hold_d, wd.at[s, c]),
            (hold_o, wo.at[s, c]),
            (hold_v, wv.at[s, y, c]),
        ],
        local.at[1],
    )
    arrived()

    def along_y(k, back):
        target = ring(y, k)
        place_in = ring(y, 4 - k) if back else y
        return [
            remote(send_v, wv.at[s, place_in, c], ysend.at[0, k - 1], yrecv.at[0, k - 1], at_chip(target, c)),
            remote(send_a.at[target], wa.at[s, place_in, c], ysend.at[1, k - 1], yrecv.at[1, k - 1], at_chip(target, c)),
            remote(send_u.at[target], wu.at[s, place_in, c], ysend.at[2, k - 1], yrecv.at[2, k - 1], at_chip(target, c)),
        ]

    def along_z(layer):
        return [
            remote(wv.at[layer, :, c], wv.at[layer, :, c], zsend.at[0], zrecv.at[0], near),
            remote(wa.at[layer, 0:2, c], wa.at[layer, 0:2, c], zsend.at[1], zrecv.at[1], near),
            remote(wa.at[layer, 2:4, c], wa.at[layer, 2:4, c], zsend.at[2], zrecv.at[2], far),
            remote(wo.at[layer, c], wo.at[layer, c], zsend.at[3], zrecv.at[3], far),
            remote(wu.at[layer, 0:2, c], wu.at[layer, 0:2, c], zsend.at[4], zrecv.at[4], near),
            remote(wu.at[layer, 2:4, c], wu.at[layer, 2:4, c], zsend.at[5], zrecv.at[5], far),
            remote(wd.at[layer, c, 0:272], wd.at[layer, c, 0:272], zsend.at[6], zrecv.at[6], near),
            remote(wd.at[layer, c, 272:544], wd.at[layer, c, 272:544], zsend.at[7], zrecv.at[7], far),
        ]

    def across(layer, i, core):
        return [
            remote(wv.at[layer, :, core], wv.at[layer, :, core], csend.at[i, 0], crecv.at[i, 0], sibling),
            remote(wa.at[layer, :, core], wa.at[layer, :, core], csend.at[i, 1], crecv.at[i, 1], sibling),
            remote(wo.at[layer, core], wo.at[layer, core], csend.at[i, 2], crecv.at[i, 2], sibling),
            remote(wu.at[layer, :, core], wu.at[layer, :, core], csend.at[i, 3], crecv.at[i, 3], sibling),
            remote(wd.at[layer, core], wd.at[layer, core], csend.at[i, 4], crecv.at[i, 4], sibling),
        ]

    sent_y = [along_y(k, False) for k in (1, 2, 3)]
    got_y = [along_y(k, True) for k in (1, 2, 3)]
    sent_z, got_z = along_z(s), along_z(1 - s)
    sent_c = [across(s, 0, c), across(1 - s, 1, c)]
    got_c = [across(s, 0, 1 - c), across(1 - s, 1, 1 - c)]
    for kind in (0, 1):
        for k in (1, 0, 2):
            sent_y[k][kind].start()
    keeps[3].wait()
    sent_z[3].start()
    sent_c[0][2].start()
    keeps[2].wait()
    sent_z[6].start()
    sent_z[7].start()
    sent_c[0][4].start()
    for kind, keep, zs, cross in ((0, 4, (0,), 0), (1, 0, (1, 2), 1)):
        keeps[keep].wait()
        for k in range(3):
            got_y[k][kind].wait_recv()
        for z in zs:
            sent_z[z].start()
        sent_c[0][cross].start()
    for k in (1, 0, 2):
        sent_y[k][2].start()
    for zs, cross in (((3,), 2), ((6, 7), 4), ((0,), 0), ((1, 2), 1)):
        for z in zs:
            got_z[z].wait_recv()
        sent_c[1][cross].start()
    keeps[1].wait()
    for k in range(3):
        got_y[k][2].wait_recv()
    for z in (4, 5):
        sent_z[z].start()
    sent_c[0][3].start()
    for z in (4, 5):
        got_z[z].wait_recv()
    sent_c[1][3].start()
    for i in range(2):
        for cross in range(5):
            got_c[i][cross].wait_recv()
    for k in range(3):
        for kind in range(3):
            sent_y[k][kind].wait_send()
    for z in range(8):
        sent_z[z].wait_send()
    for i in range(2):
        for cross in range(5):
            sent_c[i][cross].wait_send()


def run_spread(a, u, d, o, v):
    outs = [
        shape((2, 4, 2, 136, TQKV), BF),
        shape((2, 4, 2, 136, D), BF),
        shape((2, 2, 544, D), BF),
        shape((2, 2, 192, D), BF),
        shape((2, 4, 2, 16, D), BF),
    ]
    return pl.pallas_call(
        spread,
        name="spread",
        out_shape=outs,
        in_specs=[ANY] * 5,
        out_specs=[ANY] * 5,
        scratch_shapes=[
            pltpu.VMEM((136, TQKV), BF),
            pltpu.VMEM((136, D), BF),
            pltpu.VMEM((544, D), BF),
            pltpu.VMEM((192, D), BF),
            pltpu.VMEM((16, D), BF),
            DMA((2, 5)), DMA((3, 3)), DMA((3, 3)), DMA((8,)), DMA((8,)), DMA((2, 5)), DMA((2, 5)),
        ],
        compiler_params=pltpu.CompilerParams(collective_id=8, has_side_effects=True),
    )(a, u, d, o, v)


def build_small(buf, one, two, heads, y):
    buf[...] = jnp.zeros_like(buf)
    buf[0:2] = one[0:2]
    buf[2:4] = two[0:2]
    buf[4:5] = one[2:3]
    buf[5:6] = two[3:4]
    buf[6:10] = chip_row(y, two[2:3])
    for row, at in ((10, 2 * TH), (11, TH)):
        buf[row : row + 1, pl.ds(pl.multiple_of(256 * y, 256), 256)] = heads[0:1, at : at + 256]

        @pl.when(y == 3)
        def _(row=row, at=at):
            buf[row : row + 1, 1024:D] = heads[0:1, at + 256 : at + TH]


class Gather:
    def __init__(self, pair, moved, out, number, keep_from, ts, tr, gs, gr):
        self.pair, self.moved, self.out, self.i, self.keep_from = pair, moved, out, number, keep_from
        self.ts, self.tr, self.gs, self.gr = ts, tr, gs, gr

    def transpose(self):
        y, c = place()
        s, x, h, me = plane()
        source = self.pair if self.keep_from else self.pair.at[0]
        return remote(source, self.moved, self.ts.at[self.i], self.tr.at[self.i], {"fsdp": 2 * x + c, "replica": 2 * y + h})

    def start(self):
        y, c = place()
        s, x, h, me = plane()
        pl.when(x != y)(self.transpose().start)

    def copies(self):
        s, x, h, me = plane()
        targets = x_peers(x, h)
        for k in ORDER:
            yield k, remote(self.pair, self.out.at[x], self.gs.at[self.i, k - 1], self.gr.at[self.i, k - 1], targets[k - 1])

    def spread(self):
        y, c = place()
        s, x, h, me = plane()

        @pl.when(x != y)
        def _():
            self.transpose().wait()
            if self.keep_from:
                self.pair[0] = self.moved[0]
                lane = lax.broadcasted_iota(jnp.int32, self.pair.shape[1:], 1)
                merged = jnp.where(lane < self.keep_from, self.moved[1].astype(F32), self.pair[1].astype(F32))
                self.pair[1] = merged.astype(BF)
            else:
                self.pair[0] = self.moved[...]

        for k, copy in self.copies():
            copy.start()
        self.out[x] = self.pair[...]

    def finish(self):
        s, x, h, me = plane()
        targets = x_peers(x, h)
        for k, copy in self.copies():
            copy.wait_send()
            place_in = self.out.at[lax.rem(x + 4 - k, 4)]
            remote(place_in, place_in, self.gs.at[self.i, k - 1], self.gr.at[self.i, k - 1], targets[k - 1]).wait_recv()


def gather_pieces(wide, rows, half_u, done_u, done_a, one_0, two_0, heads_0, one_1, two_1, heads_1,
                  act_0, act_1, back_0, back_1, out_u, out_a, out_small, out_act, out_back,
                  swap_act, swap_back, ws, wr, piece_u, moved_u, piece_a, moved_a, half_a, small, small_c, small_y, small_x, small_z,
                  ts, tr, gs, gr, cs, cr, ys, yr, zs, zr, *extra):
    y, c = place()
    s, x, h, me = plane()
    sibling = at_chip(y, 1 - c)
    peers = [at_chip(ring(y, k), c) for k in (1, 2, 3)]
    reduce = AttendReduce(wide, rows, half_a, *extra[: len(ATTEND_SCRATCH)])
    extra = extra[len(ATTEND_SCRATCH) :]
    z_u = AlongZ(0, half_u, extra[0], piece_u, extra[1], extra[2])
    z_a = AlongZ(0, half_a, extra[3], piece_a, extra[4], extra[5])
    g_u = Gather(piece_u, moved_u, out_u, 0, 0, ts, tr, gs, gr)
    g_a = Gather(piece_a, moved_a, out_a, 1, 320, ts, tr, gs, gr)
    barrier = pltpu.get_barrier_semaphore()
    for target in peers + [sibling] + [at_plane(lax.rem(me + j, 16)) for j in range(1, 16)]:
        pl.semaphore_signal(barrier, inc=1, device_id=target, device_id_type=MESH)

    @pl.when(x != y)
    def _():
        pl.semaphore_signal(barrier, inc=1, device_id={"fsdp": 2 * x + c, "replica": 2 * y + h}, device_id_type=MESH)

    build_small(small.at[0], one_0, two_0, heads_0, y)
    build_small(small.at[1], one_1, two_1, heads_1, y)
    pl.semaphore_wait(barrier, 19 + jnp.where(x == y, 0, 1))
    z_u.start()
    reduce.begin(y, c)
    swap_act[...] = jnp.where(s == 0, act_1[...].astype(F32), act_0[...].astype(F32)).astype(BF)
    swap_back[...] = jnp.where(s == 0, back_1[...].astype(F32), back_0[...].astype(F32)).astype(BF)
    swaps = [
        remote(swap_act, out_act.at[s], ws.at[0], wr.at[0], {"section": 1 - s}),
        remote(swap_back, out_back.at[s], ws.at[1], wr.at[1], {"section": 1 - s}),
    ]
    out_act[s] = jnp.where(s == 0, act_0[...].astype(F32), act_1[...].astype(F32)).astype(BF)
    out_back[s] = jnp.where(s == 0, back_0[...].astype(F32), back_1[...].astype(F32)).astype(BF)
    cross = remote(small, small_c, cs, cr, sibling)
    cross.start()
    reduce.middle(y, c)
    cross.wait()
    small[...] = small[...] + small_c[...]
    hops = [remote(small, small_y.at[k - 1], ys.at[k - 1], yr.at[k - 1], peers[k - 1]) for k in (1, 2, 3)]
    for hop in hops:
        hop.start()
    z_u.finish()

    @pl.when(s == 1)
    def _():
        piece_u[...] = done_u[...]

    g_u.start()
    reduce.finish()
    z_a.start()
    g_u.spread()
    for hop in hops:
        hop.wait()
    small_x[...] = (small[...] + small_y[0] + small_y[1] + small_y[2]).astype(BF)

    def plane_copies():
        for j in range(1, 16):
            q = lax.rem(me + j, 16)
            yield remote(small_x.at[q // 8], small_z.at[15 - j], zs.at[j - 1], zr.at[15 - j], at_plane(q))

    for copy in plane_copies():
        copy.start()
    z_a.finish()

    @pl.when(s == 1)
    def _():
        piece_a[...] = done_a[...]

    g_a.start()
    for swap in swaps:
        swap.start()
    g_a.spread()
    total = small_x[s].astype(F32)
    for copy in plane_copies():
        copy.wait_send()
    for j in range(15):
        remote(small_x.at[0], small_z.at[j], zs.at[j], zr.at[j], sibling).wait_recv()
        total = total + small_z[j].astype(F32)
    out_small[...] = total
    for i, swap in enumerate(swaps):
        swap.wait_send()
        place_in = (out_act, out_back)[i].at[1 - s]
        remote(place_in, place_in, ws.at[i], wr.at[i], {"section": 1 - s}).wait_recv()
    g_u.finish()
    g_a.finish()


def run_gather_pieces(wide, rows, half_u, done_u, done_a, smalls, acts, backs):
    both = shape((2, BLK, D), BF)
    outs = [shape((4, 2, 136, D), BF), shape((4, 2, 136, 640), BF), shape((16, D), F32), both, both]
    scratch = [
        pltpu.VMEM((BLK, D), BF),
        pltpu.VMEM((BLK, D), BF),
        DMA((2,)),
        DMA((2,)),
        pltpu.VMEM((2, 136, D), BF),
        pltpu.VMEM((136, D), BF),
        pltpu.VMEM((2, 136, 640), BF),
        pltpu.VMEM((2, 136, 640), BF),
        pltpu.VMEM((2, 136, 640), BF),
        pltpu.VMEM((2, 16, D), F32),
        pltpu.VMEM((2, 16, D), F32),
        pltpu.VMEM((3, 2, 16, D), F32),
        pltpu.VMEM((2, 16, D), BF),
        pltpu.VMEM((15, 16, D), BF),
        DMA((2,)),
        DMA((2,)),
        DMA((2, 3)),
        DMA((2, 3)),
        DMA,
        DMA,
        DMA((3,)),
        DMA((3,)),
        DMA((15,)),
        DMA((15,)),
    ] + ATTEND_SCRATCH + z_scratch(D) + z_scratch(640)
    return call(gather_pieces, "gather_pieces", 9, outs, [ANY, ANY] + [VMEM] * 13, scratch)(
        wide, rows, half_u, done_u, done_a, *smalls, *acts, *backs
    )


def assemble(all_u, all_a, small, attn, out, up, down, b_attn, b_out, b_up, b_down, gain, shift):
    y, c = place()
    f = 2 * y + c
    for j in range(CHIPS):
        up[:, j * D : (j + 1) * D] = all_u[j, 0].astype(F32)
        down[j * 136 : (j + 1) * 136] = all_u[j, 1].astype(F32)
        first, second = all_a[j, 0].astype(F32), all_a[j, 1].astype(F32)
        parts = ((0, second[:, :TH]), (D, first[:, :TH]), (2 * D, first[:, TH:]))
        for base, part in parts:
            attn[:, base + 256 * j : base + 256 * j + 256] = part[:, :256]
        out[:, 256 * j : 256 * j + 256] = second[:, TH : TH + 256]
        if j == CHIPS - 1:
            for base, part in parts:
                attn[:, base + 1024 : base + D] = part[:, 256:]
            out[:, 1024:] = second[:, TH + 256 :]

    def pick(index, options):
        total = jnp.where(index == 0, options[0], 0.0)
        for i, option in enumerate(options[1:], 1):
            total = total + jnp.where(index == i, option, 0.0)
        return total

    for row, ref, place_in in ((0, gain, 0), (1, shift, 0), (2, gain, 1), (3, shift, 1), (4, b_out, 0), (5, b_down, 0)):
        ref[place_in : place_in + 1] = pick(f, [small[row : row + 1, 136 * i : 136 * i + 136] for i in range(8)])
    b_up[...] = pick(f, [small[6 + i // 2 : 7 + i // 2, 544 * (i % 2) : 544 * (i % 2) + 544] for i in range(8)])
    b_attn[...] = pick(f, [small[10 + i // 4 : 11 + i // 4, 272 * (i % 4) : 272 * (i % 4) + 272] for i in range(8)])


def run_assemble(all_u, all_a, small):
    sizes = [(136, 3 * D), (136, D), (136, FF), (544, D), (1, 272), (1, 136), (1, 544), (1, 136), (2, 136), (2, 136)]
    return pl.pallas_call(
        assemble,
        name="assemble",
        out_shape=[shape(dims, F32) for dims in sizes],
        in_specs=[VMEM] * 3,
        out_specs=[VMEM] * len(sizes),
        compiler_params=pltpu.CompilerParams(vmem_limit_bytes=LIMIT),
    )(all_u, all_a, small)


def split_heads(block):
    zero = jnp.zeros(block.shape[:-1] + (HD,), block.dtype)
    return [
        jnp.concatenate([block[..., 256 * j : 256 * j + 256], block[..., 1024:] if j == 3 else zero], axis=-1)
        for j in range(CHIPS)
    ]


def on_device(inputs, cotangent, weight_attn, weight_out, weight_up, weight_down, bias_attn, bias_out, bias_up,
              bias_down, norm_gain, norm_bias):
    s = lax.axis_index("section")
    f = lax.axis_index("fsdp")
    y, c = f // 2, f % 2
    wa = weight_attn[0]
    q_blocks, k_blocks, v_blocks = (split_heads(wa[:, i * D : (i + 1) * D]) for i in range(3))
    send_a = jnp.stack(
        [jnp.concatenate([k_blocks[j], v_blocks[j], q_blocks[j]], axis=-1) for j in range(CHIPS)]
    )
    send_u = jnp.stack([weight_up[0][:, j * D : (j + 1) * D] for j in range(CHIPS)])
    tail = lax.ppermute(weight_out[0, 88:], "fsdp", [(i, (i + 2) % 8) for i in range(8)])
    send_o = jnp.concatenate([weight_out[0], tail, jnp.zeros((8, D), BF)], axis=0)
    vectors = jnp.stack([norm_gain[0, 0], norm_bias[0, 0], norm_gain[0, 1], norm_bias[0, 1], bias_out[0], bias_down[0]])
    send_v = jnp.concatenate(
        [
            lax.dynamic_update_slice(jnp.zeros((6, D), BF), vectors, (0, 136 * f)),
            lax.dynamic_update_slice(jnp.zeros((4, D), BF), bias_up, (y, 544 * c)),
            lax.dynamic_update_slice(jnp.zeros((6, D), BF), bias_attn, (f // 4, 272 * (f % 4))),
        ]
    )
    wa, wu, wd, wo, wv = run_spread(send_a, send_u, weight_down[0], send_o, send_v)
    wa = wa.reshape(2, D, TQKV)
    wu = wu.reshape(2, D, D)
    wd = wd.reshape(2, D, D)
    wo = jnp.concatenate([wo[:, 1, 136:184], wo[:, 0, :136], wo[:, 1, :136]], axis=1)
    vecs = jnp.sum(wv.astype(F32), axis=(1, 2))
    stream = lax.dynamic_index_in_dim(inputs, s, 0, keepdims=False)[0]
    saved, acts = [], []
    for e in range(2):
        middle, *kept = run_attend_forward(e, stream, wa, wo, vecs[e])
        result, *kept_two = run_feed_forward(e, middle, wu, wd, vecs[e])
        saved.append((stream, kept, middle, kept_two))
        acts.append(result)
        stream = result
    grad = lax.dynamic_index_in_dim(cotangent, s, 0, keepdims=False)[0]
    in_grads, smalls, before, half_a = [None, None], [None, None], None, None
    for e in (1, 0):
        x, kept, middle, kept_two = saved[e]
        grad_middle, grad_up, grad_down, two, *reduced = run_feed_back(
            e, grad, wu, wd, vecs[e], middle, *kept_two, before=before
        )
        if reduced:
            half_a, done_u = reduced
        grad, grad_attn, grad_out, one, heads, half_u, *done_a = run_attend_back(
            e, grad_middle, wa, wo, vecs[e], x, kept, grad_up.reshape(4, 2, 136, D), grad_down.reshape(2, 4, 136, D),
            half_a,
        )
        in_grads[e] = grad
        before = (grad_attn.reshape(4, 2, 136, TQKV), grad_out.reshape(2, 136, D), half_u)
        smalls[e] = (one, two, heads)
    all_u, all_a, small, all_acts, all_grads = run_gather_pieces(
        *before, done_u, *done_a, smalls[0] + smalls[1], acts, in_grads
    )
    attn, out, up, down, b_attn, b_out, b_up, b_down, gain, shift = run_assemble(all_u, all_a, small)
    return (
        all_acts[None, :, None],
        all_grads[None, :, None],
        attn[None],
        out[None],
        up[None],
        down[None],
        b_attn,
        b_out,
        b_up,
        b_down,
        gain[None],
        shift[None],
    )


def solution(mesh):
    placed = (
        P(None, "replica", "fsdp", None),
        P(None, "replica", "fsdp", None),
        P("section", "fsdp", None),
        P("section", "fsdp", None),
        P("section", "fsdp", None),
        P("section", "fsdp", None),
        P("section", "fsdp"),
        P("section", "fsdp"),
        P("section", "fsdp"),
        P("section", "fsdp"),
        P("section", None, "fsdp"),
        P("section", None, "fsdp"),
    )
    return jax.shard_map(
        on_device,
        mesh=mesh,
        in_specs=placed,
        out_specs=(
            P("section", None, "replica", "fsdp", None),
            P("section", None, "replica", "fsdp", None),
        )
        + placed[2:],
        check_vma=False,
    )
```

```python
import functools

import jax
import jax.numpy as jnp
from jax import lax
from jax.experimental import pallas as pl
from jax.experimental.pallas import tpu as pltpu
from jax.sharding import PartitionSpec as P

D = 1088
FF = 4352
HEADS = 17
HD = 64
BLK = 64
CHIPS = 4
ROWS = BLK * CHIPS
SLOTS = 5
TH = SLOTS * HD
TQKV = 3 * TH
SCALE = HD**-0.5
EPS = 1e-5
MESH = pl.DeviceIdType.MESH
BF = jnp.bfloat16
F32 = jnp.float32
ANY = pl.BlockSpec(memory_space=pl.ANY)
VMEM = pl.BlockSpec(memory_space=pltpu.VMEM)
DMA = pltpu.SemaphoreType.DMA
LIMIT = 56 * 1024 * 1024
COST = pl.CostEstimate(flops=10_000_000, bytes_accessed=10_000, transcendentals=0)


def dot(a, b):
    return lax.dot_general(a, b, (((1,), (0,)), ((), ())), preferred_element_type=F32)


def dot_nt(a, b):
    return lax.dot_general(a, b, (((1,), (1,)), ((), ())), preferred_element_type=F32)


def dot_tn(a, b):
    return lax.dot_general(a, b, (((0,), (0,)), ((), ())), preferred_element_type=F32)


def chunks(n, size=256):
    return [(i, min(size, n - i)) for i in range(0, n, size)]


def place():
    f = lax.axis_index("fsdp")
    return f // 2, f % 2


def ring(y, k):
    return lax.rem(y + k, CHIPS)


def at_chip(y, c):
    return {"fsdp": 2 * y + c}


def greet(targets):
    barrier = pltpu.get_barrier_semaphore()
    for target in targets:
        pl.semaphore_signal(barrier, inc=1, device_id=target, device_id_type=MESH)
    return functools.partial(pl.semaphore_wait, barrier, len(targets))


def remote(src, dst, send, recv, target):
    return pltpu.make_async_remote_copy(
        src_ref=src, dst_ref=dst, send_sem=send, recv_sem=recv, device_id=target, device_id_type=MESH
    )


def slot(ref, y):
    return ref.at[pl.ds(pl.multiple_of(y * BLK, BLK), BLK)]


ORDER = (2, 1, 3)


def gather_start(full, y, c, send, recv):
    for k in ORDER:
        remote(slot(full, y), slot(full, y), send.at[k - 1], recv.at[k - 1], at_chip(ring(y, k), c)).start()


def gather_wait(full, y, c, send, recv):
    for k in (1, 3, 2):
        source = ring(y, 4 - k)
        remote(slot(full, source), slot(full, source), send.at[k - 1], recv.at[k - 1], at_chip(ring(y, k), c)).wait()


def scatter_start(acc, out_buf, in_buf, y, c, send, recv):
    for k in ORDER:
        target = ring(y, k)
        out_buf[k - 1] = slot(acc, target)[...].astype(BF)
        remote(out_buf.at[k - 1], in_buf.at[k - 1], send.at[k - 1], recv.at[k - 1], at_chip(target, c)).start()


def scatter_wait(acc, out_buf, in_buf, y, c, send, recv):
    total = slot(acc, y)[...]
    for k in (1, 3, 2):
        remote(out_buf.at[k - 1], in_buf.at[k - 1], send.at[k - 1], recv.at[k - 1], at_chip(ring(y, k), c)).wait()
        total = total + in_buf[k - 1].astype(F32)
    return total


def stats(v):
    centre = v - jnp.mean(v, axis=-1, keepdims=True)
    scale = lax.rsqrt(jnp.mean(centre * centre, axis=-1, keepdims=True) + EPS)
    return centre * scale, scale


def norm(v, gain, shift):
    return stats(v)[0] * gain + shift


def norm_back(d, v, gain):
    vh, scale = stats(v)
    q = d * gain
    grad = scale * (q - jnp.mean(q, axis=-1, keepdims=True) - vh * jnp.mean(q * vh, axis=-1, keepdims=True))
    return grad, jnp.sum(d * vh, axis=0, keepdims=True), jnp.sum(d, axis=0, keepdims=True)


GELU_A = 0.7978845608028654
GELU_B = 0.044715


def gelu(h):
    return 0.5 * h * (1.0 + jnp.tanh(GELU_A * (h + GELU_B * h * h * h)))


def gelu_slope(h):
    t = jnp.tanh(GELU_A * (h + GELU_B * h * h * h))
    return 0.5 * (1.0 + t) + 0.5 * h * (1.0 - t * t) * (GELU_A * (1.0 + 3.0 * GELU_B * h * h))


def masks(c):
    row = lax.broadcasted_iota(jnp.int32, (ROWS, ROWS), 0)
    col = lax.broadcasted_iota(jnp.int32, (ROWS, ROWS), 1)
    own = row >= col
    other = (row // BLK) >= (col // BLK) + (1 - c)
    return own, other


def load(pairs, sems):
    copies = [pltpu.make_async_copy(src, dst, sems.at[i]) for i, (src, dst) in enumerate(pairs)]
    for copy in copies:
        copy.start()
    return copies


def out_rows(wo_hbm, wo, e, y):
    start = pl.multiple_of(48 - 16 * y, 16)
    return [(wo_hbm.at[e, pl.ds(start, 256)], wo.at[0:256]), (wo_hbm.at[e, 256:320], wo.at[256:320])]


def out_wait(weights, wo, y):
    weights[1].wait()
    weights[2].wait()

    @pl.when(y < 3)
    def _():
        wo[256:320] = jnp.zeros((HD, D), BF)


def chip_row(y, rows):
    return jnp.where(lax.broadcasted_iota(jnp.int32, (CHIPS, 1), 0) == y, rows, 0.0)


def head_bias(vecs, row, y):
    last = jnp.where(y == 3, vecs[row : row + 1, 1024:D], 0.0)
    return jnp.concatenate([vecs[row : row + 1, pl.ds(pl.multiple_of(256 * y, 256), 256)], last], axis=-1)


def attend_forward(e, x, w_hbm, wo_hbm, vecs, middle, normed, queries, kv, kv_other, logsum, attended,
                   w, wo, acc, out_buf, in_buf, ls, gs, gr, ss, sr, ks, kr):
    y, c = place()
    peers = [at_chip(ring(y, k), c) for k in (1, 2, 3)]
    sibling = at_chip(y, 1 - c)
    arrived = greet(peers + [sibling])
    weights = load([(w_hbm.at[e], w)] + out_rows(wo_hbm, wo, e, y), ls)
    slot(normed, y)[...] = norm(x[...].astype(F32), vecs[0:1], vecs[1:2]).astype(BF)
    arrived()
    gather_start(normed, y, c, gs, gr)
    own, other = masks(c)
    weights[0].wait()
    gather_wait(normed, y, c, gs, gr)
    rows = normed[...]
    bias = jnp.concatenate([jnp.zeros((1, TH), F32), head_bias(vecs, 11, y)], axis=-1)
    for at, size in chunks(2 * TH):
        kv[:, at : at + size] = (dot(rows, w[:, at : at + size]) + bias[:, at : at + size]).astype(BF)
    swap = remote(kv, kv_other, ks, kr, sibling)
    swap.start()
    queries[...] = (dot(rows, w[:, 2 * TH :]) + head_bias(vecs, 10, y)).astype(BF)
    swap.wait()
    for h in range(SLOTS):
        at = h * HD
        q = queries[:, at : at + HD]
        s_own = jnp.where(own, dot_nt(q, kv[:, at : at + HD]) * SCALE, -1e30)
        s_other = jnp.where(other, dot_nt(q, kv_other[:, at : at + HD]) * SCALE, -1e30)
        top = jnp.maximum(jnp.max(s_own, axis=-1, keepdims=True), jnp.max(s_other, axis=-1, keepdims=True))
        e_own = jnp.exp(s_own - top)
        e_other = jnp.exp(s_other - top)
        total = jnp.sum(e_own, axis=-1, keepdims=True) + jnp.sum(e_other, axis=-1, keepdims=True)
        logsum[:, h : h + 1] = top + jnp.log(total)
        inverse = 1.0 / total
        a_own = (e_own * inverse).astype(BF)
        a_other = (e_other * inverse).astype(BF)
        out = dot(a_own, kv[:, TH + at : TH + at + HD]) + dot(a_other, kv_other[:, TH + at : TH + at + HD])
        attended[:, at : at + HD] = out.astype(BF)
    out_wait(weights, wo, y)
    mixed = attended[...]
    for at, size in chunks(D):
        acc[:, at : at + size] = dot(mixed, wo[:, at : at + size])
    scatter_start(acc, out_buf, in_buf, y, c, ss, sr)
    base = x[...].astype(F32) + vecs[4:5]
    middle[...] = base + scatter_wait(acc, out_buf, in_buf, y, c, ss, sr)


def feed_forward(e, middle, wu_hbm, wd_hbm, vecs, result, normed, hidden, active,
                 wu, wd, acc, out_buf, in_buf, ls, gs, gr, ss, sr):
    y, c = place()
    arrived = greet([at_chip(ring(y, k), c) for k in (1, 2, 3)])
    weights = load([(wu_hbm.at[e], wu), (wd_hbm.at[e], wd)], ls)
    slot(normed, y)[...] = norm(middle[...], vecs[2:3], vecs[3:4]).astype(BF)
    arrived()
    gather_start(normed, y, c, gs, gr)
    bias = jnp.sum(chip_row(y, vecs[6:10]), axis=0, keepdims=True)
    weights[0].wait()
    gather_wait(normed, y, c, gs, gr)
    rows = normed[...]
    for at, size in chunks(D):
        h = dot(rows, wu[:, at : at + size]) + bias[:, at : at + size]
        hidden[:, at : at + size] = h
        active[:, at : at + size] = gelu(h).astype(BF)
    weights[1].wait()
    rows = active[...]
    for at, size in chunks(D):
        acc[:, at : at + size] = dot(rows, wd[:, at : at + size])
    scatter_start(acc, out_buf, in_buf, y, c, ss, sr)
    base = middle[...] + vecs[5:6]
    result[...] = (base + scatter_wait(acc, out_buf, in_buf, y, c, ss, sr)).astype(BF)


def feed_back(e, grad, wu_hbm, wd_hbm, vecs, middle, normed, hidden, active, grad_middle, grad_up, grad_down, small,
              wu, wd, full, gh, acc, out_buf, in_buf, ls, gs, gr, ss, sr, arrived, reduce=None, weights=None):
    y, c = place()
    if weights is None:
        weights = load([(wu_hbm.at[e], wu), (wd_hbm.at[e], wd)], ls)
    own_rows = grad[...]
    slot(full, y)[...] = own_rows
    arrived()
    gather_start(full, y, c, gs, gr)
    if reduce is not None:
        reduce.begin(y, c)
    small[...] = jnp.zeros_like(small)
    small[3:4] = jnp.sum(own_rows.astype(F32), axis=0, keepdims=True)
    weights[1].wait()
    if reduce is not None:
        reduce.middle(y, c)
    gather_wait(full, y, c, gs, gr)
    rows = full[...]
    for at, size in chunks(D):
        slope = gelu_slope(hidden[:, at : at + size])
        part = (dot_nt(rows, wd[at : at + size, :]) * slope).astype(BF)
        gh[:, at : at + size] = part
        small[2:3, at : at + size] = jnp.sum(part.astype(F32), axis=0, keepdims=True)
    weights[0].wait()
    rows = gh[...]
    for at, size in chunks(D):
        acc[:, at : at + size] = dot_nt(rows, wu[at : at + size, :])
    scatter_start(acc, out_buf, in_buf, y, c, ss, sr)
    if reduce is not None:
        reduce.late()
    for at, size in chunks(D):
        grad_up[at : at + size, :] = dot_tn(normed[:, at : at + size], gh[...]).astype(BF)
        grad_down[at : at + size, :] = dot_tn(active[:, at : at + size], full[...]).astype(BF)
    d = scatter_wait(acc, out_buf, in_buf, y, c, ss, sr)
    back, gain, shift = norm_back(d, middle[...], vecs[2:3])
    small[0:1] = gain
    small[1:2] = shift
    grad_middle[...] = grad[...].astype(F32) + back
    if reduce is not None:
        reduce.finish()


def attend_back(e, grad, w_hbm, wo_hbm, vecs, x, normed, queries, kv, kv_other, logsum, attended,
                grad_x, grad_attn, grad_out, small, small_bias,
                w, wo, full, ga, gj, part_out, part_in, part_own, rows_out, edge, acc, out_buf, in_buf, ls, gs, gr, ss, sr, ks, kr, es, er,
                arrived, reduce):
    y, c = place()
    sibling = at_chip(y, 1 - c)
    weights = load([(w_hbm.at[e], w)] + out_rows(wo_hbm, wo, e, y), ls)
    own_rows = grad[...].astype(BF)
    slot(full, y)[...] = own_rows
    arrived()
    gather_start(full, y, c, gs, gr)
    reduce.begin(y, c)
    small[...] = jnp.zeros_like(small)
    small[2:3] = jnp.sum(own_rows.astype(F32), axis=0, keepdims=True)
    own, other = masks(c)
    out_wait(weights, wo, y)
    reduce.middle(y, c)
    gather_wait(full, y, c, gs, gr)
    ga[...] = dot_nt(full[...], wo[...]).astype(BF)
    for h in range(SLOTS):
        at = h * HD
        q = queries[:, at : at + HD]
        g = ga[:, at : at + HD]
        lse = logsum[:, h : h + 1]
        k_own, k_other = kv[:, at : at + HD], kv_other[:, at : at + HD]
        v_own, v_other = kv[:, TH + at : TH + at + HD], kv_other[:, TH + at : TH + at + HD]
        p_own = jnp.exp(jnp.where(own, dot_nt(q, k_own) * SCALE, -1e30) - lse)
        p_other = jnp.exp(jnp.where(other, dot_nt(q, k_other) * SCALE, -1e30) - lse)
        gp_own = dot_nt(g, v_own)
        gp_other = dot_nt(g, v_other)
        delta = jnp.sum(p_own * gp_own, axis=-1, keepdims=True) + jnp.sum(p_other * gp_other, axis=-1, keepdims=True)
        s_own = (p_own * (gp_own - delta)).astype(BF)
        s_other = (p_other * (gp_other - delta)).astype(BF)
        gj[:, 2 * TH + at : 2 * TH + at + HD] = ((dot(s_own, k_own) + dot(s_other, k_other)) * SCALE).astype(BF)
        part_own[:, at : at + HD] = dot_tn(s_own, q) * SCALE
        part_out[:, at : at + HD] = (dot_tn(s_other, q) * SCALE).astype(BF)
        part_own[:, TH + at : TH + at + HD] = dot_tn(p_own.astype(BF), g)
        part_out[:, TH + at : TH + at + HD] = dot_tn(p_other.astype(BF), g).astype(BF)
    swap = remote(part_out, part_in, ks, kr, sibling)
    swap.start()
    for at, size in chunks(D):
        rows_out[:, at : at + size] = dot_tn(attended[...], full[:, at : at + size]).astype(BF)
    lend = remote(rows_out.at[0:HD], edge, es, er, at_chip(ring(y, 3), c))
    lend.start()
    weights[0].wait()
    swap.wait()
    gj[:, : 2 * TH] = (part_own[...] + part_in[...].astype(F32)).astype(BF)
    rows = gj[...]
    for at, size in chunks(D):
        acc[:, at : at + size] = dot_nt(rows, w[at : at + size, :])
    scatter_start(acc, out_buf, in_buf, y, c, ss, sr)
    for j in range(CHIPS):
        part = dot_tn(normed[:, 272 * j : 272 * j + 272], gj[...])
        grad_attn[j, 0] = part[:136].astype(BF)
        grad_attn[j, 1] = part[136:].astype(BF)
    lend.wait()

    @pl.when(y < 3)
    def _():
        rows_out[256:320] = edge[...]

    chip_rows = rows_out[pl.ds(pl.multiple_of(16 * y, 16), 272)].astype(F32)
    grad_out[0] = chip_rows[:136].astype(BF)
    grad_out[1] = chip_rows[136:].astype(BF)
    reduce.ready(y, c)
    small_bias[...] = jnp.zeros_like(small_bias)
    small_bias[0:1] = jnp.sum(gj[...].astype(F32), axis=0, keepdims=True)
    d = scatter_wait(acc, out_buf, in_buf, y, c, ss, sr)
    back, gain, shift = norm_back(d, x[...].astype(F32), vecs[0:1])
    small[0:1] = gain
    small[1:2] = shift
    grad_x[...] = (grad[...] + back).astype(BF)
    reduce.finish()


def plane():
    s, r = lax.axis_index("section"), lax.axis_index("replica")
    return s, r // 2, r % 2, s * 8 + r


def at_plane(q):
    return {"section": q // 8, "replica": lax.rem(q, 8)}


def x_peers(x, h):
    return [{"replica": 2 * lax.rem(x + k, 4) + h} for k in (1, 2, 3)]


def z_peers(s, h):
    x = lax.axis_index("replica") // 2
    return [
        {"section": 1 - s},
        {"section": 1 - s, "replica": 2 * x + 1 - h},
        {"replica": 2 * x + 1 - h},
    ]


def plane_peers():
    s, x, h, me = plane()
    return x_peers(x, h) + z_peers(s, h)


class AlongX:
    def __init__(self, blocks, landing, out, send, recv):
        self.blocks, self.landing, self.out, self.send, self.recv = blocks, landing, out, send, recv

    def copies(self):
        s, x, h, me = plane()
        targets = x_peers(x, h)
        for k in ORDER:
            yield remote(
                self.blocks.at[lax.rem(x + k, 4)], self.landing.at[k - 1], self.send.at[k - 1], self.recv.at[k - 1],
                targets[k - 1],
            )

    def start(self):
        for copy in self.copies():
            copy.start()

    def finish(self):
        s, x, h, me = plane()
        for copy in self.copies():
            copy.wait()

        def add(i, carry):
            rows = pl.ds(pl.multiple_of(8 * (i % 17), 8), 8)
            total = self.blocks[x, i // 17, rows].astype(F32)
            for k in range(3):
                total = total + self.landing[k, i // 17, rows].astype(F32)
            self.out[i // 17, rows] = total.astype(BF)
            return carry

        lax.fori_loop(0, 34, add, 0)


def x_scratch(width):
    return [pltpu.VMEM((4, 2, 136, width), BF), pltpu.VMEM((3, 2, 136, width), BF), DMA((3,)), DMA((3,))]


class AlongZ:
    def __init__(self, layer, blocks, landing, out, send, recv):
        self.layer, self.blocks, self.landing, self.out, self.send, self.recv = layer, blocks, landing, out, send, recv

    def copies(self):
        s, x, h, me = plane()
        for half in (0, 1):
            owner = 2 * half + self.layer
            rel = lax.rem(2 * h + s - owner + 3, 4)
            target = {"section": jnp.int32(self.layer), "replica": 2 * x + half}
            copy = remote(self.blocks, self.landing.at[rel], self.send.at[half], self.recv.at[rel], target)
            yield 2 * h + s != owner, copy

    def start(self):
        for sends, copy in self.copies():
            pl.when(sends)(copy.start)

    def finish(self):
        s, x, h, me = plane()
        for sends, copy in self.copies():
            pl.when(sends)(copy.wait_send)

        @pl.when(s == self.layer)
        def _():
            for rel in range(3):
                remote(self.blocks, self.landing.at[rel], self.send.at[0], self.recv.at[rel], {"section": 1 - s}).wait_recv()

            def add(i, carry):
                rows = pl.ds(pl.multiple_of(8 * (i % 17), 8), 8)
                total = self.blocks[i // 17, rows].astype(F32)
                for rel in range(3):
                    total = total + self.landing[rel, i // 17, rows].astype(F32)
                self.out[i // 17, rows] = total.astype(BF)
                return carry

            lax.fori_loop(0, 34, add, 0)

        @pl.when(s != self.layer)
        def _():
            self.out[...] = jnp.zeros_like(self.out)


def z_scratch(width):
    return [pltpu.VMEM((3, 2, 136, width), BF), DMA((2,)), DMA((3,))]


class FeedReduce:
    def __init__(self, up, down, out, other, ls, cs, cr, *scratch):
        self.sources = (up, down)
        self.other, self.ls, self.cs, self.cr = other, ls, cs, cr
        self.along = AlongX(scratch[0], scratch[1], out, scratch[2], scratch[3])
        self.blocks = scratch[0]

    def keeps(self, c):
        up, down = self.sources
        return [
            pltpu.make_async_copy(up.at[:, c], self.blocks.at[:, 0], self.ls.at[0]),
            pltpu.make_async_copy(down.at[c], self.blocks.at[:, 1], self.ls.at[1]),
        ]

    def swaps(self, y, c):
        up, down = self.sources
        sibling = at_chip(y, 1 - c)
        return [
            remote(up.at[:, 1 - c], self.other.at[:, 0], self.cs.at[0], self.cr.at[0], sibling),
            remote(down.at[1 - c], self.other.at[:, 1], self.cs.at[1], self.cr.at[1], sibling),
        ]

    def begin(self, y, c):
        for copy in self.keeps(c) + self.swaps(y, c):
            copy.start()

    def middle(self, y, c):
        for copy in self.keeps(c) + self.swaps(y, c):
            copy.wait()

        def add(i, carry):
            self.blocks[i // 2, i % 2] = (
                self.blocks[i // 2, i % 2].astype(F32) + self.other[i // 2, i % 2].astype(F32)
            ).astype(BF)
            return carry

        lax.fori_loop(0, 8, add, 0)
        self.along.start()

    def finish(self):
        self.along.finish()


FEED_SCRATCH = [pltpu.VMEM((4, 2, 136, D), BF), DMA((2,)), DMA((2,)), DMA((2,))] + x_scratch(D)


class AttendReduce:
    def __init__(self, wide, rows, out, other_w, other_r, cs, cr, *scratch):
        self.wide, self.rows = wide, rows
        self.other_w, self.other_r = other_w, other_r
        self.cs, self.cr = cs, cr
        self.along = AlongX(scratch[0], scratch[1], out, scratch[2], scratch[3])
        self.blocks = scratch[0]

    def swaps(self, y, c):
        sibling = at_chip(y, 1 - c)
        return [
            remote(self.wide.at[:, 1 - c], self.other_w, self.cs.at[0], self.cr.at[0], sibling),
            remote(self.rows.at[1 - c], self.other_r, self.cs.at[1], self.cr.at[1], sibling),
        ]

    def begin(self, y, c):
        for copy in self.swaps(y, c):
            copy.start()

    def middle(self, y, c):
        for copy in self.swaps(y, c):
            copy.wait()
        blocks = self.blocks
        for i in range(4):
            block = self.wide[i, c].astype(F32) + self.other_w[i].astype(F32)
            blocks[i, 0] = block[:, :640].astype(BF)
            blocks[i, 1, :, :320] = block[:, 640:].astype(BF)
            chunk = self.rows[c, :, 256 * i : 256 * i + 256].astype(F32) + self.other_r[:, 256 * i : 256 * i + 256].astype(F32)
            blocks[i, 1, :, 320:576] = chunk.astype(BF)
            if i < 3:
                blocks[i, 1, :, 576:] = jnp.zeros((136, HD), BF)
        chunk = self.rows[c, :, 1024:].astype(F32) + self.other_r[:, 1024:].astype(F32)
        blocks[3, 1, :, 576:] = chunk.astype(BF)
        self.along.start()

    def finish(self):
        self.along.finish()


ATTEND_SCRATCH = [
    pltpu.VMEM((4, 136, TQKV), BF),
    pltpu.VMEM((136, D), BF),
    DMA((2,)),
    DMA((2,)),
] + x_scratch(640)


BLOCKS = [pltpu.VMEM((4, 2, 136, TQKV), BF), pltpu.VMEM((2, 136, D), BF)]


class Hooks:
    def __init__(self, begin=(), middle=(), late=(), ready=()):
        self.steps = begin, middle, late, ready

    def begin(self, y, c):
        for step in self.steps[0]:
            step(y, c)

    def middle(self, y, c):
        for step in self.steps[1]:
            step(y, c)

    def late(self):
        for step in self.steps[2]:
            step()

    def ready(self, y, c):
        for step in self.steps[3]:
            step(y, c)

    def finish(self):
        pass


def split(refs, *counts):
    parts, at = [], 0
    for count in counts:
        parts.append(refs[at : at + count])
        at += count
    assert at == len(refs)
    return parts


def feed_back_alone(e, *refs):
    y, c = place()
    feed_back(e, *refs, greet([at_chip(ring(y, k), c) for k in (1, 2, 3)]))


def backward_middle(*refs):
    a_in, updown, f_in, a_out, half_u, f_out, half_a, a_scr, u_scr, f_scr, grads, w_scr = split(
        refs, 11, 2, 7, 3, 1, 4, 1, len(ATTEND_OWN), len(FEED_SCRATCH), len(FEED_OWN), 2, len(ATTEND_SCRATCH)
    )
    y, c = place()
    s, x, h, me = plane()
    arrived = greet([at_chip(ring(y, k), c) for k in (1, 2, 3)] + [at_chip(y, 1 - c)] + x_peers(x, h))
    wu_hbm, wd_hbm, vecs, *kept = f_in
    weights = load([(wu_hbm.at[0], f_scr[0]), (wd_hbm.at[0], f_scr[1])], f_scr[7])
    feed = FeedReduce(*updown, half_u[0], *u_scr)
    attend = AttendReduce(*grads, half_a[0], *w_scr)
    grad_x, small, small_bias = a_out
    attend_back(1, *a_in, grad_x, *grads, small, small_bias, *a_scr, arrived,
                Hooks(begin=[feed.begin], middle=[feed.middle], ready=[attend.begin]))
    feed_back(0, grad_x, wu_hbm, wd_hbm, vecs, *kept, *f_out, *f_scr, lambda: None,
              Hooks(middle=[attend.middle], late=[feed.finish]), weights)
    attend.finish()


def backward_end(*refs):
    a_in, updown, halves, rest, a_out, g_out, a_scr, u_scr, grads, w_scr, z_scr, g_scr = split(
        refs, 11, 2, 2, 8, 1, 5, len(ATTEND_OWN), len(FEED_SCRATCH), 2, len(ATTEND_SCRATCH), 12 + 4 + 3, len(GATHER_OWN)
    )
    y, c = place()
    s, x, h, me = plane()
    sibling = at_chip(y, 1 - c)
    peers = [at_chip(ring(y, k), c) for k in (1, 2, 3)]
    barrier = pltpu.get_barrier_semaphore()
    for target in peers + [sibling] + [at_plane(lax.rem(me + j, 16)) for j in range(1, 16)]:
        pl.semaphore_signal(barrier, inc=1, device_id=target, device_id_type=MESH)

    @pl.when(x != y)
    def _():
        pl.semaphore_signal(barrier, inc=1, device_id={"fsdp": 2 * x + c, "replica": 2 * y + h}, device_id_type=MESH)

    def arrived():
        pl.semaphore_wait(barrier, 19 + jnp.where(x == y, 0, 1))

    half_u1, half_a1 = halves
    z_u1, z_a1, z_u0, z_a0 = z_scr[0:3], z_scr[3:6], z_scr[6:9], z_scr[9:12]
    pair_u1, pair_a1, half_u0, half_a0, small, small_bias, grad_back = z_scr[12:]
    (grad_x,) = a_out
    feed = FeedReduce(*updown, half_u0, *u_scr)
    attend = AttendReduce(*grads, half_a0, *w_scr)
    first_u = AlongZ(1, half_u1, z_u1[0], pair_u1, z_u1[1], z_u1[2])
    first_a = AlongZ(1, half_a1, z_a1[0], pair_a1, z_a1[1], z_a1[2])

    def start_first(y, c):
        first_u.start()
        first_a.start()

    attend_back(0, *a_in, grad_x, *grads, small, small_bias, *a_scr, arrived,
                Hooks(begin=[feed.begin, start_first], middle=[feed.middle], ready=[attend.begin]))
    gather_pieces(feed, attend, first_u, first_a, half_u0, half_a0, z_u0, z_a0, pair_u1, pair_a1,
                  small, small_bias, *rest, grad_x, *g_out, *g_scr)


def shape(dims, kind):
    return jax.ShapeDtypeStruct(dims, kind)


MOVE = [
    pltpu.VMEM((ROWS, D), F32),
    pltpu.VMEM((3, BLK, D), BF),
    pltpu.VMEM((3, BLK, D), BF),
    DMA((3,)),
    DMA((3,)),
    DMA((3,)),
    DMA((3,)),
    DMA((3,)),
]


def call(body, name, number, outs, ins, scratch):
    return pl.pallas_call(
        body,
        name=name,
        out_shape=outs,
        in_specs=ins,
        out_specs=[VMEM] * len(outs),
        scratch_shapes=scratch,
        cost_estimate=COST,
        compiler_params=pltpu.CompilerParams(collective_id=number, has_side_effects=True, vmem_limit_bytes=LIMIT),
    )


def run_attend_forward(e, x, w, wo, vecs):
    outs = [
        shape((BLK, D), F32),
        shape((ROWS, D), BF),
        shape((ROWS, TH), BF),
        shape((ROWS, 2 * TH), BF),
        shape((ROWS, 2 * TH), BF),
        shape((ROWS, 128), F32),
        shape((ROWS, TH), BF),
    ]
    scratch = [pltpu.VMEM((D, TQKV), BF), pltpu.VMEM((TH, D), BF)] + MOVE + [DMA, DMA]
    return call(functools.partial(attend_forward, e), "attend_forward_%d" % e, e, outs, [VMEM, ANY, ANY, VMEM], scratch)(x, w, wo, vecs)


def run_feed_forward(e, middle, wu, wd, vecs):
    outs = [shape((BLK, D), BF), shape((ROWS, D), BF), shape((ROWS, D), F32), shape((ROWS, D), BF)]
    scratch = [pltpu.VMEM((D, D), BF), pltpu.VMEM((D, D), BF)] + MOVE
    return call(functools.partial(feed_forward, e), "feed_forward_%d" % e, 2 + e, outs, [VMEM, ANY, ANY, VMEM], scratch)(middle, wu, wd, vecs)


HALF_A, HALF_U = shape((2, 136, 640), BF), shape((2, 136, D), BF)


FEED_OWN = [
    pltpu.VMEM((D, D), BF),
    pltpu.VMEM((D, D), BF),
    pltpu.VMEM((ROWS, D), BF),
    pltpu.VMEM((ROWS, D), BF),
] + MOVE
ATTEND_OWN = [
    pltpu.VMEM((D, TQKV), BF),
    pltpu.VMEM((TH, D), BF),
    pltpu.VMEM((ROWS, D), BF),
    pltpu.VMEM((ROWS, TH), BF),
    pltpu.VMEM((ROWS, TQKV), BF),
    pltpu.VMEM((ROWS, 2 * TH), BF),
    pltpu.VMEM((ROWS, 2 * TH), BF),
    pltpu.VMEM((ROWS, 2 * TH), F32),
    pltpu.VMEM((TH, D), BF),
    pltpu.VMEM((HD, D), BF),
] + MOVE + [DMA, DMA, DMA, DMA]
GATHER_OWN = [
    pltpu.VMEM((BLK, D), BF),
    pltpu.VMEM((BLK, D), BF),
    DMA((2,)),
    DMA((2,)),
    pltpu.VMEM((2, 136, D), BF),
    pltpu.VMEM((136, D), BF),
    pltpu.VMEM((2, 136, 640), BF),
    pltpu.VMEM((2, 136, 640), BF),
    pltpu.VMEM((2, 16, D), F32),
    pltpu.VMEM((2, 16, D), F32),
    pltpu.VMEM((3, 2, 16, D), F32),
    pltpu.VMEM((2, 16, D), BF),
    pltpu.VMEM((15, 16, D), BF),
    DMA((2,)),
    DMA((2,)),
    DMA((2, 3)),
    DMA((2, 3)),
    DMA,
    DMA,
    DMA((3,)),
    DMA((3,)),
    DMA((15,)),
    DMA((15,)),
]
FEED_OUTS = [shape((BLK, D), F32), shape((D, D), BF), shape((D, D), BF), shape((8, D), F32)]
SMALLS = [shape((8, D), F32), shape((8, TQKV), F32)]


def run_feed_back(grad, wu, wd, vecs, middle, normed, hidden, active):
    return call(functools.partial(feed_back_alone, 1), "feed_back_1", 4, FEED_OUTS, [VMEM, ANY, ANY] + [VMEM] * 5, FEED_OWN)(
        grad, wu, wd, vecs, middle, normed, hidden, active
    )


def run_backward_middle(attend_args, up, down, feed_args):
    outs = [shape((BLK, D), BF)] + SMALLS + [HALF_U] + FEED_OUTS + [HALF_A]
    ins = [VMEM, ANY, ANY] + [VMEM] * 8 + [ANY] * 4 + [VMEM] * 5
    scratch = ATTEND_OWN + FEED_SCRATCH + FEED_OWN + BLOCKS + ATTEND_SCRATCH
    return call(backward_middle, "backward_middle", 5, outs, ins, scratch)(*attend_args, up, down, *feed_args)


def run_backward_end(attend_args, up, down, half_u, half_a, rest):
    both = shape((2, BLK, D), BF)
    outs = [shape((BLK, D), BF)]
    outs += [shape((4, 2, 136, D), BF), shape((4, 2, 136, 640), BF), shape((16, D), F32), both, both]
    ins = [VMEM, ANY, ANY] + [VMEM] * 8 + [ANY] * 2 + [VMEM] * (2 + len(rest))
    pairs = [
        pltpu.VMEM((2, 136, D), BF),
        pltpu.VMEM((2, 136, 640), BF),
        pltpu.VMEM((2, 136, D), BF),
        pltpu.VMEM((2, 136, 640), BF),
        pltpu.VMEM((8, D), F32),
        pltpu.VMEM((8, TQKV), F32),
        pltpu.VMEM((8, 128), F32),
    ]
    zs = (z_scratch(D) + z_scratch(640)) * 2
    scratch = ATTEND_OWN + FEED_SCRATCH + BLOCKS + ATTEND_SCRATCH + zs + pairs + GATHER_OWN
    return call(backward_end, "backward_end", 6, outs, ins, scratch)(
        *attend_args, up, down, half_u, half_a, *rest
    )


def spread(send_a, send_u, send_d, send_o, send_v, wa, wu, wd, wo, wv, hold_a, hold_u, hold_d, hold_o, hold_v, local, ysend, yrecv, zsend, zrecv, csend, crecv):
    s = lax.axis_index("section")
    y, c = place()
    replica = lax.axis_index("replica")
    flipped = replica // 2 * 2 + (1 - replica % 2)
    near = {"section": 1 - s}
    far = {"section": 1 - s, "replica": flipped}
    sibling = at_chip(y, 1 - c)
    peers = [at_chip(ring(y, k), c) for k in (1, 2, 3)]
    arrived = greet(peers + [sibling, near, far])
    brought = load(
        [(send_a.at[y], hold_a), (send_u.at[y], hold_u), (send_d, hold_d), (send_o, hold_o), (send_v, hold_v)], local.at[0]
    )
    for copy in brought:
        copy.wait()
    keeps = load(
        [
            (hold_a, wa.at[s, y, c]),
            (hold_u, wu.at[s, y, c]),
            (hold_d, wd.at[s, c]),
            (hold_o, wo.at[s, c]),
            (hold_v, wv.at[s, y, c]),
        ],
        local.at[1],
    )
    arrived()

    def along_y(k, back):
        target = ring(y, k)
        place_in = ring(y, 4 - k) if back else y
        return [
            remote(send_v, wv.at[s, place_in, c], ysend.at[0, k - 1], yrecv.at[0, k - 1], at_chip(target, c)),
            remote(send_a.at[target], wa.at[s, place_in, c], ysend.at[1, k - 1], yrecv.at[1, k - 1], at_chip(target, c)),
            remote(send_u.at[target], wu.at[s, place_in, c], ysend.at[2, k - 1], yrecv.at[2, k - 1], at_chip(target, c)),
        ]

    def along_z(layer):
        return [
            remote(wv.at[layer, :, c], wv.at[layer, :, c], zsend.at[0], zrecv.at[0], near),
            remote(wa.at[layer, 0:2, c], wa.at[layer, 0:2, c], zsend.at[1], zrecv.at[1], near),
            remote(wa.at[layer, 2:4, c], wa.at[layer, 2:4, c], zsend.at[2], zrecv.at[2], far),
            remote(wo.at[layer, c], wo.at[layer, c], zsend.at[3], zrecv.at[3], far),
            remote(wu.at[layer, 0:2, c], wu.at[layer, 0:2, c], zsend.at[4], zrecv.at[4], near),
            remote(wu.at[layer, 2:4, c], wu.at[layer, 2:4, c], zsend.at[5], zrecv.at[5], far),
            remote(wd.at[layer, c, 0:272], wd.at[layer, c, 0:272], zsend.at[6], zrecv.at[6], near),
            remote(wd.at[layer, c, 272:544], wd.at[layer, c, 272:544], zsend.at[7], zrecv.at[7], far),
        ]

    def across(layer, i, core):
        return [
            remote(wv.at[layer, :, core], wv.at[layer, :, core], csend.at[i, 0], crecv.at[i, 0], sibling),
            remote(wa.at[layer, :, core], wa.at[layer, :, core], csend.at[i, 1], crecv.at[i, 1], sibling),
            remote(wo.at[layer, core], wo.at[layer, core], csend.at[i, 2], crecv.at[i, 2], sibling),
            remote(wu.at[layer, :, core], wu.at[layer, :, core], csend.at[i, 3], crecv.at[i, 3], sibling),
            remote(wd.at[layer, core], wd.at[layer, core], csend.at[i, 4], crecv.at[i, 4], sibling),
        ]

    sent_y = [along_y(k, False) for k in (1, 2, 3)]
    got_y = [along_y(k, True) for k in (1, 2, 3)]
    sent_z, got_z = along_z(s), along_z(1 - s)
    sent_c = [across(s, 0, c), across(1 - s, 1, c)]
    got_c = [across(s, 0, 1 - c), across(1 - s, 1, 1 - c)]
    for kind in (0, 1):
        for k in (1, 0, 2):
            sent_y[k][kind].start()
    keeps[3].wait()
    sent_z[3].start()
    sent_c[0][2].start()
    keeps[2].wait()
    sent_z[6].start()
    sent_z[7].start()
    sent_c[0][4].start()
    for kind, keep, zs, cross in ((0, 4, (0,), 0), (1, 0, (1, 2), 1)):
        keeps[keep].wait()
        for k in range(3):
            got_y[k][kind].wait_recv()
        for z in zs:
            sent_z[z].start()
        sent_c[0][cross].start()
    for k in (1, 0, 2):
        sent_y[k][2].start()
    for zs, cross in (((3,), 2), ((6, 7), 4), ((0,), 0), ((1, 2), 1)):
        for z in zs:
            got_z[z].wait_recv()
        sent_c[1][cross].start()
    keeps[1].wait()
    for k in range(3):
        got_y[k][2].wait_recv()
    for z in (4, 5):
        sent_z[z].start()
    sent_c[0][3].start()
    for z in (4, 5):
        got_z[z].wait_recv()
    sent_c[1][3].start()
    for i in range(2):
        for cross in range(5):
            got_c[i][cross].wait_recv()
    for k in range(3):
        for kind in range(3):
            sent_y[k][kind].wait_send()
    for z in range(8):
        sent_z[z].wait_send()
    for i in range(2):
        for cross in range(5):
            sent_c[i][cross].wait_send()


def run_spread(a, u, d, o, v):
    outs = [
        shape((2, 4, 2, 136, TQKV), BF),
        shape((2, 4, 2, 136, D), BF),
        shape((2, 2, 544, D), BF),
        shape((2, 2, 192, D), BF),
        shape((2, 4, 2, 16, D), BF),
    ]
    return pl.pallas_call(
        spread,
        name="spread",
        out_shape=outs,
        in_specs=[ANY] * 5,
        out_specs=[ANY] * 5,
        scratch_shapes=[
            pltpu.VMEM((136, TQKV), BF),
            pltpu.VMEM((136, D), BF),
            pltpu.VMEM((544, D), BF),
            pltpu.VMEM((192, D), BF),
            pltpu.VMEM((16, D), BF),
            DMA((2, 5)), DMA((3, 3)), DMA((3, 3)), DMA((8,)), DMA((8,)), DMA((2, 5)), DMA((2, 5)),
        ],
        compiler_params=pltpu.CompilerParams(collective_id=8, has_side_effects=True),
    )(a, u, d, o, v)


def build_small(buf, one, two, heads, y):
    buf[...] = jnp.zeros_like(buf)
    buf[0:2] = one[0:2]
    buf[2:4] = two[0:2]
    buf[4:5] = one[2:3]
    buf[5:6] = two[3:4]
    buf[6:10] = chip_row(y, two[2:3])
    for row, at in ((10, 2 * TH), (11, TH)):
        buf[row : row + 1, pl.ds(pl.multiple_of(256 * y, 256), 256)] = heads[0:1, at : at + 256]

        @pl.when(y == 3)
        def _(row=row, at=at):
            buf[row : row + 1, 1024:D] = heads[0:1, at + 256 : at + TH]


class Gather:
    def __init__(self, pair, moved, out, number, keep_from, ts, tr, gs, gr):
        self.pair, self.moved, self.out, self.i, self.keep_from = pair, moved, out, number, keep_from
        self.ts, self.tr, self.gs, self.gr = ts, tr, gs, gr

    def transpose(self):
        y, c = place()
        s, x, h, me = plane()
        source = self.pair if self.keep_from else self.pair.at[0]
        return remote(source, self.moved, self.ts.at[self.i], self.tr.at[self.i], {"fsdp": 2 * x + c, "replica": 2 * y + h})

    def start(self):
        y, c = place()
        s, x, h, me = plane()
        pl.when(x != y)(self.transpose().start)

    def copies(self):
        s, x, h, me = plane()
        targets = x_peers(x, h)
        for k in ORDER:
            yield k, remote(self.pair, self.out.at[x], self.gs.at[self.i, k - 1], self.gr.at[self.i, k - 1], targets[k - 1])

    def spread(self):
        y, c = place()
        s, x, h, me = plane()

        @pl.when(x != y)
        def _():
            self.transpose().wait()
            if self.keep_from:
                self.pair[0] = self.moved[0]
                lane = lax.broadcasted_iota(jnp.int32, self.pair.shape[1:], 1)
                merged = jnp.where(lane < self.keep_from, self.moved[1].astype(F32), self.pair[1].astype(F32))
                self.pair[1] = merged.astype(BF)
            else:
                self.pair[0] = self.moved[...]

        for k, copy in self.copies():
            copy.start()
        self.out[x] = self.pair[...]

    def finish(self):
        s, x, h, me = plane()
        targets = x_peers(x, h)
        for k, copy in self.copies():
            copy.wait_send()
            place_in = self.out.at[lax.rem(x + 4 - k, 4)]
            remote(place_in, place_in, self.gs.at[self.i, k - 1], self.gr.at[self.i, k - 1], targets[k - 1]).wait_recv()


def gather_pieces(feed, attend, first_u, first_a, half_u, half_a, z_u, z_a, done_u, done_a, one_0, heads_0,
                  two_0, one_1, two_1, heads_1, act_0, act_1, back_1, spare, back_0, out_u, out_a, out_small, out_act, out_back,
                  swap_act, swap_back, ws, wr, piece_u, moved_u, piece_a, moved_a, small, small_c, small_y, small_x, small_z,
                  ts, tr, gs, gr, cs, cr, ys, yr, zs, zr):
    y, c = place()
    s, x, h, me = plane()
    sibling = at_chip(y, 1 - c)
    peers = [at_chip(ring(y, k), c) for k in (1, 2, 3)]
    z_u = AlongZ(0, half_u, z_u[0], piece_u, z_u[1], z_u[2])
    z_a = AlongZ(0, half_a, z_a[0], piece_a, z_a[1], z_a[2])
    g_u = Gather(piece_u, moved_u, out_u, 0, 0, ts, tr, gs, gr)
    g_a = Gather(piece_a, moved_a, out_a, 1, 320, ts, tr, gs, gr)
    attend.middle(y, c)
    feed.finish()
    z_u.start()
    build_small(small.at[0], one_0, two_0, heads_0, y)
    build_small(small.at[1], one_1, two_1, heads_1, y)
    swap_act[...] = jnp.where(s == 0, act_1[...].astype(F32), act_0[...].astype(F32)).astype(BF)
    swap_back[...] = jnp.where(s == 0, back_1[...].astype(F32), back_0[...].astype(F32)).astype(BF)
    swaps = [
        remote(swap_act, out_act.at[s], ws.at[0], wr.at[0], {"section": 1 - s}),
        remote(swap_back, out_back.at[s], ws.at[1], wr.at[1], {"section": 1 - s}),
    ]
    out_act[s] = jnp.where(s == 0, act_0[...].astype(F32), act_1[...].astype(F32)).astype(BF)
    out_back[s] = jnp.where(s == 0, back_0[...].astype(F32), back_1[...].astype(F32)).astype(BF)
    cross = remote(small, small_c, cs, cr, sibling)
    cross.start()
    cross.wait()
    small[...] = small[...] + small_c[...]
    hops = [remote(small, small_y.at[k - 1], ys.at[k - 1], yr.at[k - 1], peers[k - 1]) for k in (1, 2, 3)]
    for hop in hops:
        hop.start()
    first_u.finish()
    first_a.finish()
    attend.finish()
    z_a.start()
    z_u.finish()

    @pl.when(s == 1)
    def _():
        piece_u[...] = done_u[...]

    g_u.start()
    g_u.spread()
    for hop in hops:
        hop.wait()
    small_x[...] = (small[...] + small_y[0] + small_y[1] + small_y[2]).astype(BF)

    def plane_copies():
        for j in range(1, 16):
            q = lax.rem(me + j, 16)
            yield remote(small_x.at[q // 8], small_z.at[15 - j], zs.at[j - 1], zr.at[15 - j], at_plane(q))

    for copy in plane_copies():
        copy.start()
    z_a.finish()

    @pl.when(s == 1)
    def _():
        piece_a[...] = done_a[...]

    g_a.start()
    for swap in swaps:
        swap.start()
    g_a.spread()
    total = small_x[s].astype(F32)
    for copy in plane_copies():
        copy.wait_send()
    for j in range(15):
        remote(small_x.at[0], small_z.at[j], zs.at[j], zr.at[j], sibling).wait_recv()
        total = total + small_z[j].astype(F32)
    out_small[...] = total
    for i, swap in enumerate(swaps):
        swap.wait_send()
        place_in = (out_act, out_back)[i].at[1 - s]
        remote(place_in, place_in, ws.at[i], wr.at[i], {"section": 1 - s}).wait_recv()
    g_u.finish()
    g_a.finish()


def assemble(all_u, all_a, small, attn, out, up, down, b_attn, b_out, b_up, b_down, gain, shift):
    y, c = place()
    f = 2 * y + c
    for j in range(CHIPS):
        up[:, j * D : (j + 1) * D] = all_u[j, 0].astype(F32)
        down[j * 136 : (j + 1) * 136] = all_u[j, 1].astype(F32)
        first, second = all_a[j, 0].astype(F32), all_a[j, 1].astype(F32)
        parts = ((0, second[:, :TH]), (D, first[:, :TH]), (2 * D, first[:, TH:]))
        for base, part in parts:
            attn[:, base + 256 * j : base + 256 * j + 256] = part[:, :256]
        out[:, 256 * j : 256 * j + 256] = second[:, TH : TH + 256]
        if j == CHIPS - 1:
            for base, part in parts:
                attn[:, base + 1024 : base + D] = part[:, 256:]
            out[:, 1024:] = second[:, TH + 256 :]

    def pick(index, options):
        total = jnp.where(index == 0, options[0], 0.0)
        for i, option in enumerate(options[1:], 1):
            total = total + jnp.where(index == i, option, 0.0)
        return total

    for row, ref, place_in in ((0, gain, 0), (1, shift, 0), (2, gain, 1), (3, shift, 1), (4, b_out, 0), (5, b_down, 0)):
        ref[place_in : place_in + 1] = pick(f, [small[row : row + 1, 136 * i : 136 * i + 136] for i in range(8)])
    b_up[...] = pick(f, [small[6 + i // 2 : 7 + i // 2, 544 * (i % 2) : 544 * (i % 2) + 544] for i in range(8)])
    b_attn[...] = pick(f, [small[10 + i // 4 : 11 + i // 4, 272 * (i % 4) : 272 * (i % 4) + 272] for i in range(8)])


def run_assemble(all_u, all_a, small):
    sizes = [(136, 3 * D), (136, D), (136, FF), (544, D), (1, 272), (1, 136), (1, 544), (1, 136), (2, 136), (2, 136)]
    return pl.pallas_call(
        assemble,
        name="assemble",
        out_shape=[shape(dims, F32) for dims in sizes],
        in_specs=[VMEM] * 3,
        out_specs=[VMEM] * len(sizes),
        compiler_params=pltpu.CompilerParams(vmem_limit_bytes=LIMIT),
    )(all_u, all_a, small)


def split_heads(block):
    zero = jnp.zeros(block.shape[:-1] + (HD,), block.dtype)
    return [
        jnp.concatenate([block[..., 256 * j : 256 * j + 256], block[..., 1024:] if j == 3 else zero], axis=-1)
        for j in range(CHIPS)
    ]


def on_device(inputs, cotangent, weight_attn, weight_out, weight_up, weight_down, bias_attn, bias_out, bias_up,
              bias_down, norm_gain, norm_bias):
    s = lax.axis_index("section")
    f = lax.axis_index("fsdp")
    y, c = f // 2, f % 2
    wa = weight_attn[0]
    q_blocks, k_blocks, v_blocks = (split_heads(wa[:, i * D : (i + 1) * D]) for i in range(3))
    send_a = jnp.stack(
        [jnp.concatenate([k_blocks[j], v_blocks[j], q_blocks[j]], axis=-1) for j in range(CHIPS)]
    )
    send_u = jnp.stack([weight_up[0][:, j * D : (j + 1) * D] for j in range(CHIPS)])
    tail = lax.ppermute(weight_out[0, 88:], "fsdp", [(i, (i + 2) % 8) for i in range(8)])
    send_o = jnp.concatenate([weight_out[0], tail, jnp.zeros((8, D), BF)], axis=0)
    vectors = jnp.stack([norm_gain[0, 0], norm_bias[0, 0], norm_gain[0, 1], norm_bias[0, 1], bias_out[0], bias_down[0]])
    send_v = jnp.concatenate(
        [
            lax.dynamic_update_slice(jnp.zeros((6, D), BF), vectors, (0, 136 * f)),
            lax.dynamic_update_slice(jnp.zeros((4, D), BF), bias_up, (y, 544 * c)),
            lax.dynamic_update_slice(jnp.zeros((6, D), BF), bias_attn, (f // 4, 272 * (f % 4))),
        ]
    )
    wa, wu, wd, wo, wv = run_spread(send_a, send_u, weight_down[0], send_o, send_v)
    wa = wa.reshape(2, D, TQKV)
    wu = wu.reshape(2, D, D)
    wd = wd.reshape(2, D, D)
    wo = jnp.concatenate([wo[:, 1, 136:184], wo[:, 0, :136], wo[:, 1, :136]], axis=1)
    vecs = jnp.sum(wv.astype(F32), axis=(1, 2))
    stream = lax.dynamic_index_in_dim(inputs, s, 0, keepdims=False)[0]
    saved, acts = [], []
    for e in range(2):
        middle, *kept = run_attend_forward(e, stream, wa, wo, vecs[e])
        result, *kept_two = run_feed_forward(e, middle, wu, wd, vecs[e])
        saved.append((stream, kept, middle, kept_two))
        acts.append(result)
        stream = result
    grad = lax.dynamic_index_in_dim(cotangent, s, 0, keepdims=False)[0]
    x_1, kept_1, middle_1, kept_two_1 = saved[1]
    x_0, kept_0, middle_0, kept_two_0 = saved[0]
    grad_middle, up, down, two_1 = run_feed_back(grad, wu, wd, vecs[1], middle_1, *kept_two_1)
    back_1, one_1, heads_1, half_u, grad_middle, up_0, down_0, two_0, half_a = run_backward_middle(
        (grad_middle, wa, wo, vecs[1], x_1, *kept_1),
        up.reshape(4, 2, 136, D),
        down.reshape(2, 4, 136, D),
        (wu, wd, vecs[0], middle_0, *kept_two_0),
    )
    back_0, all_u, all_a, small, all_acts, all_grads = run_backward_end(
        (grad_middle, wa, wo, vecs[0], x_0, *kept_0),
        up_0.reshape(4, 2, 136, D),
        down_0.reshape(2, 4, 136, D),
        half_u,
        half_a,
        (two_0, one_1, two_1, heads_1, *acts, back_1, two_0),
    )
    attn, out, up, down, b_attn, b_out, b_up, b_down, gain, shift = run_assemble(all_u, all_a, small)
    return (
        all_acts[None, :, None],
        all_grads[None, :, None],
        attn[None],
        out[None],
        up[None],
        down[None],
        b_attn,
        b_out,
        b_up,
        b_down,
        gain[None],
        shift[None],
    )


def solution(mesh):
    placed = (
        P(None, "replica", "fsdp", None),
        P(None, "replica", "fsdp", None),
        P("section", "fsdp", None),
        P("section", "fsdp", None),
        P("section", "fsdp", None),
        P("section", "fsdp", None),
        P("section", "fsdp"),
        P("section", "fsdp"),
        P("section", "fsdp"),
        P("section", "fsdp"),
        P("section", None, "fsdp"),
        P("section", None, "fsdp"),
    )
    return jax.shard_map(
        on_device,
        mesh=mesh,
        in_specs=placed,
        out_specs=(
            P("section", None, "replica", "fsdp", None),
            P("section", None, "replica", "fsdp", None),
        )
        + placed[2:],
        check_vma=False,
    )
```

```python
import functools

import jax
import jax.numpy as jnp
from jax import lax
from jax.experimental import pallas as pl
from jax.experimental.pallas import tpu as pltpu
from jax.sharding import PartitionSpec as P

D = 1088
FF = 4352
HEADS = 17
HD = 64
BLK = 64
CHIPS = 4
ROWS = BLK * CHIPS
SLOTS = 5
TH = SLOTS * HD
TQKV = 3 * TH
SCALE = HD**-0.5
EPS = 1e-5
MESH = pl.DeviceIdType.MESH
BF = jnp.bfloat16
F32 = jnp.float32
ANY = pl.BlockSpec(memory_space=pl.ANY)
VMEM = pl.BlockSpec(memory_space=pltpu.VMEM)
DMA = pltpu.SemaphoreType.DMA
LIMIT = 56 * 1024 * 1024
COST = pl.CostEstimate(flops=10_000_000, bytes_accessed=10_000, transcendentals=0)


def dot(a, b):
    return lax.dot_general(a, b, (((1,), (0,)), ((), ())), preferred_element_type=F32)


def dot_nt(a, b):
    return lax.dot_general(a, b, (((1,), (1,)), ((), ())), preferred_element_type=F32)


def dot_tn(a, b):
    return lax.dot_general(a, b, (((0,), (0,)), ((), ())), preferred_element_type=F32)


def chunks(n, size=256):
    return [(i, min(size, n - i)) for i in range(0, n, size)]


def place():
    f = lax.axis_index("fsdp")
    return f // 2, f % 2


def ring(y, k):
    return lax.rem(y + k, CHIPS)


def at_chip(y, c):
    return {"fsdp": 2 * y + c}


def greet(targets):
    barrier = pltpu.get_barrier_semaphore()
    for target in targets:
        pl.semaphore_signal(barrier, inc=1, device_id=target, device_id_type=MESH)
    return functools.partial(pl.semaphore_wait, barrier, len(targets))


def remote(src, dst, send, recv, target):
    return pltpu.make_async_remote_copy(
        src_ref=src, dst_ref=dst, send_sem=send, recv_sem=recv, device_id=target, device_id_type=MESH
    )


def slot(ref, y):
    return ref.at[pl.ds(pl.multiple_of(y * BLK, BLK), BLK)]


ORDER = (2, 1, 3)


def gather_start(full, y, c, send, recv):
    for k in ORDER:
        remote(slot(full, y), slot(full, y), send.at[k - 1], recv.at[k - 1], at_chip(ring(y, k), c)).start()


def gather_wait(full, y, c, send, recv):
    for k in (1, 3, 2):
        source = ring(y, 4 - k)
        remote(slot(full, source), slot(full, source), send.at[k - 1], recv.at[k - 1], at_chip(ring(y, k), c)).wait()


def scatter_start(acc, out_buf, in_buf, y, c, send, recv):
    for k in ORDER:
        target = ring(y, k)
        out_buf[k - 1] = slot(acc, target)[...].astype(BF)
        remote(out_buf.at[k - 1], in_buf.at[k - 1], send.at[k - 1], recv.at[k - 1], at_chip(target, c)).start()


def scatter_wait(acc, out_buf, in_buf, y, c, send, recv):
    total = slot(acc, y)[...]
    for k in (1, 3, 2):
        remote(out_buf.at[k - 1], in_buf.at[k - 1], send.at[k - 1], recv.at[k - 1], at_chip(ring(y, k), c)).wait()
        total = total + in_buf[k - 1].astype(F32)
    return total


def stats(v):
    centre = v - jnp.mean(v, axis=-1, keepdims=True)
    scale = lax.rsqrt(jnp.mean(centre * centre, axis=-1, keepdims=True) + EPS)
    return centre * scale, scale


def norm(v, gain, shift):
    return stats(v)[0] * gain + shift


def norm_back(d, v, gain):
    vh, scale = stats(v)
    q = d * gain
    grad = scale * (q - jnp.mean(q, axis=-1, keepdims=True) - vh * jnp.mean(q * vh, axis=-1, keepdims=True))
    return grad, jnp.sum(d * vh, axis=0, keepdims=True), jnp.sum(d, axis=0, keepdims=True)


GELU_A = 0.7978845608028654
GELU_B = 0.044715


def gelu(h):
    return 0.5 * h * (1.0 + jnp.tanh(GELU_A * (h + GELU_B * h * h * h)))


def gelu_slope(h):
    t = jnp.tanh(GELU_A * (h + GELU_B * h * h * h))
    return 0.5 * (1.0 + t) + 0.5 * h * (1.0 - t * t) * (GELU_A * (1.0 + 3.0 * GELU_B * h * h))


def masks(c):
    row = lax.broadcasted_iota(jnp.int32, (ROWS, ROWS), 0)
    col = lax.broadcasted_iota(jnp.int32, (ROWS, ROWS), 1)
    own = row >= col
    other = (row // BLK) >= (col // BLK) + (1 - c)
    return own, other


def load(pairs, sems):
    copies = [pltpu.make_async_copy(src, dst, sems.at[i]) for i, (src, dst) in enumerate(pairs)]
    for copy in copies:
        copy.start()
    return copies


def out_rows(wo_hbm, wo, e, y):
    start = pl.multiple_of(48 - 16 * y, 16)
    return [(wo_hbm.at[e, pl.ds(start, 256)], wo.at[0:256]), (wo_hbm.at[e, 256:320], wo.at[256:320])]


def out_wait(weights, wo, y):
    weights[1].wait()
    weights[2].wait()

    @pl.when(y < 3)
    def _():
        wo[256:320] = jnp.zeros((HD, D), BF)


def chip_row(y, rows):
    return jnp.where(lax.broadcasted_iota(jnp.int32, (CHIPS, 1), 0) == y, rows, 0.0)


def head_bias(vecs, row, y):
    last = jnp.where(y == 3, vecs[row : row + 1, 1024:D], 0.0)
    return jnp.concatenate([vecs[row : row + 1, pl.ds(pl.multiple_of(256 * y, 256), 256)], last], axis=-1)


def attend_forward(e, x, w_hbm, wo_hbm, vecs, middle, normed, queries, kv, kv_other, logsum, attended,
                   w, wo, acc, out_buf, in_buf, ls, gs, gr, ss, sr, ks, kr):
    y, c = place()
    peers = [at_chip(ring(y, k), c) for k in (1, 2, 3)]
    sibling = at_chip(y, 1 - c)
    arrived = greet(peers + [sibling])
    weights = load([(w_hbm.at[e], w)] + out_rows(wo_hbm, wo, e, y), ls)
    slot(normed, y)[...] = norm(x[...].astype(F32), vecs[0:1], vecs[1:2]).astype(BF)
    arrived()
    gather_start(normed, y, c, gs, gr)
    own, other = masks(c)
    weights[0].wait()
    gather_wait(normed, y, c, gs, gr)
    rows = normed[...]
    bias = jnp.concatenate([jnp.zeros((1, TH), F32), head_bias(vecs, 11, y)], axis=-1)
    for at, size in chunks(2 * TH):
        kv[:, at : at + size] = (dot(rows, w[:, at : at + size]) + bias[:, at : at + size]).astype(BF)
    swap = remote(kv, kv_other, ks, kr, sibling)
    swap.start()
    queries[...] = (dot(rows, w[:, 2 * TH :]) + head_bias(vecs, 10, y)).astype(BF)
    swap.wait()
    for h in range(SLOTS):
        at = h * HD
        q = queries[:, at : at + HD]
        s_own = jnp.where(own, dot_nt(q, kv[:, at : at + HD]) * SCALE, -1e30)
        s_other = jnp.where(other, dot_nt(q, kv_other[:, at : at + HD]) * SCALE, -1e30)
        top = jnp.maximum(jnp.max(s_own, axis=-1, keepdims=True), jnp.max(s_other, axis=-1, keepdims=True))
        e_own = jnp.exp(s_own - top)
        e_other = jnp.exp(s_other - top)
        total = jnp.sum(e_own, axis=-1, keepdims=True) + jnp.sum(e_other, axis=-1, keepdims=True)
        logsum[:, h : h + 1] = top + jnp.log(total)
        inverse = 1.0 / total
        a_own = (e_own * inverse).astype(BF)
        a_other = (e_other * inverse).astype(BF)
        out = dot(a_own, kv[:, TH + at : TH + at + HD]) + dot(a_other, kv_other[:, TH + at : TH + at + HD])
        attended[:, at : at + HD] = out.astype(BF)
    out_wait(weights, wo, y)
    mixed = attended[...]
    for at, size in chunks(D):
        acc[:, at : at + size] = dot(mixed, wo[:, at : at + size])
    scatter_start(acc, out_buf, in_buf, y, c, ss, sr)
    base = x[...].astype(F32) + vecs[4:5]
    middle[...] = base + scatter_wait(acc, out_buf, in_buf, y, c, ss, sr)


def feed_forward(e, middle, wu_hbm, wd_hbm, vecs, result, normed, hidden, active,
                 wu, wd, acc, out_buf, in_buf, ls, gs, gr, ss, sr):
    y, c = place()
    arrived = greet([at_chip(ring(y, k), c) for k in (1, 2, 3)])
    weights = load([(wu_hbm.at[e], wu), (wd_hbm.at[e], wd)], ls)
    slot(normed, y)[...] = norm(middle[...], vecs[2:3], vecs[3:4]).astype(BF)
    arrived()
    gather_start(normed, y, c, gs, gr)
    bias = jnp.sum(chip_row(y, vecs[6:10]), axis=0, keepdims=True)
    weights[0].wait()
    gather_wait(normed, y, c, gs, gr)
    rows = normed[...]
    for at, size in chunks(D):
        h = dot(rows, wu[:, at : at + size]) + bias[:, at : at + size]
        hidden[:, at : at + size] = h
        active[:, at : at + size] = gelu(h).astype(BF)
    weights[1].wait()
    rows = active[...]
    for at, size in chunks(D):
        acc[:, at : at + size] = dot(rows, wd[:, at : at + size])
    scatter_start(acc, out_buf, in_buf, y, c, ss, sr)
    base = middle[...] + vecs[5:6]
    result[...] = (base + scatter_wait(acc, out_buf, in_buf, y, c, ss, sr)).astype(BF)


def feed_back(e, grad, wu_hbm, wd_hbm, vecs, middle, normed, hidden, active, grad_middle, grad_up, grad_down, small,
              wu, wd, full, gh, acc, out_buf, in_buf, ls, gs, gr, ss, sr, arrived, reduce=None, weights=None):
    y, c = place()
    if weights is None:
        weights = load([(wu_hbm.at[e], wu), (wd_hbm.at[e], wd)], ls)
    own_rows = grad[...]
    slot(full, y)[...] = own_rows
    arrived()
    gather_start(full, y, c, gs, gr)
    if reduce is not None:
        reduce.begin(y, c)
    small[...] = jnp.zeros_like(small)
    small[3:4] = jnp.sum(own_rows.astype(F32), axis=0, keepdims=True)
    weights[1].wait()
    if reduce is not None:
        reduce.middle(y, c)
    gather_wait(full, y, c, gs, gr)
    rows = full[...]
    for at, size in chunks(D):
        slope = gelu_slope(hidden[:, at : at + size])
        part = (dot_nt(rows, wd[at : at + size, :]) * slope).astype(BF)
        gh[:, at : at + size] = part
        small[2:3, at : at + size] = jnp.sum(part.astype(F32), axis=0, keepdims=True)
    weights[0].wait()
    rows = gh[...]
    for at, size in chunks(D):
        acc[:, at : at + size] = dot_nt(rows, wu[at : at + size, :])
    scatter_start(acc, out_buf, in_buf, y, c, ss, sr)
    if reduce is not None:
        reduce.late()
    for at, size in chunks(D):
        grad_up[at : at + size, :] = dot_tn(normed[:, at : at + size], gh[...]).astype(BF)
        grad_down[at : at + size, :] = dot_tn(active[:, at : at + size], full[...]).astype(BF)
    d = scatter_wait(acc, out_buf, in_buf, y, c, ss, sr)
    back, gain, shift = norm_back(d, middle[...], vecs[2:3])
    small[0:1] = gain
    small[1:2] = shift
    grad_middle[...] = grad[...].astype(F32) + back
    if reduce is not None:
        reduce.finish()


def attend_back(e, grad, w_hbm, wo_hbm, vecs, x, normed, queries, kv, kv_other, logsum, attended,
                grad_x, grad_attn, grad_out, small, small_bias,
                w, wo, full, ga, gj, part_out, part_in, part_own, rows_out, edge, acc, out_buf, in_buf, ls, gs, gr, ss, sr, ks, kr, es, er,
                arrived, reduce):
    y, c = place()
    sibling = at_chip(y, 1 - c)
    weights = load([(w_hbm.at[e], w)] + out_rows(wo_hbm, wo, e, y), ls)
    own_rows = grad[...].astype(BF)
    slot(full, y)[...] = own_rows
    arrived()
    gather_start(full, y, c, gs, gr)
    reduce.begin(y, c)
    small[...] = jnp.zeros_like(small)
    small[2:3] = jnp.sum(own_rows.astype(F32), axis=0, keepdims=True)
    own, other = masks(c)
    out_wait(weights, wo, y)
    reduce.middle(y, c)
    gather_wait(full, y, c, gs, gr)
    ga[...] = dot_nt(full[...], wo[...]).astype(BF)
    for h in range(SLOTS):
        at = h * HD
        q = queries[:, at : at + HD]
        g = ga[:, at : at + HD]
        lse = logsum[:, h : h + 1]
        k_own, k_other = kv[:, at : at + HD], kv_other[:, at : at + HD]
        v_own, v_other = kv[:, TH + at : TH + at + HD], kv_other[:, TH + at : TH + at + HD]
        p_own = jnp.exp(jnp.where(own, dot_nt(q, k_own) * SCALE, -1e30) - lse)
        p_other = jnp.exp(jnp.where(other, dot_nt(q, k_other) * SCALE, -1e30) - lse)
        gp_own = dot_nt(g, v_own)
        gp_other = dot_nt(g, v_other)
        delta = jnp.sum(p_own * gp_own, axis=-1, keepdims=True) + jnp.sum(p_other * gp_other, axis=-1, keepdims=True)
        s_own = (p_own * (gp_own - delta)).astype(BF)
        s_other = (p_other * (gp_other - delta)).astype(BF)
        gj[:, 2 * TH + at : 2 * TH + at + HD] = ((dot(s_own, k_own) + dot(s_other, k_other)) * SCALE).astype(BF)
        part_own[:, at : at + HD] = dot_tn(s_own, q) * SCALE
        part_out[:, at : at + HD] = (dot_tn(s_other, q) * SCALE).astype(BF)
        part_own[:, TH + at : TH + at + HD] = dot_tn(p_own.astype(BF), g)
        part_out[:, TH + at : TH + at + HD] = dot_tn(p_other.astype(BF), g).astype(BF)
    swap = remote(part_out, part_in, ks, kr, sibling)
    swap.start()
    for at, size in chunks(D):
        rows_out[:, at : at + size] = dot_tn(attended[...], full[:, at : at + size]).astype(BF)
    lend = remote(rows_out.at[0:HD], edge, es, er, at_chip(ring(y, 3), c))
    lend.start()
    weights[0].wait()
    swap.wait()
    gj[:, : 2 * TH] = (part_own[...] + part_in[...].astype(F32)).astype(BF)
    rows = gj[...]
    for at, size in chunks(D):
        acc[:, at : at + size] = dot_nt(rows, w[at : at + size, :])
    scatter_start(acc, out_buf, in_buf, y, c, ss, sr)
    for j in range(CHIPS):
        part = dot_tn(normed[:, 272 * j : 272 * j + 272], gj[...])
        grad_attn[j, 0] = part[:136].astype(BF)
        grad_attn[j, 1] = part[136:].astype(BF)
    lend.wait()

    @pl.when(y < 3)
    def _():
        rows_out[256:320] = edge[...]

    chip_rows = rows_out[pl.ds(pl.multiple_of(16 * y, 16), 272)].astype(F32)
    grad_out[0] = chip_rows[:136].astype(BF)
    grad_out[1] = chip_rows[136:].astype(BF)
    reduce.ready(y, c)
    small_bias[...] = jnp.zeros_like(small_bias)
    small_bias[0:1] = jnp.sum(gj[...].astype(F32), axis=0, keepdims=True)
    d = scatter_wait(acc, out_buf, in_buf, y, c, ss, sr)
    back, gain, shift = norm_back(d, x[...].astype(F32), vecs[0:1])
    small[0:1] = gain
    small[1:2] = shift
    grad_x[...] = (grad[...] + back).astype(BF)
    reduce.finish()


def plane():
    s, r = lax.axis_index("section"), lax.axis_index("replica")
    return s, r // 2, r % 2, s * 8 + r


def at_plane(q):
    return {"section": q // 8, "replica": lax.rem(q, 8)}


def x_peers(x, h):
    return [{"replica": 2 * lax.rem(x + k, 4) + h} for k in (1, 2, 3)]


def z_peers(s, h):
    x = lax.axis_index("replica") // 2
    return [
        {"section": 1 - s},
        {"section": 1 - s, "replica": 2 * x + 1 - h},
        {"replica": 2 * x + 1 - h},
    ]


def plane_peers():
    s, x, h, me = plane()
    return x_peers(x, h) + z_peers(s, h)


def block_of(x, y):
    return lax.rem(x - y + 8, 4)


class AlongX:
    def __init__(self, blocks, landing, out, send, recv):
        self.blocks, self.landing, self.out, self.send, self.recv = blocks, landing, out, send, recv

    def copies(self):
        y, c = place()
        s, x, h, me = plane()
        targets = x_peers(x, h)
        for k in ORDER:
            yield remote(
                self.blocks.at[block_of(x + k, y)], self.landing.at[k - 1], self.send.at[k - 1], self.recv.at[k - 1],
                targets[k - 1],
            )

    def start(self):
        for copy in self.copies():
            copy.start()

    def finish(self):
        y, c = place()
        s, x, h, me = plane()
        own = block_of(x, y)
        for copy in self.copies():
            copy.wait()

        def add(i, carry):
            rows = pl.ds(pl.multiple_of(8 * (i % 17), 8), 8)
            total = self.blocks[own, i // 17, rows].astype(F32)
            for k in range(3):
                total = total + self.landing[k, i // 17, rows].astype(F32)
            self.out[i // 17, rows] = total.astype(BF)
            return carry

        lax.fori_loop(0, 17 * self.out.shape[0], add, 0)


def x_scratch(count, width):
    return [pltpu.VMEM((4, count, 136, width), BF), pltpu.VMEM((3, count, 136, width), BF), DMA((3,)), DMA((3,))]


class AlongZ:
    def __init__(self, layer, blocks, out, landing, send, recv):
        self.layer, self.blocks, self.landing, self.out, self.send, self.recv = layer, blocks, landing, out, send, recv

    def copies(self):
        s, x, h, me = plane()
        for half in (0, 1):
            owner = 2 * half + self.layer
            rel = lax.rem(2 * h + s - owner + 3, 4)
            target = {"section": jnp.int32(self.layer), "replica": 2 * x + half}
            copy = remote(self.blocks, self.landing.at[rel], self.send.at[half], self.recv.at[rel], target)
            yield 2 * h + s != owner, copy

    def start(self):
        for sends, copy in self.copies():
            pl.when(sends)(copy.start)

    def finish(self):
        s, x, h, me = plane()
        for sends, copy in self.copies():
            pl.when(sends)(copy.wait_send)

        @pl.when(s == self.layer)
        def _():
            for rel in range(3):
                remote(self.blocks, self.landing.at[rel], self.send.at[0], self.recv.at[rel], {"section": 1 - s}).wait_recv()

            def add(i, carry):
                rows = pl.ds(pl.multiple_of(8 * (i % 17), 8), 8)
                total = self.blocks[i // 17, rows].astype(F32)
                for rel in range(3):
                    total = total + self.landing[rel, i // 17, rows].astype(F32)
                self.out[i // 17, rows] = total.astype(BF)
                return carry

            lax.fori_loop(0, 17 * self.out.shape[0], add, 0)


def z_scratch(count, width):
    return [pltpu.VMEM((3, count, 136, width), BF), DMA((2,)), DMA((3,))]


class FeedReduce:
    def __init__(self, up, down, out_up, out_down, other, ls, cs, cr, *scratch):
        self.sources = (up, down)
        self.other, self.ls, self.cs, self.cr = other, ls, cs, cr
        self.up = AlongX(scratch[0], scratch[1], out_up, *scratch[2:4])
        self.down = AlongX(scratch[4], scratch[5], out_down, *scratch[6:8])

    def copies(self, y, c):
        up, down = self.sources
        sibling = at_chip(y, 1 - c)
        for i, (unit, own, theirs) in enumerate(
            ((self.up, up.at[:, c], up.at[:, 1 - c]), (self.down, down.at[c], down.at[1 - c]))
        ):
            keep = pltpu.make_async_copy(own, unit.blocks.at[:, 0], self.ls.at[i])
            swap = remote(theirs, self.other.at[:, i], self.cs.at[i], self.cr.at[i], sibling)
            yield unit, keep, swap

    def begin(self, y, c):
        for unit, keep, swap in self.copies(y, c):
            swap.start()
            keep.start()

    def middle(self, y, c):
        for at, (unit, keep, swap) in enumerate(self.copies(y, c)):
            keep.wait()
            swap.wait()

            def add(i, carry, unit=unit, at=at):
                unit.blocks[i, 0] = (unit.blocks[i, 0].astype(F32) + self.other[i, at].astype(F32)).astype(BF)
                return carry

            lax.fori_loop(0, 4, add, 0)
            unit.start()


FEED_SCRATCH = [pltpu.VMEM((4, 2, 136, D), BF), DMA((2,)), DMA((2,)), DMA((2,))] + x_scratch(1, D) * 2


class AttendReduce:
    def __init__(self, wide, rows, out, other_w, other_r, cs, cr, *scratch):
        self.wide, self.rows = wide, rows
        self.other_w, self.other_r = other_w, other_r
        self.cs, self.cr = cs, cr
        self.along = AlongX(scratch[0], scratch[1], out, scratch[2], scratch[3])
        self.blocks = scratch[0]

    def swaps(self, y, c):
        sibling = at_chip(y, 1 - c)
        return [
            remote(self.wide.at[:, 1 - c], self.other_w, self.cs.at[0], self.cr.at[0], sibling),
            remote(self.rows.at[1 - c], self.other_r, self.cs.at[1], self.cr.at[1], sibling),
        ]

    def begin(self, y, c):
        for copy in self.swaps(y, c):
            copy.start()

    def middle(self, y, c):
        for copy in self.swaps(y, c):
            copy.wait()
        blocks = self.blocks
        for i in range(4):
            block = self.wide[i, c].astype(F32) + self.other_w[i].astype(F32)
            blocks[i, 0] = block[:, :640].astype(BF)
            blocks[i, 1, :, :320] = block[:, 640:].astype(BF)
            chunk = self.rows[c, :, 256 * i : 256 * i + 256].astype(F32) + self.other_r[:, 256 * i : 256 * i + 256].astype(F32)
            blocks[i, 1, :, 320:576] = chunk.astype(BF)
            if i < 3:
                blocks[i, 1, :, 576:] = jnp.zeros((136, HD), BF)
        chunk = self.rows[c, :, 1024:].astype(F32) + self.other_r[:, 1024:].astype(F32)
        blocks[3, 1, :, 576:] = chunk.astype(BF)
        self.along.start()

    def finish(self):
        self.along.finish()


ATTEND_SCRATCH = [
    pltpu.VMEM((4, 136, TQKV), BF),
    pltpu.VMEM((136, D), BF),
    DMA((2,)),
    DMA((2,)),
] + x_scratch(2, 640)


BLOCKS = [pltpu.VMEM((4, 2, 136, TQKV), BF), pltpu.VMEM((2, 136, D), BF)]


class Hooks:
    def __init__(self, begin=(), middle=(), late=(), ready=()):
        self.steps = begin, middle, late, ready

    def begin(self, y, c):
        for step in self.steps[0]:
            step(y, c)

    def middle(self, y, c):
        for step in self.steps[1]:
            step(y, c)

    def late(self):
        for step in self.steps[2]:
            step()

    def ready(self, y, c):
        for step in self.steps[3]:
            step(y, c)

    def finish(self):
        pass


def split(refs, *counts):
    parts, at = [], 0
    for count in counts:
        parts.append(refs[at : at + count])
        at += count
    assert at == len(refs)
    return parts


def feed_back_alone(e, *refs):
    y, c = place()
    feed_back(e, *refs, greet([at_chip(ring(y, k), c) for k in (1, 2, 3)]))


def backward_middle(*refs):
    a_in, updown, f_in, a_out, half_u, f_out, half_a, a_scr, u_scr, f_scr, grads, w_scr = split(
        refs, 11, 2, 7, 3, 2, 4, 1, len(ATTEND_OWN), len(FEED_SCRATCH), len(FEED_OWN), 2, len(ATTEND_SCRATCH)
    )
    y, c = place()
    s, x, h, me = plane()
    arrived = greet([at_chip(ring(y, k), c) for k in (1, 2, 3)] + [at_chip(y, 1 - c)] + x_peers(x, h))
    wu_hbm, wd_hbm, vecs, *kept = f_in
    weights = load([(wu_hbm.at[0], f_scr[0]), (wd_hbm.at[0], f_scr[1])], f_scr[7])
    feed = FeedReduce(*updown, *half_u, *u_scr)
    attend = AttendReduce(*grads, half_a[0], *w_scr)
    grad_x, small, small_bias = a_out
    attend_back(1, *a_in, grad_x, *grads, small, small_bias, *a_scr, arrived,
                Hooks(begin=[feed.begin], middle=[feed.middle], ready=[attend.begin]))
    feed_back(0, grad_x, wu_hbm, wd_hbm, vecs, *kept, *f_out, *f_scr, lambda: None,
              Hooks(middle=[attend.middle], late=[feed.up.finish, feed.down.finish]), weights)
    attend.finish()


def backward_end(*refs):
    a_in, updown, halves, rest, a_out, g_out, a_scr, u_scr, grads, w_scr, z_scr, own, g_scr = split(
        refs, 11, 2, 3, 7, 1, 6, len(ATTEND_OWN), len(FEED_SCRATCH), 2, len(ATTEND_SCRATCH), 18, 11, len(GATHER_OWN)
    )
    y, c = place()
    s, x, h, me = plane()
    sibling = at_chip(y, 1 - c)
    peers = [at_chip(ring(y, k), c) for k in (1, 2, 3)]
    arrived = greet(peers + [sibling] + [at_plane(lax.rem(me + j, 16)) for j in range(1, 16)])
    half_up, half_down, half_a, sum_up, sum_down, sum_a, late_up, late_down, late_a, small, small_bias = own
    (grad_x,) = a_out
    feed = FeedReduce(*updown, half_up, half_down, *u_scr)
    attend = AttendReduce(*grads, half_a, *w_scr)
    first = [AlongZ(1, half, out, *z_scr[3 * i : 3 * i + 3]) for i, (half, out) in enumerate(zip(halves, (sum_up, sum_down, sum_a)))]
    last = [
        AlongZ(0, half, out, *z_scr[9 + 3 * i : 12 + 3 * i])
        for i, (half, out) in enumerate(zip((half_up, half_down, half_a), (late_up, late_down, late_a)))
    ]

    def start_first(y, c):
        for unit in first:
            unit.start()

    def up_along_z(y, c):
        feed.up.finish()
        last[0].start()

    attend_back(0, *a_in, grad_x, *grads, small, small_bias, *a_scr, arrived,
                Hooks(begin=[feed.begin, start_first], middle=[feed.middle], ready=[attend.begin, up_along_z]))
    gather_pieces(feed, attend, first, last, small, small_bias, *rest, grad_x, *g_out, *g_scr)


def shape(dims, kind):
    return jax.ShapeDtypeStruct(dims, kind)


MOVE = [
    pltpu.VMEM((ROWS, D), F32),
    pltpu.VMEM((3, BLK, D), BF),
    pltpu.VMEM((3, BLK, D), BF),
    DMA((3,)),
    DMA((3,)),
    DMA((3,)),
    DMA((3,)),
    DMA((3,)),
]


def call(body, name, number, outs, ins, scratch):
    return pl.pallas_call(
        body,
        name=name,
        out_shape=outs,
        in_specs=ins,
        out_specs=[VMEM] * len(outs),
        scratch_shapes=scratch,
        cost_estimate=COST,
        compiler_params=pltpu.CompilerParams(collective_id=number, has_side_effects=True, vmem_limit_bytes=LIMIT),
    )


def run_attend_forward(e, x, w, wo, vecs):
    outs = [
        shape((BLK, D), F32),
        shape((ROWS, D), BF),
        shape((ROWS, TH), BF),
        shape((ROWS, 2 * TH), BF),
        shape((ROWS, 2 * TH), BF),
        shape((ROWS, 128), F32),
        shape((ROWS, TH), BF),
    ]
    scratch = [pltpu.VMEM((D, TQKV), BF), pltpu.VMEM((TH, D), BF)] + MOVE + [DMA, DMA]
    return call(functools.partial(attend_forward, e), "attend_forward_%d" % e, e, outs, [VMEM, ANY, ANY, VMEM], scratch)(x, w, wo, vecs)


def run_feed_forward(e, middle, wu, wd, vecs):
    outs = [shape((BLK, D), BF), shape((ROWS, D), BF), shape((ROWS, D), F32), shape((ROWS, D), BF)]
    scratch = [pltpu.VMEM((D, D), BF), pltpu.VMEM((D, D), BF)] + MOVE
    return call(functools.partial(feed_forward, e), "feed_forward_%d" % e, 2 + e, outs, [VMEM, ANY, ANY, VMEM], scratch)(middle, wu, wd, vecs)


HALF_A, HALF_U = shape((2, 136, 640), BF), shape((1, 136, D), BF)


FEED_OWN = [
    pltpu.VMEM((D, D), BF),
    pltpu.VMEM((D, D), BF),
    pltpu.VMEM((ROWS, D), BF),
    pltpu.VMEM((ROWS, D), BF),
] + MOVE
ATTEND_OWN = [
    pltpu.VMEM((D, TQKV), BF),
    pltpu.VMEM((TH, D), BF),
    pltpu.VMEM((ROWS, D), BF),
    pltpu.VMEM((ROWS, TH), BF),
    pltpu.VMEM((ROWS, TQKV), BF),
    pltpu.VMEM((ROWS, 2 * TH), BF),
    pltpu.VMEM((ROWS, 2 * TH), BF),
    pltpu.VMEM((ROWS, 2 * TH), F32),
    pltpu.VMEM((TH, D), BF),
    pltpu.VMEM((HD, D), BF),
] + MOVE + [DMA, DMA, DMA, DMA]
GATHER_OWN = [
    pltpu.VMEM((BLK, D), BF),
    pltpu.VMEM((BLK, D), BF),
    DMA((2,)),
    DMA((2,)),
    pltpu.VMEM((1, 136, D), BF),
    pltpu.VMEM((2, 136, 640), BF),
    pltpu.VMEM((2, 16, D), F32),
    pltpu.VMEM((2, 16, D), F32),
    pltpu.VMEM((3, 2, 16, D), F32),
    pltpu.VMEM((2, 16, D), BF),
    pltpu.VMEM((15, 16, D), BF),
    DMA((3,)),
    DMA((3,)),
    DMA((3, 3)),
    DMA((3, 3)),
    DMA,
    DMA,
    DMA((3,)),
    DMA((3,)),
    DMA((15,)),
    DMA((15,)),
]
FEED_OUTS = [shape((BLK, D), F32), shape((D, D), BF), shape((D, D), BF), shape((8, D), F32)]
SMALLS = [shape((8, D), F32), shape((8, TQKV), F32)]


def run_feed_back(grad, wu, wd, vecs, middle, normed, hidden, active):
    return call(functools.partial(feed_back_alone, 1), "feed_back_1", 4, FEED_OUTS, [VMEM, ANY, ANY] + [VMEM] * 5, FEED_OWN)(
        grad, wu, wd, vecs, middle, normed, hidden, active
    )


def run_backward_middle(attend_args, up, down, feed_args):
    outs = [shape((BLK, D), BF)] + SMALLS + [HALF_U, HALF_U] + FEED_OUTS + [HALF_A]
    ins = [VMEM, ANY, ANY] + [VMEM] * 8 + [ANY] * 4 + [VMEM] * 5
    scratch = ATTEND_OWN + FEED_SCRATCH + FEED_OWN + BLOCKS + ATTEND_SCRATCH
    return call(backward_middle, "backward_middle", 5, outs, ins, scratch)(*attend_args, up, down, *feed_args)


def run_backward_end(attend_args, up, down, halves, rest):
    both = shape((2, BLK, D), BF)
    outs = [shape((BLK, D), BF), shape((4, 1, 136, D), BF), shape((4, 1, 136, D), BF), shape((4, 2, 136, 640), BF)]
    outs += [shape((16, D), F32), both, both]
    ins = [VMEM, ANY, ANY] + [VMEM] * 8 + [ANY] * 2 + [VMEM] * (3 + len(rest))
    units = [pltpu.VMEM((1, 136, D), BF), pltpu.VMEM((1, 136, D), BF), pltpu.VMEM((2, 136, 640), BF)]
    zs = (z_scratch(1, D) + z_scratch(1, D) + z_scratch(2, 640)) * 2
    smalls = [pltpu.VMEM((8, D), F32), pltpu.VMEM((8, TQKV), F32)]
    scratch = ATTEND_OWN + FEED_SCRATCH + BLOCKS + ATTEND_SCRATCH + zs + units * 3 + smalls + GATHER_OWN
    return call(backward_end, "backward_end", 6, outs, ins, scratch)(*attend_args, up, down, *halves, *rest)


def spread(send_a, send_u, send_d, send_o, send_v, wa, wu, wd, wo, wv, hold_a, hold_u, hold_d, hold_o, hold_v, local, ysend, yrecv, zsend, zrecv, csend, crecv):
    s = lax.axis_index("section")
    y, c = place()
    replica = lax.axis_index("replica")
    flipped = replica // 2 * 2 + (1 - replica % 2)
    near = {"section": 1 - s}
    far = {"section": 1 - s, "replica": flipped}
    sibling = at_chip(y, 1 - c)
    peers = [at_chip(ring(y, k), c) for k in (1, 2, 3)]
    arrived = greet(peers + [sibling, near, far])
    brought = load(
        [(send_a.at[y], hold_a), (send_u.at[y], hold_u), (send_d, hold_d), (send_o, hold_o), (send_v, hold_v)], local.at[0]
    )
    for copy in brought:
        copy.wait()
    keeps = load(
        [
            (hold_a, wa.at[s, y, c]),
            (hold_u, wu.at[s, y, c]),
            (hold_d, wd.at[s, c]),
            (hold_o, wo.at[s, c]),
            (hold_v, wv.at[s, y, c]),
        ],
        local.at[1],
    )
    arrived()

    def along_y(k, back):
        target = ring(y, k)
        place_in = ring(y, 4 - k) if back else y
        return [
            remote(send_v, wv.at[s, place_in, c], ysend.at[0, k - 1], yrecv.at[0, k - 1], at_chip(target, c)),
            remote(send_a.at[target], wa.at[s, place_in, c], ysend.at[1, k - 1], yrecv.at[1, k - 1], at_chip(target, c)),
            remote(send_u.at[target], wu.at[s, place_in, c], ysend.at[2, k - 1], yrecv.at[2, k - 1], at_chip(target, c)),
        ]

    def along_z(layer):
        return [
            remote(wv.at[layer, :, c], wv.at[layer, :, c], zsend.at[0], zrecv.at[0], near),
            remote(wa.at[layer, 0:2, c], wa.at[layer, 0:2, c], zsend.at[1], zrecv.at[1], near),
            remote(wa.at[layer, 2:4, c], wa.at[layer, 2:4, c], zsend.at[2], zrecv.at[2], far),
            remote(wo.at[layer, c], wo.at[layer, c], zsend.at[3], zrecv.at[3], far),
            remote(wu.at[layer, 0:2, c], wu.at[layer, 0:2, c], zsend.at[4], zrecv.at[4], near),
            remote(wu.at[layer, 2:4, c], wu.at[layer, 2:4, c], zsend.at[5], zrecv.at[5], far),
            remote(wd.at[layer, c, 0:272], wd.at[layer, c, 0:272], zsend.at[6], zrecv.at[6], near),
            remote(wd.at[layer, c, 272:544], wd.at[layer, c, 272:544], zsend.at[7], zrecv.at[7], far),
        ]

    def across(layer, i, core):
        return [
            remote(wv.at[layer, :, core], wv.at[layer, :, core], csend.at[i, 0], crecv.at[i, 0], sibling),
            remote(wa.at[layer, :, core], wa.at[layer, :, core], csend.at[i, 1], crecv.at[i, 1], sibling),
            remote(wo.at[layer, core], wo.at[layer, core], csend.at[i, 2], crecv.at[i, 2], sibling),
            remote(wu.at[layer, :, core], wu.at[layer, :, core], csend.at[i, 3], crecv.at[i, 3], sibling),
            remote(wd.at[layer, core], wd.at[layer, core], csend.at[i, 4], crecv.at[i, 4], sibling),
        ]

    sent_y = [along_y(k, False) for k in (1, 2, 3)]
    got_y = [along_y(k, True) for k in (1, 2, 3)]
    sent_z, got_z = along_z(s), along_z(1 - s)
    sent_c = [across(s, 0, c), across(1 - s, 1, c)]
    got_c = [across(s, 0, 1 - c), across(1 - s, 1, 1 - c)]
    for kind in (0, 1):
        for k in (1, 0, 2):
            sent_y[k][kind].start()
    keeps[3].wait()
    sent_z[3].start()
    sent_c[0][2].start()
    keeps[2].wait()
    sent_z[6].start()
    sent_z[7].start()
    sent_c[0][4].start()
    for kind, keep, zs, cross in ((0, 4, (0,), 0), (1, 0, (1, 2), 1)):
        keeps[keep].wait()
        for k in range(3):
            got_y[k][kind].wait_recv()
        for z in zs:
            sent_z[z].start()
        sent_c[0][cross].start()
    for k in (1, 0, 2):
        sent_y[k][2].start()
    for zs, cross in (((3,), 2), ((6, 7), 4), ((0,), 0), ((1, 2), 1)):
        for z in zs:
            got_z[z].wait_recv()
        sent_c[1][cross].start()
    keeps[1].wait()
    for k in range(3):
        got_y[k][2].wait_recv()
    for z in (4, 5):
        sent_z[z].start()
    sent_c[0][3].start()
    for z in (4, 5):
        got_z[z].wait_recv()
    sent_c[1][3].start()
    for i in range(2):
        for cross in range(5):
            got_c[i][cross].wait_recv()
    for k in range(3):
        for kind in range(3):
            sent_y[k][kind].wait_send()
    for z in range(8):
        sent_z[z].wait_send()
    for i in range(2):
        for cross in range(5):
            sent_c[i][cross].wait_send()


def run_spread(a, u, d, o, v):
    outs = [
        shape((2, 4, 2, 136, TQKV), BF),
        shape((2, 4, 2, 136, D), BF),
        shape((2, 2, 544, D), BF),
        shape((2, 2, 192, D), BF),
        shape((2, 4, 2, 16, D), BF),
    ]
    return pl.pallas_call(
        spread,
        name="spread",
        out_shape=outs,
        in_specs=[ANY] * 5,
        out_specs=[ANY] * 5,
        scratch_shapes=[
            pltpu.VMEM((136, TQKV), BF),
            pltpu.VMEM((136, D), BF),
            pltpu.VMEM((544, D), BF),
            pltpu.VMEM((192, D), BF),
            pltpu.VMEM((16, D), BF),
            DMA((2, 5)), DMA((3, 3)), DMA((3, 3)), DMA((8,)), DMA((8,)), DMA((2, 5)), DMA((2, 5)),
        ],
        compiler_params=pltpu.CompilerParams(collective_id=8, has_side_effects=True),
    )(a, u, d, o, v)


def build_small(buf, one, two, heads, y):
    buf[...] = jnp.zeros_like(buf)
    buf[0:2] = one[0:2]
    buf[2:4] = two[0:2]
    buf[4:5] = one[2:3]
    buf[5:6] = two[3:4]
    buf[6:10] = chip_row(y, two[2:3])
    for row, at in ((10, 2 * TH), (11, TH)):
        buf[row : row + 1, pl.ds(pl.multiple_of(256 * y, 256), 256)] = heads[0:1, at : at + 256]

        @pl.when(y == 3)
        def _(row=row, at=at):
            buf[row : row + 1, 1024:D] = heads[0:1, at + 256 : at + TH]


class Gather:
    def __init__(self, unit, moved, keep_from, out, ts, tr, gs, gr):
        self.unit, self.moved, self.out, self.keep_from = unit, moved, out, keep_from
        self.ts, self.tr, self.gs, self.gr = ts, tr, gs, gr

    def transpose(self):
        y, c = place()
        s, x, h, me = plane()
        return remote(self.unit, self.moved, self.ts, self.tr, at_chip(block_of(x, y), c))

    def elsewhere(self):
        y, c = place()
        s, x, h, me = plane()
        return block_of(x, y) != y

    def start(self):
        pl.when(self.elsewhere())(self.transpose().start)

    def arrive(self):
        @pl.when(self.elsewhere())
        def _():
            self.transpose().wait()
            self.unit[0] = self.moved[0]
            if self.keep_from:
                lane = lax.broadcasted_iota(jnp.int32, self.unit.shape[1:], 1)
                merged = jnp.where(lane < self.keep_from, self.moved[1].astype(F32), self.unit[1].astype(F32))
                self.unit[1] = merged.astype(BF)

    def copies(self):
        y, c = place()
        s, x, h, me = plane()
        targets = x_peers(x, h)
        for k in ORDER:
            yield k, remote(self.unit, self.out.at[block_of(x, y)], self.gs.at[k - 1], self.gr.at[k - 1], targets[k - 1])

    def spread(self):
        y, c = place()
        s, x, h, me = plane()
        for k, copy in self.copies():
            copy.start()
        self.out[block_of(x, y)] = self.unit[...]

    def finish(self):
        y, c = place()
        s, x, h, me = plane()
        targets = x_peers(x, h)
        for k, copy in self.copies():
            copy.wait_send()
            place_in = self.out.at[block_of(x - k + 4, y)]
            remote(place_in, place_in, self.gs.at[k - 1], self.gr.at[k - 1], targets[k - 1]).wait_recv()


def gather_pieces(feed, attend, first, last, one_0, heads_0,
                  two_0, one_1, two_1, heads_1, act_0, act_1, back_1, back_0,
                  out_up, out_down, out_a, out_small, out_act, out_back,
                  swap_act, swap_back, ws, wr, moved_up, moved_a, small, small_c, small_y, small_x, small_z,
                  ts, tr, gs, gr, cs, cr, ys, yr, zs, zr):
    y, c = place()
    s, x, h, me = plane()
    sibling = at_chip(y, 1 - c)
    peers = [at_chip(ring(y, k), c) for k in (1, 2, 3)]
    gathers = [
        Gather(last[i].out, moved, keep, out, ts.at[i], tr.at[i], gs.at[i], gr.at[i])
        for i, (moved, keep, out) in enumerate(((moved_up, 0, out_up), (None, 0, out_down), (moved_a, 320, out_a)))
    ]

    def sum_along_z(i):
        first[i].finish()
        last[i].finish()

        @pl.when(s == 1)
        def _():
            last[i].out[...] = first[i].out[...]

    attend.middle(y, c)
    feed.down.finish()
    last[1].start()
    build_small(small.at[0], one_0, two_0, heads_0, y)
    build_small(small.at[1], one_1, two_1, heads_1, y)
    cross = remote(small, small_c, cs, cr, sibling)
    cross.start()
    swap_act[...] = jnp.where(s == 0, act_1[...].astype(F32), act_0[...].astype(F32)).astype(BF)
    swap_back[...] = jnp.where(s == 0, back_1[...].astype(F32), back_0[...].astype(F32)).astype(BF)
    swaps = [
        remote(swap_act, out_act.at[s], ws.at[0], wr.at[0], {"section": 1 - s}),
        remote(swap_back, out_back.at[s], ws.at[1], wr.at[1], {"section": 1 - s}),
    ]
    out_act[s] = jnp.where(s == 0, act_0[...].astype(F32), act_1[...].astype(F32)).astype(BF)
    out_back[s] = jnp.where(s == 0, back_0[...].astype(F32), back_1[...].astype(F32)).astype(BF)
    cross.wait()
    small[...] = small[...] + small_c[...]
    hops = [remote(small, small_y.at[k - 1], ys.at[k - 1], yr.at[k - 1], peers[k - 1]) for k in (1, 2, 3)]
    for hop in hops:
        hop.start()
    sum_along_z(0)
    gathers[0].start()
    for hop in hops:
        hop.wait()
    small_x[...] = (small[...] + small_y[0] + small_y[1] + small_y[2]).astype(BF)

    def plane_copies():
        for j in range(1, 16):
            q = lax.rem(me + j, 16)
            yield remote(small_x.at[q // 8], small_z.at[15 - j], zs.at[j - 1], zr.at[15 - j], at_plane(q))

    attend.finish()
    last[2].start()
    gathers[0].arrive()
    gathers[0].spread()
    sum_along_z(1)
    gathers[1].spread()
    for copy in plane_copies():
        copy.start()
    sum_along_z(2)
    gathers[2].start()
    for swap in swaps:
        swap.start()
    gathers[2].arrive()
    gathers[2].spread()
    total = small_x[s].astype(F32)
    for copy in plane_copies():
        copy.wait_send()
    for j in range(15):
        remote(small_x.at[0], small_z.at[j], zs.at[j], zr.at[j], sibling).wait_recv()
        total = total + small_z[j].astype(F32)
    out_small[...] = total
    for i, swap in enumerate(swaps):
        swap.wait_send()
        place_in = (out_act, out_back)[i].at[1 - s]
        remote(place_in, place_in, ws.at[i], wr.at[i], {"section": 1 - s}).wait_recv()
    for gather in gathers:
        gather.finish()


def assemble(all_up, all_down, all_a, small, attn, out, up, down, b_attn, b_out, b_up, b_down, gain, shift):
    y, c = place()
    f = 2 * y + c
    for j in range(CHIPS):
        up[:, j * D : (j + 1) * D] = all_up[j, 0].astype(F32)
        down[j * 136 : (j + 1) * 136] = all_down[j, 0].astype(F32)
        first, second = all_a[j, 0].astype(F32), all_a[j, 1].astype(F32)
        parts = ((0, second[:, :TH]), (D, first[:, :TH]), (2 * D, first[:, TH:]))
        for base, part in parts:
            attn[:, base + 256 * j : base + 256 * j + 256] = part[:, :256]
        out[:, 256 * j : 256 * j + 256] = second[:, TH : TH + 256]
        if j == CHIPS - 1:
            for base, part in parts:
                attn[:, base + 1024 : base + D] = part[:, 256:]
            out[:, 1024:] = second[:, TH + 256 :]

    def pick(index, options):
        total = jnp.where(index == 0, options[0], 0.0)
        for i, option in enumerate(options[1:], 1):
            total = total + jnp.where(index == i, option, 0.0)
        return total

    for row, ref, place_in in ((0, gain, 0), (1, shift, 0), (2, gain, 1), (3, shift, 1), (4, b_out, 0), (5, b_down, 0)):
        ref[place_in : place_in + 1] = pick(f, [small[row : row + 1, 136 * i : 136 * i + 136] for i in range(8)])
    b_up[...] = pick(f, [small[6 + i // 2 : 7 + i // 2, 544 * (i % 2) : 544 * (i % 2) + 544] for i in range(8)])
    b_attn[...] = pick(f, [small[10 + i // 4 : 11 + i // 4, 272 * (i % 4) : 272 * (i % 4) + 272] for i in range(8)])


def run_assemble(*gathered):
    sizes = [(136, 3 * D), (136, D), (136, FF), (544, D), (1, 272), (1, 136), (1, 544), (1, 136), (2, 136), (2, 136)]
    return pl.pallas_call(
        assemble,
        name="assemble",
        out_shape=[shape(dims, F32) for dims in sizes],
        in_specs=[VMEM] * 4,
        out_specs=[VMEM] * len(sizes),
        compiler_params=pltpu.CompilerParams(vmem_limit_bytes=LIMIT),
    )(*gathered)


def split_heads(block):
    zero = jnp.zeros(block.shape[:-1] + (HD,), block.dtype)
    return [
        jnp.concatenate([block[..., 256 * j : 256 * j + 256], block[..., 1024:] if j == 3 else zero], axis=-1)
        for j in range(CHIPS)
    ]


def on_device(inputs, cotangent, weight_attn, weight_out, weight_up, weight_down, bias_attn, bias_out, bias_up,
              bias_down, norm_gain, norm_bias):
    s = lax.axis_index("section")
    f = lax.axis_index("fsdp")
    y, c = f // 2, f % 2
    wa = weight_attn[0]
    q_blocks, k_blocks, v_blocks = (split_heads(wa[:, i * D : (i + 1) * D]) for i in range(3))
    send_a = jnp.stack(
        [jnp.concatenate([k_blocks[j], v_blocks[j], q_blocks[j]], axis=-1) for j in range(CHIPS)]
    )
    send_u = jnp.stack([weight_up[0][:, j * D : (j + 1) * D] for j in range(CHIPS)])
    tail = lax.ppermute(weight_out[0, 88:], "fsdp", [(i, (i + 2) % 8) for i in range(8)])
    send_o = jnp.concatenate([weight_out[0], tail, jnp.zeros((8, D), BF)], axis=0)
    vectors = jnp.stack([norm_gain[0, 0], norm_bias[0, 0], norm_gain[0, 1], norm_bias[0, 1], bias_out[0], bias_down[0]])
    send_v = jnp.concatenate(
        [
            lax.dynamic_update_slice(jnp.zeros((6, D), BF), vectors, (0, 136 * f)),
            lax.dynamic_update_slice(jnp.zeros((4, D), BF), bias_up, (y, 544 * c)),
            lax.dynamic_update_slice(jnp.zeros((6, D), BF), bias_attn, (f // 4, 272 * (f % 4))),
        ]
    )
    wa, wu, wd, wo, wv = run_spread(send_a, send_u, weight_down[0], send_o, send_v)
    wa = wa.reshape(2, D, TQKV)
    wu = wu.reshape(2, D, D)
    wd = wd.reshape(2, D, D)
    wo = jnp.concatenate([wo[:, 1, 136:184], wo[:, 0, :136], wo[:, 1, :136]], axis=1)
    vecs = jnp.sum(wv.astype(F32), axis=(1, 2))
    stream = lax.dynamic_index_in_dim(inputs, s, 0, keepdims=False)[0]
    saved, acts = [], []
    for e in range(2):
        middle, *kept = run_attend_forward(e, stream, wa, wo, vecs[e])
        result, *kept_two = run_feed_forward(e, middle, wu, wd, vecs[e])
        saved.append((stream, kept, middle, kept_two))
        acts.append(result)
        stream = result
    grad = lax.dynamic_index_in_dim(cotangent, s, 0, keepdims=False)[0]
    x_1, kept_1, middle_1, kept_two_1 = saved[1]
    x_0, kept_0, middle_0, kept_two_0 = saved[0]
    grad_middle, up, down, two_1 = run_feed_back(grad, wu, wd, vecs[1], middle_1, *kept_two_1)
    back_1, one_1, heads_1, half_up, half_down, grad_middle, up_0, down_0, two_0, half_a = run_backward_middle(
        (grad_middle, wa, wo, vecs[1], x_1, *kept_1),
        up.reshape(4, 2, 136, D),
        down.reshape(2, 4, 136, D),
        (wu, wd, vecs[0], middle_0, *kept_two_0),
    )
    back_0, all_up, all_down, all_a, small, all_acts, all_grads = run_backward_end(
        (grad_middle, wa, wo, vecs[0], x_0, *kept_0),
        up_0.reshape(4, 2, 136, D),
        down_0.reshape(2, 4, 136, D),
        (half_up, half_down, half_a),
        (two_0, one_1, two_1, heads_1, *acts, back_1),
    )
    attn, out, up, down, b_attn, b_out, b_up, b_down, gain, shift = run_assemble(all_up, all_down, all_a, small)
    return (
        all_acts[None, :, None],
        all_grads[None, :, None],
        attn[None],
        out[None],
        up[None],
        down[None],
        b_attn,
        b_out,
        b_up,
        b_down,
        gain[None],
        shift[None],
    )


def solution(mesh):
    placed = (
        P(None, "replica", "fsdp", None),
        P(None, "replica", "fsdp", None),
        P("section", "fsdp", None),
        P("section", "fsdp", None),
        P("section", "fsdp", None),
        P("section", "fsdp", None),
        P("section", "fsdp"),
        P("section", "fsdp"),
        P("section", "fsdp"),
        P("section", "fsdp"),
        P("section", None, "fsdp"),
        P("section", None, "fsdp"),
    )
    return jax.shard_map(
        on_device,
        mesh=mesh,
        in_specs=placed,
        out_specs=(
            P("section", None, "replica", "fsdp", None),
            P("section", None, "replica", "fsdp", None),
        )
        + placed[2:],
        check_vma=False,
    )
```

```python
import functools

import jax
import jax.numpy as jnp
from jax import lax
from jax.experimental import pallas as pl
from jax.experimental.pallas import tpu as pltpu
from jax.sharding import PartitionSpec as P

D = 1088
FF = 4352
HEADS = 17
HD = 64
BLK = 64
CHIPS = 4
ROWS = BLK * CHIPS
SLOTS = 5
TH = SLOTS * HD
TQKV = 3 * TH
SCALE = HD**-0.5
EPS = 1e-5
MESH = pl.DeviceIdType.MESH
BF = jnp.bfloat16
F32 = jnp.float32
ANY = pl.BlockSpec(memory_space=pl.ANY)
VMEM = pl.BlockSpec(memory_space=pltpu.VMEM)
DMA = pltpu.SemaphoreType.DMA
LIMIT = 56 * 1024 * 1024
COST = pl.CostEstimate(flops=10_000_000, bytes_accessed=10_000, transcendentals=0)


def dot(a, b):
    return lax.dot_general(a, b, (((1,), (0,)), ((), ())), preferred_element_type=F32)


def dot_nt(a, b):
    return lax.dot_general(a, b, (((1,), (1,)), ((), ())), preferred_element_type=F32)


def dot_tn(a, b):
    return lax.dot_general(a, b, (((0,), (0,)), ((), ())), preferred_element_type=F32)


def chunks(n, size=256):
    return [(i, min(size, n - i)) for i in range(0, n, size)]


def place():
    f = lax.axis_index("fsdp")
    return f // 2, f % 2


def ring(y, k):
    return lax.rem(y + k, CHIPS)


def at_chip(y, c):
    return {"fsdp": 2 * y + c}


def greet(targets):
    barrier = pltpu.get_barrier_semaphore()
    for target in targets:
        pl.semaphore_signal(barrier, inc=1, device_id=target, device_id_type=MESH)
    return functools.partial(pl.semaphore_wait, barrier, len(targets))


def remote(src, dst, send, recv, target):
    return pltpu.make_async_remote_copy(
        src_ref=src, dst_ref=dst, send_sem=send, recv_sem=recv, device_id=target, device_id_type=MESH
    )


def slot(ref, y):
    return ref.at[pl.ds(pl.multiple_of(y * BLK, BLK), BLK)]


ORDER = (2, 1, 3)


def gather_start(full, y, c, send, recv):
    for k in ORDER:
        remote(slot(full, y), slot(full, y), send.at[k - 1], recv.at[k - 1], at_chip(ring(y, k), c)).start()


def gather_wait(full, y, c, send, recv):
    for k in (1, 3, 2):
        source = ring(y, 4 - k)
        remote(slot(full, source), slot(full, source), send.at[k - 1], recv.at[k - 1], at_chip(ring(y, k), c)).wait()


def scatter_start(acc, out_buf, in_buf, y, c, send, recv):
    for k in ORDER:
        target = ring(y, k)
        out_buf[k - 1] = slot(acc, target)[...].astype(BF)
        remote(out_buf.at[k - 1], in_buf.at[k - 1], send.at[k - 1], recv.at[k - 1], at_chip(target, c)).start()


def scatter_wait(acc, out_buf, in_buf, y, c, send, recv):
    total = slot(acc, y)[...]
    for k in (1, 3, 2):
        remote(out_buf.at[k - 1], in_buf.at[k - 1], send.at[k - 1], recv.at[k - 1], at_chip(ring(y, k), c)).wait()
        total = total + in_buf[k - 1].astype(F32)
    return total


def stats(v):
    centre = v - jnp.mean(v, axis=-1, keepdims=True)
    scale = lax.rsqrt(jnp.mean(centre * centre, axis=-1, keepdims=True) + EPS)
    return centre * scale, scale


def norm(v, gain, shift):
    return stats(v)[0] * gain + shift


def norm_back(d, v, gain):
    vh, scale = stats(v)
    q = d * gain
    grad = scale * (q - jnp.mean(q, axis=-1, keepdims=True) - vh * jnp.mean(q * vh, axis=-1, keepdims=True))
    return grad, jnp.sum(d * vh, axis=0, keepdims=True), jnp.sum(d, axis=0, keepdims=True)


GELU_A = 0.7978845608028654
GELU_B = 0.044715


def gelu(h):
    return 0.5 * h * (1.0 + jnp.tanh(GELU_A * (h + GELU_B * h * h * h)))


def gelu_slope(h):
    t = jnp.tanh(GELU_A * (h + GELU_B * h * h * h))
    return 0.5 * (1.0 + t) + 0.5 * h * (1.0 - t * t) * (GELU_A * (1.0 + 3.0 * GELU_B * h * h))


def masks(c):
    row = lax.broadcasted_iota(jnp.int32, (ROWS, ROWS), 0)
    col = lax.broadcasted_iota(jnp.int32, (ROWS, ROWS), 1)
    own = row >= col
    other = (row // BLK) >= (col // BLK) + (1 - c)
    return own, other


def load(pairs, sems):
    copies = [pltpu.make_async_copy(src, dst, sems.at[i]) for i, (src, dst) in enumerate(pairs)]
    for copy in copies:
        copy.start()
    return copies


def out_rows(wo_hbm, wo, e, y):
    start = pl.multiple_of(48 - 16 * y, 16)
    return [(wo_hbm.at[e, pl.ds(start, 256)], wo.at[0:256]), (wo_hbm.at[e, 256:320], wo.at[256:320])]


def out_wait(weights, wo, y):
    weights[1].wait()
    weights[2].wait()

    @pl.when(y < 3)
    def _():
        wo[256:320] = jnp.zeros((HD, D), BF)


def chip_row(y, rows):
    return jnp.where(lax.broadcasted_iota(jnp.int32, (CHIPS, 1), 0) == y, rows, 0.0)


def head_bias(vecs, row, y):
    last = jnp.where(y == 3, vecs[row : row + 1, 1024:D], 0.0)
    return jnp.concatenate([vecs[row : row + 1, pl.ds(pl.multiple_of(256 * y, 256), 256)], last], axis=-1)


def attend_forward(e, x, w_hbm, wo_hbm, vecs, middle, normed, queries, kv, kv_other, logsum, attended,
                   w, wo, acc, out_buf, in_buf, ls, gs, gr, ss, sr, ks, kr, arrived, weights=None):
    y, c = place()
    sibling = at_chip(y, 1 - c)
    if weights is None:
        weights = load([(w_hbm.at[e], w)] + out_rows(wo_hbm, wo, e, y), ls)
    slot(normed, y)[...] = norm(x[...].astype(F32), vecs[0:1], vecs[1:2]).astype(BF)
    arrived()
    gather_start(normed, y, c, gs, gr)
    own, other = masks(c)
    weights[0].wait()
    gather_wait(normed, y, c, gs, gr)
    rows = normed[...]
    bias = jnp.concatenate([jnp.zeros((1, TH), F32), head_bias(vecs, 11, y)], axis=-1)
    for at, size in chunks(2 * TH):
        kv[:, at : at + size] = (dot(rows, w[:, at : at + size]) + bias[:, at : at + size]).astype(BF)
    swap = remote(kv, kv_other, ks, kr, sibling)
    swap.start()
    queries[...] = (dot(rows, w[:, 2 * TH :]) + head_bias(vecs, 10, y)).astype(BF)
    swap.wait()
    for h in range(SLOTS):
        at = h * HD
        q = queries[:, at : at + HD]
        s_own = jnp.where(own, dot_nt(q, kv[:, at : at + HD]) * SCALE, -1e30)
        s_other = jnp.where(other, dot_nt(q, kv_other[:, at : at + HD]) * SCALE, -1e30)
        top = jnp.maximum(jnp.max(s_own, axis=-1, keepdims=True), jnp.max(s_other, axis=-1, keepdims=True))
        e_own = jnp.exp(s_own - top)
        e_other = jnp.exp(s_other - top)
        total = jnp.sum(e_own, axis=-1, keepdims=True) + jnp.sum(e_other, axis=-1, keepdims=True)
        logsum[:, h : h + 1] = top + jnp.log(total)
        inverse = 1.0 / total
        a_own = (e_own * inverse).astype(BF)
        a_other = (e_other * inverse).astype(BF)
        out = dot(a_own, kv[:, TH + at : TH + at + HD]) + dot(a_other, kv_other[:, TH + at : TH + at + HD])
        attended[:, at : at + HD] = out.astype(BF)
    out_wait(weights, wo, y)
    mixed = attended[...]
    for at, size in chunks(D):
        acc[:, at : at + size] = dot(mixed, wo[:, at : at + size])
    scatter_start(acc, out_buf, in_buf, y, c, ss, sr)
    base = x[...].astype(F32) + vecs[4:5]
    middle[...] = base + scatter_wait(acc, out_buf, in_buf, y, c, ss, sr)


def feed_forward(middle, vecs, result, normed, hidden, active,
                 wu, wd, acc, out_buf, in_buf, gs, gr, ss, sr, arrived, weights, defer=False):
    y, c = place()
    slot(normed, y)[...] = norm(middle[...], vecs[2:3], vecs[3:4]).astype(BF)
    arrived()
    gather_start(normed, y, c, gs, gr)
    bias = jnp.sum(chip_row(y, vecs[6:10]), axis=0, keepdims=True)
    weights[0].wait()
    gather_wait(normed, y, c, gs, gr)
    rows = normed[...]
    for at, size in chunks(D):
        h = dot(rows, wu[:, at : at + size]) + bias[:, at : at + size]
        hidden[:, at : at + size] = h
        active[:, at : at + size] = gelu(h).astype(BF)
    weights[1].wait()
    rows = active[...]
    for at, size in chunks(D):
        acc[:, at : at + size] = dot(rows, wd[:, at : at + size])
    scatter_start(acc, out_buf, in_buf, y, c, ss, sr)

    def finish():
        base = middle[...] + vecs[5:6]
        result[...] = (base + scatter_wait(acc, out_buf, in_buf, y, c, ss, sr)).astype(BF)

    if defer:
        return finish
    finish()


def feed_back(e, grad, wu_hbm, wd_hbm, vecs, middle, normed, hidden, active, grad_middle, grad_up, grad_down, small,
              wu, wd, full, gh, acc, out_buf, in_buf, ls, gs, gr, ss, sr, arrived, reduce=None, weights=None, early=False):
    y, c = place()
    if weights is None:
        weights = load([(wu_hbm.at[e], wu), (wd_hbm.at[e], wd)], ls)
    own_rows = grad[...]
    if not early:
        slot(full, y)[...] = own_rows
        arrived()
        gather_start(full, y, c, gs, gr)
    if reduce is not None:
        reduce.begin(y, c)
    small[...] = jnp.zeros_like(small)
    small[3:4] = jnp.sum(own_rows.astype(F32), axis=0, keepdims=True)
    weights[1].wait()
    if reduce is not None:
        reduce.middle(y, c)
    gather_wait(full, y, c, gs, gr)
    rows = full[...]
    for at, size in chunks(D):
        slope = gelu_slope(hidden[:, at : at + size])
        part = (dot_nt(rows, wd[at : at + size, :]) * slope).astype(BF)
        gh[:, at : at + size] = part
        small[2:3, at : at + size] = jnp.sum(part.astype(F32), axis=0, keepdims=True)
    weights[0].wait()
    rows = gh[...]
    for at, size in chunks(D):
        acc[:, at : at + size] = dot_nt(rows, wu[at : at + size, :])
    scatter_start(acc, out_buf, in_buf, y, c, ss, sr)
    if reduce is not None:
        reduce.late()
    for at, size in chunks(D):
        grad_up[at : at + size, :] = dot_tn(normed[:, at : at + size], gh[...]).astype(BF)
        grad_down[at : at + size, :] = dot_tn(active[:, at : at + size], full[...]).astype(BF)
    d = scatter_wait(acc, out_buf, in_buf, y, c, ss, sr)
    back, gain, shift = norm_back(d, middle[...], vecs[2:3])
    small[0:1] = gain
    small[1:2] = shift
    grad_middle[...] = grad[...].astype(F32) + back
    if reduce is not None:
        reduce.finish()


def attend_back(e, grad, w_hbm, wo_hbm, vecs, x, normed, queries, kv, kv_other, logsum, attended,
                grad_x, grad_attn, grad_out, small, small_bias,
                w, wo, full, ga, gj, part_out, part_in, part_own, rows_out, edge, acc, out_buf, in_buf, ls, gs, gr, ss, sr, ks, kr, es, er,
                arrived, reduce):
    y, c = place()
    sibling = at_chip(y, 1 - c)
    weights = load([(w_hbm.at[e], w)] + out_rows(wo_hbm, wo, e, y), ls)
    own_rows = grad[...].astype(BF)
    slot(full, y)[...] = own_rows
    arrived()
    gather_start(full, y, c, gs, gr)
    reduce.begin(y, c)
    small[...] = jnp.zeros_like(small)
    small[2:3] = jnp.sum(own_rows.astype(F32), axis=0, keepdims=True)
    own, other = masks(c)
    out_wait(weights, wo, y)
    reduce.middle(y, c)
    gather_wait(full, y, c, gs, gr)
    ga[...] = dot_nt(full[...], wo[...]).astype(BF)
    for h in range(SLOTS):
        at = h * HD
        q = queries[:, at : at + HD]
        g = ga[:, at : at + HD]
        lse = logsum[:, h : h + 1]
        k_own, k_other = kv[:, at : at + HD], kv_other[:, at : at + HD]
        v_own, v_other = kv[:, TH + at : TH + at + HD], kv_other[:, TH + at : TH + at + HD]
        p_own = jnp.exp(jnp.where(own, dot_nt(q, k_own) * SCALE, -1e30) - lse)
        p_other = jnp.exp(jnp.where(other, dot_nt(q, k_other) * SCALE, -1e30) - lse)
        gp_own = dot_nt(g, v_own)
        gp_other = dot_nt(g, v_other)
        delta = jnp.sum(p_own * gp_own, axis=-1, keepdims=True) + jnp.sum(p_other * gp_other, axis=-1, keepdims=True)
        s_own = (p_own * (gp_own - delta)).astype(BF)
        s_other = (p_other * (gp_other - delta)).astype(BF)
        gj[:, 2 * TH + at : 2 * TH + at + HD] = ((dot(s_own, k_own) + dot(s_other, k_other)) * SCALE).astype(BF)
        part_own[:, at : at + HD] = dot_tn(s_own, q) * SCALE
        part_out[:, at : at + HD] = (dot_tn(s_other, q) * SCALE).astype(BF)
        part_own[:, TH + at : TH + at + HD] = dot_tn(p_own.astype(BF), g)
        part_out[:, TH + at : TH + at + HD] = dot_tn(p_other.astype(BF), g).astype(BF)
    swap = remote(part_out, part_in, ks, kr, sibling)
    swap.start()
    for at, size in chunks(D):
        rows_out[:, at : at + size] = dot_tn(attended[...], full[:, at : at + size]).astype(BF)
    lend = remote(rows_out.at[0:HD], edge, es, er, at_chip(ring(y, 3), c))
    lend.start()
    weights[0].wait()
    swap.wait()
    gj[:, : 2 * TH] = (part_own[...] + part_in[...].astype(F32)).astype(BF)
    rows = gj[...]
    for at, size in chunks(D):
        acc[:, at : at + size] = dot_nt(rows, w[at : at + size, :])
    scatter_start(acc, out_buf, in_buf, y, c, ss, sr)
    for j in range(CHIPS):
        part = dot_tn(normed[:, 272 * j : 272 * j + 272], gj[...])
        grad_attn[j, 0] = part[:136].astype(BF)
        grad_attn[j, 1] = part[136:].astype(BF)
    lend.wait()

    @pl.when(y < 3)
    def _():
        rows_out[256:320] = edge[...]

    chip_rows = rows_out[pl.ds(pl.multiple_of(16 * y, 16), 272)].astype(F32)
    grad_out[0] = chip_rows[:136].astype(BF)
    grad_out[1] = chip_rows[136:].astype(BF)
    reduce.ready(y, c)
    small_bias[...] = jnp.zeros_like(small_bias)
    small_bias[0:1] = jnp.sum(gj[...].astype(F32), axis=0, keepdims=True)
    d = scatter_wait(acc, out_buf, in_buf, y, c, ss, sr)
    back, gain, shift = norm_back(d, x[...].astype(F32), vecs[0:1])
    small[0:1] = gain
    small[1:2] = shift
    grad_x[...] = (grad[...] + back).astype(BF)
    reduce.finish()


def plane():
    s, r = lax.axis_index("section"), lax.axis_index("replica")
    return s, r // 2, r % 2, s * 8 + r


def at_plane(q):
    return {"section": q // 8, "replica": lax.rem(q, 8)}


def x_peers(x, h):
    return [{"replica": 2 * lax.rem(x + k, 4) + h} for k in (1, 2, 3)]


def z_peers(s, h):
    x = lax.axis_index("replica") // 2
    return [
        {"section": 1 - s},
        {"section": 1 - s, "replica": 2 * x + 1 - h},
        {"replica": 2 * x + 1 - h},
    ]


def plane_peers():
    s, x, h, me = plane()
    return x_peers(x, h) + z_peers(s, h)


def block_of(x, y):
    return lax.rem(x - y + 8, 4)


class AlongX:
    def __init__(self, blocks, landing, out, send, recv):
        self.blocks, self.landing, self.out, self.send, self.recv = blocks, landing, out, send, recv

    def copies(self):
        y, c = place()
        s, x, h, me = plane()
        targets = x_peers(x, h)
        for k in ORDER:
            yield remote(
                self.blocks.at[block_of(x + k, y)], self.landing.at[k - 1], self.send.at[k - 1], self.recv.at[k - 1],
                targets[k - 1],
            )

    def start(self):
        for copy in self.copies():
            copy.start()

    def finish(self):
        y, c = place()
        s, x, h, me = plane()
        own = block_of(x, y)
        for copy in self.copies():
            copy.wait()

        def add(i, carry):
            rows = pl.ds(pl.multiple_of(8 * (i % 17), 8), 8)
            total = self.blocks[own, i // 17, rows].astype(F32)
            for k in range(3):
                total = total + self.landing[k, i // 17, rows].astype(F32)
            self.out[i // 17, rows] = total.astype(BF)
            return carry

        lax.fori_loop(0, 17 * self.out.shape[0], add, 0)


def x_scratch(count, width):
    return [pltpu.VMEM((4, count, 136, width), BF), pltpu.VMEM((3, count, 136, width), BF), DMA((3,)), DMA((3,))]


class AlongZ:
    def __init__(self, layer, blocks, out, landing, send, recv):
        self.layer, self.blocks, self.landing, self.out, self.send, self.recv = layer, blocks, landing, out, send, recv

    def copies(self):
        s, x, h, me = plane()
        for half in (0, 1):
            owner = 2 * half + self.layer
            rel = lax.rem(2 * h + s - owner + 3, 4)
            target = {"section": jnp.int32(self.layer), "replica": 2 * x + half}
            copy = remote(self.blocks, self.landing.at[rel], self.send.at[half], self.recv.at[rel], target)
            yield 2 * h + s != owner, copy

    def start(self):
        for sends, copy in self.copies():
            pl.when(sends)(copy.start)

    def finish(self):
        s, x, h, me = plane()
        for sends, copy in self.copies():
            pl.when(sends)(copy.wait_send)

        @pl.when(s == self.layer)
        def _():
            for rel in range(3):
                remote(self.blocks, self.landing.at[rel], self.send.at[0], self.recv.at[rel], {"section": 1 - s}).wait_recv()

            def add(i, carry):
                rows = pl.ds(pl.multiple_of(8 * (i % 17), 8), 8)
                total = self.blocks[i // 17, rows].astype(F32)
                for rel in range(3):
                    total = total + self.landing[rel, i // 17, rows].astype(F32)
                self.out[i // 17, rows] = total.astype(BF)
                return carry

            lax.fori_loop(0, 17 * self.out.shape[0], add, 0)


def z_scratch(count, width):
    return [pltpu.VMEM((3, count, 136, width), BF), DMA((2,)), DMA((3,))]


class FeedReduce:
    def __init__(self, up, down, out_up, out_down, other, ls, cs, cr, *scratch):
        self.sources = (up, down)
        self.other, self.ls, self.cs, self.cr = other, ls, cs, cr
        self.up = AlongX(scratch[0], scratch[1], out_up, *scratch[2:4])
        self.down = AlongX(scratch[4], scratch[5], out_down, *scratch[6:8])

    def copies(self, y, c):
        up, down = self.sources
        sibling = at_chip(y, 1 - c)
        for i, (unit, own, theirs) in enumerate(
            ((self.up, up.at[:, c], up.at[:, 1 - c]), (self.down, down.at[c], down.at[1 - c]))
        ):
            keep = pltpu.make_async_copy(own, unit.blocks.at[:, 0], self.ls.at[i])
            swap = remote(theirs, self.other.at[:, i], self.cs.at[i], self.cr.at[i], sibling)
            yield unit, keep, swap

    def begin(self, y, c):
        for unit, keep, swap in self.copies(y, c):
            swap.start()
            keep.start()

    def middle(self, y, c):
        for at, (unit, keep, swap) in enumerate(self.copies(y, c)):
            keep.wait()
            swap.wait()

            def add(i, carry, unit=unit, at=at):
                unit.blocks[i, 0] = (unit.blocks[i, 0].astype(F32) + self.other[i, at].astype(F32)).astype(BF)
                return carry

            lax.fori_loop(0, 4, add, 0)
            unit.start()


FEED_SCRATCH = [pltpu.VMEM((4, 2, 136, D), BF), DMA((2,)), DMA((2,)), DMA((2,))] + x_scratch(1, D) * 2


class AttendReduce:
    def __init__(self, wide, rows, out, other_w, other_r, cs, cr, *scratch):
        self.wide, self.rows = wide, rows
        self.other_w, self.other_r = other_w, other_r
        self.cs, self.cr = cs, cr
        self.along = AlongX(scratch[0], scratch[1], out, scratch[2], scratch[3])
        self.blocks = scratch[0]

    def swaps(self, y, c):
        sibling = at_chip(y, 1 - c)
        return [
            remote(self.wide.at[:, 1 - c], self.other_w, self.cs.at[0], self.cr.at[0], sibling),
            remote(self.rows.at[1 - c], self.other_r, self.cs.at[1], self.cr.at[1], sibling),
        ]

    def begin(self, y, c):
        for copy in self.swaps(y, c):
            copy.start()

    def middle(self, y, c):
        for copy in self.swaps(y, c):
            copy.wait()
        blocks = self.blocks
        for i in range(4):
            block = self.wide[i, c].astype(F32) + self.other_w[i].astype(F32)
            blocks[i, 0] = block[:, :640].astype(BF)
            blocks[i, 1, :, :320] = block[:, 640:].astype(BF)
            chunk = self.rows[c, :, 256 * i : 256 * i + 256].astype(F32) + self.other_r[:, 256 * i : 256 * i + 256].astype(F32)
            blocks[i, 1, :, 320:576] = chunk.astype(BF)
            if i < 3:
                blocks[i, 1, :, 576:] = jnp.zeros((136, HD), BF)
        chunk = self.rows[c, :, 1024:].astype(F32) + self.other_r[:, 1024:].astype(F32)
        blocks[3, 1, :, 576:] = chunk.astype(BF)
        self.along.start()

    def finish(self):
        self.along.finish()


ATTEND_SCRATCH = [
    pltpu.VMEM((4, 136, TQKV), BF),
    pltpu.VMEM((136, D), BF),
    DMA((2,)),
    DMA((2,)),
] + x_scratch(2, 640)


BLOCKS = [pltpu.VMEM((4, 2, 136, TQKV), BF), pltpu.VMEM((2, 136, D), BF)]


class Hooks:
    def __init__(self, begin=(), middle=(), late=(), ready=()):
        self.steps = begin, middle, late, ready

    def begin(self, y, c):
        for step in self.steps[0]:
            step(y, c)

    def middle(self, y, c):
        for step in self.steps[1]:
            step(y, c)

    def late(self):
        for step in self.steps[2]:
            step()

    def ready(self, y, c):
        for step in self.steps[3]:
            step(y, c)

    def finish(self):
        pass


def split(refs, *counts):
    parts, at = [], 0
    for count in counts:
        parts.append(refs[at : at + count])
        at += count
    assert at == len(refs)
    return parts


def attend_forward_first(*refs):
    y, c = place()
    arrived = greet([at_chip(ring(y, k), c) for k in (1, 2, 3)] + [at_chip(y, 1 - c)])
    attend_forward(0, refs[0].at[lax.axis_index("section"), 0], *refs[1:], arrived)


class Loaded:
    def wait(self):
        pass


def forward_rest(middle_0, wu_hbm, wd_hbm, w_hbm, wo_hbm, vecs_0, vecs_1, cotangent, *refs):
    f0_out, a_out, result_1, back_out, f0_scr, a_scr, f1_kept, f1_scr, b_scr, loads = split(
        refs, 4, 7, 1, 4, 2 + len(FEED_MOVE), 2 + len(MOVE) + 2, 3, 2 + len(FEED_MOVE), 2 + len(MOVE), 1
    )
    y, c = place()
    arrived = greet([at_chip(ring(y, k), c) for k in (1, 2, 3)] + [at_chip(y, 1 - c)])
    weights_0 = load([(wu_hbm.at[0], f0_scr[0]), (wd_hbm.at[0], f0_scr[1])], loads[0].at[0])
    weights_a = load([(w_hbm.at[1], a_scr[0])] + out_rows(wo_hbm, a_scr[1], 1, y), a_scr[5])
    weights_1 = load([(wu_hbm.at[1], f1_scr[0]), (wd_hbm.at[1], f1_scr[1])], loads[0].at[1])
    grad = cotangent.at[lax.axis_index("section"), 0]
    full, gs, gr = b_scr[0], b_scr[6], b_scr[7]
    slot(full, y)[...] = grad[...]

    def begin():
        arrived()

    result_0 = f0_out[0]
    feed_forward(middle_0, vecs_0, *f0_out, *f0_scr, begin, weights_0)
    gather_start(full, y, c, gs, gr)
    attend_forward(1, result_0, w_hbm, wo_hbm, vecs_1, *a_out, *a_scr, lambda: None, weights_a)
    middle_1 = a_out[0]
    normed, hidden, active = f1_kept
    finish = feed_forward(middle_1, vecs_1, result_1[0], normed, hidden, active, *f1_scr, lambda: None, weights_1, True)
    feed_back(1, grad, wu_hbm, wd_hbm, vecs_1, middle_1, normed, hidden, active, *back_out,
              f1_scr[0], f1_scr[1], *b_scr, lambda: None, Hooks(late=[finish]), [Loaded(), Loaded()], True)


def backward_middle(*refs):
    a_in, updown, f_in, a_out, half_u, f_out, half_a, a_scr, u_scr, f_scr, grads, w_scr = split(
        refs, 11, 2, 7, 3, 2, 4, 1, len(ATTEND_OWN), len(FEED_SCRATCH), len(FEED_OWN), 2, len(ATTEND_SCRATCH)
    )
    y, c = place()
    s, x, h, me = plane()
    arrived = greet([at_chip(ring(y, k), c) for k in (1, 2, 3)] + [at_chip(y, 1 - c)] + x_peers(x, h))
    wu_hbm, wd_hbm, vecs, *kept = f_in
    weights = load([(wu_hbm.at[0], f_scr[0]), (wd_hbm.at[0], f_scr[1])], f_scr[7])
    feed = FeedReduce(*updown, *half_u, *u_scr)
    attend = AttendReduce(*grads, half_a[0], *w_scr)
    grad_x, small, small_bias = a_out
    attend_back(1, *a_in, grad_x, *grads, small, small_bias, *a_scr, arrived,
                Hooks(begin=[feed.begin], middle=[feed.middle], ready=[attend.begin]))
    feed_back(0, grad_x, wu_hbm, wd_hbm, vecs, *kept, *f_out, *f_scr, lambda: None,
              Hooks(middle=[attend.middle], late=[feed.up.finish, feed.down.finish]), weights)
    attend.finish()


def backward_end(*refs):
    a_in, updown, halves, rest, a_out, g_out, a_scr, u_scr, grads, w_scr, z_scr, own, g_scr = split(
        refs, 11, 2, 3, 7, 1, 6, len(ATTEND_OWN), len(FEED_SCRATCH), 2, len(ATTEND_SCRATCH), 18, 11, len(GATHER_OWN)
    )
    y, c = place()
    s, x, h, me = plane()
    sibling = at_chip(y, 1 - c)
    peers = [at_chip(ring(y, k), c) for k in (1, 2, 3)]
    arrived = greet(peers + [sibling] + [at_plane(lax.rem(me + j, 16)) for j in range(1, 16)])
    half_up, half_down, half_a, sum_up, sum_down, sum_a, late_up, late_down, late_a, small, small_bias = own
    (grad_x,) = a_out
    a_in = [*a_in[:4], a_in[4].at[s, 0], *a_in[5:]]
    feed = FeedReduce(*updown, half_up, half_down, *u_scr)
    attend = AttendReduce(*grads, half_a, *w_scr)
    first = [AlongZ(1, half, out, *z_scr[3 * i : 3 * i + 3]) for i, (half, out) in enumerate(zip(halves, (sum_up, sum_down, sum_a)))]
    last = [
        AlongZ(0, half, out, *z_scr[9 + 3 * i : 12 + 3 * i])
        for i, (half, out) in enumerate(zip((half_up, half_down, half_a), (late_up, late_down, late_a)))
    ]

    def start_first(y, c):
        for unit in first:
            unit.start()

    def up_along_z(y, c):
        feed.up.finish()
        last[0].start()

    attend_back(0, *a_in, grad_x, *grads, small, small_bias, *a_scr, arrived,
                Hooks(begin=[feed.begin, start_first], middle=[feed.middle], ready=[attend.begin, up_along_z]))
    gather_pieces(feed, attend, first, last, small, small_bias, *rest, grad_x, *g_out, *g_scr)


def shape(dims, kind):
    return jax.ShapeDtypeStruct(dims, kind)


MOVE = [
    pltpu.VMEM((ROWS, D), F32),
    pltpu.VMEM((3, BLK, D), BF),
    pltpu.VMEM((3, BLK, D), BF),
    DMA((3,)),
    DMA((3,)),
    DMA((3,)),
    DMA((3,)),
    DMA((3,)),
]


def call(body, name, number, outs, ins, scratch):
    return pl.pallas_call(
        body,
        name=name,
        out_shape=outs,
        in_specs=ins,
        out_specs=[VMEM] * len(outs),
        scratch_shapes=scratch,
        cost_estimate=COST,
        compiler_params=pltpu.CompilerParams(collective_id=number, has_side_effects=True, vmem_limit_bytes=LIMIT),
    )


HALF_A, HALF_U = shape((2, 136, 640), BF), shape((1, 136, D), BF)
FEED_OUTS = [shape((BLK, D), F32), shape((D, D), BF), shape((D, D), BF), shape((8, D), F32)]
ATTEND_KEPT = [
    shape((BLK, D), F32),
    shape((ROWS, D), BF),
    shape((ROWS, TH), BF),
    shape((ROWS, 2 * TH), BF),
    shape((ROWS, 2 * TH), BF),
    shape((ROWS, 128), F32),
    shape((ROWS, TH), BF),
]
FEED_KEPT = [shape((ROWS, D), BF), shape((ROWS, D), F32), shape((ROWS, D), BF)]
ATTEND_WEIGHTS = [pltpu.VMEM((D, TQKV), BF), pltpu.VMEM((TH, D), BF)]
FEED_WEIGHTS = [pltpu.VMEM((D, D), BF), pltpu.VMEM((D, D), BF)]
FEED_MOVE = MOVE[:3] + MOVE[4:]


def run_attend_forward(x, w, wo, vecs):
    scratch = ATTEND_WEIGHTS + MOVE + [DMA, DMA]
    return call(attend_forward_first, "attend_forward_0", 0, ATTEND_KEPT, [VMEM, ANY, ANY, VMEM], scratch)(x, w, wo, vecs)


def run_forward_rest(middle, wu, wd, wa, wo, vecs, cotangent):
    outs = [shape((BLK, D), BF)] + FEED_KEPT + ATTEND_KEPT + [shape((BLK, D), BF)] + FEED_OUTS
    kept = [pltpu.VMEM(kind.shape, kind.dtype) for kind in FEED_KEPT]
    rows = pltpu.VMEM((ROWS, D), BF)
    scratch = FEED_WEIGHTS + FEED_MOVE + ATTEND_WEIGHTS + MOVE + [DMA, DMA] + kept + FEED_WEIGHTS + FEED_MOVE
    scratch = scratch + [rows, rows] + MOVE + [DMA((2, 2))]
    return call(forward_rest, "forward_rest", 2, outs, [VMEM] + [ANY] * 4 + [VMEM] * 3, scratch)(
        middle, wu, wd, wa, wo, vecs[0], vecs[1], cotangent
    )


FEED_OWN = [
    pltpu.VMEM((D, D), BF),
    pltpu.VMEM((D, D), BF),
    pltpu.VMEM((ROWS, D), BF),
    pltpu.VMEM((ROWS, D), BF),
] + MOVE
ATTEND_OWN = [
    pltpu.VMEM((D, TQKV), BF),
    pltpu.VMEM((TH, D), BF),
    pltpu.VMEM((ROWS, D), BF),
    pltpu.VMEM((ROWS, TH), BF),
    pltpu.VMEM((ROWS, TQKV), BF),
    pltpu.VMEM((ROWS, 2 * TH), BF),
    pltpu.VMEM((ROWS, 2 * TH), BF),
    pltpu.VMEM((ROWS, 2 * TH), F32),
    pltpu.VMEM((TH, D), BF),
    pltpu.VMEM((HD, D), BF),
] + MOVE + [DMA, DMA, DMA, DMA]
GATHER_OWN = [
    pltpu.VMEM((BLK, D), BF),
    pltpu.VMEM((BLK, D), BF),
    DMA((2,)),
    DMA((2,)),
    pltpu.VMEM((1, 136, D), BF),
    pltpu.VMEM((2, 136, 640), BF),
    pltpu.VMEM((2, 16, D), F32),
    pltpu.VMEM((2, 16, D), F32),
    pltpu.VMEM((3, 2, 16, D), F32),
    pltpu.VMEM((2, 16, D), BF),
    pltpu.VMEM((15, 16, D), BF),
    DMA((3,)),
    DMA((3,)),
    DMA((3, 3)),
    DMA((3, 3)),
    DMA,
    DMA,
    DMA((3,)),
    DMA((3,)),
    DMA((15,)),
    DMA((15,)),
]
SMALLS = [shape((8, D), F32), shape((8, TQKV), F32)]


def run_backward_middle(attend_args, up, down, feed_args):
    outs = [shape((BLK, D), BF)] + SMALLS + [HALF_U, HALF_U] + FEED_OUTS + [HALF_A]
    ins = [VMEM, ANY, ANY] + [VMEM] * 8 + [ANY] * 4 + [VMEM] * 5
    scratch = ATTEND_OWN + FEED_SCRATCH + FEED_OWN + BLOCKS + ATTEND_SCRATCH
    return call(backward_middle, "backward_middle", 5, outs, ins, scratch)(*attend_args, up, down, *feed_args)


def run_backward_end(attend_args, up, down, halves, rest):
    both = shape((2, BLK, D), BF)
    outs = [shape((BLK, D), BF), shape((4, 1, 136, D), BF), shape((4, 1, 136, D), BF), shape((4, 2, 136, 640), BF)]
    outs += [shape((16, D), F32), both, both]
    ins = [VMEM, ANY, ANY] + [VMEM] * 8 + [ANY] * 2 + [VMEM] * (3 + len(rest))
    units = [pltpu.VMEM((1, 136, D), BF), pltpu.VMEM((1, 136, D), BF), pltpu.VMEM((2, 136, 640), BF)]
    zs = (z_scratch(1, D) + z_scratch(1, D) + z_scratch(2, 640)) * 2
    smalls = [pltpu.VMEM((8, D), F32), pltpu.VMEM((8, TQKV), F32)]
    scratch = ATTEND_OWN + FEED_SCRATCH + BLOCKS + ATTEND_SCRATCH + zs + units * 3 + smalls + GATHER_OWN
    return call(backward_end, "backward_end", 6, outs, ins, scratch)(*attend_args, up, down, *halves, *rest)


def spread(send_a, send_u, send_d, send_o, send_v, wa, wu, wd, wo, wv, hold_a, hold_u, hold_d, hold_o, hold_v, local, ysend, yrecv, zsend, zrecv, csend, crecv):
    s = lax.axis_index("section")
    y, c = place()
    replica = lax.axis_index("replica")
    flipped = replica // 2 * 2 + (1 - replica % 2)
    near = {"section": 1 - s}
    far = {"section": 1 - s, "replica": flipped}
    sibling = at_chip(y, 1 - c)
    peers = [at_chip(ring(y, k), c) for k in (1, 2, 3)]
    arrived = greet(peers + [sibling, near, far])
    brought = load(
        [(send_a.at[y], hold_a), (send_u.at[y], hold_u), (send_d, hold_d), (send_o, hold_o), (send_v, hold_v)], local.at[0]
    )
    for copy in brought:
        copy.wait()
    keeps = load(
        [
            (hold_a, wa.at[s, y, c]),
            (hold_u, wu.at[s, y, c]),
            (hold_d, wd.at[s, c]),
            (hold_o, wo.at[s, c]),
            (hold_v, wv.at[s, y, c]),
        ],
        local.at[1],
    )
    arrived()

    def along_y(k, back):
        target = ring(y, k)
        place_in = ring(y, 4 - k) if back else y
        return [
            remote(send_v, wv.at[s, place_in, c], ysend.at[0, k - 1], yrecv.at[0, k - 1], at_chip(target, c)),
            remote(send_a.at[target], wa.at[s, place_in, c], ysend.at[1, k - 1], yrecv.at[1, k - 1], at_chip(target, c)),
            remote(send_u.at[target], wu.at[s, place_in, c], ysend.at[2, k - 1], yrecv.at[2, k - 1], at_chip(target, c)),
        ]

    def along_z(layer):
        return [
            remote(wv.at[layer, :, c], wv.at[layer, :, c], zsend.at[0], zrecv.at[0], near),
            remote(wa.at[layer, 0:2, c], wa.at[layer, 0:2, c], zsend.at[1], zrecv.at[1], near),
            remote(wa.at[layer, 2:4, c], wa.at[layer, 2:4, c], zsend.at[2], zrecv.at[2], far),
            remote(wo.at[layer, c], wo.at[layer, c], zsend.at[3], zrecv.at[3], far),
            remote(wu.at[layer, 0:2, c], wu.at[layer, 0:2, c], zsend.at[4], zrecv.at[4], near),
            remote(wu.at[layer, 2:4, c], wu.at[layer, 2:4, c], zsend.at[5], zrecv.at[5], far),
            remote(wd.at[layer, c, 0:272], wd.at[layer, c, 0:272], zsend.at[6], zrecv.at[6], near),
            remote(wd.at[layer, c, 272:544], wd.at[layer, c, 272:544], zsend.at[7], zrecv.at[7], far),
        ]

    def across(layer, i, core):
        return [
            remote(wv.at[layer, :, core], wv.at[layer, :, core], csend.at[i, 0], crecv.at[i, 0], sibling),
            remote(wa.at[layer, :, core], wa.at[layer, :, core], csend.at[i, 1], crecv.at[i, 1], sibling),
            remote(wo.at[layer, core], wo.at[layer, core], csend.at[i, 2], crecv.at[i, 2], sibling),
            remote(wu.at[layer, :, core], wu.at[layer, :, core], csend.at[i, 3], crecv.at[i, 3], sibling),
            remote(wd.at[layer, core], wd.at[layer, core], csend.at[i, 4], crecv.at[i, 4], sibling),
        ]

    sent_y = [along_y(k, False) for k in (1, 2, 3)]
    got_y = [along_y(k, True) for k in (1, 2, 3)]
    sent_z, got_z = along_z(s), along_z(1 - s)
    sent_c = [across(s, 0, c), across(1 - s, 1, c)]
    got_c = [across(s, 0, 1 - c), across(1 - s, 1, 1 - c)]
    for kind in (0, 1):
        for k in (1, 0, 2):
            sent_y[k][kind].start()
    keeps[3].wait()
    sent_z[3].start()
    sent_c[0][2].start()
    keeps[2].wait()
    sent_z[6].start()
    sent_z[7].start()
    sent_c[0][4].start()
    for kind, keep, zs, cross in ((0, 4, (0,), 0), (1, 0, (1, 2), 1)):
        keeps[keep].wait()
        for k in range(3):
            got_y[k][kind].wait_recv()
        for z in zs:
            sent_z[z].start()
        sent_c[0][cross].start()
    for k in (1, 0, 2):
        sent_y[k][2].start()
    for zs, cross in (((3,), 2), ((6, 7), 4), ((0,), 0), ((1, 2), 1)):
        for z in zs:
            got_z[z].wait_recv()
        sent_c[1][cross].start()
    keeps[1].wait()
    for k in range(3):
        got_y[k][2].wait_recv()
    for z in (4, 5):
        sent_z[z].start()
    sent_c[0][3].start()
    for z in (4, 5):
        got_z[z].wait_recv()
    sent_c[1][3].start()
    for i in range(2):
        for cross in range(5):
            got_c[i][cross].wait_recv()
    for k in range(3):
        for kind in range(3):
            sent_y[k][kind].wait_send()
    for z in range(8):
        sent_z[z].wait_send()
    for i in range(2):
        for cross in range(5):
            sent_c[i][cross].wait_send()


def run_spread(a, u, d, o, v):
    outs = [
        shape((2, 4, 2, 136, TQKV), BF),
        shape((2, 4, 2, 136, D), BF),
        shape((2, 2, 544, D), BF),
        shape((2, 2, 192, D), BF),
        shape((2, 4, 2, 16, D), BF),
    ]
    return pl.pallas_call(
        spread,
        name="spread",
        out_shape=outs,
        in_specs=[ANY] * 5,
        out_specs=[ANY] * 5,
        scratch_shapes=[
            pltpu.VMEM((136, TQKV), BF),
            pltpu.VMEM((136, D), BF),
            pltpu.VMEM((544, D), BF),
            pltpu.VMEM((192, D), BF),
            pltpu.VMEM((16, D), BF),
            DMA((2, 5)), DMA((3, 3)), DMA((3, 3)), DMA((8,)), DMA((8,)), DMA((2, 5)), DMA((2, 5)),
        ],
        compiler_params=pltpu.CompilerParams(collective_id=8, has_side_effects=True),
    )(a, u, d, o, v)


def build_small(buf, one, two, heads, y):
    buf[...] = jnp.zeros_like(buf)
    buf[0:2] = one[0:2]
    buf[2:4] = two[0:2]
    buf[4:5] = one[2:3]
    buf[5:6] = two[3:4]
    buf[6:10] = chip_row(y, two[2:3])
    for row, at in ((10, 2 * TH), (11, TH)):
        buf[row : row + 1, pl.ds(pl.multiple_of(256 * y, 256), 256)] = heads[0:1, at : at + 256]

        @pl.when(y == 3)
        def _(row=row, at=at):
            buf[row : row + 1, 1024:D] = heads[0:1, at + 256 : at + TH]


class Gather:
    def __init__(self, unit, moved, keep_from, out, ts, tr, gs, gr):
        self.unit, self.moved, self.out, self.keep_from = unit, moved, out, keep_from
        self.ts, self.tr, self.gs, self.gr = ts, tr, gs, gr

    def transpose(self):
        y, c = place()
        s, x, h, me = plane()
        return remote(self.unit, self.moved, self.ts, self.tr, at_chip(block_of(x, y), c))

    def elsewhere(self):
        y, c = place()
        s, x, h, me = plane()
        return block_of(x, y) != y

    def start(self):
        pl.when(self.elsewhere())(self.transpose().start)

    def arrive(self):
        @pl.when(self.elsewhere())
        def _():
            self.transpose().wait()
            self.unit[0] = self.moved[0]
            if self.keep_from:
                lane = lax.broadcasted_iota(jnp.int32, self.unit.shape[1:], 1)
                merged = jnp.where(lane < self.keep_from, self.moved[1].astype(F32), self.unit[1].astype(F32))
                self.unit[1] = merged.astype(BF)

    def copies(self):
        y, c = place()
        s, x, h, me = plane()
        targets = x_peers(x, h)
        for k in ORDER:
            yield k, remote(self.unit, self.out.at[block_of(x, y)], self.gs.at[k - 1], self.gr.at[k - 1], targets[k - 1])

    def spread(self):
        y, c = place()
        s, x, h, me = plane()
        for k, copy in self.copies():
            copy.start()
        self.out[block_of(x, y)] = self.unit[...]

    def finish(self):
        y, c = place()
        s, x, h, me = plane()
        targets = x_peers(x, h)
        for k, copy in self.copies():
            copy.wait_send()
            place_in = self.out.at[block_of(x - k + 4, y)]
            remote(place_in, place_in, self.gs.at[k - 1], self.gr.at[k - 1], targets[k - 1]).wait_recv()


def gather_pieces(feed, attend, first, last, one_0, heads_0,
                  two_0, one_1, two_1, heads_1, act_0, act_1, back_1, back_0,
                  out_up, out_down, out_a, out_small, out_act, out_back,
                  swap_act, swap_back, ws, wr, moved_up, moved_a, small, small_c, small_y, small_x, small_z,
                  ts, tr, gs, gr, cs, cr, ys, yr, zs, zr):
    y, c = place()
    s, x, h, me = plane()
    sibling = at_chip(y, 1 - c)
    peers = [at_chip(ring(y, k), c) for k in (1, 2, 3)]
    gathers = [
        Gather(last[i].out, moved, keep, out, ts.at[i], tr.at[i], gs.at[i], gr.at[i])
        for i, (moved, keep, out) in enumerate(((moved_up, 0, out_up), (None, 0, out_down), (moved_a, 320, out_a)))
    ]

    def sum_along_z(i):
        first[i].finish()
        last[i].finish()

        @pl.when(s == 1)
        def _():
            last[i].out[...] = first[i].out[...]

    attend.middle(y, c)
    feed.down.finish()
    last[1].start()
    build_small(small.at[0], one_0, two_0, heads_0, y)
    build_small(small.at[1], one_1, two_1, heads_1, y)
    cross = remote(small, small_c, cs, cr, sibling)
    cross.start()
    swap_act[...] = jnp.where(s == 0, act_1[...].astype(F32), act_0[...].astype(F32)).astype(BF)
    swap_back[...] = jnp.where(s == 0, back_1[...].astype(F32), back_0[...].astype(F32)).astype(BF)
    swaps = [
        remote(swap_act, out_act.at[s], ws.at[0], wr.at[0], {"section": 1 - s}),
        remote(swap_back, out_back.at[s], ws.at[1], wr.at[1], {"section": 1 - s}),
    ]
    out_act[s] = jnp.where(s == 0, act_0[...].astype(F32), act_1[...].astype(F32)).astype(BF)
    out_back[s] = jnp.where(s == 0, back_0[...].astype(F32), back_1[...].astype(F32)).astype(BF)
    cross.wait()
    small[...] = small[...] + small_c[...]
    hops = [remote(small, small_y.at[k - 1], ys.at[k - 1], yr.at[k - 1], peers[k - 1]) for k in (1, 2, 3)]
    for hop in hops:
        hop.start()
    sum_along_z(0)
    gathers[0].start()
    for hop in hops:
        hop.wait()
    small_x[...] = (small[...] + small_y[0] + small_y[1] + small_y[2]).astype(BF)

    def plane_copies():
        for j in range(1, 16):
            q = lax.rem(me + j, 16)
            yield remote(small_x.at[q // 8], small_z.at[15 - j], zs.at[j - 1], zr.at[15 - j], at_plane(q))

    attend.finish()
    last[2].start()
    gathers[0].arrive()
    gathers[0].spread()
    sum_along_z(1)
    gathers[1].spread()
    for copy in plane_copies():
        copy.start()
    sum_along_z(2)
    gathers[2].start()
    for swap in swaps:
        swap.start()
    gathers[2].arrive()
    gathers[2].spread()
    total = small_x[s].astype(F32)
    for copy in plane_copies():
        copy.wait_send()
    for j in range(15):
        remote(small_x.at[0], small_z.at[j], zs.at[j], zr.at[j], sibling).wait_recv()
        total = total + small_z[j].astype(F32)
    out_small[...] = total
    for i, swap in enumerate(swaps):
        swap.wait_send()
        place_in = (out_act, out_back)[i].at[1 - s]
        remote(place_in, place_in, ws.at[i], wr.at[i], {"section": 1 - s}).wait_recv()
    for gather in gathers:
        gather.finish()


def assemble(all_up, all_down, all_a, small, attn, out, up, down, b_attn, b_out, b_up, b_down, gain, shift):
    y, c = place()
    f = 2 * y + c
    for j in range(CHIPS):
        up[:, j * D : (j + 1) * D] = all_up[j, 0].astype(F32)
        down[j * 136 : (j + 1) * 136] = all_down[j, 0].astype(F32)
        first, second = all_a[j, 0].astype(F32), all_a[j, 1].astype(F32)
        parts = ((0, second[:, :TH]), (D, first[:, :TH]), (2 * D, first[:, TH:]))
        for base, part in parts:
            attn[:, base + 256 * j : base + 256 * j + 256] = part[:, :256]
        out[:, 256 * j : 256 * j + 256] = second[:, TH : TH + 256]
        if j == CHIPS - 1:
            for base, part in parts:
                attn[:, base + 1024 : base + D] = part[:, 256:]
            out[:, 1024:] = second[:, TH + 256 :]

    def pick(index, options):
        total = jnp.where(index == 0, options[0], 0.0)
        for i, option in enumerate(options[1:], 1):
            total = total + jnp.where(index == i, option, 0.0)
        return total

    for row, ref, place_in in ((0, gain, 0), (1, shift, 0), (2, gain, 1), (3, shift, 1), (4, b_out, 0), (5, b_down, 0)):
        ref[place_in : place_in + 1] = pick(f, [small[row : row + 1, 136 * i : 136 * i + 136] for i in range(8)])
    b_up[...] = pick(f, [small[6 + i // 2 : 7 + i // 2, 544 * (i % 2) : 544 * (i % 2) + 544] for i in range(8)])
    b_attn[...] = pick(f, [small[10 + i // 4 : 11 + i // 4, 272 * (i % 4) : 272 * (i % 4) + 272] for i in range(8)])


def run_assemble(*gathered):
    sizes = [(136, 3 * D), (136, D), (136, FF), (544, D), (1, 272), (1, 136), (1, 544), (1, 136), (2, 136), (2, 136)]
    return pl.pallas_call(
        assemble,
        name="assemble",
        out_shape=[shape(dims, F32) for dims in sizes],
        in_specs=[VMEM] * 4,
        out_specs=[VMEM] * len(sizes),
        compiler_params=pltpu.CompilerParams(vmem_limit_bytes=LIMIT),
    )(*gathered)


def split_heads(block):
    zero = jnp.zeros(block.shape[:-1] + (HD,), block.dtype)
    return [
        jnp.concatenate([block[..., 256 * j : 256 * j + 256], block[..., 1024:] if j == 3 else zero], axis=-1)
        for j in range(CHIPS)
    ]


def on_device(inputs, cotangent, weight_attn, weight_out, weight_up, weight_down, bias_attn, bias_out, bias_up,
              bias_down, norm_gain, norm_bias):
    s = lax.axis_index("section")
    f = lax.axis_index("fsdp")
    y, c = f // 2, f % 2
    wa = weight_attn[0]
    q_blocks, k_blocks, v_blocks = (split_heads(wa[:, i * D : (i + 1) * D]) for i in range(3))
    send_a = jnp.stack(
        [jnp.concatenate([k_blocks[j], v_blocks[j], q_blocks[j]], axis=-1) for j in range(CHIPS)]
    )
    send_u = jnp.stack([weight_up[0][:, j * D : (j + 1) * D] for j in range(CHIPS)])
    tail = lax.ppermute(weight_out[0, 88:], "fsdp", [(i, (i + 2) % 8) for i in range(8)])
    send_o = jnp.concatenate([weight_out[0], tail, jnp.zeros((8, D), BF)], axis=0)
    vectors = jnp.stack([norm_gain[0, 0], norm_bias[0, 0], norm_gain[0, 1], norm_bias[0, 1], bias_out[0], bias_down[0]])
    send_v = jnp.concatenate(
        [
            lax.dynamic_update_slice(jnp.zeros((6, D), BF), vectors, (0, 136 * f)),
            lax.dynamic_update_slice(jnp.zeros((4, D), BF), bias_up, (y, 544 * c)),
            lax.dynamic_update_slice(jnp.zeros((6, D), BF), bias_attn, (f // 4, 272 * (f % 4))),
        ]
    )
    wa, wu, wd, wo, wv = run_spread(send_a, send_u, weight_down[0], send_o, send_v)
    wa = wa.reshape(2, D, TQKV)
    wu = wu.reshape(2, D, D)
    wd = wd.reshape(2, D, D)
    wo = jnp.concatenate([wo[:, 1, 136:184], wo[:, 0, :136], wo[:, 1, :136]], axis=1)
    vecs = jnp.sum(wv.astype(F32), axis=(1, 2))
    middle_0, *kept_0 = run_attend_forward(inputs, wa, wo, vecs[0])
    rest = run_forward_rest(middle_0, wu, wd, wa, wo, vecs, cotangent)
    (x_1, *kept_two_0), (middle_1, *kept_1), (result_1,), (grad_middle, up, down, two_1) = split(rest, 4, 7, 1, 4)
    acts = [x_1, result_1]
    back_1, one_1, heads_1, half_up, half_down, grad_middle, up_0, down_0, two_0, half_a = run_backward_middle(
        (grad_middle, wa, wo, vecs[1], x_1, *kept_1),
        up.reshape(4, 2, 136, D),
        down.reshape(2, 4, 136, D),
        (wu, wd, vecs[0], middle_0, *kept_two_0),
    )
    back_0, all_up, all_down, all_a, small, all_acts, all_grads = run_backward_end(
        (grad_middle, wa, wo, vecs[0], inputs, *kept_0),
        up_0.reshape(4, 2, 136, D),
        down_0.reshape(2, 4, 136, D),
        (half_up, half_down, half_a),
        (two_0, one_1, two_1, heads_1, *acts, back_1),
    )
    attn, out, up, down, b_attn, b_out, b_up, b_down, gain, shift = run_assemble(all_up, all_down, all_a, small)
    return (
        all_acts[None, :, None],
        all_grads[None, :, None],
        attn[None],
        out[None],
        up[None],
        down[None],
        b_attn,
        b_out,
        b_up,
        b_down,
        gain[None],
        shift[None],
    )


def solution(mesh):
    placed = (
        P(None, "replica", "fsdp", None),
        P(None, "replica", "fsdp", None),
        P("section", "fsdp", None),
        P("section", "fsdp", None),
        P("section", "fsdp", None),
        P("section", "fsdp", None),
        P("section", "fsdp"),
        P("section", "fsdp"),
        P("section", "fsdp"),
        P("section", "fsdp"),
        P("section", None, "fsdp"),
        P("section", None, "fsdp"),
    )
    return jax.shard_map(
        on_device,
        mesh=mesh,
        in_specs=placed,
        out_specs=(
            P("section", None, "replica", "fsdp", None),
            P("section", None, "replica", "fsdp", None),
        )
        + placed[2:],
        check_vma=False,
    )
```

```python
import functools

import jax
import jax.numpy as jnp
from jax import lax
from jax.experimental import pallas as pl
from jax.experimental.pallas import tpu as pltpu
from jax.sharding import PartitionSpec as P

D = 1088
FF = 4352
HEADS = 17
HD = 64
BLK = 64
CHIPS = 4
ROWS = BLK * CHIPS
SLOTS = 5
TH = SLOTS * HD
TQKV = 3 * TH
SCALE = HD**-0.5
EPS = 1e-5
MESH = pl.DeviceIdType.MESH
BF = jnp.bfloat16
F32 = jnp.float32
ANY = pl.BlockSpec(memory_space=pl.ANY)
VMEM = pl.BlockSpec(memory_space=pltpu.VMEM)
DMA = pltpu.SemaphoreType.DMA
LIMIT = 56 * 1024 * 1024
COST = pl.CostEstimate(flops=10_000_000, bytes_accessed=10_000, transcendentals=0)


def dot(a, b):
    return lax.dot_general(a, b, (((1,), (0,)), ((), ())), preferred_element_type=F32)


def dot_nt(a, b):
    return lax.dot_general(a, b, (((1,), (1,)), ((), ())), preferred_element_type=F32)


def dot_tn(a, b):
    return lax.dot_general(a, b, (((0,), (0,)), ((), ())), preferred_element_type=F32)


def chunks(n, size=256):
    return [(i, min(size, n - i)) for i in range(0, n, size)]


def place():
    f = lax.axis_index("fsdp")
    return f // 2, f % 2


def ring(y, k):
    return lax.rem(y + k, CHIPS)


def at_chip(y, c):
    return {"fsdp": 2 * y + c}


def greet(targets):
    barrier = pltpu.get_barrier_semaphore()
    for target in targets:
        pl.semaphore_signal(barrier, inc=1, device_id=target, device_id_type=MESH)
    return functools.partial(pl.semaphore_wait, barrier, len(targets))


def remote(src, dst, send, recv, target):
    return pltpu.make_async_remote_copy(
        src_ref=src, dst_ref=dst, send_sem=send, recv_sem=recv, device_id=target, device_id_type=MESH
    )


def slot(ref, y):
    return ref.at[pl.ds(pl.multiple_of(y * BLK, BLK), BLK)]


ORDER = (2, 1, 3)


def gather_start(full, y, c, send, recv):
    for k in ORDER:
        remote(slot(full, y), slot(full, y), send.at[k - 1], recv.at[k - 1], at_chip(ring(y, k), c)).start()


def gather_wait(full, y, c, send, recv):
    for k in (1, 3, 2):
        source = ring(y, 4 - k)
        remote(slot(full, source), slot(full, source), send.at[k - 1], recv.at[k - 1], at_chip(ring(y, k), c)).wait()


def scatter_start(acc, out_buf, in_buf, y, c, send, recv):
    for k in ORDER:
        target = ring(y, k)
        out_buf[k - 1] = slot(acc, target)[...].astype(BF)
        remote(out_buf.at[k - 1], in_buf.at[k - 1], send.at[k - 1], recv.at[k - 1], at_chip(target, c)).start()


def scatter_wait(acc, out_buf, in_buf, y, c, send, recv):
    total = slot(acc, y)[...]
    for k in (1, 3, 2):
        remote(out_buf.at[k - 1], in_buf.at[k - 1], send.at[k - 1], recv.at[k - 1], at_chip(ring(y, k), c)).wait()
        total = total + in_buf[k - 1].astype(F32)
    return total


def stats(v):
    centre = v - jnp.mean(v, axis=-1, keepdims=True)
    scale = lax.rsqrt(jnp.mean(centre * centre, axis=-1, keepdims=True) + EPS)
    return centre * scale, scale


def norm(v, gain, shift):
    return stats(v)[0] * gain + shift


def norm_back(d, v, gain):
    vh, scale = stats(v)
    q = d * gain
    grad = scale * (q - jnp.mean(q, axis=-1, keepdims=True) - vh * jnp.mean(q * vh, axis=-1, keepdims=True))
    return grad, jnp.sum(d * vh, axis=0, keepdims=True), jnp.sum(d, axis=0, keepdims=True)


GELU_A = 0.7978845608028654
GELU_B = 0.044715


def gelu(h):
    return 0.5 * h * (1.0 + jnp.tanh(GELU_A * (h + GELU_B * h * h * h)))


def gelu_slope(h):
    t = jnp.tanh(GELU_A * (h + GELU_B * h * h * h))
    return 0.5 * (1.0 + t) + 0.5 * h * (1.0 - t * t) * (GELU_A * (1.0 + 3.0 * GELU_B * h * h))


def masks(c):
    row = lax.broadcasted_iota(jnp.int32, (ROWS, ROWS), 0)
    col = lax.broadcasted_iota(jnp.int32, (ROWS, ROWS), 1)
    own = row >= col
    other = (row // BLK) >= (col // BLK) + (1 - c)
    return own, other


def load(pairs, sems):
    copies = [pltpu.make_async_copy(src, dst, sems.at[i]) for i, (src, dst) in enumerate(pairs)]
    for copy in copies:
        copy.start()
    return copies


def out_rows(wo_hbm, wo, e, y):
    start = pl.multiple_of(48 - 16 * y, 16)
    return [(wo_hbm.at[e, pl.ds(start, 256)], wo.at[0:256]), (wo_hbm.at[e, 256:320], wo.at[256:320])]


def out_wait(weights, wo, y):
    weights[1].wait()
    weights[2].wait()

    @pl.when(y < 3)
    def _():
        wo[256:320] = jnp.zeros((HD, D), BF)


def chip_row(y, rows):
    return jnp.where(lax.broadcasted_iota(jnp.int32, (CHIPS, 1), 0) == y, rows, 0.0)


def head_bias(vecs, row, y):
    last = jnp.where(y == 3, vecs[row : row + 1, 1024:D], 0.0)
    return jnp.concatenate([vecs[row : row + 1, pl.ds(pl.multiple_of(256 * y, 256), 256)], last], axis=-1)


def attend_forward(e, x, w_hbm, wo_hbm, vecs, middle, normed, queries, kv, kv_other, logsum, attended,
                   w, wo, acc, out_buf, in_buf, ls, gs, gr, ss, sr, ks, kr, arrived, weights=None, hooks=None):
    y, c = place()
    sibling = at_chip(y, 1 - c)
    if weights is None:
        weights = load([(w_hbm.at[e], w)] + out_rows(wo_hbm, wo, e, y), ls)
    slot(normed, y)[...] = norm(x[...].astype(F32), vecs[0:1], vecs[1:2]).astype(BF)
    arrived()
    gather_start(normed, y, c, gs, gr)
    if hooks is not None:
        hooks.begin(y, c)
    own, other = masks(c)
    weights[0].wait()
    gather_wait(normed, y, c, gs, gr)
    rows = normed[...]
    bias = jnp.concatenate([jnp.zeros((1, TH), F32), head_bias(vecs, 11, y)], axis=-1)
    for at, size in chunks(2 * TH):
        kv[:, at : at + size] = (dot(rows, w[:, at : at + size]) + bias[:, at : at + size]).astype(BF)
    swap = remote(kv, kv_other, ks, kr, sibling)
    swap.start()
    queries[...] = (dot(rows, w[:, 2 * TH :]) + head_bias(vecs, 10, y)).astype(BF)
    swap.wait()
    for h in range(SLOTS):
        at = h * HD
        q = queries[:, at : at + HD]
        s_own = jnp.where(own, dot_nt(q, kv[:, at : at + HD]) * SCALE, -1e30)
        s_other = jnp.where(other, dot_nt(q, kv_other[:, at : at + HD]) * SCALE, -1e30)
        top = jnp.maximum(jnp.max(s_own, axis=-1, keepdims=True), jnp.max(s_other, axis=-1, keepdims=True))
        e_own = jnp.exp(s_own - top)
        e_other = jnp.exp(s_other - top)
        total = jnp.sum(e_own, axis=-1, keepdims=True) + jnp.sum(e_other, axis=-1, keepdims=True)
        logsum[:, h : h + 1] = top + jnp.log(total)
        inverse = 1.0 / total
        a_own = (e_own * inverse).astype(BF)
        a_other = (e_other * inverse).astype(BF)
        out = dot(a_own, kv[:, TH + at : TH + at + HD]) + dot(a_other, kv_other[:, TH + at : TH + at + HD])
        attended[:, at : at + HD] = out.astype(BF)
    out_wait(weights, wo, y)
    mixed = attended[...]
    for at, size in chunks(D):
        acc[:, at : at + size] = dot(mixed, wo[:, at : at + size])
    scatter_start(acc, out_buf, in_buf, y, c, ss, sr)
    if hooks is not None:
        hooks.late()
    base = x[...].astype(F32) + vecs[4:5]
    middle[...] = base + scatter_wait(acc, out_buf, in_buf, y, c, ss, sr)


def feed_forward(middle, vecs, result, normed, hidden, active,
                 wu, wd, acc, out_buf, in_buf, gs, gr, ss, sr, arrived, weights, defer=False):
    y, c = place()
    slot(normed, y)[...] = norm(middle[...], vecs[2:3], vecs[3:4]).astype(BF)
    arrived()
    gather_start(normed, y, c, gs, gr)
    bias = jnp.sum(chip_row(y, vecs[6:10]), axis=0, keepdims=True)
    weights[0].wait()
    gather_wait(normed, y, c, gs, gr)
    rows = normed[...]
    for at, size in chunks(D):
        h = dot(rows, wu[:, at : at + size]) + bias[:, at : at + size]
        hidden[:, at : at + size] = h
        active[:, at : at + size] = gelu(h).astype(BF)
    weights[1].wait()
    rows = active[...]
    for at, size in chunks(D):
        acc[:, at : at + size] = dot(rows, wd[:, at : at + size])
    scatter_start(acc, out_buf, in_buf, y, c, ss, sr)

    def finish():
        base = middle[...] + vecs[5:6]
        result[...] = (base + scatter_wait(acc, out_buf, in_buf, y, c, ss, sr)).astype(BF)

    if defer:
        return finish
    finish()


def feed_back(e, grad, wu_hbm, wd_hbm, vecs, middle, normed, hidden, active, grad_middle, grad_up, grad_down, small,
              wu, wd, full, gh, acc, out_buf, in_buf, ls, gs, gr, ss, sr, arrived, reduce=None, weights=None, early=False):
    y, c = place()
    if weights is None:
        weights = load([(wu_hbm.at[e], wu), (wd_hbm.at[e], wd)], ls)
    own_rows = grad[...]
    if not early:
        slot(full, y)[...] = own_rows
        arrived()
        gather_start(full, y, c, gs, gr)
    if reduce is not None:
        reduce.begin(y, c)
    small[...] = jnp.zeros_like(small)
    small[3:4] = jnp.sum(own_rows.astype(F32), axis=0, keepdims=True)
    weights[1].wait()
    if reduce is not None:
        reduce.middle(y, c)
    gather_wait(full, y, c, gs, gr)
    rows = full[...]
    for at, size in chunks(D):
        slope = gelu_slope(hidden[:, at : at + size])
        part = (dot_nt(rows, wd[at : at + size, :]) * slope).astype(BF)
        gh[:, at : at + size] = part
        small[2:3, at : at + size] = jnp.sum(part.astype(F32), axis=0, keepdims=True)
    weights[0].wait()
    rows = gh[...]
    for at, size in chunks(D):
        acc[:, at : at + size] = dot_nt(rows, wu[at : at + size, :])
    scatter_start(acc, out_buf, in_buf, y, c, ss, sr)
    if reduce is not None:
        reduce.late()
    for at, size in chunks(D):
        grad_up[at : at + size, :] = dot_tn(normed[:, at : at + size], gh[...]).astype(BF)
        grad_down[at : at + size, :] = dot_tn(active[:, at : at + size], full[...]).astype(BF)
    d = scatter_wait(acc, out_buf, in_buf, y, c, ss, sr)
    back, gain, shift = norm_back(d, middle[...], vecs[2:3])
    small[0:1] = gain
    small[1:2] = shift
    grad_middle[...] = grad[...].astype(F32) + back
    if reduce is not None:
        reduce.finish()


def attend_back(e, grad, w_hbm, wo_hbm, vecs, x, normed, queries, kv, kv_other, logsum, attended,
                grad_x, grad_attn, grad_out, small, small_bias,
                w, wo, full, ga, gj, part_out, part_in, part_own, rows_out, edge, acc, out_buf, in_buf, ls, gs, gr, ss, sr, ks, kr, es, er,
                arrived, reduce):
    y, c = place()
    sibling = at_chip(y, 1 - c)
    weights = load([(w_hbm.at[e], w)] + out_rows(wo_hbm, wo, e, y), ls)
    own_rows = grad[...].astype(BF)
    slot(full, y)[...] = own_rows
    arrived()
    gather_start(full, y, c, gs, gr)
    reduce.begin(y, c)
    small[...] = jnp.zeros_like(small)
    small[2:3] = jnp.sum(own_rows.astype(F32), axis=0, keepdims=True)
    own, other = masks(c)
    out_wait(weights, wo, y)
    reduce.middle(y, c)
    gather_wait(full, y, c, gs, gr)
    ga[...] = dot_nt(full[...], wo[...]).astype(BF)
    for h in range(SLOTS):
        at = h * HD
        q = queries[:, at : at + HD]
        g = ga[:, at : at + HD]
        lse = logsum[:, h : h + 1]
        k_own, k_other = kv[:, at : at + HD], kv_other[:, at : at + HD]
        v_own, v_other = kv[:, TH + at : TH + at + HD], kv_other[:, TH + at : TH + at + HD]
        p_own = jnp.exp(jnp.where(own, dot_nt(q, k_own) * SCALE, -1e30) - lse)
        p_other = jnp.exp(jnp.where(other, dot_nt(q, k_other) * SCALE, -1e30) - lse)
        gp_own = dot_nt(g, v_own)
        gp_other = dot_nt(g, v_other)
        delta = jnp.sum(p_own * gp_own, axis=-1, keepdims=True) + jnp.sum(p_other * gp_other, axis=-1, keepdims=True)
        s_own = (p_own * (gp_own - delta)).astype(BF)
        s_other = (p_other * (gp_other - delta)).astype(BF)
        gj[:, 2 * TH + at : 2 * TH + at + HD] = ((dot(s_own, k_own) + dot(s_other, k_other)) * SCALE).astype(BF)
        part_own[:, at : at + HD] = dot_tn(s_own, q) * SCALE
        part_out[:, at : at + HD] = (dot_tn(s_other, q) * SCALE).astype(BF)
        part_own[:, TH + at : TH + at + HD] = dot_tn(p_own.astype(BF), g)
        part_out[:, TH + at : TH + at + HD] = dot_tn(p_other.astype(BF), g).astype(BF)
    swap = remote(part_out, part_in, ks, kr, sibling)
    swap.start()
    for at, size in chunks(D):
        rows_out[:, at : at + size] = dot_tn(attended[...], full[:, at : at + size]).astype(BF)
    lend = remote(rows_out.at[0:HD], edge, es, er, at_chip(ring(y, 3), c))
    lend.start()
    weights[0].wait()
    swap.wait()
    gj[:, : 2 * TH] = (part_own[...] + part_in[...].astype(F32)).astype(BF)
    rows = gj[...]
    for at, size in chunks(D):
        acc[:, at : at + size] = dot_nt(rows, w[at : at + size, :])
    scatter_start(acc, out_buf, in_buf, y, c, ss, sr)
    for j in range(CHIPS):
        part = dot_tn(normed[:, 272 * j : 272 * j + 272], gj[...])
        grad_attn[j, 0] = part[:136].astype(BF)
        grad_attn[j, 1] = part[136:].astype(BF)
    lend.wait()

    @pl.when(y < 3)
    def _():
        rows_out[256:320] = edge[...]

    chip_rows = rows_out[pl.ds(pl.multiple_of(16 * y, 16), 272)].astype(F32)
    grad_out[0] = chip_rows[:136].astype(BF)
    grad_out[1] = chip_rows[136:].astype(BF)
    reduce.ready(y, c)
    small_bias[...] = jnp.zeros_like(small_bias)
    small_bias[0:1] = jnp.sum(gj[...].astype(F32), axis=0, keepdims=True)
    d = scatter_wait(acc, out_buf, in_buf, y, c, ss, sr)
    back, gain, shift = norm_back(d, x[...].astype(F32), vecs[0:1])
    small[0:1] = gain
    small[1:2] = shift
    grad_x[...] = (grad[...] + back).astype(BF)
    reduce.finish()


def plane():
    s, r = lax.axis_index("section"), lax.axis_index("replica")
    return s, r // 2, r % 2, s * 8 + r


def at_plane(q):
    return {"section": q // 8, "replica": lax.rem(q, 8)}


def x_peers(x, h):
    return [{"replica": 2 * lax.rem(x + k, 4) + h} for k in (1, 2, 3)]


def z_peers(s, h):
    x = lax.axis_index("replica") // 2
    return [
        {"section": 1 - s},
        {"section": 1 - s, "replica": 2 * x + 1 - h},
        {"replica": 2 * x + 1 - h},
    ]


def plane_peers():
    s, x, h, me = plane()
    return x_peers(x, h) + z_peers(s, h)


def block_of(x, y):
    return lax.rem(x - y + 8, 4)


class AlongX:
    def __init__(self, blocks, landing, out, send, recv):
        self.blocks, self.landing, self.out, self.send, self.recv = blocks, landing, out, send, recv

    def copies(self):
        y, c = place()
        s, x, h, me = plane()
        targets = x_peers(x, h)
        for k in ORDER:
            yield remote(
                self.blocks.at[block_of(x + k, y)], self.landing.at[k - 1], self.send.at[k - 1], self.recv.at[k - 1],
                targets[k - 1],
            )

    def start(self):
        for copy in self.copies():
            copy.start()

    def finish(self):
        y, c = place()
        s, x, h, me = plane()
        own = block_of(x, y)
        for copy in self.copies():
            copy.wait()

        def add(i, carry):
            rows = pl.ds(pl.multiple_of(8 * (i % 17), 8), 8)
            total = self.blocks[own, i // 17, rows].astype(F32)
            for k in range(3):
                total = total + self.landing[k, i // 17, rows].astype(F32)
            self.out[i // 17, rows] = total.astype(BF)
            return carry

        lax.fori_loop(0, 17 * self.out.shape[0], add, 0)


def x_scratch(count, width):
    return [pltpu.VMEM((4, count, 136, width), BF), pltpu.VMEM((3, count, 136, width), BF), DMA((3,)), DMA((3,))]


class AlongZ:
    def __init__(self, layer, blocks, out, landing, send, recv):
        self.layer, self.blocks, self.landing, self.out, self.send, self.recv = layer, blocks, landing, out, send, recv

    def copies(self):
        s, x, h, me = plane()
        for half in (0, 1):
            owner = 2 * half + self.layer
            rel = lax.rem(2 * h + s - owner + 3, 4)
            target = {"section": jnp.int32(self.layer), "replica": 2 * x + half}
            copy = remote(self.blocks, self.landing.at[rel], self.send.at[half], self.recv.at[rel], target)
            yield 2 * h + s != owner, copy

    def start(self):
        for sends, copy in self.copies():
            pl.when(sends)(copy.start)

    def finish(self):
        s, x, h, me = plane()
        for sends, copy in self.copies():
            pl.when(sends)(copy.wait_send)

        @pl.when(s == self.layer)
        def _():
            for rel in range(3):
                remote(self.blocks, self.landing.at[rel], self.send.at[0], self.recv.at[rel], {"section": 1 - s}).wait_recv()

            def add(i, carry):
                rows = pl.ds(pl.multiple_of(8 * (i % 17), 8), 8)
                total = self.blocks[i // 17, rows].astype(F32)
                for rel in range(3):
                    total = total + self.landing[rel, i // 17, rows].astype(F32)
                self.out[i // 17, rows] = total.astype(BF)
                return carry

            lax.fori_loop(0, 17 * self.out.shape[0], add, 0)


def z_scratch(count, width):
    return [pltpu.VMEM((3, count, 136, width), BF), DMA((2,)), DMA((3,))]


class FeedReduce:
    def __init__(self, up, down, out_up, out_down, other, ls, cs, cr, *scratch):
        self.sources = (up, down)
        self.other, self.ls, self.cs, self.cr = other, ls, cs, cr
        self.up = AlongX(scratch[0], scratch[1], out_up, *scratch[2:4])
        self.down = AlongX(scratch[4], scratch[5], out_down, *scratch[6:8])

    def copies(self, y, c):
        up, down = self.sources
        sibling = at_chip(y, 1 - c)
        for i, (unit, own, theirs) in enumerate(
            ((self.up, up.at[:, c], up.at[:, 1 - c]), (self.down, down.at[c], down.at[1 - c]))
        ):
            keep = pltpu.make_async_copy(own, unit.blocks.at[:, 0], self.ls.at[i])
            swap = remote(theirs, self.other.at[:, i], self.cs.at[i], self.cr.at[i], sibling)
            yield unit, keep, swap

    def begin(self, y, c):
        for unit, keep, swap in self.copies(y, c):
            swap.start()
            keep.start()

    def middle(self, y, c):
        for at, (unit, keep, swap) in enumerate(self.copies(y, c)):
            keep.wait()
            swap.wait()

            def add(i, carry, unit=unit, at=at):
                unit.blocks[i, 0] = (unit.blocks[i, 0].astype(F32) + self.other[i, at].astype(F32)).astype(BF)
                return carry

            lax.fori_loop(0, 4, add, 0)
            unit.start()


FEED_SCRATCH = [pltpu.VMEM((4, 2, 136, D), BF), DMA((2,)), DMA((2,)), DMA((2,))] + x_scratch(1, D) * 2


class AttendReduce:
    def __init__(self, wide, rows, out, other_w, other_r, cs, cr, *scratch):
        self.wide, self.rows = wide, rows
        self.other_w, self.other_r = other_w, other_r
        self.cs, self.cr = cs, cr
        self.along = AlongX(scratch[0], scratch[1], out, scratch[2], scratch[3])
        self.blocks = scratch[0]

    def swaps(self, y, c):
        sibling = at_chip(y, 1 - c)
        return [
            remote(self.wide.at[:, 1 - c], self.other_w, self.cs.at[0], self.cr.at[0], sibling),
            remote(self.rows.at[1 - c], self.other_r, self.cs.at[1], self.cr.at[1], sibling),
        ]

    def begin(self, y, c):
        for copy in self.swaps(y, c):
            copy.start()

    def middle(self, y, c):
        for copy in self.swaps(y, c):
            copy.wait()
        blocks = self.blocks
        for i in range(4):
            block = self.wide[i, c].astype(F32) + self.other_w[i].astype(F32)
            blocks[i, 0] = block[:, :640].astype(BF)
            blocks[i, 1, :, :320] = block[:, 640:].astype(BF)
            chunk = self.rows[c, :, 256 * i : 256 * i + 256].astype(F32) + self.other_r[:, 256 * i : 256 * i + 256].astype(F32)
            blocks[i, 1, :, 320:576] = chunk.astype(BF)
            if i < 3:
                blocks[i, 1, :, 576:] = jnp.zeros((136, HD), BF)
        chunk = self.rows[c, :, 1024:].astype(F32) + self.other_r[:, 1024:].astype(F32)
        blocks[3, 1, :, 576:] = chunk.astype(BF)
        self.along.start()

    def finish(self):
        self.along.finish()


ATTEND_SCRATCH = [
    pltpu.VMEM((4, 136, TQKV), BF),
    pltpu.VMEM((136, D), BF),
    DMA((2,)),
    DMA((2,)),
] + x_scratch(2, 640)


BLOCKS = [pltpu.VMEM((4, 2, 136, TQKV), BF), pltpu.VMEM((2, 136, D), BF)]


class Hooks:
    def __init__(self, begin=(), middle=(), late=(), ready=()):
        self.steps = begin, middle, late, ready

    def begin(self, y, c):
        for step in self.steps[0]:
            step(y, c)

    def middle(self, y, c):
        for step in self.steps[1]:
            step(y, c)

    def late(self):
        for step in self.steps[2]:
            step()

    def ready(self, y, c):
        for step in self.steps[3]:
            step(y, c)

    def finish(self):
        pass


def split(refs, *counts):
    parts, at = [], 0
    for count in counts:
        parts.append(refs[at : at + count])
        at += count
    assert at == len(refs)
    return parts


def attend_forward_first(x, w_hbm, wo_hbm, vecs, part, *refs):
    kept, (wu,), own, (hold, ls, zs, zr, cs, cr) = split(refs, 7, 1, 2 + len(MOVE) + 2, 6)
    y, c = place()
    s, _, h, me = plane()
    sibling = at_chip(y, 1 - c)
    near, far = z_peers(s, h)[:2]
    arrived = greet([at_chip(ring(y, k), c) for k in (1, 2, 3)] + [sibling, near, far])
    bring = pltpu.make_async_copy(part, hold, ls.at[0])
    bring.start()

    def along_z(layer):
        return [
            remote(hold.at[0:2], wu.at[layer, 0:2, c], zs.at[0], zr.at[0], near),
            remote(hold.at[2:4], wu.at[layer, 2:4, c], zs.at[1], zr.at[1], far),
        ]

    def across(layer, i, core):
        rows = wu.at[layer, :, core]
        return remote(hold if i == 0 else rows, rows, cs.at[i], cr.at[i], sibling)

    keep = pltpu.make_async_copy(hold, wu.at[s, :, c], ls.at[1])

    def begin(y, c):
        bring.wait()
        keep.start()
        for copy in along_z(s):
            copy.start()
        across(s, 0, c).start()

    def late():
        for copy in along_z(1 - s):
            copy.wait_recv()
        across(1 - s, 1, c).start()

    attend_forward(0, x.at[s, 0], w_hbm, wo_hbm, vecs, *kept, *own, arrived, hooks=Hooks(begin=[begin], late=[late]))
    across(s, 0, 1 - c).wait_recv()
    across(1 - s, 1, 1 - c).wait_recv()
    for copy in along_z(s):
        copy.wait_send()
    across(s, 0, c).wait_send()
    across(1 - s, 1, c).wait_send()
    keep.wait()


class Loaded:
    def wait(self):
        pass


def forward_rest(middle_0, wu_hbm, wd_hbm, w_hbm, wo_hbm, vecs_0, vecs_1, cotangent, *refs):
    f0_out, a_out, result_1, back_out, f0_scr, a_scr, f1_kept, f1_scr, b_scr, loads = split(
        refs, 4, 7, 1, 4, 2 + len(FEED_MOVE), 2 + len(MOVE) + 2, 3, 2 + len(FEED_MOVE), 2 + len(MOVE), 1
    )
    y, c = place()
    arrived = greet([at_chip(ring(y, k), c) for k in (1, 2, 3)] + [at_chip(y, 1 - c)])
    weights_0 = load([(wu_hbm.at[0], f0_scr[0]), (wd_hbm.at[0], f0_scr[1])], loads[0].at[0])
    weights_a = load([(w_hbm.at[1], a_scr[0])] + out_rows(wo_hbm, a_scr[1], 1, y), a_scr[5])
    weights_1 = load([(wu_hbm.at[1], f1_scr[0]), (wd_hbm.at[1], f1_scr[1])], loads[0].at[1])
    grad = cotangent.at[lax.axis_index("section"), 0]
    full, gs, gr = b_scr[0], b_scr[6], b_scr[7]
    slot(full, y)[...] = grad[...]

    def begin():
        arrived()

    result_0 = f0_out[0]
    feed_forward(middle_0, vecs_0, *f0_out, *f0_scr, begin, weights_0)
    gather_start(full, y, c, gs, gr)
    attend_forward(1, result_0, w_hbm, wo_hbm, vecs_1, *a_out, *a_scr, lambda: None, weights_a)
    middle_1 = a_out[0]
    normed, hidden, active = f1_kept
    finish = feed_forward(middle_1, vecs_1, result_1[0], normed, hidden, active, *f1_scr, lambda: None, weights_1, True)
    feed_back(1, grad, wu_hbm, wd_hbm, vecs_1, middle_1, normed, hidden, active, *back_out,
              f1_scr[0], f1_scr[1], *b_scr, lambda: None, Hooks(late=[finish]), [Loaded(), Loaded()], True)


def backward_middle(*refs):
    a_in, updown, f_in, a_out, half_u, f_out, half_a, a_scr, u_scr, f_scr, grads, w_scr = split(
        refs, 11, 2, 7, 3, 2, 4, 1, len(ATTEND_OWN), len(FEED_SCRATCH), len(FEED_OWN), 2, len(ATTEND_SCRATCH)
    )
    y, c = place()
    s, x, h, me = plane()
    arrived = greet([at_chip(ring(y, k), c) for k in (1, 2, 3)] + [at_chip(y, 1 - c)] + x_peers(x, h))
    wu_hbm, wd_hbm, vecs, *kept = f_in
    weights = load([(wu_hbm.at[0], f_scr[0]), (wd_hbm.at[0], f_scr[1])], f_scr[7])
    feed = FeedReduce(*updown, *half_u, *u_scr)
    attend = AttendReduce(*grads, half_a[0], *w_scr)
    grad_x, small, small_bias = a_out
    attend_back(1, *a_in, grad_x, *grads, small, small_bias, *a_scr, arrived,
                Hooks(begin=[feed.begin], middle=[feed.middle], ready=[attend.begin]))
    feed_back(0, grad_x, wu_hbm, wd_hbm, vecs, *kept, *f_out, *f_scr, lambda: None,
              Hooks(middle=[attend.middle], late=[feed.up.finish, feed.down.finish]), weights)
    attend.finish()


def backward_end(*refs):
    a_in, updown, halves, rest, a_out, g_out, a_scr, u_scr, grads, w_scr, z_scr, own, g_scr = split(
        refs, 11, 2, 3, 7, 1, 6, len(ATTEND_OWN), len(FEED_SCRATCH), 2, len(ATTEND_SCRATCH), 18, 11, len(GATHER_OWN)
    )
    y, c = place()
    s, x, h, me = plane()
    sibling = at_chip(y, 1 - c)
    peers = [at_chip(ring(y, k), c) for k in (1, 2, 3)]
    arrived = greet(peers + [sibling] + [at_plane(lax.rem(me + j, 16)) for j in range(1, 16)])
    half_up, half_down, half_a, sum_up, sum_down, sum_a, late_up, late_down, late_a, small, small_bias = own
    (grad_x,) = a_out
    a_in = [*a_in[:4], a_in[4].at[s, 0], *a_in[5:]]
    feed = FeedReduce(*updown, half_up, half_down, *u_scr)
    attend = AttendReduce(*grads, half_a, *w_scr)
    first = [AlongZ(1, half, out, *z_scr[3 * i : 3 * i + 3]) for i, (half, out) in enumerate(zip(halves, (sum_up, sum_down, sum_a)))]
    last = [
        AlongZ(0, half, out, *z_scr[9 + 3 * i : 12 + 3 * i])
        for i, (half, out) in enumerate(zip((half_up, half_down, half_a), (late_up, late_down, late_a)))
    ]

    def start_first(y, c):
        for unit in first:
            unit.start()

    def up_along_z(y, c):
        feed.up.finish()
        last[0].start()

    attend_back(0, *a_in, grad_x, *grads, small, small_bias, *a_scr, arrived,
                Hooks(begin=[feed.begin, start_first], middle=[feed.middle], ready=[attend.begin, up_along_z]))
    gather_pieces(feed, attend, first, last, small, small_bias, *rest, grad_x, *g_out, *g_scr)


def shape(dims, kind):
    return jax.ShapeDtypeStruct(dims, kind)


MOVE = [
    pltpu.VMEM((ROWS, D), F32),
    pltpu.VMEM((3, BLK, D), BF),
    pltpu.VMEM((3, BLK, D), BF),
    DMA((3,)),
    DMA((3,)),
    DMA((3,)),
    DMA((3,)),
    DMA((3,)),
]


def call(body, name, number, outs, ins, scratch, out_specs=None):
    return pl.pallas_call(
        body,
        name=name,
        out_shape=outs,
        in_specs=ins,
        out_specs=out_specs or [VMEM] * len(outs),
        scratch_shapes=scratch,
        cost_estimate=COST,
        compiler_params=pltpu.CompilerParams(collective_id=number, has_side_effects=True, vmem_limit_bytes=LIMIT),
    )


HALF_A, HALF_U = shape((2, 136, 640), BF), shape((1, 136, D), BF)
FEED_OUTS = [shape((BLK, D), F32), shape((D, D), BF), shape((D, D), BF), shape((8, D), F32)]
ATTEND_KEPT = [
    shape((BLK, D), F32),
    shape((ROWS, D), BF),
    shape((ROWS, TH), BF),
    shape((ROWS, 2 * TH), BF),
    shape((ROWS, 2 * TH), BF),
    shape((ROWS, 128), F32),
    shape((ROWS, TH), BF),
]
FEED_KEPT = [shape((ROWS, D), BF), shape((ROWS, D), F32), shape((ROWS, D), BF)]
ATTEND_WEIGHTS = [pltpu.VMEM((D, TQKV), BF), pltpu.VMEM((TH, D), BF)]
FEED_WEIGHTS = [pltpu.VMEM((D, D), BF), pltpu.VMEM((D, D), BF)]
FEED_MOVE = MOVE[:3] + MOVE[4:]


def run_attend_forward(x, w, wo, vecs, part):
    scratch = ATTEND_WEIGHTS + MOVE + [DMA, DMA]
    scratch += [pltpu.VMEM((4, 136, D), BF), DMA((2,)), DMA((2,)), DMA((2,)), DMA((2,)), DMA((2,))]
    outs = ATTEND_KEPT + [shape((2, 4, 2, 136, D), BF)]
    return call(attend_forward_first, "attend_forward_0", 0, outs, [VMEM, ANY, ANY, VMEM, ANY], scratch,
                [VMEM] * 7 + [ANY])(x, w, wo, vecs, part)


def run_forward_rest(middle, wu, wd, wa, wo, vecs, cotangent):
    outs = [shape((BLK, D), BF)] + FEED_KEPT + ATTEND_KEPT + [shape((BLK, D), BF)] + FEED_OUTS
    kept = [pltpu.VMEM(kind.shape, kind.dtype) for kind in FEED_KEPT]
    rows = pltpu.VMEM((ROWS, D), BF)
    scratch = FEED_WEIGHTS + FEED_MOVE + ATTEND_WEIGHTS + MOVE + [DMA, DMA] + kept + FEED_WEIGHTS + FEED_MOVE
    scratch = scratch + [rows, rows] + MOVE + [DMA((2, 2))]
    return call(forward_rest, "forward_rest", 2, outs, [VMEM] + [ANY] * 4 + [VMEM] * 3, scratch)(
        middle, wu, wd, wa, wo, vecs[0], vecs[1], cotangent
    )


FEED_OWN = [
    pltpu.VMEM((D, D), BF),
    pltpu.VMEM((D, D), BF),
    pltpu.VMEM((ROWS, D), BF),
    pltpu.VMEM((ROWS, D), BF),
] + MOVE
ATTEND_OWN = [
    pltpu.VMEM((D, TQKV), BF),
    pltpu.VMEM((TH, D), BF),
    pltpu.VMEM((ROWS, D), BF),
    pltpu.VMEM((ROWS, TH), BF),
    pltpu.VMEM((ROWS, TQKV), BF),
    pltpu.VMEM((ROWS, 2 * TH), BF),
    pltpu.VMEM((ROWS, 2 * TH), BF),
    pltpu.VMEM((ROWS, 2 * TH), F32),
    pltpu.VMEM((TH, D), BF),
    pltpu.VMEM((HD, D), BF),
] + MOVE + [DMA, DMA, DMA, DMA]
GATHER_OWN = [
    pltpu.VMEM((BLK, D), BF),
    pltpu.VMEM((BLK, D), BF),
    DMA((2,)),
    DMA((2,)),
    pltpu.VMEM((1, 136, D), BF),
    pltpu.VMEM((2, 136, 640), BF),
    pltpu.VMEM((2, 16, D), F32),
    pltpu.VMEM((2, 16, D), F32),
    pltpu.VMEM((3, 2, 16, D), F32),
    pltpu.VMEM((2, 16, D), BF),
    pltpu.VMEM((15, 16, D), BF),
    DMA((3,)),
    DMA((3,)),
    DMA((3, 4)),
    DMA((3, 4)),
    DMA,
    DMA,
    DMA((3,)),
    DMA((3,)),
    DMA((15,)),
    DMA((15,)),
]
SMALLS = [shape((8, D), F32), shape((8, TQKV), F32)]


def run_backward_middle(attend_args, up, down, feed_args):
    outs = [shape((BLK, D), BF)] + SMALLS + [HALF_U, HALF_U] + FEED_OUTS + [HALF_A]
    ins = [VMEM, ANY, ANY] + [VMEM] * 8 + [ANY] * 4 + [VMEM] * 5
    scratch = ATTEND_OWN + FEED_SCRATCH + FEED_OWN + BLOCKS + ATTEND_SCRATCH
    return call(backward_middle, "backward_middle", 5, outs, ins, scratch)(*attend_args, up, down, *feed_args)


def run_backward_end(attend_args, up, down, halves, rest):
    both = shape((2, BLK, D), BF)
    outs = [shape((BLK, D), BF), shape((4, 1, 136, D), BF), shape((4, 1, 136, D), BF), shape((4, 2, 136, 640), BF)]
    outs += [shape((16, D), F32), both, both]
    ins = [VMEM, ANY, ANY] + [VMEM] * 8 + [ANY] * 2 + [VMEM] * (3 + len(rest))
    units = [pltpu.VMEM((1, 136, D), BF), pltpu.VMEM((1, 136, D), BF), pltpu.VMEM((2, 136, 640), BF)]
    zs = (z_scratch(1, D) + z_scratch(1, D) + z_scratch(2, 640)) * 2
    smalls = [pltpu.VMEM((8, D), F32), pltpu.VMEM((8, TQKV), F32)]
    scratch = ATTEND_OWN + FEED_SCRATCH + BLOCKS + ATTEND_SCRATCH + zs + units * 3 + smalls + GATHER_OWN
    return call(backward_end, "backward_end", 6, outs, ins, scratch)(*attend_args, up, down, *halves, *rest)


def spread(send_a, send_u, send_d, send_o, send_v, wa, wu, wd, wo, wv, hold_a, hold_u, hold_d, hold_o, hold_v, local, ysend, yrecv, zsend, zrecv, csend, crecv):
    s = lax.axis_index("section")
    y, c = place()
    replica = lax.axis_index("replica")
    flipped = replica // 2 * 2 + (1 - replica % 2)
    near = {"section": 1 - s}
    far = {"section": 1 - s, "replica": flipped}
    sibling = at_chip(y, 1 - c)
    peers = [at_chip(ring(y, k), c) for k in (1, 2, 3)]
    arrived = greet(peers + [sibling, near, far])
    brought = load(
        [(send_a.at[y], hold_a), (send_u.at[y], hold_u), (send_d, hold_d), (send_o, hold_o), (send_v, hold_v)], local.at[0]
    )
    for copy in brought:
        copy.wait()
    keeps = load(
        [
            (hold_a, wa.at[s, y, c]),
            (hold_u, wu.at[y]),
            (hold_d, wd.at[s, c]),
            (hold_o, wo.at[s, c]),
            (hold_v, wv.at[s, y, c]),
        ],
        local.at[1],
    )
    arrived()

    def along_y(k, back):
        target = ring(y, k)
        place_in = ring(y, 4 - k) if back else y
        return [
            remote(send_v, wv.at[s, place_in, c], ysend.at[0, k - 1], yrecv.at[0, k - 1], at_chip(target, c)),
            remote(send_a.at[target], wa.at[s, place_in, c], ysend.at[1, k - 1], yrecv.at[1, k - 1], at_chip(target, c)),
            remote(send_u.at[target], wu.at[place_in], ysend.at[2, k - 1], yrecv.at[2, k - 1], at_chip(target, c)),
        ]

    def along_z(layer):
        return [
            remote(wv.at[layer, :, c], wv.at[layer, :, c], zsend.at[0], zrecv.at[0], near),
            remote(wa.at[layer, 0:2, c], wa.at[layer, 0:2, c], zsend.at[1], zrecv.at[1], near),
            remote(wa.at[layer, 2:4, c], wa.at[layer, 2:4, c], zsend.at[2], zrecv.at[2], far),
            remote(wo.at[layer, c], wo.at[layer, c], zsend.at[3], zrecv.at[3], far),
            remote(wd.at[layer, c, 0:272], wd.at[layer, c, 0:272], zsend.at[4], zrecv.at[4], near),
            remote(wd.at[layer, c, 272:544], wd.at[layer, c, 272:544], zsend.at[5], zrecv.at[5], far),
        ]

    def across(layer, i, core):
        return [
            remote(wv.at[layer, :, core], wv.at[layer, :, core], csend.at[i, 0], crecv.at[i, 0], sibling),
            remote(wa.at[layer, :, core], wa.at[layer, :, core], csend.at[i, 1], crecv.at[i, 1], sibling),
            remote(wo.at[layer, core], wo.at[layer, core], csend.at[i, 2], crecv.at[i, 2], sibling),
            remote(wd.at[layer, core], wd.at[layer, core], csend.at[i, 3], crecv.at[i, 3], sibling),
        ]

    sent_y = [along_y(k, False) for k in (1, 2, 3)]
    got_y = [along_y(k, True) for k in (1, 2, 3)]
    sent_z, got_z = along_z(s), along_z(1 - s)
    sent_c = [across(s, 0, c), across(1 - s, 1, c)]
    got_c = [across(s, 0, 1 - c), across(1 - s, 1, 1 - c)]
    for kind in (0, 1):
        for k in (1, 0, 2):
            sent_y[k][kind].start()
    keeps[3].wait()
    sent_z[3].start()
    sent_c[0][2].start()
    keeps[2].wait()
    sent_z[4].start()
    sent_z[5].start()
    sent_c[0][3].start()
    for kind, keep, zs, cross in ((0, 4, (0,), 0), (1, 0, (1, 2), 1)):
        keeps[keep].wait()
        for k in range(3):
            got_y[k][kind].wait_recv()
        for z in zs:
            sent_z[z].start()
        sent_c[0][cross].start()
    for k in (1, 0, 2):
        sent_y[k][2].start()
    for zs, cross in (((3,), 2), ((4, 5), 3), ((0,), 0), ((1, 2), 1)):
        for z in zs:
            got_z[z].wait_recv()
        sent_c[1][cross].start()
    keeps[1].wait()
    for k in range(3):
        got_y[k][2].wait_recv()
    for i in range(2):
        for cross in range(4):
            got_c[i][cross].wait_recv()
    for k in range(3):
        for kind in range(3):
            sent_y[k][kind].wait_send()
    for z in range(6):
        sent_z[z].wait_send()
    for i in range(2):
        for cross in range(4):
            sent_c[i][cross].wait_send()


def run_spread(a, u, d, o, v):
    outs = [
        shape((2, 4, 2, 136, TQKV), BF),
        shape((4, 136, D), BF),
        shape((2, 2, 544, D), BF),
        shape((2, 2, 192, D), BF),
        shape((2, 4, 2, 16, D), BF),
    ]
    return pl.pallas_call(
        spread,
        name="spread",
        out_shape=outs,
        in_specs=[ANY] * 5,
        out_specs=[ANY] * 5,
        scratch_shapes=[
            pltpu.VMEM((136, TQKV), BF),
            pltpu.VMEM((136, D), BF),
            pltpu.VMEM((544, D), BF),
            pltpu.VMEM((192, D), BF),
            pltpu.VMEM((16, D), BF),
            DMA((2, 5)), DMA((3, 3)), DMA((3, 3)), DMA((6,)), DMA((6,)), DMA((2, 4)), DMA((2, 4)),
        ],
        compiler_params=pltpu.CompilerParams(collective_id=8, has_side_effects=True),
    )(a, u, d, o, v)


def build_small(buf, one, two, heads, y):
    buf[...] = jnp.zeros_like(buf)
    buf[0:2] = one[0:2]
    buf[2:4] = two[0:2]
    buf[4:5] = one[2:3]
    buf[5:6] = two[3:4]
    buf[6:10] = chip_row(y, two[2:3])
    for row, at in ((10, 2 * TH), (11, TH)):
        buf[row : row + 1, pl.ds(pl.multiple_of(256 * y, 256), 256)] = heads[0:1, at : at + 256]

        @pl.when(y == 3)
        def _(row=row, at=at):
            buf[row : row + 1, 1024:D] = heads[0:1, at + 256 : at + TH]


class Gather:
    def __init__(self, unit, moved, keep_from, out, ts, tr, gs, gr):
        self.unit, self.moved, self.out, self.keep_from = unit, moved, out, keep_from
        self.ts, self.tr, self.gs, self.gr = ts, tr, gs, gr

    def transpose(self):
        y, c = place()
        s, x, h, me = plane()
        return remote(self.unit, self.moved, self.ts, self.tr, at_chip(block_of(x, y), c))

    def elsewhere(self):
        y, c = place()
        s, x, h, me = plane()
        return block_of(x, y) != y

    def start(self):
        pl.when(self.elsewhere())(self.transpose().start)

    def arrive(self):
        @pl.when(self.elsewhere())
        def _():
            self.transpose().wait()
            self.unit[0] = self.moved[0]
            if self.keep_from:
                lane = lax.broadcasted_iota(jnp.int32, self.unit.shape[1:], 1)
                merged = jnp.where(lane < self.keep_from, self.moved[1].astype(F32), self.unit[1].astype(F32))
                self.unit[1] = merged.astype(BF)

    def copies(self):
        y, c = place()
        s, x, h, me = plane()
        targets = x_peers(x, h)
        for k in (1, 3):
            yield remote(self.unit, self.out.at[block_of(x, y)], self.gs.at[k], self.gr.at[k], targets[k - 1])

    def half(self, x, second):
        y, c = place()
        block = self.out.at[block_of(x, y)]
        if self.unit.shape[0] == 2:
            return block.at[1] if second else block.at[0]
        return block.at[0, :, 512:] if second else block.at[0, :, 0:512]

    def arrivals(self):
        s, x, h, me = plane()
        targets = x_peers(x, h)
        y, c = place()
        for k in (1, 3):
            place_in = self.out.at[block_of(x - k + 4, y)]
            yield remote(place_in, place_in, self.gs.at[k], self.gr.at[k], targets[k - 1])

    def forwards(self):
        s, x, h, me = plane()
        targets = x_peers(x, h)
        for i, k in enumerate((1, 3)):
            part = self.half(x - k + 4, i)
            yield remote(part, part, self.gs.at[2 * i], self.gr.at[2 * i], targets[k - 1])

    def spread(self):
        y, c = place()
        s, x, h, me = plane()
        for copy in self.copies():
            copy.start()
        self.out[block_of(x, y)] = self.unit[...]

    def forward(self):
        for copy in self.arrivals():
            copy.wait_recv()
        for copy in self.forwards():
            copy.start()

    def finish(self):
        s, x, h, me = plane()
        targets = x_peers(x, h)
        for copy in self.copies():
            copy.wait_send()
        for copy in self.forwards():
            copy.wait_send()
        for i, k in enumerate((1, 3)):
            part = self.half(x + 2, i)
            remote(part, part, self.gs.at[2 * i], self.gr.at[2 * i], targets[k - 1]).wait_recv()


def gather_pieces(feed, attend, first, last, one_0, heads_0,
                  two_0, one_1, two_1, heads_1, act_0, act_1, back_1, back_0,
                  out_up, out_down, out_a, out_small, out_act, out_back,
                  swap_act, swap_back, ws, wr, moved_up, moved_a, small, small_c, small_y, small_x, small_z,
                  ts, tr, gs, gr, cs, cr, ys, yr, zs, zr):
    y, c = place()
    s, x, h, me = plane()
    sibling = at_chip(y, 1 - c)
    peers = [at_chip(ring(y, k), c) for k in (1, 2, 3)]
    gathers = [
        Gather(last[i].out, moved, keep, out, ts.at[i], tr.at[i], gs.at[i], gr.at[i])
        for i, (moved, keep, out) in enumerate(((moved_up, 0, out_up), (None, 0, out_down), (moved_a, 320, out_a)))
    ]

    def sum_along_z(i):
        first[i].finish()
        last[i].finish()

        @pl.when(s == 1)
        def _():
            last[i].out[...] = first[i].out[...]

    attend.middle(y, c)
    feed.down.finish()
    last[1].start()
    build_small(small.at[0], one_0, two_0, heads_0, y)
    build_small(small.at[1], one_1, two_1, heads_1, y)
    cross = remote(small, small_c, cs, cr, sibling)
    cross.start()
    swap_act[...] = jnp.where(s == 0, act_1[...].astype(F32), act_0[...].astype(F32)).astype(BF)
    swap_back[...] = jnp.where(s == 0, back_1[...].astype(F32), back_0[...].astype(F32)).astype(BF)
    swaps = [
        remote(swap_act, out_act.at[s], ws.at[0], wr.at[0], {"section": 1 - s}),
        remote(swap_back, out_back.at[s], ws.at[1], wr.at[1], {"section": 1 - s}),
    ]
    out_act[s] = jnp.where(s == 0, act_0[...].astype(F32), act_1[...].astype(F32)).astype(BF)
    out_back[s] = jnp.where(s == 0, back_0[...].astype(F32), back_1[...].astype(F32)).astype(BF)
    cross.wait()
    small[...] = small[...] + small_c[...]
    hops = [remote(small, small_y.at[k - 1], ys.at[k - 1], yr.at[k - 1], peers[k - 1]) for k in (1, 2, 3)]
    for hop in hops:
        hop.start()
    sum_along_z(0)
    gathers[0].start()
    for hop in hops:
        hop.wait()
    small_x[...] = (small[...] + small_y[0] + small_y[1] + small_y[2]).astype(BF)

    def plane_copies():
        for j in range(1, 16):
            q = lax.rem(me + j, 16)
            yield remote(small_x.at[q // 8], small_z.at[15 - j], zs.at[j - 1], zr.at[15 - j], at_plane(q))

    attend.finish()
    last[2].start()
    gathers[0].arrive()
    gathers[0].spread()
    sum_along_z(1)
    gathers[1].spread()
    for copy in plane_copies():
        copy.start()
    gathers[0].forward()
    sum_along_z(2)
    gathers[2].start()
    for swap in swaps:
        swap.start()
    gathers[1].forward()
    gathers[2].arrive()
    gathers[2].spread()
    total = small_x[s].astype(F32)
    for copy in plane_copies():
        copy.wait_send()
    for j in range(15):
        remote(small_x.at[0], small_z.at[j], zs.at[j], zr.at[j], sibling).wait_recv()
        total = total + small_z[j].astype(F32)
    out_small[...] = total
    gathers[2].forward()
    for i, swap in enumerate(swaps):
        swap.wait_send()
        place_in = (out_act, out_back)[i].at[1 - s]
        remote(place_in, place_in, ws.at[i], wr.at[i], {"section": 1 - s}).wait_recv()
    for gather in gathers:
        gather.finish()


def assemble(all_up, all_down, all_a, small, attn, out, up, down, b_attn, b_out, b_up, b_down, gain, shift):
    y, c = place()
    f = 2 * y + c
    for j in range(CHIPS):
        up[:, j * D : (j + 1) * D] = all_up[j, 0].astype(F32)
        down[j * 136 : (j + 1) * 136] = all_down[j, 0].astype(F32)
        first, second = all_a[j, 0].astype(F32), all_a[j, 1].astype(F32)
        parts = ((0, second[:, :TH]), (D, first[:, :TH]), (2 * D, first[:, TH:]))
        for base, part in parts:
            attn[:, base + 256 * j : base + 256 * j + 256] = part[:, :256]
        out[:, 256 * j : 256 * j + 256] = second[:, TH : TH + 256]
        if j == CHIPS - 1:
            for base, part in parts:
                attn[:, base + 1024 : base + D] = part[:, 256:]
            out[:, 1024:] = second[:, TH + 256 :]

    def pick(index, options):
        total = jnp.where(index == 0, options[0], 0.0)
        for i, option in enumerate(options[1:], 1):
            total = total + jnp.where(index == i, option, 0.0)
        return total

    for row, ref, place_in in ((0, gain, 0), (1, shift, 0), (2, gain, 1), (3, shift, 1), (4, b_out, 0), (5, b_down, 0)):
        ref[place_in : place_in + 1] = pick(f, [small[row : row + 1, 136 * i : 136 * i + 136] for i in range(8)])
    b_up[...] = pick(f, [small[6 + i // 2 : 7 + i // 2, 544 * (i % 2) : 544 * (i % 2) + 544] for i in range(8)])
    b_attn[...] = pick(f, [small[10 + i // 4 : 11 + i // 4, 272 * (i % 4) : 272 * (i % 4) + 272] for i in range(8)])


def run_assemble(*gathered):
    sizes = [(136, 3 * D), (136, D), (136, FF), (544, D), (1, 272), (1, 136), (1, 544), (1, 136), (2, 136), (2, 136)]
    return pl.pallas_call(
        assemble,
        name="assemble",
        out_shape=[shape(dims, F32) for dims in sizes],
        in_specs=[VMEM] * 4,
        out_specs=[VMEM] * len(sizes),
        compiler_params=pltpu.CompilerParams(vmem_limit_bytes=LIMIT),
    )(*gathered)


def split_heads(block):
    zero = jnp.zeros(block.shape[:-1] + (HD,), block.dtype)
    return [
        jnp.concatenate([block[..., 256 * j : 256 * j + 256], block[..., 1024:] if j == 3 else zero], axis=-1)
        for j in range(CHIPS)
    ]


def on_device(inputs, cotangent, weight_attn, weight_out, weight_up, weight_down, bias_attn, bias_out, bias_up,
              bias_down, norm_gain, norm_bias):
    s = lax.axis_index("section")
    f = lax.axis_index("fsdp")
    y, c = f // 2, f % 2
    wa = weight_attn[0]
    q_blocks, k_blocks, v_blocks = (split_heads(wa[:, i * D : (i + 1) * D]) for i in range(3))
    send_a = jnp.stack(
        [jnp.concatenate([k_blocks[j], v_blocks[j], q_blocks[j]], axis=-1) for j in range(CHIPS)]
    )
    send_u = jnp.stack([weight_up[0][:, j * D : (j + 1) * D] for j in range(CHIPS)])
    tail = lax.ppermute(weight_out[0, 88:], "fsdp", [(i, (i + 2) % 8) for i in range(8)])
    send_o = jnp.concatenate([weight_out[0], tail, jnp.zeros((8, D), BF)], axis=0)
    vectors = jnp.stack([norm_gain[0, 0], norm_bias[0, 0], norm_gain[0, 1], norm_bias[0, 1], bias_out[0], bias_down[0]])
    send_v = jnp.concatenate(
        [
            lax.dynamic_update_slice(jnp.zeros((6, D), BF), vectors, (0, 136 * f)),
            lax.dynamic_update_slice(jnp.zeros((4, D), BF), bias_up, (y, 544 * c)),
            lax.dynamic_update_slice(jnp.zeros((6, D), BF), bias_attn, (f // 4, 272 * (f % 4))),
        ]
    )
    wa, wu, wd, wo, wv = run_spread(send_a, send_u, weight_down[0], send_o, send_v)
    wa = wa.reshape(2, D, TQKV)
    wd = wd.reshape(2, D, D)
    wo = jnp.concatenate([wo[:, 1, 136:184], wo[:, 0, :136], wo[:, 1, :136]], axis=1)
    vecs = jnp.sum(wv.astype(F32), axis=(1, 2))
    middle_0, *kept_0, wu = run_attend_forward(inputs, wa, wo, vecs[0], wu)
    wu = wu.reshape(2, D, D)
    rest = run_forward_rest(middle_0, wu, wd, wa, wo, vecs, cotangent)
    (x_1, *kept_two_0), (middle_1, *kept_1), (result_1,), (grad_middle, up, down, two_1) = split(rest, 4, 7, 1, 4)
    acts = [x_1, result_1]
    back_1, one_1, heads_1, half_up, half_down, grad_middle, up_0, down_0, two_0, half_a = run_backward_middle(
        (grad_middle, wa, wo, vecs[1], x_1, *kept_1),
        up.reshape(4, 2, 136, D),
        down.reshape(2, 4, 136, D),
        (wu, wd, vecs[0], middle_0, *kept_two_0),
    )
    back_0, all_up, all_down, all_a, small, all_acts, all_grads = run_backward_end(
        (grad_middle, wa, wo, vecs[0], inputs, *kept_0),
        up_0.reshape(4, 2, 136, D),
        down_0.reshape(2, 4, 136, D),
        (half_up, half_down, half_a),
        (two_0, one_1, two_1, heads_1, *acts, back_1),
    )
    attn, out, up, down, b_attn, b_out, b_up, b_down, gain, shift = run_assemble(all_up, all_down, all_a, small)
    return (
        all_acts[None, :, None],
        all_grads[None, :, None],
        attn[None],
        out[None],
        up[None],
        down[None],
        b_attn,
        b_out,
        b_up,
        b_down,
        gain[None],
        shift[None],
    )


def solution(mesh):
    placed = (
        P(None, "replica", "fsdp", None),
        P(None, "replica", "fsdp", None),
        P("section", "fsdp", None),
        P("section", "fsdp", None),
        P("section", "fsdp", None),
        P("section", "fsdp", None),
        P("section", "fsdp"),
        P("section", "fsdp"),
        P("section", "fsdp"),
        P("section", "fsdp"),
        P("section", None, "fsdp"),
        P("section", None, "fsdp"),
    )
    return jax.shard_map(
        on_device,
        mesh=mesh,
        in_specs=placed,
        out_specs=(
            P("section", None, "replica", "fsdp", None),
            P("section", None, "replica", "fsdp", None),
        )
        + placed[2:],
        check_vma=False,
    )
```

```python
import functools

import jax
import jax.numpy as jnp
from jax import lax
from jax.experimental import pallas as pl
from jax.experimental.pallas import tpu as pltpu
from jax.sharding import PartitionSpec as P

D = 1088
FF = 4352
HEADS = 17
HD = 64
BLK = 64
CHIPS = 4
ROWS = BLK * CHIPS
SLOTS = 5
TH = SLOTS * HD
TQKV = 3 * TH
SCALE = HD**-0.5
EPS = 1e-5
MESH = pl.DeviceIdType.MESH
BF = jnp.bfloat16
F32 = jnp.float32
ANY = pl.BlockSpec(memory_space=pl.ANY)
VMEM = pl.BlockSpec(memory_space=pltpu.VMEM)
DMA = pltpu.SemaphoreType.DMA
LIMIT = 56 * 1024 * 1024
COST = pl.CostEstimate(flops=10_000_000, bytes_accessed=10_000, transcendentals=0)


def dot(a, b):
    return lax.dot_general(a, b, (((1,), (0,)), ((), ())), preferred_element_type=F32)


def dot_nt(a, b):
    return lax.dot_general(a, b, (((1,), (1,)), ((), ())), preferred_element_type=F32)


def dot_tn(a, b):
    return lax.dot_general(a, b, (((0,), (0,)), ((), ())), preferred_element_type=F32)


def chunks(n, size=256):
    return [(i, min(size, n - i)) for i in range(0, n, size)]


def place():
    f = lax.axis_index("fsdp")
    return f // 2, f % 2


def ring(y, k):
    return lax.rem(y + k, CHIPS)


def at_chip(y, c):
    return {"fsdp": 2 * y + c}


def greet(targets):
    barrier = pltpu.get_barrier_semaphore()
    for target in targets:
        pl.semaphore_signal(barrier, inc=1, device_id=target, device_id_type=MESH)
    return functools.partial(pl.semaphore_wait, barrier, len(targets))


def remote(src, dst, send, recv, target):
    return pltpu.make_async_remote_copy(
        src_ref=src, dst_ref=dst, send_sem=send, recv_sem=recv, device_id=target, device_id_type=MESH
    )


def slot(ref, y):
    return ref.at[pl.ds(pl.multiple_of(y * BLK, BLK), BLK)]


ORDER = (2, 1, 3)


def gather_start(full, y, c, send, recv):
    for k in ORDER:
        remote(slot(full, y), slot(full, y), send.at[k - 1], recv.at[k - 1], at_chip(ring(y, k), c)).start()


def gather_wait(full, y, c, send, recv):
    for k in (1, 3, 2):
        source = ring(y, 4 - k)
        remote(slot(full, source), slot(full, source), send.at[k - 1], recv.at[k - 1], at_chip(ring(y, k), c)).wait()


def scatter_start(acc, out_buf, in_buf, y, c, send, recv):
    for k in ORDER:
        target = ring(y, k)
        out_buf[k - 1] = slot(acc, target)[...].astype(BF)
        remote(out_buf.at[k - 1], in_buf.at[k - 1], send.at[k - 1], recv.at[k - 1], at_chip(target, c)).start()


def scatter_wait(acc, out_buf, in_buf, y, c, send, recv):
    total = slot(acc, y)[...]
    for k in (1, 3, 2):
        remote(out_buf.at[k - 1], in_buf.at[k - 1], send.at[k - 1], recv.at[k - 1], at_chip(ring(y, k), c)).wait()
        total = total + in_buf[k - 1].astype(F32)
    return total


def stats(v):
    centre = v - jnp.mean(v, axis=-1, keepdims=True)
    scale = lax.rsqrt(jnp.mean(centre * centre, axis=-1, keepdims=True) + EPS)
    return centre * scale, scale


def norm(v, gain, shift):
    return stats(v)[0] * gain + shift


def norm_back(d, v, gain):
    vh, scale = stats(v)
    q = d * gain
    grad = scale * (q - jnp.mean(q, axis=-1, keepdims=True) - vh * jnp.mean(q * vh, axis=-1, keepdims=True))
    return grad, jnp.sum(d * vh, axis=0, keepdims=True), jnp.sum(d, axis=0, keepdims=True)


GELU_A = 0.7978845608028654
GELU_B = 0.044715


def gelu(h):
    return 0.5 * h * (1.0 + jnp.tanh(GELU_A * (h + GELU_B * h * h * h)))


def gelu_slope(h):
    t = jnp.tanh(GELU_A * (h + GELU_B * h * h * h))
    return 0.5 * (1.0 + t) + 0.5 * h * (1.0 - t * t) * (GELU_A * (1.0 + 3.0 * GELU_B * h * h))


def masks(c):
    row = lax.broadcasted_iota(jnp.int32, (ROWS, ROWS), 0)
    col = lax.broadcasted_iota(jnp.int32, (ROWS, ROWS), 1)
    own = row >= col
    other = (row // BLK) >= (col // BLK) + (1 - c)
    return own, other


def load(pairs, sems):
    copies = [pltpu.make_async_copy(src, dst, sems.at[i]) for i, (src, dst) in enumerate(pairs)]
    for copy in copies:
        copy.start()
    return copies


def out_rows(wo_hbm, wo, e, y):
    start = pl.multiple_of(48 - 16 * y, 16)
    return [(wo_hbm.at[e, pl.ds(start, 256)], wo.at[0:256]), (wo_hbm.at[e, 256:320], wo.at[256:320])]


def out_wait(weights, wo, y):
    weights[1].wait()
    weights[2].wait()

    @pl.when(y < 3)
    def _():
        wo[256:320] = jnp.zeros((HD, D), BF)


def chip_row(y, rows):
    return jnp.where(lax.broadcasted_iota(jnp.int32, (CHIPS, 1), 0) == y, rows, 0.0)


def head_bias(vecs, row, y):
    last = jnp.where(y == 3, vecs[row : row + 1, 1024:D], 0.0)
    return jnp.concatenate([vecs[row : row + 1, pl.ds(pl.multiple_of(256 * y, 256), 256)], last], axis=-1)


def attend_forward(e, x, w_hbm, wo_hbm, vecs, middle, normed, queries, kv, kv_other, logsum, attended,
                   w, wo, acc, out_buf, in_buf, ls, gs, gr, ss, sr, ks, kr, arrived, weights=None, hooks=None):
    y, c = place()
    sibling = at_chip(y, 1 - c)
    if weights is None:
        weights = load([(w_hbm.at[e], w)] + out_rows(wo_hbm, wo, e, y), ls)
    slot(normed, y)[...] = norm(x[...].astype(F32), vecs[0:1], vecs[1:2]).astype(BF)
    arrived()
    gather_start(normed, y, c, gs, gr)
    if hooks is not None:
        hooks.begin(y, c)
    own, other = masks(c)
    weights[0].wait()
    gather_wait(normed, y, c, gs, gr)
    rows = normed[...]
    bias = jnp.concatenate([jnp.zeros((1, TH), F32), head_bias(vecs, 11, y)], axis=-1)
    for at, size in chunks(2 * TH):
        kv[:, at : at + size] = (dot(rows, w[:, at : at + size]) + bias[:, at : at + size]).astype(BF)
    swap = remote(kv, kv_other, ks, kr, sibling)
    swap.start()
    queries[...] = (dot(rows, w[:, 2 * TH :]) + head_bias(vecs, 10, y)).astype(BF)
    swap.wait()
    for h in range(SLOTS):
        at = h * HD
        q = queries[:, at : at + HD]
        s_own = jnp.where(own, dot_nt(q, kv[:, at : at + HD]) * SCALE, -1e30)
        s_other = jnp.where(other, dot_nt(q, kv_other[:, at : at + HD]) * SCALE, -1e30)
        top = jnp.maximum(jnp.max(s_own, axis=-1, keepdims=True), jnp.max(s_other, axis=-1, keepdims=True))
        e_own = jnp.exp(s_own - top)
        e_other = jnp.exp(s_other - top)
        total = jnp.sum(e_own, axis=-1, keepdims=True) + jnp.sum(e_other, axis=-1, keepdims=True)
        logsum[:, h : h + 1] = top + jnp.log(total)
        inverse = 1.0 / total
        a_own = (e_own * inverse).astype(BF)
        a_other = (e_other * inverse).astype(BF)
        out = dot(a_own, kv[:, TH + at : TH + at + HD]) + dot(a_other, kv_other[:, TH + at : TH + at + HD])
        attended[:, at : at + HD] = out.astype(BF)
    out_wait(weights, wo, y)
    mixed = attended[...]
    for at, size in chunks(D):
        acc[:, at : at + size] = dot(mixed, wo[:, at : at + size])
    scatter_start(acc, out_buf, in_buf, y, c, ss, sr)
    if hooks is not None:
        hooks.late()
    base = x[...].astype(F32) + vecs[4:5]
    middle[...] = base + scatter_wait(acc, out_buf, in_buf, y, c, ss, sr)


def feed_forward(middle, vecs, result, normed, hidden, active,
                 wu, wd, acc, out_buf, in_buf, gs, gr, ss, sr, arrived, weights, defer=False):
    y, c = place()
    slot(normed, y)[...] = norm(middle[...], vecs[2:3], vecs[3:4]).astype(BF)
    arrived()
    gather_start(normed, y, c, gs, gr)
    bias = jnp.sum(chip_row(y, vecs[6:10]), axis=0, keepdims=True)
    weights[0].wait()
    gather_wait(normed, y, c, gs, gr)
    rows = normed[...]
    for at, size in chunks(D):
        h = dot(rows, wu[:, at : at + size]) + bias[:, at : at + size]
        hidden[:, at : at + size] = h
        active[:, at : at + size] = gelu(h).astype(BF)
    weights[1].wait()
    rows = active[...]
    for at, size in chunks(D):
        acc[:, at : at + size] = dot(rows, wd[:, at : at + size])
    scatter_start(acc, out_buf, in_buf, y, c, ss, sr)

    def finish():
        base = middle[...] + vecs[5:6]
        result[...] = (base + scatter_wait(acc, out_buf, in_buf, y, c, ss, sr)).astype(BF)

    if defer:
        return finish
    finish()


def feed_back(e, grad, wu_hbm, wd_hbm, vecs, middle, normed, hidden, active, grad_middle, grad_up, grad_down, small,
              wu, wd, full, gh, acc, out_buf, in_buf, ls, gs, gr, ss, sr, arrived, reduce=None, weights=None, early=False):
    y, c = place()
    if weights is None:
        weights = load([(wu_hbm.at[e], wu), (wd_hbm.at[e], wd)], ls)
    own_rows = grad[...]
    if not early:
        slot(full, y)[...] = own_rows
        arrived()
        gather_start(full, y, c, gs, gr)
    if reduce is not None:
        reduce.begin(y, c)
    small[...] = jnp.zeros_like(small)
    small[3:4] = jnp.sum(own_rows.astype(F32), axis=0, keepdims=True)
    weights[1].wait()
    if reduce is not None:
        reduce.middle(y, c)
    gather_wait(full, y, c, gs, gr)
    rows = full[...]
    for at, size in chunks(D):
        slope = gelu_slope(hidden[:, at : at + size])
        part = (dot_nt(rows, wd[at : at + size, :]) * slope).astype(BF)
        gh[:, at : at + size] = part
        small[2:3, at : at + size] = jnp.sum(part.astype(F32), axis=0, keepdims=True)
    if reduce is not None:
        reduce.relay(y, c)
    weights[0].wait()
    rows = gh[...]
    for at, size in chunks(D):
        acc[:, at : at + size] = dot_nt(rows, wu[at : at + size, :])
    scatter_start(acc, out_buf, in_buf, y, c, ss, sr)
    if reduce is not None:
        reduce.late()
    for at, size in chunks(D):
        grad_up[at : at + size, :] = dot_tn(normed[:, at : at + size], gh[...]).astype(BF)
        grad_down[at : at + size, :] = dot_tn(active[:, at : at + size], full[...]).astype(BF)
    d = scatter_wait(acc, out_buf, in_buf, y, c, ss, sr)
    back, gain, shift = norm_back(d, middle[...], vecs[2:3])
    small[0:1] = gain
    small[1:2] = shift
    grad_middle[...] = grad[...].astype(F32) + back
    if reduce is not None:
        reduce.finish()


def attend_back(e, grad, w_hbm, wo_hbm, vecs, x, normed, queries, kv, kv_other, logsum, attended,
                grad_x, grad_attn, grad_out, small, small_bias,
                w, wo, full, ga, gj, part_out, part_in, part_own, rows_out, edge, acc, out_buf, in_buf, ls, gs, gr, ss, sr, ks, kr, es, er,
                arrived, reduce):
    y, c = place()
    sibling = at_chip(y, 1 - c)
    weights = load([(w_hbm.at[e], w)] + out_rows(wo_hbm, wo, e, y), ls)
    own_rows = grad[...].astype(BF)
    slot(full, y)[...] = own_rows
    arrived()
    gather_start(full, y, c, gs, gr)
    reduce.begin(y, c)
    small[...] = jnp.zeros_like(small)
    small[2:3] = jnp.sum(own_rows.astype(F32), axis=0, keepdims=True)
    own, other = masks(c)
    out_wait(weights, wo, y)
    reduce.middle(y, c)
    gather_wait(full, y, c, gs, gr)
    ga[...] = dot_nt(full[...], wo[...]).astype(BF)
    reduce.relay(y, c)
    for h in range(SLOTS):
        at = h * HD
        q = queries[:, at : at + HD]
        g = ga[:, at : at + HD]
        lse = logsum[:, h : h + 1]
        k_own, k_other = kv[:, at : at + HD], kv_other[:, at : at + HD]
        v_own, v_other = kv[:, TH + at : TH + at + HD], kv_other[:, TH + at : TH + at + HD]
        p_own = jnp.exp(jnp.where(own, dot_nt(q, k_own) * SCALE, -1e30) - lse)
        p_other = jnp.exp(jnp.where(other, dot_nt(q, k_other) * SCALE, -1e30) - lse)
        gp_own = dot_nt(g, v_own)
        gp_other = dot_nt(g, v_other)
        delta = jnp.sum(p_own * gp_own, axis=-1, keepdims=True) + jnp.sum(p_other * gp_other, axis=-1, keepdims=True)
        s_own = (p_own * (gp_own - delta)).astype(BF)
        s_other = (p_other * (gp_other - delta)).astype(BF)
        gj[:, 2 * TH + at : 2 * TH + at + HD] = ((dot(s_own, k_own) + dot(s_other, k_other)) * SCALE).astype(BF)
        part_own[:, at : at + HD] = dot_tn(s_own, q) * SCALE
        part_out[:, at : at + HD] = (dot_tn(s_other, q) * SCALE).astype(BF)
        part_own[:, TH + at : TH + at + HD] = dot_tn(p_own.astype(BF), g)
        part_out[:, TH + at : TH + at + HD] = dot_tn(p_other.astype(BF), g).astype(BF)
    swap = remote(part_out, part_in, ks, kr, sibling)
    swap.start()
    for at, size in chunks(D):
        rows_out[:, at : at + size] = dot_tn(attended[...], full[:, at : at + size]).astype(BF)
    lend = remote(rows_out.at[0:HD], edge, es, er, at_chip(ring(y, 3), c))
    lend.start()
    weights[0].wait()
    swap.wait()
    gj[:, : 2 * TH] = (part_own[...] + part_in[...].astype(F32)).astype(BF)
    rows = gj[...]
    for at, size in chunks(D):
        acc[:, at : at + size] = dot_nt(rows, w[at : at + size, :])
    scatter_start(acc, out_buf, in_buf, y, c, ss, sr)
    for j in range(CHIPS):
        part = dot_tn(normed[:, 272 * j : 272 * j + 272], gj[...])
        grad_attn[j, 0] = part[:136].astype(BF)
        grad_attn[j, 1] = part[136:].astype(BF)
    lend.wait()

    @pl.when(y < 3)
    def _():
        rows_out[256:320] = edge[...]

    chip_rows = rows_out[pl.ds(pl.multiple_of(16 * y, 16), 272)].astype(F32)
    grad_out[0] = chip_rows[:136].astype(BF)
    grad_out[1] = chip_rows[136:].astype(BF)
    reduce.ready(y, c)
    small_bias[...] = jnp.zeros_like(small_bias)
    small_bias[0:1] = jnp.sum(gj[...].astype(F32), axis=0, keepdims=True)
    d = scatter_wait(acc, out_buf, in_buf, y, c, ss, sr)
    back, gain, shift = norm_back(d, x[...].astype(F32), vecs[0:1])
    small[0:1] = gain
    small[1:2] = shift
    grad_x[...] = (grad[...] + back).astype(BF)
    reduce.finish()


def plane():
    s, r = lax.axis_index("section"), lax.axis_index("replica")
    return s, r // 2, r % 2, s * 8 + r


def at_plane(q):
    return {"section": q // 8, "replica": lax.rem(q, 8)}


def x_peers(x, h):
    return [{"replica": 2 * lax.rem(x + k, 4) + h} for k in (1, 2, 3)]


def z_peers(s, h):
    x = lax.axis_index("replica") // 2
    return [
        {"section": 1 - s},
        {"section": 1 - s, "replica": 2 * x + 1 - h},
        {"replica": 2 * x + 1 - h},
    ]


def plane_peers():
    s, x, h, me = plane()
    return x_peers(x, h) + z_peers(s, h)


def block_of(x, y):
    return lax.rem(x - y + 8, 4)


def halves(block, second):
    cut = 512 if block.shape[-1] == D else 384
    return block.at[:, :, cut:] if second else block.at[:, :, 0:cut]


class AlongX:
    def __init__(self, blocks, landing, passing, out, send, recv):
        self.blocks, self.landing, self.passing, self.out = blocks, landing, passing, out
        self.send, self.recv = send, recv

    def parts(self):
        y, c = place()
        s, x, h, me = plane()
        targets = x_peers(x, h)
        ahead, behind = targets[0], targets[2]
        opposite = self.blocks.at[block_of(x + 2, y)]
        to_ahead, to_behind = self.blocks.at[block_of(x + 1, y)], self.blocks.at[block_of(x + 3, y)]
        moves = [
            (halves(opposite, 0), halves(self.passing, 0), ahead),
            (halves(opposite, 1), halves(self.passing, 1), behind),
            (halves(to_ahead, 1), halves(self.landing.at[0], 1), ahead),
            (halves(to_behind, 0), halves(self.landing.at[1], 0), behind),
            (halves(to_ahead, 0), halves(self.landing.at[0], 0), ahead),
            (halves(to_behind, 1), halves(self.landing.at[1], 1), behind),
        ]
        return [remote(source, to, self.send.at[i], self.recv.at[i], target) for i, (source, to, target) in enumerate(moves)]

    def start(self):
        for copy in self.parts()[:4]:
            copy.start()

    def relay(self):
        y, c = place()
        s, x, h, me = plane()
        copies = self.parts()
        for second, step in ((0, 1), (1, 3)):
            copies[second].wait_recv()
            block, passed = halves(self.blocks.at[block_of(x + step, y)], second), halves(self.passing, second)
            block[...] = (block[...].astype(F32) + passed[...].astype(F32)).astype(BF)
            copies[4 + second].start()

    def finish(self):
        y, c = place()
        s, x, h, me = plane()
        own = block_of(x, y)
        copies = self.parts()
        for copy in copies:
            copy.wait_send()
        for copy in copies[2:]:
            copy.wait_recv()

        def add(i, carry):
            rows = pl.ds(pl.multiple_of(8 * i, 8), 8)
            total = self.blocks[own, 0, rows].astype(F32)
            total = total + self.landing[0, 0, rows].astype(F32) + self.landing[1, 0, rows].astype(F32)
            self.out[0, rows] = total.astype(BF)
            return carry

        lax.fori_loop(0, 17, add, 0)


def x_scratch(width):
    return [
        pltpu.VMEM((4, 1, 136, width), BF),
        pltpu.VMEM((2, 1, 136, width), BF),
        pltpu.VMEM((1, 136, width), BF),
        DMA((6,)),
        DMA((6,)),
    ]


class AlongZ:
    def __init__(self, layer, blocks, out, landing, send, recv):
        self.layer, self.blocks, self.landing, self.out, self.send, self.recv = layer, blocks, landing, out, send, recv

    def copies(self):
        s, x, h, me = plane()
        for half in (0, 1):
            owner = 2 * half + self.layer
            rel = lax.rem(2 * h + s - owner + 3, 4)
            target = {"section": jnp.int32(self.layer), "replica": 2 * x + half}
            copy = remote(self.blocks, self.landing.at[rel], self.send.at[half], self.recv.at[rel], target)
            yield 2 * h + s != owner, copy

    def start(self):
        for sends, copy in self.copies():
            pl.when(sends)(copy.start)

    def finish(self):
        s, x, h, me = plane()
        for sends, copy in self.copies():
            pl.when(sends)(copy.wait_send)

        @pl.when(s == self.layer)
        def _():
            for rel in range(3):
                remote(self.blocks, self.landing.at[rel], self.send.at[0], self.recv.at[rel], {"section": 1 - s}).wait_recv()

            def add(i, carry):
                rows = pl.ds(pl.multiple_of(8 * (i % 17), 8), 8)
                total = self.blocks[i // 17, rows].astype(F32)
                for rel in range(3):
                    total = total + self.landing[rel, i // 17, rows].astype(F32)
                self.out[i // 17, rows] = total.astype(BF)
                return carry

            lax.fori_loop(0, 17 * self.out.shape[0], add, 0)


def z_scratch(count, width):
    return [pltpu.VMEM((3, count, 136, width), BF), DMA((2,)), DMA((3,))]


class FeedReduce:
    def __init__(self, up, down, out_up, out_down, other, ls, cs, cr, *scratch):
        self.sources = (up, down)
        self.other, self.ls, self.cs, self.cr = other, ls, cs, cr
        self.up = AlongX(*scratch[0:3], out_up, *scratch[3:5])
        self.down = AlongX(*scratch[5:8], out_down, *scratch[8:10])

    def copies(self, y, c):
        up, down = self.sources
        sibling = at_chip(y, 1 - c)
        for i, (unit, own, theirs) in enumerate(
            ((self.up, up.at[:, c], up.at[:, 1 - c]), (self.down, down.at[c], down.at[1 - c]))
        ):
            keep = pltpu.make_async_copy(own, unit.blocks.at[:, 0], self.ls.at[i])
            swap = remote(theirs, self.other.at[:, i], self.cs.at[i], self.cr.at[i], sibling)
            yield unit, keep, swap

    def begin(self, y, c):
        for unit, keep, swap in self.copies(y, c):
            swap.start()
            keep.start()

    def middle(self, y, c):
        for at, (unit, keep, swap) in enumerate(self.copies(y, c)):
            keep.wait()
            swap.wait()

            def add(i, carry, unit=unit, at=at):
                unit.blocks[i, 0] = (unit.blocks[i, 0].astype(F32) + self.other[i, at].astype(F32)).astype(BF)
                return carry

            lax.fori_loop(0, 4, add, 0)
            unit.start()

    def relay(self, y, c):
        self.up.relay()
        self.down.relay()


FEED_SCRATCH = [pltpu.VMEM((4, 2, 136, D), BF), DMA((2,)), DMA((2,)), DMA((2,))] + x_scratch(D) * 2


class AttendReduce:
    def __init__(self, wide, rows, outs, other_w, other_r, cs, cr, *scratch):
        self.wide, self.rows = wide, rows
        self.other_w, self.other_r = other_w, other_r
        self.cs, self.cr = cs, cr
        self.units = [AlongX(*scratch[0:3], outs[0], *scratch[3:5]), AlongX(*scratch[5:8], outs[1], *scratch[8:10])]

    def swaps(self, y, c):
        sibling = at_chip(y, 1 - c)
        return [
            remote(self.wide.at[:, 1 - c], self.other_w, self.cs.at[0], self.cr.at[0], sibling),
            remote(self.rows.at[1 - c], self.other_r, self.cs.at[1], self.cr.at[1], sibling),
        ]

    def begin(self, y, c):
        for copy in self.swaps(y, c):
            copy.start()

    def middle(self, y, c):
        for copy in self.swaps(y, c):
            copy.wait()
        first, second = (unit.blocks for unit in self.units)
        for i in range(4):
            block = self.wide[i, c].astype(F32) + self.other_w[i].astype(F32)
            first[i, 0] = block[:, :640].astype(BF)
            second[i, 0, :, :320] = block[:, 640:].astype(BF)
        self.units[0].start()
        for i in range(4):
            chunk = self.rows[c, :, 256 * i : 256 * i + 256].astype(F32) + self.other_r[:, 256 * i : 256 * i + 256].astype(F32)
            second[i, 0, :, 320:576] = chunk.astype(BF)
            if i < 3:
                second[i, 0, :, 576:] = jnp.zeros((136, HD), BF)
        chunk = self.rows[c, :, 1024:].astype(F32) + self.other_r[:, 1024:].astype(F32)
        second[3, 0, :, 576:] = chunk.astype(BF)
        self.units[1].start()

    def relay(self, y, c):
        for unit in self.units:
            unit.relay()


ATTEND_SCRATCH = [
    pltpu.VMEM((4, 136, TQKV), BF),
    pltpu.VMEM((136, D), BF),
    DMA((2,)),
    DMA((2,)),
] + x_scratch(640) * 2


BLOCKS = [pltpu.VMEM((4, 2, 136, TQKV), BF), pltpu.VMEM((2, 136, D), BF)]


class Hooks:
    def __init__(self, begin=(), middle=(), late=(), ready=(), relay=()):
        self.steps = begin, middle, late, ready, relay

    def begin(self, y, c):
        for step in self.steps[0]:
            step(y, c)

    def middle(self, y, c):
        for step in self.steps[1]:
            step(y, c)

    def late(self):
        for step in self.steps[2]:
            step()

    def ready(self, y, c):
        for step in self.steps[3]:
            step(y, c)

    def relay(self, y, c):
        for step in self.steps[4]:
            step(y, c)

    def finish(self):
        pass


def split(refs, *counts):
    parts, at = [], 0
    for count in counts:
        parts.append(refs[at : at + count])
        at += count
    assert at == len(refs)
    return parts


def attend_forward_first(x, w_hbm, wo_hbm, vecs, part, *refs):
    kept, (wu,), own, (hold, ls, zs, zr, cs, cr) = split(refs, 7, 1, 2 + len(MOVE) + 2, 6)
    y, c = place()
    s, _, h, me = plane()
    sibling = at_chip(y, 1 - c)
    near, far = z_peers(s, h)[:2]
    arrived = greet([at_chip(ring(y, k), c) for k in (1, 2, 3)] + [sibling, near, far])
    bring = pltpu.make_async_copy(part, hold, ls.at[0])
    bring.start()

    def along_z(layer):
        return [
            remote(hold.at[0:2], wu.at[layer, 0:2, c], zs.at[0], zr.at[0], near),
            remote(hold.at[2:4], wu.at[layer, 2:4, c], zs.at[1], zr.at[1], far),
        ]

    def across(layer, i, core):
        rows = wu.at[layer, :, core]
        return remote(hold if i == 0 else rows, rows, cs.at[i], cr.at[i], sibling)

    keep = pltpu.make_async_copy(hold, wu.at[s, :, c], ls.at[1])

    def begin(y, c):
        bring.wait()
        keep.start()
        for copy in along_z(s):
            copy.start()
        across(s, 0, c).start()

    def late():
        for copy in along_z(1 - s):
            copy.wait_recv()
        across(1 - s, 1, c).start()

    attend_forward(0, x.at[s, 0], w_hbm, wo_hbm, vecs, *kept, *own, arrived, hooks=Hooks(begin=[begin], late=[late]))
    across(s, 0, 1 - c).wait_recv()
    across(1 - s, 1, 1 - c).wait_recv()
    for copy in along_z(s):
        copy.wait_send()
    across(s, 0, c).wait_send()
    across(1 - s, 1, c).wait_send()
    keep.wait()


class Loaded:
    def wait(self):
        pass


def forward_rest(middle_0, wu_hbm, wd_hbm, w_hbm, wo_hbm, vecs_0, vecs_1, cotangent, *refs):
    f0_out, a_out, result_1, back_out, f0_scr, a_scr, f1_kept, f1_scr, b_scr, loads = split(
        refs, 4, 7, 1, 4, 2 + len(FEED_MOVE), 2 + len(MOVE) + 2, 3, 2 + len(FEED_MOVE), 2 + len(MOVE), 1
    )
    y, c = place()
    arrived = greet([at_chip(ring(y, k), c) for k in (1, 2, 3)] + [at_chip(y, 1 - c)])
    weights_0 = load([(wu_hbm.at[0], f0_scr[0]), (wd_hbm.at[0], f0_scr[1])], loads[0].at[0])
    weights_a = load([(w_hbm.at[1], a_scr[0])] + out_rows(wo_hbm, a_scr[1], 1, y), a_scr[5])
    weights_1 = load([(wu_hbm.at[1], f1_scr[0]), (wd_hbm.at[1], f1_scr[1])], loads[0].at[1])
    grad = cotangent.at[lax.axis_index("section"), 0]
    full, gs, gr = b_scr[0], b_scr[6], b_scr[7]
    slot(full, y)[...] = grad[...]

    def begin():
        arrived()

    result_0 = f0_out[0]
    feed_forward(middle_0, vecs_0, *f0_out, *f0_scr, begin, weights_0)
    gather_start(full, y, c, gs, gr)
    attend_forward(1, result_0, w_hbm, wo_hbm, vecs_1, *a_out, *a_scr, lambda: None, weights_a)
    middle_1 = a_out[0]
    normed, hidden, active = f1_kept
    finish = feed_forward(middle_1, vecs_1, result_1[0], normed, hidden, active, *f1_scr, lambda: None, weights_1, True)
    feed_back(1, grad, wu_hbm, wd_hbm, vecs_1, middle_1, normed, hidden, active, *back_out,
              f1_scr[0], f1_scr[1], *b_scr, lambda: None, Hooks(late=[finish]), [Loaded(), Loaded()], True)


def backward_middle(*refs):
    a_in, updown, f_in, a_out, half_u, f_out, half_a, a_scr, u_scr, f_scr, grads, w_scr = split(
        refs, 11, 2, 7, 3, 2, 4, 2, len(ATTEND_OWN), len(FEED_SCRATCH), len(FEED_OWN), 2, len(ATTEND_SCRATCH)
    )
    y, c = place()
    s, x, h, me = plane()
    arrived = greet([at_chip(ring(y, k), c) for k in (1, 2, 3)] + [at_chip(y, 1 - c)] + x_peers(x, h))
    wu_hbm, wd_hbm, vecs, *kept = f_in
    weights = load([(wu_hbm.at[0], f_scr[0]), (wd_hbm.at[0], f_scr[1])], f_scr[7])
    feed = FeedReduce(*updown, *half_u, *u_scr)
    attend = AttendReduce(*grads, half_a, *w_scr)
    grad_x, small, small_bias = a_out
    attend_back(1, *a_in, grad_x, *grads, small, small_bias, *a_scr, arrived,
                Hooks(begin=[feed.begin], middle=[feed.middle], relay=[feed.relay], ready=[attend.begin]))
    feed_back(0, grad_x, wu_hbm, wd_hbm, vecs, *kept, *f_out, *f_scr, lambda: None,
              Hooks(middle=[attend.middle], relay=[attend.relay], late=[feed.up.finish, feed.down.finish]), weights)
    for unit in attend.units:
        unit.finish()


def backward_end(*refs):
    a_in, updown, halves, rest, a_out, g_out, a_scr, u_scr, grads, w_scr, z_scr, own, g_scr = split(
        refs, 11, 2, 4, 7, 1, 7, len(ATTEND_OWN), len(FEED_SCRATCH), 2, len(ATTEND_SCRATCH), 24, 14, len(GATHER_OWN)
    )
    y, c = place()
    s, x, h, me = plane()
    sibling = at_chip(y, 1 - c)
    peers = [at_chip(ring(y, k), c) for k in (1, 2, 3)]
    arrived = greet(peers + [sibling] + [at_plane(lax.rem(me + j, 16)) for j in range(1, 16)])
    mine, sums, lates, (small, small_bias) = split(own, 4, 4, 4, 2)
    (grad_x,) = a_out
    a_in = [*a_in[:4], a_in[4].at[s, 0], *a_in[5:]]
    feed = FeedReduce(*updown, mine[0], mine[1], *u_scr)
    attend = AttendReduce(*grads, mine[2:], *w_scr)
    first = [AlongZ(1, half, out, *z_scr[3 * i : 3 * i + 3]) for i, (half, out) in enumerate(zip(halves, sums))]
    last = [
        AlongZ(0, half, out, *z_scr[12 + 3 * i : 15 + 3 * i])
        for i, (half, out) in enumerate(zip(mine, lates))
    ]

    def start_first(y, c):
        for unit in first:
            unit.start()

    def up_along_z(y, c):
        feed.up.finish()
        last[0].start()

    attend_back(0, *a_in, grad_x, *grads, small, small_bias, *a_scr, arrived,
                Hooks(begin=[feed.begin, start_first], middle=[feed.middle], relay=[feed.relay], ready=[attend.begin, up_along_z]))
    gather_pieces(feed, attend, first, last, small, small_bias, *rest, grad_x, *g_out, *g_scr)


def shape(dims, kind):
    return jax.ShapeDtypeStruct(dims, kind)


MOVE = [
    pltpu.VMEM((ROWS, D), F32),
    pltpu.VMEM((3, BLK, D), BF),
    pltpu.VMEM((3, BLK, D), BF),
    DMA((3,)),
    DMA((3,)),
    DMA((3,)),
    DMA((3,)),
    DMA((3,)),
]


def call(body, name, number, outs, ins, scratch, out_specs=None):
    return pl.pallas_call(
        body,
        name=name,
        out_shape=outs,
        in_specs=ins,
        out_specs=out_specs or [VMEM] * len(outs),
        scratch_shapes=scratch,
        cost_estimate=COST,
        compiler_params=pltpu.CompilerParams(collective_id=number, has_side_effects=True, vmem_limit_bytes=LIMIT),
    )


HALF_A, HALF_U = shape((1, 136, 640), BF), shape((1, 136, D), BF)
FEED_OUTS = [shape((BLK, D), F32), shape((D, D), BF), shape((D, D), BF), shape((8, D), F32)]
ATTEND_KEPT = [
    shape((BLK, D), F32),
    shape((ROWS, D), BF),
    shape((ROWS, TH), BF),
    shape((ROWS, 2 * TH), BF),
    shape((ROWS, 2 * TH), BF),
    shape((ROWS, 128), F32),
    shape((ROWS, TH), BF),
]
FEED_KEPT = [shape((ROWS, D), BF), shape((ROWS, D), F32), shape((ROWS, D), BF)]
ATTEND_WEIGHTS = [pltpu.VMEM((D, TQKV), BF), pltpu.VMEM((TH, D), BF)]
FEED_WEIGHTS = [pltpu.VMEM((D, D), BF), pltpu.VMEM((D, D), BF)]
FEED_MOVE = MOVE[:3] + MOVE[4:]


def run_attend_forward(x, w, wo, vecs, part):
    scratch = ATTEND_WEIGHTS + MOVE + [DMA, DMA]
    scratch += [pltpu.VMEM((4, 136, D), BF), DMA((2,)), DMA((2,)), DMA((2,)), DMA((2,)), DMA((2,))]
    outs = ATTEND_KEPT + [shape((2, 4, 2, 136, D), BF)]
    return call(attend_forward_first, "attend_forward_0", 0, outs, [VMEM, ANY, ANY, VMEM, ANY], scratch,
                [VMEM] * 7 + [ANY])(x, w, wo, vecs, part)


def run_forward_rest(middle, wu, wd, wa, wo, vecs, cotangent):
    outs = [shape((BLK, D), BF)] + FEED_KEPT + ATTEND_KEPT + [shape((BLK, D), BF)] + FEED_OUTS
    kept = [pltpu.VMEM(kind.shape, kind.dtype) for kind in FEED_KEPT]
    rows = pltpu.VMEM((ROWS, D), BF)
    scratch = FEED_WEIGHTS + FEED_MOVE + ATTEND_WEIGHTS + MOVE + [DMA, DMA] + kept + FEED_WEIGHTS + FEED_MOVE
    scratch = scratch + [rows, rows] + MOVE + [DMA((2, 2))]
    return call(forward_rest, "forward_rest", 2, outs, [VMEM] + [ANY] * 4 + [VMEM] * 3, scratch)(
        middle, wu, wd, wa, wo, vecs[0], vecs[1], cotangent
    )


FEED_OWN = [
    pltpu.VMEM((D, D), BF),
    pltpu.VMEM((D, D), BF),
    pltpu.VMEM((ROWS, D), BF),
    pltpu.VMEM((ROWS, D), BF),
] + MOVE
ATTEND_OWN = [
    pltpu.VMEM((D, TQKV), BF),
    pltpu.VMEM((TH, D), BF),
    pltpu.VMEM((ROWS, D), BF),
    pltpu.VMEM((ROWS, TH), BF),
    pltpu.VMEM((ROWS, TQKV), BF),
    pltpu.VMEM((ROWS, 2 * TH), BF),
    pltpu.VMEM((ROWS, 2 * TH), BF),
    pltpu.VMEM((ROWS, 2 * TH), F32),
    pltpu.VMEM((TH, D), BF),
    pltpu.VMEM((HD, D), BF),
] + MOVE + [DMA, DMA, DMA, DMA]
GATHER_OWN = [
    pltpu.VMEM((BLK, D), BF),
    pltpu.VMEM((BLK, D), BF),
    DMA((2,)),
    DMA((2,)),
    pltpu.VMEM((1, 136, D), BF),
    pltpu.VMEM((1, 136, 640), BF),
    pltpu.VMEM((1, 136, 640), BF),
    pltpu.VMEM((2, 16, D), F32),
    pltpu.VMEM((2, 16, D), F32),
    pltpu.VMEM((3, 2, 16, D), F32),
    pltpu.VMEM((2, 16, D), BF),
    pltpu.VMEM((15, 16, D), BF),
    DMA((4,)),
    DMA((4,)),
    DMA((4, 4)),
    DMA((4, 4)),
    DMA,
    DMA,
    DMA((3,)),
    DMA((3,)),
    DMA((15,)),
    DMA((15,)),
]
SMALLS = [shape((8, D), F32), shape((8, TQKV), F32)]


def run_backward_middle(attend_args, up, down, feed_args):
    outs = [shape((BLK, D), BF)] + SMALLS + [HALF_U, HALF_U] + FEED_OUTS + [HALF_A, HALF_A]
    ins = [VMEM, ANY, ANY] + [VMEM] * 8 + [ANY] * 4 + [VMEM] * 5
    scratch = ATTEND_OWN + FEED_SCRATCH + FEED_OWN + BLOCKS + ATTEND_SCRATCH
    return call(backward_middle, "backward_middle", 5, outs, ins, scratch)(*attend_args, up, down, *feed_args)


def run_backward_end(attend_args, up, down, halves, rest):
    both = shape((2, BLK, D), BF)
    outs = [shape((BLK, D), BF), shape((4, 1, 136, D), BF), shape((4, 1, 136, D), BF), shape((4, 1, 136, 640), BF)] + [shape((4, 1, 136, 640), BF)]
    outs += [shape((16, D), F32), both, both]
    ins = [VMEM, ANY, ANY] + [VMEM] * 8 + [ANY] * 2 + [VMEM] * (4 + len(rest))
    units = [pltpu.VMEM((1, 136, D), BF), pltpu.VMEM((1, 136, D), BF)] + [pltpu.VMEM((1, 136, 640), BF)] * 2
    zs = (z_scratch(1, D) + z_scratch(1, D) + z_scratch(1, 640) * 2) * 2
    smalls = [pltpu.VMEM((8, D), F32), pltpu.VMEM((8, TQKV), F32)]
    scratch = ATTEND_OWN + FEED_SCRATCH + BLOCKS + ATTEND_SCRATCH + zs + units * 3 + smalls + GATHER_OWN
    return call(backward_end, "backward_end", 6, outs, ins, scratch)(*attend_args, up, down, *halves, *rest)


def spread(send_a, send_u, send_d, send_o, send_v, wa, wu, wd, wo, wv, hold_a, hold_u, hold_d, hold_o, hold_v, local, ysend, yrecv, zsend, zrecv, csend, crecv):
    s = lax.axis_index("section")
    y, c = place()
    replica = lax.axis_index("replica")
    flipped = replica // 2 * 2 + (1 - replica % 2)
    near = {"section": 1 - s}
    far = {"section": 1 - s, "replica": flipped}
    sibling = at_chip(y, 1 - c)
    peers = [at_chip(ring(y, k), c) for k in (1, 2, 3)]
    arrived = greet(peers + [sibling, near, far])
    brought = load(
        [(send_a.at[y], hold_a), (send_u.at[y], hold_u), (send_d, hold_d), (send_o, hold_o), (send_v, hold_v)], local.at[0]
    )
    for copy in brought:
        copy.wait()
    keeps = load(
        [
            (hold_a, wa.at[s, y, c]),
            (hold_u, wu.at[y]),
            (hold_d, wd.at[s, c]),
            (hold_o, wo.at[s, c]),
            (hold_v, wv.at[s, y, c]),
        ],
        local.at[1],
    )
    arrived()

    def along_y(k, back):
        target = ring(y, k)
        place_in = ring(y, 4 - k) if back else y
        return [
            remote(send_v, wv.at[s, place_in, c], ysend.at[0, k - 1], yrecv.at[0, k - 1], at_chip(target, c)),
            remote(send_a.at[target], wa.at[s, place_in, c], ysend.at[1, k - 1], yrecv.at[1, k - 1], at_chip(target, c)),
            remote(send_u.at[target], wu.at[place_in], ysend.at[2, k - 1], yrecv.at[2, k - 1], at_chip(target, c)),
        ]

    def along_z(layer):
        return [
            remote(wv.at[layer, :, c], wv.at[layer, :, c], zsend.at[0], zrecv.at[0], near),
            remote(wa.at[layer, 0:2, c], wa.at[layer, 0:2, c], zsend.at[1], zrecv.at[1], near),
            remote(wa.at[layer, 2:4, c], wa.at[layer, 2:4, c], zsend.at[2], zrecv.at[2], far),
            remote(wo.at[layer, c], wo.at[layer, c], zsend.at[3], zrecv.at[3], far),
            remote(wd.at[layer, c, 0:272], wd.at[layer, c, 0:272], zsend.at[4], zrecv.at[4], near),
            remote(wd.at[layer, c, 272:544], wd.at[layer, c, 272:544], zsend.at[5], zrecv.at[5], far),
        ]

    def across(layer, i, core):
        return [
            remote(wv.at[layer, :, core], wv.at[layer, :, core], csend.at[i, 0], crecv.at[i, 0], sibling),
            remote(wa.at[layer, :, core], wa.at[layer, :, core], csend.at[i, 1], crecv.at[i, 1], sibling),
            remote(wo.at[layer, core], wo.at[layer, core], csend.at[i, 2], crecv.at[i, 2], sibling),
            remote(wd.at[layer, core], wd.at[layer, core], csend.at[i, 3], crecv.at[i, 3], sibling),
        ]

    sent_y = [along_y(k, False) for k in (1, 2, 3)]
    got_y = [along_y(k, True) for k in (1, 2, 3)]
    sent_z, got_z = along_z(s), along_z(1 - s)
    sent_c = [across(s, 0, c), across(1 - s, 1, c)]
    got_c = [across(s, 0, 1 - c), across(1 - s, 1, 1 - c)]
    for kind in (0, 1):
        for k in (1, 0, 2):
            sent_y[k][kind].start()
    keeps[3].wait()
    sent_z[3].start()
    sent_c[0][2].start()
    keeps[2].wait()
    sent_z[4].start()
    sent_z[5].start()
    sent_c[0][3].start()
    for kind, keep, zs, cross in ((0, 4, (0,), 0), (1, 0, (1, 2), 1)):
        keeps[keep].wait()
        for k in range(3):
            got_y[k][kind].wait_recv()
        for z in zs:
            sent_z[z].start()
        sent_c[0][cross].start()
    for k in (1, 0, 2):
        sent_y[k][2].start()
    for zs, cross in (((3,), 2), ((4, 5), 3), ((0,), 0), ((1, 2), 1)):
        for z in zs:
            got_z[z].wait_recv()
        sent_c[1][cross].start()
    keeps[1].wait()
    for k in range(3):
        got_y[k][2].wait_recv()
    for i in range(2):
        for cross in range(4):
            got_c[i][cross].wait_recv()
    for k in range(3):
        for kind in range(3):
            sent_y[k][kind].wait_send()
    for z in range(6):
        sent_z[z].wait_send()
    for i in range(2):
        for cross in range(4):
            sent_c[i][cross].wait_send()


def run_spread(a, u, d, o, v):
    outs = [
        shape((2, 4, 2, 136, TQKV), BF),
        shape((4, 136, D), BF),
        shape((2, 2, 544, D), BF),
        shape((2, 2, 192, D), BF),
        shape((2, 4, 2, 16, D), BF),
    ]
    return pl.pallas_call(
        spread,
        name="spread",
        out_shape=outs,
        in_specs=[ANY] * 5,
        out_specs=[ANY] * 5,
        scratch_shapes=[
            pltpu.VMEM((136, TQKV), BF),
            pltpu.VMEM((136, D), BF),
            pltpu.VMEM((544, D), BF),
            pltpu.VMEM((192, D), BF),
            pltpu.VMEM((16, D), BF),
            DMA((2, 5)), DMA((3, 3)), DMA((3, 3)), DMA((6,)), DMA((6,)), DMA((2, 4)), DMA((2, 4)),
        ],
        compiler_params=pltpu.CompilerParams(collective_id=8, has_side_effects=True),
    )(a, u, d, o, v)


def build_small(buf, one, two, heads, y):
    buf[...] = jnp.zeros_like(buf)
    buf[0:2] = one[0:2]
    buf[2:4] = two[0:2]
    buf[4:5] = one[2:3]
    buf[5:6] = two[3:4]
    buf[6:10] = chip_row(y, two[2:3])
    for row, at in ((10, 2 * TH), (11, TH)):
        buf[row : row + 1, pl.ds(pl.multiple_of(256 * y, 256), 256)] = heads[0:1, at : at + 256]

        @pl.when(y == 3)
        def _(row=row, at=at):
            buf[row : row + 1, 1024:D] = heads[0:1, at + 256 : at + TH]


class Gather:
    def __init__(self, unit, moved, keep_from, out, ts, tr, gs, gr):
        self.unit, self.moved, self.out, self.keep_from = unit, moved, out, keep_from
        self.ts, self.tr, self.gs, self.gr = ts, tr, gs, gr

    def transpose(self):
        y, c = place()
        s, x, h, me = plane()
        return remote(self.unit, self.moved, self.ts, self.tr, at_chip(block_of(x, y), c))

    def elsewhere(self):
        y, c = place()
        s, x, h, me = plane()
        return block_of(x, y) != y

    def start(self):
        pl.when(self.elsewhere())(self.transpose().start)

    def arrive(self):
        @pl.when(self.elsewhere())
        def _():
            self.transpose().wait()
            if self.keep_from:
                lane = lax.broadcasted_iota(jnp.int32, self.unit.shape[1:], 1)
                merged = jnp.where(lane < self.keep_from, self.moved[0].astype(F32), self.unit[0].astype(F32))
                self.unit[0] = merged.astype(BF)
            else:
                self.unit[0] = self.moved[0]

    def copies(self):
        y, c = place()
        s, x, h, me = plane()
        targets = x_peers(x, h)
        for k in (1, 3):
            yield remote(self.unit, self.out.at[block_of(x, y)], self.gs.at[k], self.gr.at[k], targets[k - 1])

    def half(self, x, second):
        y, c = place()
        return halves(self.out.at[block_of(x, y)], second)

    def arrivals(self):
        s, x, h, me = plane()
        targets = x_peers(x, h)
        y, c = place()
        for k in (1, 3):
            place_in = self.out.at[block_of(x - k + 4, y)]
            yield remote(place_in, place_in, self.gs.at[k], self.gr.at[k], targets[k - 1])

    def forwards(self):
        s, x, h, me = plane()
        targets = x_peers(x, h)
        for i, k in enumerate((1, 3)):
            part = self.half(x - k + 4, i)
            yield remote(part, part, self.gs.at[2 * i], self.gr.at[2 * i], targets[k - 1])

    def spread(self):
        y, c = place()
        s, x, h, me = plane()
        for copy in self.copies():
            copy.start()
        self.out[block_of(x, y)] = self.unit[...]

    def forward(self):
        for copy in self.arrivals():
            copy.wait_recv()
        for copy in self.forwards():
            copy.start()

    def finish(self):
        s, x, h, me = plane()
        targets = x_peers(x, h)
        for copy in self.copies():
            copy.wait_send()
        for copy in self.forwards():
            copy.wait_send()
        for i, k in enumerate((1, 3)):
            part = self.half(x + 2, i)
            remote(part, part, self.gs.at[2 * i], self.gr.at[2 * i], targets[k - 1]).wait_recv()


def gather_pieces(feed, attend, first, last, one_0, heads_0,
                  two_0, one_1, two_1, heads_1, act_0, act_1, back_1, back_0,
                  out_up, out_down, out_a, out_b, out_small, out_act, out_back,
                  swap_act, swap_back, ws, wr, moved_up, moved_a, moved_b, small, small_c, small_y, small_x, small_z,
                  ts, tr, gs, gr, cs, cr, ys, yr, zs, zr):
    y, c = place()
    s, x, h, me = plane()
    sibling = at_chip(y, 1 - c)
    peers = [at_chip(ring(y, k), c) for k in (1, 2, 3)]
    gathers = [
        Gather(last[i].out, moved, keep, out, ts.at[i], tr.at[i], gs.at[i], gr.at[i])
        for i, (moved, keep, out) in enumerate(((moved_up, 0, out_up), (None, 0, out_down), (moved_a, 0, out_a), (moved_b, 320, out_b)))
    ]

    def sum_along_z(i):
        first[i].finish()
        last[i].finish()

        @pl.when(s == 1)
        def _():
            last[i].out[...] = first[i].out[...]

    attend.middle(y, c)
    feed.down.finish()
    last[1].start()
    attend.relay(y, c)
    build_small(small.at[0], one_0, two_0, heads_0, y)
    build_small(small.at[1], one_1, two_1, heads_1, y)
    cross = remote(small, small_c, cs, cr, sibling)
    cross.start()
    swap_act[...] = jnp.where(s == 0, act_1[...].astype(F32), act_0[...].astype(F32)).astype(BF)
    swap_back[...] = jnp.where(s == 0, back_1[...].astype(F32), back_0[...].astype(F32)).astype(BF)
    swaps = [
        remote(swap_act, out_act.at[s], ws.at[0], wr.at[0], {"section": 1 - s}),
        remote(swap_back, out_back.at[s], ws.at[1], wr.at[1], {"section": 1 - s}),
    ]
    out_act[s] = jnp.where(s == 0, act_0[...].astype(F32), act_1[...].astype(F32)).astype(BF)
    out_back[s] = jnp.where(s == 0, back_0[...].astype(F32), back_1[...].astype(F32)).astype(BF)
    cross.wait()
    small[...] = small[...] + small_c[...]
    hops = [remote(small, small_y.at[k - 1], ys.at[k - 1], yr.at[k - 1], peers[k - 1]) for k in (1, 2, 3)]
    for hop in hops:
        hop.start()
    sum_along_z(0)
    gathers[0].start()
    for hop in hops:
        hop.wait()
    small_x[...] = (small[...] + small_y[0] + small_y[1] + small_y[2]).astype(BF)

    def plane_copies():
        for j in range(1, 16):
            q = lax.rem(me + j, 16)
            yield remote(small_x.at[q // 8], small_z.at[15 - j], zs.at[j - 1], zr.at[15 - j], at_plane(q))

    attend.units[0].finish()
    last[2].start()
    gathers[0].arrive()
    gathers[0].spread()
    attend.units[1].finish()
    last[3].start()
    sum_along_z(1)
    gathers[1].spread()
    for copy in plane_copies():
        copy.start()
    gathers[0].forward()
    sum_along_z(2)
    gathers[2].start()
    gathers[1].forward()
    for swap in swaps:
        swap.start()
    gathers[2].arrive()
    gathers[2].spread()
    sum_along_z(3)
    gathers[3].start()
    gathers[2].forward()
    gathers[3].arrive()
    gathers[3].spread()
    total = small_x[s].astype(F32)
    for copy in plane_copies():
        copy.wait_send()
    for j in range(15):
        remote(small_x.at[0], small_z.at[j], zs.at[j], zr.at[j], sibling).wait_recv()
        total = total + small_z[j].astype(F32)
    out_small[...] = total
    gathers[3].forward()
    for i, swap in enumerate(swaps):
        swap.wait_send()
        place_in = (out_act, out_back)[i].at[1 - s]
        remote(place_in, place_in, ws.at[i], wr.at[i], {"section": 1 - s}).wait_recv()
    for gather in gathers:
        gather.finish()


def assemble(all_up, all_down, all_a, all_b, small, attn, out, up, down, b_attn, b_out, b_up, b_down, gain, shift):
    y, c = place()
    f = 2 * y + c
    for j in range(CHIPS):
        up[:, j * D : (j + 1) * D] = all_up[j, 0].astype(F32)
        down[j * 136 : (j + 1) * 136] = all_down[j, 0].astype(F32)
        first, second = all_a[j, 0].astype(F32), all_b[j, 0].astype(F32)
        parts = ((0, second[:, :TH]), (D, first[:, :TH]), (2 * D, first[:, TH:]))
        for base, part in parts:
            attn[:, base + 256 * j : base + 256 * j + 256] = part[:, :256]
        out[:, 256 * j : 256 * j + 256] = second[:, TH : TH + 256]
        if j == CHIPS - 1:
            for base, part in parts:
                attn[:, base + 1024 : base + D] = part[:, 256:]
            out[:, 1024:] = second[:, TH + 256 :]

    def pick(index, options):
        total = jnp.where(index == 0, options[0], 0.0)
        for i, option in enumerate(options[1:], 1):
            total = total + jnp.where(index == i, option, 0.0)
        return total

    for row, ref, place_in in ((0, gain, 0), (1, shift, 0), (2, gain, 1), (3, shift, 1), (4, b_out, 0), (5, b_down, 0)):
        ref[place_in : place_in + 1] = pick(f, [small[row : row + 1, 136 * i : 136 * i + 136] for i in range(8)])
    b_up[...] = pick(f, [small[6 + i // 2 : 7 + i // 2, 544 * (i % 2) : 544 * (i % 2) + 544] for i in range(8)])
    b_attn[...] = pick(f, [small[10 + i // 4 : 11 + i // 4, 272 * (i % 4) : 272 * (i % 4) + 272] for i in range(8)])


def run_assemble(*gathered):
    sizes = [(136, 3 * D), (136, D), (136, FF), (544, D), (1, 272), (1, 136), (1, 544), (1, 136), (2, 136), (2, 136)]
    return pl.pallas_call(
        assemble,
        name="assemble",
        out_shape=[shape(dims, F32) for dims in sizes],
        in_specs=[VMEM] * 5,
        out_specs=[VMEM] * len(sizes),
        compiler_params=pltpu.CompilerParams(vmem_limit_bytes=LIMIT),
    )(*gathered)


def split_heads(block):
    zero = jnp.zeros(block.shape[:-1] + (HD,), block.dtype)
    return [
        jnp.concatenate([block[..., 256 * j : 256 * j + 256], block[..., 1024:] if j == 3 else zero], axis=-1)
        for j in range(CHIPS)
    ]


def on_device(inputs, cotangent, weight_attn, weight_out, weight_up, weight_down, bias_attn, bias_out, bias_up,
              bias_down, norm_gain, norm_bias):
    s = lax.axis_index("section")
    f = lax.axis_index("fsdp")
    y, c = f // 2, f % 2
    wa = weight_attn[0]
    q_blocks, k_blocks, v_blocks = (split_heads(wa[:, i * D : (i + 1) * D]) for i in range(3))
    send_a = jnp.stack(
        [jnp.concatenate([k_blocks[j], v_blocks[j], q_blocks[j]], axis=-1) for j in range(CHIPS)]
    )
    send_u = jnp.stack([weight_up[0][:, j * D : (j + 1) * D] for j in range(CHIPS)])
    tail = lax.ppermute(weight_out[0, 88:], "fsdp", [(i, (i + 2) % 8) for i in range(8)])
    send_o = jnp.concatenate([weight_out[0], tail, jnp.zeros((8, D), BF)], axis=0)
    vectors = jnp.stack([norm_gain[0, 0], norm_bias[0, 0], norm_gain[0, 1], norm_bias[0, 1], bias_out[0], bias_down[0]])
    send_v = jnp.concatenate(
        [
            lax.dynamic_update_slice(jnp.zeros((6, D), BF), vectors, (0, 136 * f)),
            lax.dynamic_update_slice(jnp.zeros((4, D), BF), bias_up, (y, 544 * c)),
            lax.dynamic_update_slice(jnp.zeros((6, D), BF), bias_attn, (f // 4, 272 * (f % 4))),
        ]
    )
    wa, wu, wd, wo, wv = run_spread(send_a, send_u, weight_down[0], send_o, send_v)
    wa = wa.reshape(2, D, TQKV)
    wd = wd.reshape(2, D, D)
    wo = jnp.concatenate([wo[:, 1, 136:184], wo[:, 0, :136], wo[:, 1, :136]], axis=1)
    vecs = jnp.sum(wv.astype(F32), axis=(1, 2))
    middle_0, *kept_0, wu = run_attend_forward(inputs, wa, wo, vecs[0], wu)
    wu = wu.reshape(2, D, D)
    rest = run_forward_rest(middle_0, wu, wd, wa, wo, vecs, cotangent)
    (x_1, *kept_two_0), (middle_1, *kept_1), (result_1,), (grad_middle, up, down, two_1) = split(rest, 4, 7, 1, 4)
    acts = [x_1, result_1]
    back_1, one_1, heads_1, half_up, half_down, grad_middle, up_0, down_0, two_0, *half_a = run_backward_middle(
        (grad_middle, wa, wo, vecs[1], x_1, *kept_1),
        up.reshape(4, 2, 136, D),
        down.reshape(2, 4, 136, D),
        (wu, wd, vecs[0], middle_0, *kept_two_0),
    )
    back_0, all_up, all_down, all_a, all_b, small, all_acts, all_grads = run_backward_end(
        (grad_middle, wa, wo, vecs[0], inputs, *kept_0),
        up_0.reshape(4, 2, 136, D),
        down_0.reshape(2, 4, 136, D),
        (half_up, half_down, *half_a),
        (two_0, one_1, two_1, heads_1, *acts, back_1),
    )
    attn, out, up, down, b_attn, b_out, b_up, b_down, gain, shift = run_assemble(all_up, all_down, all_a, all_b, small)
    return (
        all_acts[None, :, None],
        all_grads[None, :, None],
        attn[None],
        out[None],
        up[None],
        down[None],
        b_attn,
        b_out,
        b_up,
        b_down,
        gain[None],
        shift[None],
    )


def solution(mesh):
    placed = (
        P(None, "replica", "fsdp", None),
        P(None, "replica", "fsdp", None),
        P("section", "fsdp", None),
        P("section", "fsdp", None),
        P("section", "fsdp", None),
        P("section", "fsdp", None),
        P("section", "fsdp"),
        P("section", "fsdp"),
        P("section", "fsdp"),
        P("section", "fsdp"),
        P("section", None, "fsdp"),
        P("section", None, "fsdp"),
    )
    return jax.shard_map(
        on_device,
        mesh=mesh,
        in_specs=placed,
        out_specs=(
            P("section", None, "replica", "fsdp", None),
            P("section", None, "replica", "fsdp", None),
        )
        + placed[2:],
        check_vma=False,
    )
```

```python
import functools

import jax
import jax.numpy as jnp
from jax import lax
from jax.experimental import pallas as pl
from jax.experimental.pallas import tpu as pltpu
from jax.sharding import PartitionSpec as P

D = 1088
FF = 4352
HEADS = 17
HD = 64
BLK = 64
CHIPS = 4
ROWS = BLK * CHIPS
SLOTS = 5
TH = SLOTS * HD
TQKV = 3 * TH
SCALE = HD**-0.5
EPS = 1e-5
MESH = pl.DeviceIdType.MESH
BF = jnp.bfloat16
F32 = jnp.float32
ANY = pl.BlockSpec(memory_space=pl.ANY)
VMEM = pl.BlockSpec(memory_space=pltpu.VMEM)
DMA = pltpu.SemaphoreType.DMA
LIMIT = 56 * 1024 * 1024
COST = pl.CostEstimate(flops=10_000_000, bytes_accessed=10_000, transcendentals=0)


def dot(a, b):
    return lax.dot_general(a, b, (((1,), (0,)), ((), ())), preferred_element_type=F32)


def dot_nt(a, b):
    return lax.dot_general(a, b, (((1,), (1,)), ((), ())), preferred_element_type=F32)


def dot_tn(a, b):
    return lax.dot_general(a, b, (((0,), (0,)), ((), ())), preferred_element_type=F32)


def chunks(n, size=256):
    return [(i, min(size, n - i)) for i in range(0, n, size)]


def place():
    f = lax.axis_index("fsdp")
    return f // 2, f % 2


def ring(y, k):
    return lax.rem(y + k, CHIPS)


def at_chip(y, c):
    return {"fsdp": 2 * y + c}


def greet(targets):
    barrier = pltpu.get_barrier_semaphore()
    for target in targets:
        pl.semaphore_signal(barrier, inc=1, device_id=target, device_id_type=MESH)
    return functools.partial(pl.semaphore_wait, barrier, len(targets))


def remote(src, dst, send, recv, target):
    return pltpu.make_async_remote_copy(
        src_ref=src, dst_ref=dst, send_sem=send, recv_sem=recv, device_id=target, device_id_type=MESH
    )


def slot(ref, y):
    return ref.at[pl.ds(pl.multiple_of(y * BLK, BLK), BLK)]


ORDER = (2, 1, 3)


def gather_start(full, y, c, send, recv):
    for k in ORDER:
        remote(slot(full, y), slot(full, y), send.at[k - 1], recv.at[k - 1], at_chip(ring(y, k), c)).start()


def gather_wait(full, y, c, send, recv):
    for k in (1, 3, 2):
        source = ring(y, 4 - k)
        remote(slot(full, source), slot(full, source), send.at[k - 1], recv.at[k - 1], at_chip(ring(y, k), c)).wait()


def scatter_start(acc, out_buf, in_buf, y, c, send, recv):
    for k in ORDER:
        target = ring(y, k)
        out_buf[k - 1] = slot(acc, target)[...].astype(BF)
        remote(out_buf.at[k - 1], in_buf.at[k - 1], send.at[k - 1], recv.at[k - 1], at_chip(target, c)).start()


def scatter_wait(acc, out_buf, in_buf, y, c, send, recv):
    total = slot(acc, y)[...]
    for k in (1, 3, 2):
        remote(out_buf.at[k - 1], in_buf.at[k - 1], send.at[k - 1], recv.at[k - 1], at_chip(ring(y, k), c)).wait()
        total = total + in_buf[k - 1].astype(F32)
    return total


def stats(v):
    centre = v - jnp.mean(v, axis=-1, keepdims=True)
    scale = lax.rsqrt(jnp.mean(centre * centre, axis=-1, keepdims=True) + EPS)
    return centre * scale, scale


def norm(v, gain, shift):
    return stats(v)[0] * gain + shift


def norm_back(d, v, gain):
    vh, scale = stats(v)
    q = d * gain
    grad = scale * (q - jnp.mean(q, axis=-1, keepdims=True) - vh * jnp.mean(q * vh, axis=-1, keepdims=True))
    return grad, jnp.sum(d * vh, axis=0, keepdims=True), jnp.sum(d, axis=0, keepdims=True)


GELU_A = 0.7978845608028654
GELU_B = 0.044715


def gelu(h):
    return 0.5 * h * (1.0 + jnp.tanh(GELU_A * (h + GELU_B * h * h * h)))


def gelu_slope(h):
    t = jnp.tanh(GELU_A * (h + GELU_B * h * h * h))
    return 0.5 * (1.0 + t) + 0.5 * h * (1.0 - t * t) * (GELU_A * (1.0 + 3.0 * GELU_B * h * h))


def masks(c):
    row = lax.broadcasted_iota(jnp.int32, (ROWS, ROWS), 0)
    col = lax.broadcasted_iota(jnp.int32, (ROWS, ROWS), 1)
    own = row >= col
    other = (row // BLK) >= (col // BLK) + (1 - c)
    return own, other


def load(pairs, sems):
    copies = [pltpu.make_async_copy(src, dst, sems.at[i]) for i, (src, dst) in enumerate(pairs)]
    for copy in copies:
        copy.start()
    return copies


def out_rows(wo_hbm, wo, e, y):
    start = pl.multiple_of(48 - 16 * y, 16)
    return [(wo_hbm.at[e, pl.ds(start, 256)], wo.at[0:256]), (wo_hbm.at[e, 256:320], wo.at[256:320])]


def out_wait(weights, wo, y):
    weights[1].wait()
    weights[2].wait()

    @pl.when(y < 3)
    def _():
        wo[256:320] = jnp.zeros((HD, D), BF)


def chip_row(y, rows):
    return jnp.where(lax.broadcasted_iota(jnp.int32, (CHIPS, 1), 0) == y, rows, 0.0)


def head_bias(vecs, row, y):
    last = jnp.where(y == 3, vecs[row : row + 1, 1024:D], 0.0)
    return jnp.concatenate([vecs[row : row + 1, pl.ds(pl.multiple_of(256 * y, 256), 256)], last], axis=-1)


def attend_forward(e, x, w_hbm, wo_hbm, vecs, middle, normed, queries, kv, kv_other, logsum, attended,
                   w, wo, acc, out_buf, in_buf, ls, gs, gr, ss, sr, ks, kr, arrived, weights=None, hooks=None):
    y, c = place()
    sibling = at_chip(y, 1 - c)
    if weights is None:
        weights = load([(w_hbm.at[e], w)] + out_rows(wo_hbm, wo, e, y), ls)
    slot(normed, y)[...] = norm(x[...].astype(F32), vecs[0:1], vecs[1:2]).astype(BF)
    arrived()
    gather_start(normed, y, c, gs, gr)
    if hooks is not None:
        hooks.begin(y, c)
    own, other = masks(c)
    weights[0].wait()
    gather_wait(normed, y, c, gs, gr)
    rows = normed[...]
    bias = jnp.concatenate([jnp.zeros((1, TH), F32), head_bias(vecs, 11, y)], axis=-1)
    for at, size in chunks(2 * TH):
        kv[:, at : at + size] = (dot(rows, w[:, at : at + size]) + bias[:, at : at + size]).astype(BF)
    swap = remote(kv, kv_other, ks, kr, sibling)
    swap.start()
    queries[...] = (dot(rows, w[:, 2 * TH :]) + head_bias(vecs, 10, y)).astype(BF)
    swap.wait()
    for h in range(SLOTS):
        at = h * HD
        q = queries[:, at : at + HD]
        s_own = jnp.where(own, dot_nt(q, kv[:, at : at + HD]) * SCALE, -1e30)
        s_other = jnp.where(other, dot_nt(q, kv_other[:, at : at + HD]) * SCALE, -1e30)
        top = jnp.maximum(jnp.max(s_own, axis=-1, keepdims=True), jnp.max(s_other, axis=-1, keepdims=True))
        e_own = jnp.exp(s_own - top)
        e_other = jnp.exp(s_other - top)
        total = jnp.sum(e_own, axis=-1, keepdims=True) + jnp.sum(e_other, axis=-1, keepdims=True)
        logsum[:, h : h + 1] = top + jnp.log(total)
        inverse = 1.0 / total
        a_own = (e_own * inverse).astype(BF)
        a_other = (e_other * inverse).astype(BF)
        out = dot(a_own, kv[:, TH + at : TH + at + HD]) + dot(a_other, kv_other[:, TH + at : TH + at + HD])
        attended[:, at : at + HD] = out.astype(BF)
    out_wait(weights, wo, y)
    mixed = attended[...]
    for at, size in chunks(D):
        acc[:, at : at + size] = dot(mixed, wo[:, at : at + size])
    scatter_start(acc, out_buf, in_buf, y, c, ss, sr)
    if hooks is not None:
        hooks.late()
    base = x[...].astype(F32) + vecs[4:5]
    middle[...] = base + scatter_wait(acc, out_buf, in_buf, y, c, ss, sr)


def feed_forward(middle, vecs, result, normed, hidden, active,
                 wu, wd, acc, out_buf, in_buf, gs, gr, ss, sr, arrived, weights, defer=False):
    y, c = place()
    slot(normed, y)[...] = norm(middle[...], vecs[2:3], vecs[3:4]).astype(BF)
    arrived()
    gather_start(normed, y, c, gs, gr)
    bias = jnp.sum(chip_row(y, vecs[6:10]), axis=0, keepdims=True)
    weights[0].wait()
    gather_wait(normed, y, c, gs, gr)
    rows = normed[...]
    for at, size in chunks(D):
        h = dot(rows, wu[:, at : at + size]) + bias[:, at : at + size]
        hidden[:, at : at + size] = h
        active[:, at : at + size] = gelu(h).astype(BF)
    weights[1].wait()
    rows = active[...]
    for at, size in chunks(D):
        acc[:, at : at + size] = dot(rows, wd[:, at : at + size])
    scatter_start(acc, out_buf, in_buf, y, c, ss, sr)

    def finish():
        base = middle[...] + vecs[5:6]
        result[...] = (base + scatter_wait(acc, out_buf, in_buf, y, c, ss, sr)).astype(BF)

    if defer:
        return finish
    finish()


def feed_back(e, grad, wu_hbm, wd_hbm, vecs, middle, normed, hidden, active, grad_middle, grad_up, grad_down, small,
              wu, wd, full, gh, acc, out_buf, in_buf, ls, gs, gr, ss, sr, arrived, reduce=None, weights=None, early=False):
    y, c = place()
    if weights is None:
        weights = load([(wu_hbm.at[e], wu), (wd_hbm.at[e], wd)], ls)
    own_rows = grad[...]
    if not early:
        slot(full, y)[...] = own_rows
        arrived()
        gather_start(full, y, c, gs, gr)
    if reduce is not None:
        reduce.begin(y, c)
    small[...] = jnp.zeros_like(small)
    small[3:4] = jnp.sum(own_rows.astype(F32), axis=0, keepdims=True)
    weights[1].wait()
    if reduce is not None:
        reduce.middle(y, c)
    gather_wait(full, y, c, gs, gr)
    rows = full[...]
    for at, size in chunks(D):
        slope = gelu_slope(hidden[:, at : at + size])
        part = (dot_nt(rows, wd[at : at + size, :]) * slope).astype(BF)
        gh[:, at : at + size] = part
        small[2:3, at : at + size] = jnp.sum(part.astype(F32), axis=0, keepdims=True)
    weights[0].wait()
    rows = gh[...]
    for at, size in chunks(D):
        acc[:, at : at + size] = dot_nt(rows, wu[at : at + size, :])
    scatter_start(acc, out_buf, in_buf, y, c, ss, sr)
    if reduce is not None:
        reduce.relay(y, c)
        reduce.late()
    for at, size in chunks(D):
        grad_up[at : at + size, :] = dot_tn(normed[:, at : at + size], gh[...]).astype(BF)
        grad_down[at : at + size, :] = dot_tn(active[:, at : at + size], full[...]).astype(BF)
    d = scatter_wait(acc, out_buf, in_buf, y, c, ss, sr)
    back, gain, shift = norm_back(d, middle[...], vecs[2:3])
    small[0:1] = gain
    small[1:2] = shift
    grad_middle[...] = grad[...].astype(F32) + back
    if reduce is not None:
        reduce.finish()


def attend_back(e, grad, w_hbm, wo_hbm, vecs, x, normed, queries, kv, kv_other, logsum, attended,
                grad_x, grad_attn, grad_out, small, small_bias,
                w, wo, full, ga, gj, part_out, part_in, part_own, rows_out, edge, acc, out_buf, in_buf, ls, gs, gr, ss, sr, ks, kr, es, er,
                arrived, reduce):
    y, c = place()
    sibling = at_chip(y, 1 - c)
    weights = load([(w_hbm.at[e], w)] + out_rows(wo_hbm, wo, e, y), ls)
    own_rows = grad[...].astype(BF)
    slot(full, y)[...] = own_rows
    arrived()
    gather_start(full, y, c, gs, gr)
    reduce.begin(y, c)
    small[...] = jnp.zeros_like(small)
    small[2:3] = jnp.sum(own_rows.astype(F32), axis=0, keepdims=True)
    own, other = masks(c)
    out_wait(weights, wo, y)
    reduce.middle(y, c)
    gather_wait(full, y, c, gs, gr)
    ga[...] = dot_nt(full[...], wo[...]).astype(BF)
    for h in range(SLOTS):
        at = h * HD
        q = queries[:, at : at + HD]
        g = ga[:, at : at + HD]
        lse = logsum[:, h : h + 1]
        k_own, k_other = kv[:, at : at + HD], kv_other[:, at : at + HD]
        v_own, v_other = kv[:, TH + at : TH + at + HD], kv_other[:, TH + at : TH + at + HD]
        p_own = jnp.exp(jnp.where(own, dot_nt(q, k_own) * SCALE, -1e30) - lse)
        p_other = jnp.exp(jnp.where(other, dot_nt(q, k_other) * SCALE, -1e30) - lse)
        gp_own = dot_nt(g, v_own)
        gp_other = dot_nt(g, v_other)
        delta = jnp.sum(p_own * gp_own, axis=-1, keepdims=True) + jnp.sum(p_other * gp_other, axis=-1, keepdims=True)
        s_own = (p_own * (gp_own - delta)).astype(BF)
        s_other = (p_other * (gp_other - delta)).astype(BF)
        gj[:, 2 * TH + at : 2 * TH + at + HD] = ((dot(s_own, k_own) + dot(s_other, k_other)) * SCALE).astype(BF)
        part_own[:, at : at + HD] = dot_tn(s_own, q) * SCALE
        part_out[:, at : at + HD] = (dot_tn(s_other, q) * SCALE).astype(BF)
        part_own[:, TH + at : TH + at + HD] = dot_tn(p_own.astype(BF), g)
        part_out[:, TH + at : TH + at + HD] = dot_tn(p_other.astype(BF), g).astype(BF)
    swap = remote(part_out, part_in, ks, kr, sibling)
    swap.start()
    for at, size in chunks(D):
        rows_out[:, at : at + size] = dot_tn(attended[...], full[:, at : at + size]).astype(BF)
    lend = remote(rows_out.at[0:HD], edge, es, er, at_chip(ring(y, 3), c))
    lend.start()
    reduce.relay(y, c)
    weights[0].wait()
    swap.wait()
    gj[:, : 2 * TH] = (part_own[...] + part_in[...].astype(F32)).astype(BF)
    rows = gj[...]
    for at, size in chunks(D):
        acc[:, at : at + size] = dot_nt(rows, w[at : at + size, :])
    scatter_start(acc, out_buf, in_buf, y, c, ss, sr)
    for j in range(CHIPS):
        part = dot_tn(normed[:, 272 * j : 272 * j + 272], gj[...])
        grad_attn[j, 0] = part[:136].astype(BF)
        grad_attn[j, 1] = part[136:].astype(BF)
    lend.wait()

    @pl.when(y < 3)
    def _():
        rows_out[256:320] = edge[...]

    chip_rows = rows_out[pl.ds(pl.multiple_of(16 * y, 16), 272)].astype(F32)
    grad_out[0] = chip_rows[:136].astype(BF)
    grad_out[1] = chip_rows[136:].astype(BF)
    reduce.ready(y, c)
    small_bias[...] = jnp.zeros_like(small_bias)
    small_bias[0:1] = jnp.sum(gj[...].astype(F32), axis=0, keepdims=True)
    d = scatter_wait(acc, out_buf, in_buf, y, c, ss, sr)
    back, gain, shift = norm_back(d, x[...].astype(F32), vecs[0:1])
    small[0:1] = gain
    small[1:2] = shift
    grad_x[...] = (grad[...] + back).astype(BF)
    reduce.finish()


def plane():
    s, r = lax.axis_index("section"), lax.axis_index("replica")
    return s, r // 2, r % 2, s * 8 + r


def at_plane(q):
    return {"section": q // 8, "replica": lax.rem(q, 8)}


def x_peers(x, h):
    return [{"replica": 2 * lax.rem(x + k, 4) + h} for k in (1, 2, 3)]


def z_peers(s, h):
    x = lax.axis_index("replica") // 2
    return [
        {"section": 1 - s},
        {"section": 1 - s, "replica": 2 * x + 1 - h},
        {"replica": 2 * x + 1 - h},
    ]


def plane_peers():
    s, x, h, me = plane()
    return x_peers(x, h) + z_peers(s, h)


def block_of(x, y):
    return lax.rem(x - y + 8, 4)


def halves(block, second):
    cut = 512 if block.shape[-1] == D else 384
    return block.at[:, :, cut:] if second else block.at[:, :, 0:cut]


class AlongX:
    def __init__(self, blocks, landing, passing, out, send, recv):
        self.blocks, self.landing, self.passing, self.out = blocks, landing, passing, out
        self.send, self.recv = send, recv

    def parts(self):
        y, c = place()
        s, x, h, me = plane()
        targets = x_peers(x, h)
        ahead, behind = targets[0], targets[2]
        opposite = self.blocks.at[block_of(x + 2, y)]
        to_ahead, to_behind = self.blocks.at[block_of(x + 1, y)], self.blocks.at[block_of(x + 3, y)]
        moves = [
            (halves(opposite, 0), halves(self.passing, 0), ahead),
            (halves(opposite, 1), halves(self.passing, 1), behind),
            (halves(to_ahead, 1), halves(self.landing.at[0], 1), ahead),
            (halves(to_behind, 0), halves(self.landing.at[1], 0), behind),
            (halves(to_ahead, 0), halves(self.landing.at[0], 0), ahead),
            (halves(to_behind, 1), halves(self.landing.at[1], 1), behind),
        ]
        return [remote(source, to, self.send.at[i], self.recv.at[i], target) for i, (source, to, target) in enumerate(moves)]

    def start(self):
        for copy in self.parts()[:4]:
            copy.start()

    def relay(self):
        y, c = place()
        s, x, h, me = plane()
        copies = self.parts()
        for second, step in ((0, 1), (1, 3)):
            copies[second].wait_recv()
            block, passed = halves(self.blocks.at[block_of(x + step, y)], second), halves(self.passing, second)
            block[...] = (block[...].astype(F32) + passed[...].astype(F32)).astype(BF)
            copies[4 + second].start()

    def finish(self):
        y, c = place()
        s, x, h, me = plane()
        own = block_of(x, y)
        copies = self.parts()
        for copy in copies:
            copy.wait_send()
        for copy in copies[2:]:
            copy.wait_recv()

        def add(i, carry):
            rows = pl.ds(pl.multiple_of(8 * i, 8), 8)
            total = self.blocks[own, 0, rows].astype(F32)
            total = total + self.landing[0, 0, rows].astype(F32) + self.landing[1, 0, rows].astype(F32)
            self.out[0, rows] = total.astype(BF)
            return carry

        lax.fori_loop(0, 17, add, 0)


def x_scratch(width):
    return [
        pltpu.VMEM((4, 1, 136, width), BF),
        pltpu.VMEM((2, 1, 136, width), BF),
        pltpu.VMEM((1, 136, width), BF),
        DMA((6,)),
        DMA((6,)),
    ]


class AlongZ:
    def __init__(self, layer, blocks, out, landing, send, recv):
        self.layer, self.blocks, self.landing, self.out, self.send, self.recv = layer, blocks, landing, out, send, recv

    def copies(self):
        s, x, h, me = plane()
        for half in (0, 1):
            owner = 2 * half + self.layer
            rel = lax.rem(2 * h + s - owner + 3, 4)
            target = {"section": jnp.int32(self.layer), "replica": 2 * x + half}
            copy = remote(self.blocks, self.landing.at[rel], self.send.at[half], self.recv.at[rel], target)
            yield 2 * h + s != owner, copy

    def start(self):
        for sends, copy in self.copies():
            pl.when(sends)(copy.start)

    def finish(self):
        s, x, h, me = plane()
        for sends, copy in self.copies():
            pl.when(sends)(copy.wait_send)

        @pl.when(s == self.layer)
        def _():
            for rel in range(3):
                remote(self.blocks, self.landing.at[rel], self.send.at[0], self.recv.at[rel], {"section": 1 - s}).wait_recv()

            def add(i, carry):
                rows = pl.ds(pl.multiple_of(8 * (i % 17), 8), 8)
                total = self.blocks[i // 17, rows].astype(F32)
                for rel in range(3):
                    total = total + self.landing[rel, i // 17, rows].astype(F32)
                self.out[i // 17, rows] = total.astype(BF)
                return carry

            lax.fori_loop(0, 17 * self.out.shape[0], add, 0)


def z_scratch(count, width):
    return [pltpu.VMEM((3, count, 136, width), BF), DMA((2,)), DMA((3,))]


class FeedReduce:
    def __init__(self, up, down, out_up, out_down, other, ls, cs, cr, *scratch):
        self.sources = (up, down)
        self.other, self.ls, self.cs, self.cr = other, ls, cs, cr
        self.up = AlongX(*scratch[0:3], out_up, *scratch[3:5])
        self.down = AlongX(*scratch[5:8], out_down, *scratch[8:10])

    def copies(self, y, c):
        up, down = self.sources
        sibling = at_chip(y, 1 - c)
        for i, (unit, own, theirs) in enumerate(
            ((self.up, up.at[:, c], up.at[:, 1 - c]), (self.down, down.at[c], down.at[1 - c]))
        ):
            keep = pltpu.make_async_copy(own, unit.blocks.at[:, 0], self.ls.at[i])
            swap = remote(theirs, self.other.at[:, i], self.cs.at[i], self.cr.at[i], sibling)
            yield unit, keep, swap

    def begin(self, y, c):
        for unit, keep, swap in self.copies(y, c):
            swap.start()
            keep.start()

    def middle(self, y, c):
        for at, (unit, keep, swap) in enumerate(self.copies(y, c)):
            keep.wait()
            swap.wait()

            def add(i, carry, unit=unit, at=at):
                unit.blocks[i, 0] = (unit.blocks[i, 0].astype(F32) + self.other[i, at].astype(F32)).astype(BF)
                return carry

            lax.fori_loop(0, 4, add, 0)
            unit.start()

    def relay(self, y, c):
        self.up.relay()
        self.down.relay()


FEED_SCRATCH = [pltpu.VMEM((4, 2, 136, D), BF), DMA((2,)), DMA((2,)), DMA((2,))] + x_scratch(D) * 2


class AttendReduce:
    def __init__(self, wide, rows, outs, other_w, other_r, cs, cr, *scratch):
        self.wide, self.rows = wide, rows
        self.other_w, self.other_r = other_w, other_r
        self.cs, self.cr = cs, cr
        self.units = [AlongX(*scratch[0:3], outs[0], *scratch[3:5]), AlongX(*scratch[5:8], outs[1], *scratch[8:10])]

    def swaps(self, y, c):
        sibling = at_chip(y, 1 - c)
        return [
            remote(self.wide.at[:, 1 - c], self.other_w, self.cs.at[0], self.cr.at[0], sibling),
            remote(self.rows.at[1 - c], self.other_r, self.cs.at[1], self.cr.at[1], sibling),
        ]

    def begin(self, y, c):
        for copy in self.swaps(y, c):
            copy.start()

    def middle(self, y, c):
        for copy in self.swaps(y, c):
            copy.wait()
        first, second = (unit.blocks for unit in self.units)
        for i in range(4):
            block = self.wide[i, c].astype(F32) + self.other_w[i].astype(F32)
            first[i, 0] = block[:, :640].astype(BF)
            second[i, 0, :, :320] = block[:, 640:].astype(BF)
        self.units[0].start()
        for i in range(4):
            chunk = self.rows[c, :, 256 * i : 256 * i + 256].astype(F32) + self.other_r[:, 256 * i : 256 * i + 256].astype(F32)
            second[i, 0, :, 320:576] = chunk.astype(BF)
            if i < 3:
                second[i, 0, :, 576:] = jnp.zeros((136, HD), BF)
        chunk = self.rows[c, :, 1024:].astype(F32) + self.other_r[:, 1024:].astype(F32)
        second[3, 0, :, 576:] = chunk.astype(BF)
        self.units[1].start()

    def relay(self, y, c):
        for unit in self.units:
            unit.relay()


ATTEND_SCRATCH = [
    pltpu.VMEM((4, 136, TQKV), BF),
    pltpu.VMEM((136, D), BF),
    DMA((2,)),
    DMA((2,)),
] + x_scratch(640) * 2


BLOCKS = [pltpu.VMEM((4, 2, 136, TQKV), BF), pltpu.VMEM((2, 136, D), BF)]


class Hooks:
    def __init__(self, begin=(), middle=(), late=(), ready=(), relay=()):
        self.steps = begin, middle, late, ready, relay

    def begin(self, y, c):
        for step in self.steps[0]:
            step(y, c)

    def middle(self, y, c):
        for step in self.steps[1]:
            step(y, c)

    def late(self):
        for step in self.steps[2]:
            step()

    def ready(self, y, c):
        for step in self.steps[3]:
            step(y, c)

    def relay(self, y, c):
        for step in self.steps[4]:
            step(y, c)

    def finish(self):
        pass


def split(refs, *counts):
    parts, at = [], 0
    for count in counts:
        parts.append(refs[at : at + count])
        at += count
    assert at == len(refs)
    return parts


def attend_forward_first(x, w_hbm, wo_hbm, vecs, part, *refs):
    kept, (wu,), own, (hold, ls, zs, zr, cs, cr) = split(refs, 7, 1, 2 + len(MOVE) + 2, 6)
    y, c = place()
    s, _, h, me = plane()
    sibling = at_chip(y, 1 - c)
    near, far = z_peers(s, h)[:2]
    arrived = greet([at_chip(ring(y, k), c) for k in (1, 2, 3)] + [sibling, near, far])
    bring = pltpu.make_async_copy(part, hold, ls.at[0])
    bring.start()

    def along_z(layer):
        return [
            remote(hold.at[0:2], wu.at[layer, 0:2, c], zs.at[0], zr.at[0], near),
            remote(hold.at[2:4], wu.at[layer, 2:4, c], zs.at[1], zr.at[1], far),
        ]

    def across(layer, i, core):
        rows = wu.at[layer, :, core]
        return remote(hold if i == 0 else rows, rows, cs.at[i], cr.at[i], sibling)

    keep = pltpu.make_async_copy(hold, wu.at[s, :, c], ls.at[1])

    def begin(y, c):
        bring.wait()
        keep.start()
        for copy in along_z(s):
            copy.start()
        across(s, 0, c).start()

    def late():
        for copy in along_z(1 - s):
            copy.wait_recv()
        across(1 - s, 1, c).start()

    attend_forward(0, x.at[s, 0], w_hbm, wo_hbm, vecs, *kept, *own, arrived, hooks=Hooks(begin=[begin], late=[late]))
    across(s, 0, 1 - c).wait_recv()
    across(1 - s, 1, 1 - c).wait_recv()
    for copy in along_z(s):
        copy.wait_send()
    across(s, 0, c).wait_send()
    across(1 - s, 1, c).wait_send()
    keep.wait()


class Loaded:
    def wait(self):
        pass


def forward_rest(middle_0, wu_hbm, wd_hbm, w_hbm, wo_hbm, vecs_0, vecs_1, cotangent, *refs):
    f0_out, a_out, result_1, back_out, f0_scr, a_scr, f1_kept, f1_scr, b_scr, loads = split(
        refs, 4, 7, 1, 4, 2 + len(FEED_MOVE), 2 + len(MOVE) + 2, 3, 2 + len(FEED_MOVE), 2 + len(MOVE), 1
    )
    y, c = place()
    arrived = greet([at_chip(ring(y, k), c) for k in (1, 2, 3)] + [at_chip(y, 1 - c)])
    weights_0 = load([(wu_hbm.at[0], f0_scr[0]), (wd_hbm.at[0], f0_scr[1])], loads[0].at[0])
    weights_a = load([(w_hbm.at[1], a_scr[0])] + out_rows(wo_hbm, a_scr[1], 1, y), a_scr[5])
    weights_1 = load([(wu_hbm.at[1], f1_scr[0]), (wd_hbm.at[1], f1_scr[1])], loads[0].at[1])
    grad = cotangent.at[lax.axis_index("section"), 0]
    full, gs, gr = b_scr[0], b_scr[6], b_scr[7]
    slot(full, y)[...] = grad[...]

    def begin():
        arrived()

    result_0 = f0_out[0]
    feed_forward(middle_0, vecs_0, *f0_out, *f0_scr, begin, weights_0)
    gather_start(full, y, c, gs, gr)
    attend_forward(1, result_0, w_hbm, wo_hbm, vecs_1, *a_out, *a_scr, lambda: None, weights_a)
    middle_1 = a_out[0]
    normed, hidden, active = f1_kept
    finish = feed_forward(middle_1, vecs_1, result_1[0], normed, hidden, active, *f1_scr, lambda: None, weights_1, True)
    feed_back(1, grad, wu_hbm, wd_hbm, vecs_1, middle_1, normed, hidden, active, *back_out,
              f1_scr[0], f1_scr[1], *b_scr, lambda: None, Hooks(late=[finish]), [Loaded(), Loaded()], True)


def backward_middle(*refs):
    a_in, updown, f_in, a_out, half_u, f_out, half_a, a_scr, u_scr, f_scr, grads, w_scr = split(
        refs, 11, 2, 7, 3, 2, 4, 2, len(ATTEND_OWN), len(FEED_SCRATCH), len(FEED_OWN), 2, len(ATTEND_SCRATCH)
    )
    y, c = place()
    s, x, h, me = plane()
    arrived = greet([at_chip(ring(y, k), c) for k in (1, 2, 3)] + [at_chip(y, 1 - c)] + x_peers(x, h))
    wu_hbm, wd_hbm, vecs, *kept = f_in
    weights = load([(wu_hbm.at[0], f_scr[0]), (wd_hbm.at[0], f_scr[1])], f_scr[7])
    feed = FeedReduce(*updown, *half_u, *u_scr)
    attend = AttendReduce(*grads, half_a, *w_scr)
    grad_x, small, small_bias = a_out
    attend_back(1, *a_in, grad_x, *grads, small, small_bias, *a_scr, arrived,
                Hooks(begin=[feed.begin], middle=[feed.middle], relay=[feed.relay], ready=[attend.begin]))
    feed_back(0, grad_x, wu_hbm, wd_hbm, vecs, *kept, *f_out, *f_scr, lambda: None,
              Hooks(middle=[attend.middle], relay=[attend.relay], late=[feed.up.finish, feed.down.finish]), weights)
    for unit in attend.units:
        unit.finish()


def backward_end(*refs):
    a_in, updown, halves, rest, a_out, g_out, a_scr, u_scr, grads, w_scr, z_scr, own, g_scr = split(
        refs, 11, 2, 4, 7, 1, 7, len(ATTEND_OWN), len(FEED_SCRATCH), 2, len(ATTEND_SCRATCH), 24, 14, len(GATHER_OWN)
    )
    y, c = place()
    s, x, h, me = plane()
    sibling = at_chip(y, 1 - c)
    peers = [at_chip(ring(y, k), c) for k in (1, 2, 3)]
    arrived = greet(peers + [sibling] + [at_plane(lax.rem(me + j, 16)) for j in range(1, 16)])
    mine, sums, lates, (small, small_bias) = split(own, 4, 4, 4, 2)
    (grad_x,) = a_out
    a_in = [*a_in[:4], a_in[4].at[s, 0], *a_in[5:]]
    feed = FeedReduce(*updown, mine[0], mine[1], *u_scr)
    attend = AttendReduce(*grads, mine[2:], *w_scr)
    first = [AlongZ(1, half, out, *z_scr[3 * i : 3 * i + 3]) for i, (half, out) in enumerate(zip(halves, sums))]
    last = [
        AlongZ(0, half, out, *z_scr[12 + 3 * i : 15 + 3 * i])
        for i, (half, out) in enumerate(zip(mine, lates))
    ]

    def start_first(y, c):
        for unit in first:
            unit.start()

    def up_along_z(y, c):
        feed.up.finish()
        last[0].start()

    attend_back(0, *a_in, grad_x, *grads, small, small_bias, *a_scr, arrived,
                Hooks(begin=[feed.begin, start_first], middle=[feed.middle], relay=[feed.relay], ready=[attend.begin, up_along_z]))
    gather_pieces(feed, attend, first, last, small, small_bias, *rest, grad_x, *g_out, *g_scr)


def shape(dims, kind):
    return jax.ShapeDtypeStruct(dims, kind)


MOVE = [
    pltpu.VMEM((ROWS, D), F32),
    pltpu.VMEM((3, BLK, D), BF),
    pltpu.VMEM((3, BLK, D), BF),
    DMA((3,)),
    DMA((3,)),
    DMA((3,)),
    DMA((3,)),
    DMA((3,)),
]


def call(body, name, number, outs, ins, scratch, out_specs=None):
    return pl.pallas_call(
        body,
        name=name,
        out_shape=outs,
        in_specs=ins,
        out_specs=out_specs or [VMEM] * len(outs),
        scratch_shapes=scratch,
        cost_estimate=COST,
        compiler_params=pltpu.CompilerParams(collective_id=number, has_side_effects=True, vmem_limit_bytes=LIMIT),
    )


HALF_A, HALF_U = shape((1, 136, 640), BF), shape((1, 136, D), BF)
FEED_OUTS = [shape((BLK, D), F32), shape((D, D), BF), shape((D, D), BF), shape((8, D), F32)]
ATTEND_KEPT = [
    shape((BLK, D), F32),
    shape((ROWS, D), BF),
    shape((ROWS, TH), BF),
    shape((ROWS, 2 * TH), BF),
    shape((ROWS, 2 * TH), BF),
    shape((ROWS, 128), F32),
    shape((ROWS, TH), BF),
]
FEED_KEPT = [shape((ROWS, D), BF), shape((ROWS, D), F32), shape((ROWS, D), BF)]
ATTEND_WEIGHTS = [pltpu.VMEM((D, TQKV), BF), pltpu.VMEM((TH, D), BF)]
FEED_WEIGHTS = [pltpu.VMEM((D, D), BF), pltpu.VMEM((D, D), BF)]
FEED_MOVE = MOVE[:3] + MOVE[4:]


def run_attend_forward(x, w, wo, vecs, part):
    scratch = ATTEND_WEIGHTS + MOVE + [DMA, DMA]
    scratch += [pltpu.VMEM((4, 136, D), BF), DMA((2,)), DMA((2,)), DMA((2,)), DMA((2,)), DMA((2,))]
    outs = ATTEND_KEPT + [shape((2, 4, 2, 136, D), BF)]
    return call(attend_forward_first, "attend_forward_0", 0, outs, [VMEM, ANY, ANY, VMEM, ANY], scratch,
                [VMEM] * 7 + [ANY])(x, w, wo, vecs, part)


def run_forward_rest(middle, wu, wd, wa, wo, vecs, cotangent):
    outs = [shape((BLK, D), BF)] + FEED_KEPT + ATTEND_KEPT + [shape((BLK, D), BF)] + FEED_OUTS
    kept = [pltpu.VMEM(kind.shape, kind.dtype) for kind in FEED_KEPT]
    rows = pltpu.VMEM((ROWS, D), BF)
    scratch = FEED_WEIGHTS + FEED_MOVE + ATTEND_WEIGHTS + MOVE + [DMA, DMA] + kept + FEED_WEIGHTS + FEED_MOVE
    scratch = scratch + [rows, rows] + MOVE + [DMA((2, 2))]
    return call(forward_rest, "forward_rest", 2, outs, [VMEM] + [ANY] * 4 + [VMEM] * 3, scratch)(
        middle, wu, wd, wa, wo, vecs[0], vecs[1], cotangent
    )


FEED_OWN = [
    pltpu.VMEM((D, D), BF),
    pltpu.VMEM((D, D), BF),
    pltpu.VMEM((ROWS, D), BF),
    pltpu.VMEM((ROWS, D), BF),
] + MOVE
ATTEND_OWN = [
    pltpu.VMEM((D, TQKV), BF),
    pltpu.VMEM((TH, D), BF),
    pltpu.VMEM((ROWS, D), BF),
    pltpu.VMEM((ROWS, TH), BF),
    pltpu.VMEM((ROWS, TQKV), BF),
    pltpu.VMEM((ROWS, 2 * TH), BF),
    pltpu.VMEM((ROWS, 2 * TH), BF),
    pltpu.VMEM((ROWS, 2 * TH), F32),
    pltpu.VMEM((TH, D), BF),
    pltpu.VMEM((HD, D), BF),
] + MOVE + [DMA, DMA, DMA, DMA]
GATHER_OWN = [
    pltpu.VMEM((BLK, D), BF),
    pltpu.VMEM((BLK, D), BF),
    DMA((2,)),
    DMA((2,)),
    pltpu.VMEM((1, 136, D), BF),
    pltpu.VMEM((1, 136, 640), BF),
    pltpu.VMEM((1, 136, 640), BF),
    pltpu.VMEM((2, 16, D), F32),
    pltpu.VMEM((2, 16, D), F32),
    pltpu.VMEM((3, 2, 16, D), F32),
    pltpu.VMEM((2, 16, D), BF),
    pltpu.VMEM((15, 16, D), BF),
    DMA((4,)),
    DMA((4,)),
    DMA((4, 4)),
    DMA((4, 4)),
    DMA,
    DMA,
    DMA((3,)),
    DMA((3,)),
    DMA((15,)),
    DMA((15,)),
]
SMALLS = [shape((8, D), F32), shape((8, TQKV), F32)]


def run_backward_middle(attend_args, up, down, feed_args):
    outs = [shape((BLK, D), BF)] + SMALLS + [HALF_U, HALF_U] + FEED_OUTS + [HALF_A, HALF_A]
    ins = [VMEM, ANY, ANY] + [VMEM] * 8 + [ANY] * 4 + [VMEM] * 5
    scratch = ATTEND_OWN + FEED_SCRATCH + FEED_OWN + BLOCKS + ATTEND_SCRATCH
    return call(backward_middle, "backward_middle", 5, outs, ins, scratch)(*attend_args, up, down, *feed_args)


def run_backward_end(attend_args, up, down, halves, rest):
    both = shape((2, BLK, D), BF)
    outs = [shape((BLK, D), BF), shape((4, 1, 136, D), BF), shape((4, 1, 136, D), BF), shape((4, 1, 136, 640), BF)] + [shape((4, 1, 136, 640), BF)]
    outs += [shape((16, D), F32), both, both]
    ins = [VMEM, ANY, ANY] + [VMEM] * 8 + [ANY] * 2 + [VMEM] * (4 + len(rest))
    units = [pltpu.VMEM((1, 136, D), BF), pltpu.VMEM((1, 136, D), BF)] + [pltpu.VMEM((1, 136, 640), BF)] * 2
    zs = (z_scratch(1, D) + z_scratch(1, D) + z_scratch(1, 640) * 2) * 2
    smalls = [pltpu.VMEM((8, D), F32), pltpu.VMEM((8, TQKV), F32)]
    scratch = ATTEND_OWN + FEED_SCRATCH + BLOCKS + ATTEND_SCRATCH + zs + units * 3 + smalls + GATHER_OWN
    return call(backward_end, "backward_end", 6, outs, ins, scratch)(*attend_args, up, down, *halves, *rest)


def spread(send_a, send_u, send_d, send_o, send_v, send_t, wa, wu, wd, wo, wv, wt, hold_a, hold_u, hold_d, hold_o, hold_v, local, ysend, yrecv, zsend, zrecv, csend, crecv, tsend, trecv):
    s = lax.axis_index("section")
    y, c = place()
    replica = lax.axis_index("replica")
    flipped = replica // 2 * 2 + (1 - replica % 2)
    near = {"section": 1 - s}
    far = {"section": 1 - s, "replica": flipped}
    sibling = at_chip(y, 1 - c)
    peers = [at_chip(ring(y, k), c) for k in (1, 2, 3)]
    arrived = greet(peers + [sibling, near, far])
    brought = load(
        [(send_a.at[y], hold_a), (send_u.at[y], hold_u), (send_d, hold_d), (send_o, hold_o), (send_v, hold_v)], local.at[0]
    )
    for copy in brought:
        copy.wait()
    keeps = load(
        [
            (hold_a, wa.at[s, y, c]),
            (hold_u, wu.at[y]),
            (hold_d, wd.at[s, c]),
            (hold_o, wo.at[s, c]),
            (hold_v, wv.at[s, y, c]),
        ],
        local.at[1],
    )
    arrived()

    def along_y(k, back):
        target = ring(y, k)
        place_in = ring(y, 4 - k) if back else y
        return [
            remote(send_v, wv.at[s, place_in, c], ysend.at[0, k - 1], yrecv.at[0, k - 1], at_chip(target, c)),
            remote(send_a.at[target], wa.at[s, place_in, c], ysend.at[1, k - 1], yrecv.at[1, k - 1], at_chip(target, c)),
            remote(send_u.at[target], wu.at[place_in], ysend.at[2, k - 1], yrecv.at[2, k - 1], at_chip(target, c)),
        ]

    def along_z(layer):
        return [
            remote(wv.at[layer, :, c], wv.at[layer, :, c], zsend.at[0], zrecv.at[0], near),
            remote(wa.at[layer, 0:2, c], wa.at[layer, 0:2, c], zsend.at[1], zrecv.at[1], near),
            remote(wa.at[layer, 2:4, c], wa.at[layer, 2:4, c], zsend.at[2], zrecv.at[2], far),
            remote(wo.at[layer, c], wo.at[layer, c], zsend.at[3], zrecv.at[3], far),
            remote(wd.at[layer, c, 0:272], wd.at[layer, c, 0:272], zsend.at[4], zrecv.at[4], near),
            remote(wd.at[layer, c, 272:544], wd.at[layer, c, 272:544], zsend.at[5], zrecv.at[5], far),
        ]

    def across(layer, i, core):
        return [
            remote(wv.at[layer, :, core], wv.at[layer, :, core], csend.at[i, 0], crecv.at[i, 0], sibling),
            remote(wa.at[layer, :, core], wa.at[layer, :, core], csend.at[i, 1], crecv.at[i, 1], sibling),
            remote(wo.at[layer, core], wo.at[layer, core], csend.at[i, 2], crecv.at[i, 2], sibling),
            remote(wd.at[layer, core], wd.at[layer, core], csend.at[i, 3], crecv.at[i, 3], sibling),
        ]

    def tail_z(layer):
        return remote(wt.at[layer, c], wt.at[layer, c], tsend.at[1], trecv.at[1], far)

    def tail_c(layer, i, core):
        return remote(wt.at[layer, core], wt.at[layer, core], tsend.at[2 + i], trecv.at[2 + i], sibling)

    tail_y = remote(send_t, wt.at[s, c], tsend.at[0], trecv.at[0], peers[0])
    sent_y = [along_y(k, False) for k in (1, 2, 3)]
    got_y = [along_y(k, True) for k in (1, 2, 3)]
    sent_z, got_z = along_z(s), along_z(1 - s)
    sent_c = [across(s, 0, c), across(1 - s, 1, c)]
    got_c = [across(s, 0, 1 - c), across(1 - s, 1, 1 - c)]
    for kind in (0, 1):
        for k in (1, 0, 2):
            sent_y[k][kind].start()
    tail_y.start()
    keeps[3].wait()
    sent_z[3].start()
    sent_c[0][2].start()
    keeps[2].wait()
    sent_z[4].start()
    sent_z[5].start()
    sent_c[0][3].start()
    for kind, keep, zs, cross in ((0, 4, (0,), 0), (1, 0, (1, 2), 1)):
        keeps[keep].wait()
        for k in range(3):
            got_y[k][kind].wait_recv()
        for z in zs:
            sent_z[z].start()
        sent_c[0][cross].start()
    for k in (1, 0, 2):
        sent_y[k][2].start()
    tail_y.wait()
    tail_z(s).start()
    tail_c(s, 0, c).start()
    for zs, cross in (((3,), 2), ((4, 5), 3), ((0,), 0), ((1, 2), 1)):
        for z in zs:
            got_z[z].wait_recv()
        sent_c[1][cross].start()
    tail_z(1 - s).wait_recv()
    tail_c(1 - s, 1, c).start()
    keeps[1].wait()
    for k in range(3):
        got_y[k][2].wait_recv()
    for i in range(2):
        for cross in range(4):
            got_c[i][cross].wait_recv()
    tail_c(s, 0, 1 - c).wait_recv()
    tail_c(1 - s, 1, 1 - c).wait_recv()
    tail_z(s).wait_send()
    tail_c(s, 0, c).wait_send()
    tail_c(1 - s, 1, c).wait_send()
    for k in range(3):
        for kind in range(3):
            sent_y[k][kind].wait_send()
    for z in range(6):
        sent_z[z].wait_send()
    for i in range(2):
        for cross in range(4):
            sent_c[i][cross].wait_send()


def run_spread(a, u, d, o, v, t):
    outs = [
        shape((2, 4, 2, 136, TQKV), BF),
        shape((4, 136, D), BF),
        shape((2, 2, 544, D), BF),
        shape((2, 2, 136, D), BF),
        shape((2, 4, 2, 16, D), BF),
        shape((2, 2, 48, D), BF),
    ]
    return pl.pallas_call(
        spread,
        name="spread",
        out_shape=outs,
        in_specs=[ANY] * 6,
        out_specs=[ANY] * 6,
        scratch_shapes=[
            pltpu.VMEM((136, TQKV), BF),
            pltpu.VMEM((136, D), BF),
            pltpu.VMEM((544, D), BF),
            pltpu.VMEM((136, D), BF),
            pltpu.VMEM((16, D), BF),
            DMA((2, 5)), DMA((3, 3)), DMA((3, 3)), DMA((6,)), DMA((6,)), DMA((2, 4)), DMA((2, 4)), DMA((4,)), DMA((4,)),
        ],
        compiler_params=pltpu.CompilerParams(collective_id=8, has_side_effects=True),
    )(a, u, d, o, v, t)


def build_small(buf, one, two, heads, y):
    buf[...] = jnp.zeros_like(buf)
    buf[0:2] = one[0:2]
    buf[2:4] = two[0:2]
    buf[4:5] = one[2:3]
    buf[5:6] = two[3:4]
    buf[6:10] = chip_row(y, two[2:3])
    for row, at in ((10, 2 * TH), (11, TH)):
        buf[row : row + 1, pl.ds(pl.multiple_of(256 * y, 256), 256)] = heads[0:1, at : at + 256]

        @pl.when(y == 3)
        def _(row=row, at=at):
            buf[row : row + 1, 1024:D] = heads[0:1, at + 256 : at + TH]


class Gather:
    def __init__(self, unit, moved, keep_from, out, ts, tr, gs, gr):
        self.unit, self.moved, self.out, self.keep_from = unit, moved, out, keep_from
        self.ts, self.tr, self.gs, self.gr = ts, tr, gs, gr

    def transpose(self):
        y, c = place()
        s, x, h, me = plane()
        return remote(self.unit, self.moved, self.ts, self.tr, at_chip(block_of(x, y), c))

    def elsewhere(self):
        y, c = place()
        s, x, h, me = plane()
        return block_of(x, y) != y

    def start(self):
        pl.when(self.elsewhere())(self.transpose().start)

    def arrive(self):
        @pl.when(self.elsewhere())
        def _():
            self.transpose().wait()
            if self.keep_from:
                lane = lax.broadcasted_iota(jnp.int32, self.unit.shape[1:], 1)
                merged = jnp.where(lane < self.keep_from, self.moved[0].astype(F32), self.unit[0].astype(F32))
                self.unit[0] = merged.astype(BF)
            else:
                self.unit[0] = self.moved[0]

    def copies(self):
        y, c = place()
        s, x, h, me = plane()
        targets = x_peers(x, h)
        for k in (1, 3):
            yield remote(self.unit, self.out.at[block_of(x, y)], self.gs.at[k], self.gr.at[k], targets[k - 1])

    def half(self, x, second):
        y, c = place()
        return halves(self.out.at[block_of(x, y)], second)

    def arrivals(self):
        s, x, h, me = plane()
        targets = x_peers(x, h)
        y, c = place()
        for k in (1, 3):
            place_in = self.out.at[block_of(x - k + 4, y)]
            yield remote(place_in, place_in, self.gs.at[k], self.gr.at[k], targets[k - 1])

    def forwards(self):
        s, x, h, me = plane()
        targets = x_peers(x, h)
        for i, k in enumerate((1, 3)):
            part = self.half(x - k + 4, i)
            yield remote(part, part, self.gs.at[2 * i], self.gr.at[2 * i], targets[k - 1])

    def spread(self):
        y, c = place()
        s, x, h, me = plane()
        for copy in self.copies():
            copy.start()
        self.out[block_of(x, y)] = self.unit[...]

    def forward(self):
        for copy in self.arrivals():
            copy.wait_recv()
        for copy in self.forwards():
            copy.start()

    def finish(self):
        s, x, h, me = plane()
        targets = x_peers(x, h)
        for copy in self.copies():
            copy.wait_send()
        for copy in self.forwards():
            copy.wait_send()
        for i, k in enumerate((1, 3)):
            part = self.half(x + 2, i)
            remote(part, part, self.gs.at[2 * i], self.gr.at[2 * i], targets[k - 1]).wait_recv()


def gather_pieces(feed, attend, first, last, one_0, heads_0,
                  two_0, one_1, two_1, heads_1, act_0, act_1, back_1, back_0,
                  out_up, out_down, out_a, out_b, out_small, out_act, out_back,
                  swap_act, swap_back, ws, wr, moved_up, moved_a, moved_b, small, small_c, small_y, small_x, small_z,
                  ts, tr, gs, gr, cs, cr, ys, yr, zs, zr):
    y, c = place()
    s, x, h, me = plane()
    sibling = at_chip(y, 1 - c)
    peers = [at_chip(ring(y, k), c) for k in (1, 2, 3)]
    gathers = [
        Gather(last[i].out, moved, keep, out, ts.at[i], tr.at[i], gs.at[i], gr.at[i])
        for i, (moved, keep, out) in enumerate(((moved_up, 0, out_up), (None, 0, out_down), (moved_a, 0, out_a), (moved_b, 320, out_b)))
    ]

    def sum_along_z(i):
        first[i].finish()
        last[i].finish()

        @pl.when(s == 1)
        def _():
            last[i].out[...] = first[i].out[...]

    attend.middle(y, c)
    feed.down.finish()
    last[1].start()
    attend.relay(y, c)
    build_small(small.at[0], one_0, two_0, heads_0, y)
    build_small(small.at[1], one_1, two_1, heads_1, y)
    cross = remote(small, small_c, cs, cr, sibling)
    cross.start()
    swap_act[...] = jnp.where(s == 0, act_1[...].astype(F32), act_0[...].astype(F32)).astype(BF)
    swap_back[...] = jnp.where(s == 0, back_1[...].astype(F32), back_0[...].astype(F32)).astype(BF)
    swaps = [
        remote(swap_act, out_act.at[s], ws.at[0], wr.at[0], {"section": 1 - s}),
        remote(swap_back, out_back.at[s], ws.at[1], wr.at[1], {"section": 1 - s}),
    ]
    out_act[s] = jnp.where(s == 0, act_0[...].astype(F32), act_1[...].astype(F32)).astype(BF)
    out_back[s] = jnp.where(s == 0, back_0[...].astype(F32), back_1[...].astype(F32)).astype(BF)
    cross.wait()
    small[...] = small[...] + small_c[...]
    hops = [remote(small, small_y.at[k - 1], ys.at[k - 1], yr.at[k - 1], peers[k - 1]) for k in (1, 2, 3)]
    for hop in hops:
        hop.start()
    sum_along_z(0)
    gathers[0].start()
    for hop in hops:
        hop.wait()
    small_x[...] = (small[...] + small_y[0] + small_y[1] + small_y[2]).astype(BF)

    def plane_copies():
        for j in range(1, 16):
            q = lax.rem(me + j, 16)
            yield remote(small_x.at[q // 8], small_z.at[15 - j], zs.at[j - 1], zr.at[15 - j], at_plane(q))

    attend.units[0].finish()
    last[2].start()
    gathers[0].arrive()
    gathers[0].spread()
    attend.units[1].finish()
    last[3].start()
    sum_along_z(1)
    gathers[1].spread()
    for copy in plane_copies():
        copy.start()
    gathers[0].forward()
    sum_along_z(2)
    gathers[2].start()
    gathers[1].forward()
    for swap in swaps:
        swap.start()
    gathers[2].arrive()
    gathers[2].spread()
    sum_along_z(3)
    gathers[3].start()
    gathers[2].forward()
    gathers[3].arrive()
    gathers[3].spread()
    total = small_x[s].astype(F32)
    for copy in plane_copies():
        copy.wait_send()
    for j in range(15):
        remote(small_x.at[0], small_z.at[j], zs.at[j], zr.at[j], sibling).wait_recv()
        total = total + small_z[j].astype(F32)
    out_small[...] = total
    gathers[3].forward()
    for i, swap in enumerate(swaps):
        swap.wait_send()
        place_in = (out_act, out_back)[i].at[1 - s]
        remote(place_in, place_in, ws.at[i], wr.at[i], {"section": 1 - s}).wait_recv()
    for gather in gathers:
        gather.finish()


def assemble(all_up, all_down, all_a, all_b, small, attn, out, up, down, b_attn, b_out, b_up, b_down, gain, shift):
    y, c = place()
    f = 2 * y + c
    for j in range(CHIPS):
        up[:, j * D : (j + 1) * D] = all_up[j, 0].astype(F32)
        down[j * 136 : (j + 1) * 136] = all_down[j, 0].astype(F32)
        first, second = all_a[j, 0].astype(F32), all_b[j, 0].astype(F32)
        parts = ((0, second[:, :TH]), (D, first[:, :TH]), (2 * D, first[:, TH:]))
        for base, part in parts:
            attn[:, base + 256 * j : base + 256 * j + 256] = part[:, :256]
        out[:, 256 * j : 256 * j + 256] = second[:, TH : TH + 256]
        if j == CHIPS - 1:
            for base, part in parts:
                attn[:, base + 1024 : base + D] = part[:, 256:]
            out[:, 1024:] = second[:, TH + 256 :]

    def pick(index, options):
        total = jnp.where(index == 0, options[0], 0.0)
        for i, option in enumerate(options[1:], 1):
            total = total + jnp.where(index == i, option, 0.0)
        return total

    for row, ref, place_in in ((0, gain, 0), (1, shift, 0), (2, gain, 1), (3, shift, 1), (4, b_out, 0), (5, b_down, 0)):
        ref[place_in : place_in + 1] = pick(f, [small[row : row + 1, 136 * i : 136 * i + 136] for i in range(8)])
    b_up[...] = pick(f, [small[6 + i // 2 : 7 + i // 2, 544 * (i % 2) : 544 * (i % 2) + 544] for i in range(8)])
    b_attn[...] = pick(f, [small[10 + i // 4 : 11 + i // 4, 272 * (i % 4) : 272 * (i % 4) + 272] for i in range(8)])


def run_assemble(*gathered):
    sizes = [(136, 3 * D), (136, D), (136, FF), (544, D), (1, 272), (1, 136), (1, 544), (1, 136), (2, 136), (2, 136)]
    return pl.pallas_call(
        assemble,
        name="assemble",
        out_shape=[shape(dims, F32) for dims in sizes],
        in_specs=[VMEM] * 5,
        out_specs=[VMEM] * len(sizes),
        compiler_params=pltpu.CompilerParams(vmem_limit_bytes=LIMIT),
    )(*gathered)


def split_heads(block):
    zero = jnp.zeros(block.shape[:-1] + (HD,), block.dtype)
    return [
        jnp.concatenate([block[..., 256 * j : 256 * j + 256], block[..., 1024:] if j == 3 else zero], axis=-1)
        for j in range(CHIPS)
    ]


def on_device(inputs, cotangent, weight_attn, weight_out, weight_up, weight_down, bias_attn, bias_out, bias_up,
              bias_down, norm_gain, norm_bias):
    s = lax.axis_index("section")
    f = lax.axis_index("fsdp")
    y, c = f // 2, f % 2
    wa = weight_attn[0]
    q_blocks, k_blocks, v_blocks = (split_heads(wa[:, i * D : (i + 1) * D]) for i in range(3))
    send_a = jnp.stack(
        [jnp.concatenate([k_blocks[j], v_blocks[j], q_blocks[j]], axis=-1) for j in range(CHIPS)]
    )
    send_u = jnp.stack([weight_up[0][:, j * D : (j + 1) * D] for j in range(CHIPS)])
    vectors = jnp.stack([norm_gain[0, 0], norm_bias[0, 0], norm_gain[0, 1], norm_bias[0, 1], bias_out[0], bias_down[0]])
    send_v = jnp.concatenate(
        [
            lax.dynamic_update_slice(jnp.zeros((6, D), BF), vectors, (0, 136 * f)),
            lax.dynamic_update_slice(jnp.zeros((4, D), BF), bias_up, (y, 544 * c)),
            lax.dynamic_update_slice(jnp.zeros((6, D), BF), bias_attn, (f // 4, 272 * (f % 4))),
        ]
    )
    wa, wu, wd, wo, wv, wt = run_spread(
        send_a, send_u, weight_down[0], weight_out[0], send_v, weight_out[0, 88:]
    )
    wa = wa.reshape(2, D, TQKV)
    wd = wd.reshape(2, D, D)
    wo = jnp.concatenate([wt[:, 1], wo[:, 0], wo[:, 1]], axis=1)
    vecs = jnp.sum(wv.astype(F32), axis=(1, 2))
    middle_0, *kept_0, wu = run_attend_forward(inputs, wa, wo, vecs[0], wu)
    wu = wu.reshape(2, D, D)
    rest = run_forward_rest(middle_0, wu, wd, wa, wo, vecs, cotangent)
    (x_1, *kept_two_0), (middle_1, *kept_1), (result_1,), (grad_middle, up, down, two_1) = split(rest, 4, 7, 1, 4)
    acts = [x_1, result_1]
    back_1, one_1, heads_1, half_up, half_down, grad_middle, up_0, down_0, two_0, *half_a = run_backward_middle(
        (grad_middle, wa, wo, vecs[1], x_1, *kept_1),
        up.reshape(4, 2, 136, D),
        down.reshape(2, 4, 136, D),
        (wu, wd, vecs[0], middle_0, *kept_two_0),
    )
    back_0, all_up, all_down, all_a, all_b, small, all_acts, all_grads = run_backward_end(
        (grad_middle, wa, wo, vecs[0], inputs, *kept_0),
        up_0.reshape(4, 2, 136, D),
        down_0.reshape(2, 4, 136, D),
        (half_up, half_down, *half_a),
        (two_0, one_1, two_1, heads_1, *acts, back_1),
    )
    attn, out, up, down, b_attn, b_out, b_up, b_down, gain, shift = run_assemble(all_up, all_down, all_a, all_b, small)
    return (
        all_acts[None, :, None],
        all_grads[None, :, None],
        attn[None],
        out[None],
        up[None],
        down[None],
        b_attn,
        b_out,
        b_up,
        b_down,
        gain[None],
        shift[None],
    )


def solution(mesh):
    placed = (
        P(None, "replica", "fsdp", None),
        P(None, "replica", "fsdp", None),
        P("section", "fsdp", None),
        P("section", "fsdp", None),
        P("section", "fsdp", None),
        P("section", "fsdp", None),
        P("section", "fsdp"),
        P("section", "fsdp"),
        P("section", "fsdp"),
        P("section", "fsdp"),
        P("section", None, "fsdp"),
        P("section", None, "fsdp"),
    )
    return jax.shard_map(
        on_device,
        mesh=mesh,
        in_specs=placed,
        out_specs=(
            P("section", None, "replica", "fsdp", None),
            P("section", None, "replica", "fsdp", None),
        )
        + placed[2:],
        check_vma=False,
    )
```
